32 devices in a mesh: replica: 8 (over y, x, core), fsdp: 4 (over z).
Axes of the slice: x: 2, y: 2, z: 4, core: 2. Of those that a mesh axis runs over, the one named last changes fastest.
Arguments:
- tokens: bfloat16 [8192, 2048], P(('replica', 'fsdp')), may hold values from -6 to 6
- segment_ids: int32 [8, 1024], P('replica'), may hold values from 0 to 4, as said below
- attention_gain: bfloat16 [2048], P('fsdp'), may hold values from 0.5 to 1.5
- query_weight: bfloat16 [2048, 2048], P('fsdp'), may hold values from -0.1875 to 0.1875
- key_weight: bfloat16 [2048, 256], P('fsdp'), may hold values from -0.1875 to 0.1875
- value_weight: bfloat16 [2048, 256], P('fsdp'), may hold values from -0.125 to 0.125
- output_weight: bfloat16 [2048, 2048], P('fsdp'), may hold values from -0.5 to 0.5
- feed_gain: bfloat16 [2048], P('fsdp'), may hold values from 0.5 to 1.5
- gate_weight: bfloat16 [2048, 5632], P('fsdp'), may hold values from -0.125 to 0.125
- up_weight: bfloat16 [2048, 5632], P('fsdp'), may hold values from -0.125 to 0.125
- down_weight: bfloat16 [5632, 2048], P('fsdp'), may hold values from -0.15625 to 0.15625
- cotangent: bfloat16 [8192, 2048], P(('replica', 'fsdp')), may hold values from -6 to 6
Outputs:
- activations: bfloat16 [8192, 2048], P(('replica', 'fsdp'))
- input_grad: bfloat16 [8192, 2048], P(('replica', 'fsdp'))
- attention_gain_grad: float32 [2048], P('fsdp')
- query_grad: float32 [2048, 2048], P('fsdp')
- key_grad: float32 [2048, 256], P('fsdp')
- value_grad: float32 [2048, 256], P('fsdp')
- output_grad: float32 [2048, 2048], P('fsdp')
- feed_gain_grad: float32 [2048], P('fsdp')
- gate_grad: float32 [2048, 5632], P('fsdp')
- up_grad: float32 [2048, 5632], P('fsdp')
- down_grad: float32 [5632, 2048], P('fsdp')
The draws below stay inside these ranges and needn't reach their ends.
Inputs may be any that keep to these rules, and one draw needn't show every extreme that they name: `segment_ids`: in each row the document numbers start at 0 and rise by 0 or 1 from one token to the next. Every document has 60 to 800 tokens, except the last of a row, which is cut at the row's end and may be shorter. The first document of every row has exactly 800 tokens.
All inputs are finite; a program needn't handle non-finite values.
Results may differ from the reference program's by a relative error of at most 0.023.
Values may be sent and summed in bfloat16 or wider, within the bound.
A program may use at most 448 MiB of HBM per device.

```python
import math
import jax
import jax.numpy as jnp
from jax import lax

D = 2048
HEADS = 32
KV_HEADS = 4
HEAD_DIM = 64
FF = 5632
DOC_MIN = 60
DOC_MAX = 800
QW = 2048
KW = 256
LEN = 1024
SEQS = 8
TOKENS = 8192


def draw_segment_ids(key, part):
    key = jax.random.fold_in(key, 11)
    pick_key = jax.random.fold_in(key, 5)
    doc_slots = LEN // DOC_MIN + 2
    doc_lengths = jax.random.randint(key, (SEQS, doc_slots), DOC_MIN, DOC_MAX + 1)
    chosen_row = jax.random.randint(pick_key, (), 0, SEQS)
    row_index = jnp.arange(SEQS, dtype=jnp.int32)[:, None]
    doc_lengths = jnp.where(row_index == chosen_row, DOC_MIN, doc_lengths)
    slot_index = jnp.arange(doc_slots, dtype=jnp.int32)[None, :]
    doc_lengths = jnp.where(slot_index == 0, DOC_MAX, doc_lengths).astype(jnp.int32)
    doc_starts = jnp.cumsum(doc_lengths, axis=1) - doc_lengths
    places = jnp.arange(LEN, dtype=jnp.int32)
    begun = (doc_starts[:, None, :] <= places[None, :, None]).astype(jnp.int32)
    return (jnp.sum(begun, axis=2) - 1).astype(jnp.int32)


def levels(key, shape, shards, low, largest):
    def one(axis_at, parts):
        heights = jax.random.uniform(jax.random.fold_in(jax.random.fold_in(key, 6), axis_at), (parts,), jnp.float32, low / len(shards), largest / len(shards))
        return jnp.repeat(jnp.exp(heights), shape[axis_at] // parts).reshape((-1,) + (1,) * (len(shape) - axis_at - 1))

    gain = one(*shards[0])
    for cut in shards[1:]:
        gain = gain * one(*cut)
    return gain


def bell_draw(stream_key, extent, width, limit, cuts=(), kind=jnp.bfloat16):
    result = width * jax.random.normal(stream_key, extent, jnp.float32)
    if cuts:
        result = result * levels(stream_key, extent, cuts, -0.22, 0.18)
    return jnp.clip(result, -limit, limit).astype(kind)


def setup_inputs(seed: int = 0) -> dict:
    arg_keys = jax.random.split(jax.random.key(seed), 13)
    tokens = bell_draw(arg_keys[0], (TOKENS, D), 1.0, 6.0, ((0, 32),))
    segment_ids = draw_segment_ids(jax.random.fold_in(arg_keys[12], 71), 0)
    attention_gain = jnp.clip(1.0 + 0.1 * jax.random.normal(arg_keys[2], (D,), jnp.float32), 0.5, 1.5).astype(jnp.bfloat16)
    query_weight = bell_draw(arg_keys[3], (D, QW), (D // 2) ** -0.5, 0.1875, ((0, 4),))
    key_weight = bell_draw(arg_keys[4], (D, KW), (D // 2) ** -0.5, 0.1875, ((0, 4),))
    value_weight = bell_draw(arg_keys[5], (D, KW), D ** -0.5, 0.125, ((0, 4),))
    output_weight = bell_draw(arg_keys[6], (QW, D), (QW // 16) ** -0.5, 0.5, ((0, 4),))
    feed_gain = jnp.clip(1.0 + 0.1 * jax.random.normal(arg_keys[7], (D,), jnp.float32), 0.5, 1.5).astype(jnp.bfloat16)
    gate_weight = bell_draw(arg_keys[8], (D, FF), D ** -0.5, 0.125, ((0, 4),))
    up_weight = bell_draw(arg_keys[9], (D, FF), D ** -0.5, 0.125, ((0, 4),))
    down_weight = bell_draw(arg_keys[10], (FF, D), (FF // 4) ** -0.5, 0.15625, ((0, 4),))
    cotangent = bell_draw(arg_keys[11], (TOKENS, D), 1.0, 6.0, ((0, 32),))
    return dict(tokens=tokens, segment_ids=segment_ids, attention_gain=attention_gain, query_weight=query_weight, key_weight=key_weight, value_weight=value_weight, output_weight=output_weight, feed_gain=feed_gain, gate_weight=gate_weight, up_weight=up_weight, down_weight=down_weight, cotangent=cotangent)


@jax.custom_vjp
def low(v):
    return lax.optimization_barrier(v.astype(jnp.bfloat16)).astype(jnp.float32)

@jax.custom_vjp
def low_back(v):
    return v

def low_keep(v):
    return (low(v), None)

def low_pass(kept, grad):
    return (grad,)

def back_keep(v):
    return (v, None)

def back_low(kept, grad):
    return (low(grad),)
low.defvjp(low_keep, low_pass)
low_back.defvjp(back_keep, back_low)
EPSILON = 1e-05
NEGATIVE = -1e+30
HIGHEST = lax.Precision.HIGHEST

def matmul(left_side, right_side):
    return jnp.dot(left_side, right_side, precision=HIGHEST, preferred_element_type=jnp.float32)

def doc_positions(row_ids):
    places = jnp.arange(row_ids.shape[0], dtype=jnp.int32)
    fresh_start = jnp.concatenate([jnp.ones((1,), dtype=jnp.bool_), row_ids[1:] != row_ids[:-1]])
    first_place = lax.cummax(jnp.where(fresh_start, places, 0), axis=0)
    return places - first_place

def rope_tables(positions):
    half_dim = HEAD_DIM // 2
    freq_rates = jnp.exp(jnp.arange(half_dim, dtype=jnp.float32) * (-math.log(10000.0) / half_dim))
    angles = positions.astype(jnp.float32)[:, None] * freq_rates[None, :]
    return (jnp.cos(angles), jnp.sin(angles))

def rotate(tensor, cosine_table, sine_table):
    half_dim = tensor.shape[-1] // 2
    lower_half = tensor[..., :half_dim]
    upper_half = tensor[..., half_dim:]
    cos_part = cosine_table[:, None, :]
    sin_part = sine_table[:, None, :]
    return jnp.concatenate([lower_half * cos_part - upper_half * sin_part, upper_half * cos_part + lower_half * sin_part], axis=-1)

def inverse_rms(values):
    return lax.rsqrt(lax.optimization_barrier(jnp.mean(values * values, axis=1, keepdims=True)) + EPSILON)

def attention(queries, key_rows, value_rows, row_ids):
    length = queries.shape[0]
    block_rows = math.gcd(length, 512)
    places = jnp.arange(length, dtype=jnp.int32)

    def one_block(first_row):
        query_block = lax.dynamic_slice_in_dim(queries, first_row, block_rows, 0)
        block_ids = lax.dynamic_slice_in_dim(row_ids, first_row, block_rows, 0)
        block_places = first_row + jnp.arange(block_rows, dtype=jnp.int32)
        allowed = (block_ids[:, None] == row_ids[None, :]) & (places[None, :] <= block_places[:, None])
        scores = low_back(jnp.einsum('qgrd,kgd->grqk', query_block, key_rows, precision=HIGHEST) * HEAD_DIM ** (-0.5))
        masked = jnp.where(allowed, scores, NEGATIVE)
        row_top = lax.optimization_barrier(jnp.max(masked, axis=-1, keepdims=True))
        weights = jnp.where(allowed, jnp.exp(masked - row_top), 0.0)
        softmax_rows = low(weights / lax.optimization_barrier(jnp.sum(weights, axis=-1, keepdims=True)))
        return jnp.einsum('grqk,kgd->qgrd', softmax_rows, value_rows, precision=HIGHEST)
    block_starts = jnp.arange(length // block_rows, dtype=jnp.int32) * block_rows
    blocks = lax.map(jax.checkpoint(one_block), block_starts)
    return blocks.reshape(length, HEADS * HEAD_DIM)

def layer(sequence, row_ids, params):
    attention_gain, query_weight, key_weight, value_weight, output_weight, feed_gain, gate_weight, up_weight, down_weight = params
    length = sequence.shape[0]
    group_ratio = HEADS // KV_HEADS
    cosine_table, sine_table = rope_tables(doc_positions(row_ids))
    normed_in = sequence * inverse_rms(sequence)
    hidden_in = low(normed_in * attention_gain)
    queries = low_back(matmul(hidden_in, query_weight))
    key_lin = low_back(matmul(hidden_in, key_weight))
    value_rows = low(low_back(matmul(hidden_in, value_weight)))
    query_rot = low(rotate(queries.reshape(length, HEADS, HEAD_DIM), cosine_table, sine_table))
    query_rot = query_rot.reshape(length, KV_HEADS, group_ratio, HEAD_DIM)
    key_rot = low(rotate(key_lin.reshape(length, KV_HEADS, HEAD_DIM), cosine_table, sine_table))
    value_rows = value_rows.reshape(length, KV_HEADS, HEAD_DIM)
    mixed_heads = low_back(low(attention(query_rot, key_rot, value_rows, row_ids)))
    middle = sequence + low_back(matmul(mixed_heads, output_weight))
    normed_mid = middle * inverse_rms(middle)
    hidden_mid = low(normed_mid * feed_gain)
    gate_acc = low_back(matmul(hidden_mid, gate_weight))
    up_acc = low_back(matmul(hidden_mid, up_weight))
    inner_act = low(jax.nn.silu(gate_acc) * up_acc)
    return middle + matmul(inner_act, down_weight)

def reference(tokens, segment_ids, attention_gain, query_weight, key_weight, value_weight, output_weight, feed_gain, gate_weight, up_weight, down_weight, cotangent):
    params = tuple((weight_item.astype(jnp.float32) for weight_item in (attention_gain, query_weight, key_weight, value_weight, output_weight, feed_gain, gate_weight, up_weight, down_weight)))
    inputs = tokens.astype(jnp.float32).reshape(SEQS, LEN, D)

    def whole_layer(inputs, params):

        def advance(carried, pair):
            return (carried, layer(pair[0], pair[1], params))
        _, outputs = lax.scan(advance, jnp.zeros((), jnp.float32), (inputs, segment_ids))
        return outputs
    outputs, pullback = jax.vjp(whole_layer, inputs, params)
    input_grads, weight_grads = pullback(cotangent.astype(jnp.float32).reshape(SEQS, LEN, D))
    return (outputs.reshape(TOKENS, D).astype(jnp.bfloat16), input_grads.reshape(TOKENS, D).astype(jnp.bfloat16), weight_grads[0], weight_grads[1], weight_grads[2], weight_grads[3], weight_grads[4], weight_grads[5], weight_grads[6], weight_grads[7], weight_grads[8])
```

```python
import math

import jax
import jax.numpy as jnp
from jax import lax
from jax.sharding import PartitionSpec as P

HEADS = 32
KV_HEADS = 4
HEAD_DIM = 64
EPSILON = 1e-05
NEGATIVE = -1e30
R = "replica"
F = "fsdp"


def inverse_rms(values):
    return lax.rsqrt(jnp.mean(values * values, axis=1, keepdims=True) + EPSILON)


def rope_tables(positions):
    half_dim = HEAD_DIM // 2
    freq_rates = jnp.exp(jnp.arange(half_dim, dtype=jnp.float32) * (-math.log(10000.0) / half_dim))
    angles = positions.astype(jnp.float32)[:, None] * freq_rates[None, :]
    return (jnp.cos(angles), jnp.sin(angles))


def rotate(tensor, cosine_table, sine_table, sign):
    half_dim = HEAD_DIM // 2
    low, up = tensor[..., :half_dim], tensor[..., half_dim:]
    cos_part = cosine_table[:, None, :]
    sin_part = sine_table[:, None, :] * sign
    return jnp.concatenate(
        [low * cos_part - up * sin_part, up * cos_part + low * sin_part], axis=-1
    )


def dot(a, b, ca=1, cb=0):
    return lax.dot_general(a, b, (((ca,), (cb,)), ((), ())), preferred_element_type=jnp.float32)


def plane_gather(x):
    return lax.all_gather(x, R, axis=0, tiled=True)


def plane_scatter(x):
    return lax.psum_scatter(x, R, scatter_dimension=0, tiled=True)


def line_gather(x):
    return lax.all_gather(x, F, axis=0, tiled=True)


def line_scatter(x):
    return lax.psum_scatter(x, F, scatter_dimension=0, tiled=True)


def per_device(
    tokens,
    segment_ids,
    attention_gain,
    query_weight,
    key_weight,
    value_weight,
    output_weight,
    feed_gain,
    gate_weight,
    up_weight,
    down_weight,
    cotangent,
):
    f32, bf16 = jnp.float32, jnp.bfloat16
    planes, width = lax.axis_size(F), lax.axis_size(R)
    r, z = lax.axis_index(R), lax.axis_index(F)
    tok, model = tokens.shape
    length = segment_ids.shape[1]
    all_tok = width * tok
    heads = HEADS // width
    group = HEADS // KV_HEADS
    qw = heads * HEAD_DIM
    kv = (r * heads) // group
    feed = gate_weight.shape[1]
    piece = feed // (width * planes)
    hidden_units = piece * planes
    scale = HEAD_DIM ** (-0.5)

    def cols(weight, first, count):
        return lax.dynamic_slice_in_dim(weight, first, count, 1)

    def feed_cols(weight):
        return [cols(weight, p * (feed // planes) + r * piece, piece) for p in range(planes)]

    w_qkv = line_gather(
        jnp.concatenate(
            [
                cols(query_weight, r * qw, qw),
                cols(key_weight, kv * HEAD_DIM, HEAD_DIM),
                cols(value_weight, kv * HEAD_DIM, HEAD_DIM),
            ],
            axis=1,
        )
    )
    w_out = lax.all_to_all(
        line_gather(cols(output_weight, r * (model // width), model // width)),
        R,
        split_axis=0,
        concat_axis=1,
        tiled=True,
    )
    w_feed = line_gather(jnp.concatenate(feed_cols(gate_weight) + feed_cols(up_weight), axis=1))
    w_gate, w_up = w_feed[:, :hidden_units], w_feed[:, hidden_units:]
    w_down = line_gather(lax.dynamic_slice_in_dim(down_weight, r * piece, piece, 0))
    gains = lax.all_gather(jnp.stack([attention_gain, feed_gain]), F, axis=1, tiled=True)
    gain_in, gain_mid = gains[0].astype(f32), gains[1].astype(f32)

    ids = lax.all_gather(segment_ids, R, axis=0, tiled=True)
    places = jnp.arange(length, dtype=jnp.int32)
    fresh = jnp.concatenate(
        [jnp.ones((width, 1), dtype=jnp.bool_), ids[:, 1:] != ids[:, :-1]], axis=1
    )
    positions = places[None] - lax.cummax(jnp.where(fresh, places[None], 0), axis=1)
    own_ids = lax.dynamic_slice_in_dim(ids, z * tok, tok, 1)
    own_positions = lax.dynamic_slice_in_dim(positions, z * tok, tok, 1).reshape(all_tok)
    own_places = z * tok + jnp.arange(tok, dtype=jnp.int32)
    allowed = (own_ids[:, :, None] == ids[:, None, :]) & (
        places[None, None, :] <= own_places[None, :, None]
    )
    cosine, sine = rope_tables(own_positions)

    tok_float = tokens.astype(f32)
    scale_in = inverse_rms(tok_float)
    normed_in = tok_float * scale_in
    hidden_in = plane_gather((normed_in * gain_in).astype(bf16))
    qkv = dot(hidden_in, w_qkv)
    query = rotate(qkv[:, :qw].reshape(all_tok, heads, HEAD_DIM), cosine, sine, 1.0).astype(bf16)
    key = rotate(qkv[:, None, qw : qw + HEAD_DIM], cosine, sine, 1.0).astype(bf16)[:, 0]
    value = qkv[:, qw + HEAD_DIM :].astype(bf16)
    kv_rows = (
        lax.all_gather(jnp.concatenate([key, value], axis=1), F, axis=0, tiled=False)
        .reshape(planes, width, tok, 2 * HEAD_DIM)
        .transpose(1, 0, 2, 3)
        .reshape(width, length, 2 * HEAD_DIM)
    )
    key_rows, value_rows = kv_rows[..., :HEAD_DIM], kv_rows[..., HEAD_DIM:]
    query_rows = query.reshape(width, tok, heads, HEAD_DIM)

    def one_forward(items):
        q, k, v, mask = items
        raw = jnp.einsum("qhd,kd->hqk", q, k, preferred_element_type=f32) * scale
        masked = jnp.where(mask, raw, NEGATIVE)
        top = jnp.max(masked, axis=-1, keepdims=True)
        total = jnp.sum(jnp.where(mask, jnp.exp(masked - top), 0.0), axis=-1, keepdims=True)
        log_total = top + jnp.log(total)
        probs = jnp.where(mask, jnp.exp(masked - log_total), 0.0).astype(bf16)
        return jnp.einsum("hqk,kd->qhd", probs, v, preferred_element_type=f32), log_total

    mixed, log_totals = lax.map(one_forward, (query_rows, key_rows, value_rows, allowed))
    mixed = mixed.reshape(all_tok, qw).astype(bf16)
    branch = plane_scatter(dot(mixed, w_out).astype(bf16)).astype(f32)
    middle = tok_float + branch
    scale_mid = inverse_rms(middle)
    normed_mid = middle * scale_mid

    hidden_mid = plane_gather((normed_mid * gain_mid).astype(bf16))
    cot_all = plane_gather(cotangent)
    gate_acc = dot(hidden_mid, w_gate)
    up_acc = dot(hidden_mid, w_up)
    gate_sig = jax.nn.sigmoid(gate_acc)
    gate_silu = gate_acc * gate_sig
    inner_act = (gate_silu * up_acc).astype(bf16)
    feed_out = plane_scatter(dot(inner_act, w_down).astype(bf16)).astype(f32)
    activations = (middle + feed_out).astype(bf16)
    grad_inner = dot(cot_all, w_down, 1, 1)
    grad_gate = (grad_inner * up_acc * gate_sig * (1.0 + gate_acc * (1.0 - gate_sig))).astype(bf16)
    grad_up = (grad_inner * gate_silu).astype(bf16)
    grad_hidden_mid = plane_scatter(
        (dot(grad_gate, w_gate, 1, 1) + dot(grad_up, w_up, 1, 1)).astype(bf16)
    ).astype(f32)
    feed_rows = line_scatter(
        jnp.concatenate([dot(hidden_mid, grad_gate, 0, 0), dot(hidden_mid, grad_up, 0, 0)], axis=1)
        .astype(bf16)
    )
    down_rows = line_scatter(dot(inner_act, cot_all, 0, 0).astype(bf16))
    gain_mid_term = jnp.sum(grad_hidden_mid * normed_mid, axis=0)
    grad_normed_mid = grad_hidden_mid * gain_mid
    grad_middle = cotangent.astype(f32) + scale_mid * (
        grad_normed_mid - normed_mid * jnp.mean(grad_normed_mid * normed_mid, axis=1, keepdims=True)
    )

    grad_branch = plane_gather(grad_middle.astype(bf16))
    grad_mixed = dot(grad_branch, w_out, 1, 1).astype(bf16)
    out_part = dot(mixed, grad_branch, 0, 0).astype(bf16)
    out_rows = line_scatter(
        lax.all_to_all(out_part, R, split_axis=1, concat_axis=0, tiled=True)
    )

    def one_backward(items):
        q, k, v, g, mask, log_total = items
        raw = jnp.einsum("qhd,kd->hqk", q, k, preferred_element_type=f32) * scale
        probs = jnp.where(mask, jnp.exp(jnp.where(mask, raw, NEGATIVE) - log_total), 0.0)
        probs_low = probs.astype(bf16)
        grad_probs = jnp.einsum("qhd,kd->hqk", g, v, preferred_element_type=f32)
        delta = jnp.sum(grad_probs * probs, axis=-1, keepdims=True)
        grad_scores = (probs * (grad_probs - delta)).astype(bf16)
        gq = jnp.einsum("hqk,kd->qhd", grad_scores, k, preferred_element_type=f32) * scale
        gk = jnp.einsum("hqk,qhd->kd", grad_scores, q, preferred_element_type=f32) * scale
        gv = jnp.einsum("hqk,qhd->kd", probs_low, g, preferred_element_type=f32)
        return gq, jnp.concatenate([gk, gv], axis=-1).astype(bf16)

    gq, gkv = lax.map(
        one_backward,
        (
            query_rows,
            key_rows,
            value_rows,
            grad_mixed.reshape(width, tok, heads, HEAD_DIM),
            allowed,
            log_totals,
        ),
    )
    gkv = gkv.reshape(width, planes, tok, 2 * HEAD_DIM).transpose(1, 0, 2, 3)
    gkv = line_scatter(gkv.reshape(planes * all_tok, 2 * HEAD_DIM)).astype(f32)
    grad_qkv = jnp.concatenate(
        [
            rotate(gq.reshape(all_tok, heads, HEAD_DIM), cosine, sine, -1.0).reshape(all_tok, qw),
            rotate(gkv[:, None, :HEAD_DIM], cosine, sine, -1.0)[:, 0],
            gkv[:, HEAD_DIM:],
        ],
        axis=1,
    ).astype(bf16)
    grad_hidden_in = plane_scatter(dot(grad_qkv, w_qkv, 1, 1).astype(bf16)).astype(f32)
    qkv_rows = line_scatter(dot(hidden_in, grad_qkv, 0, 0).astype(bf16))
    gain_in_term = jnp.sum(grad_hidden_in * normed_in, axis=0)
    grad_normed_in = grad_hidden_in * gain_in
    input_grad = (
        grad_middle
        + scale_in
        * (
            grad_normed_in
            - normed_in * jnp.mean(grad_normed_in * normed_in, axis=1, keepdims=True)
        )
    ).astype(bf16)

    gain_terms = lax.psum(
        lax.psum_scatter(
            jnp.stack([gain_in_term, gain_mid_term]), F, scatter_dimension=1, tiled=True
        ),
        R,
    )
    rows = model // planes

    def spread(x):
        x = plane_gather(x)
        return x.reshape(width, x.shape[0] // width, x.shape[1])

    down_grad = spread(down_rows).reshape(feed // planes, model).astype(f32)
    feed_all = spread(feed_rows).reshape(width, rows, 2, planes, piece)
    feed_all = feed_all.transpose(2, 1, 3, 0, 4).reshape(2, rows, feed).astype(f32)
    out_grad = spread(out_rows).transpose(1, 0, 2).reshape(output_weight.shape).astype(f32)
    qkv_all = spread(qkv_rows)
    query_grad = qkv_all[..., :qw].transpose(1, 0, 2).reshape(query_weight.shape).astype(f32)
    kv_all = qkv_all[..., qw:].astype(f32).reshape(KV_HEADS, width // KV_HEADS, rows, 2, HEAD_DIM)
    kv_all = kv_all.sum(axis=1).transpose(2, 1, 0, 3).reshape(2, rows, KV_HEADS * HEAD_DIM)
    return (
        activations,
        input_grad,
        gain_terms[0],
        query_grad,
        kv_all[0],
        kv_all[1],
        out_grad,
        gain_terms[1],
        feed_all[0],
        feed_all[1],
        down_grad,
    )


def solution(mesh):
    tok = P((R, F), None)
    row = P(F, None)
    in_specs = (tok, P(R, None), P(F), row, row, row, row, P(F), row, row, row, tok)
    out_specs = (tok, tok, P(F), row, row, row, row, P(F), row, row, row)
    return jax.shard_map(
        per_device, mesh=mesh, in_specs=in_specs, out_specs=out_specs, check_vma=False
    )
```

```python
import functools
import math

import jax
import jax.numpy as jnp
from jax import lax
from jax.experimental import pallas as pl
from jax.experimental.pallas import tpu as pltpu
from jax.sharding import PartitionSpec as P

HEADS = 32
KV_HEADS = 4
HEAD_DIM = 64
EPSILON = 1e-05
NEGATIVE = -1e30
R = "replica"
F = "fsdp"
MESH = pl.DeviceIdType.MESH
DMA = pltpu.SemaphoreType.DMA
ANY = pl.BlockSpec(memory_space=pl.ANY)


def inverse_rms(values):
    return lax.rsqrt(jnp.mean(values * values, axis=1, keepdims=True) + EPSILON)


def rope_tables(positions):
    half_dim = HEAD_DIM // 2
    freq_rates = jnp.exp(jnp.arange(half_dim, dtype=jnp.float32) * (-math.log(10000.0) / half_dim))
    angles = positions.astype(jnp.float32)[:, None] * freq_rates[None, :]
    return (jnp.cos(angles), jnp.sin(angles))


def rotate(tensor, cosine_table, sine_table, sign):
    half_dim = HEAD_DIM // 2
    low, up = tensor[..., :half_dim], tensor[..., half_dim:]
    cos_part = cosine_table[:, None, :]
    sin_part = sine_table[:, None, :] * sign
    return jnp.concatenate(
        [low * cos_part - up * sin_part, up * cos_part + low * sin_part], axis=-1
    )


def dot(a, b, ca=1, cb=0):
    return lax.dot_general(a, b, (((ca,), (cb,)), ((), ())), preferred_element_type=jnp.float32)


def remote(src, dst, sems, index, device):
    return pltpu.make_async_remote_copy(
        src_ref=src,
        dst_ref=dst,
        send_sem=sems[0].at[index],
        recv_sem=sems[1].at[index],
        device_id={R: device},
        device_id_type=MESH,
    )


def greet(*devices):
    barrier = pltpu.get_barrier_semaphore()
    for device in devices:
        pl.semaphore_signal(barrier, inc=1, device_id={R: device}, device_id_type=MESH)
    pl.semaphore_wait(barrier, len(devices))


def gather_kernel(chunks, x, out, local_sem, to_x, at_x, to_y, at_y, to_far, at_far, to_sib, at_sib):
    me = lax.axis_index(R)
    sibling, beside_x, beside_y, across = me + 1 - 2 * lax.rem(me, 2), me ^ 2, me ^ 4, me ^ 6
    size = x.shape[0] // chunks
    half = chunks // 2
    greet(sibling, beside_x, beside_y)
    own = pltpu.make_async_copy(x, out.at[me], local_sem)
    own.start()

    def copy(owner, chunk, device, sems, index):
        part = pl.ds(chunk * size, size)
        src = x.at[part] if owner is me else out.at[owner, part]
        return remote(src, out.at[owner, part], sems, index, device)

    x_sems, y_sems, far_sems, sib_sems = (to_x, at_x), (to_y, at_y), (to_far, at_far), (to_sib, at_sib)
    x_copies, y_copies, far_copies, sib_copies = [], [], [], []
    for i in range(chunks):
        j = (i + half) % chunks
        x_copies.append(copy(me, i, beside_x, x_sems, i))
        y_copies.append(copy(me, j, beside_y, y_sems, j))
        x_copies[-1].start()
        y_copies[-1].start()
    for i in range(chunks):
        sib_copies.append(copy(me, i, sibling, sib_sems, (0, i)))
        sib_copies[-1].start()
    for i in range(chunks):
        j = (i + half) % chunks
        x_copies[i].wait_recv()
        if i < half:
            far_copies.append((i, copy(beside_x, i, beside_y, far_sems, i)))
            far_copies[-1][1].start()
        sib_copies.append(copy(beside_x, i, sibling, sib_sems, (1, i)))
        sib_copies[-1].start()
        y_copies[i].wait_recv()
        if j >= half:
            far_copies.append((j, copy(beside_y, j, beside_x, far_sems, j)))
            far_copies[-1][1].start()
        sib_copies.append(copy(beside_y, j, sibling, sib_sems, (2, j)))
        sib_copies[-1].start()
    for i, far in far_copies:
        far.wait_recv()
        sib_copies.append(copy(across, i, sibling, sib_sems, (3, i)))
        sib_copies[-1].start()
    for sent in sib_copies:
        sent.wait()
    for sent in x_copies + y_copies + [far for _, far in far_copies]:
        sent.wait_send()
    own.wait()


def scatter_kernel(
    chunks, part, out, own, from_sib, give, got, give_far, got_far, total,
    own_sem, out_sem, to_sib, at_sib, to_near, at_near, to_far, at_far,
):
    f32, bf16 = jnp.float32, jnp.bfloat16
    me = lax.axis_index(R)
    flip = 1 - 2 * lax.rem(me, 2)
    sibling, beside_x, beside_y = me + flip, me ^ 2, me ^ 4
    rows = out.shape[0]
    size = rows // chunks
    half = chunks // 2
    owners = [me, beside_x, beside_y, me ^ 6]
    order = [c for j in range(half) for c in (j, half + j)]

    def rows_of(device, j):
        return part.at[pl.ds(pl.multiple_of(device * rows + j * size, 16), size)]

    def own_copy(d, j):
        return pltpu.make_async_copy(rows_of(owners[d], j), own.at[d, j], own_sem.at[d, j])

    def sib_copy(d, j):
        return remote(rows_of(owners[d] + flip, j), from_sib.at[d, j], (to_sib, at_sib), (d, j), sibling)

    def near_copy(j):
        device = beside_x if j < half else beside_y
        return remote(give.at[j], got.at[j], (to_near, at_near), j, device)

    def far_copy(j):
        device = beside_y if j < half else beside_x
        return remote(give_far.at[j], got_far.at[j], (to_far, at_far), j, device)

    def out_copy(j):
        return pltpu.make_async_copy(total.at[j], out.at[pl.ds(j * size, size)], out_sem.at[j])

    def summed(d, j):
        own_copy(d, j).wait()
        sib_copy(d, j).wait_recv()
        return own[d, j].astype(f32) + from_sib[d, j].astype(f32)

    for j in order:
        for d in (1, 2, 3, 0):
            own_copy(d, j).start()
    greet(sibling, beside_x, beside_y)
    for j in order:
        for d in (1, 3, 2, 0) if j < half else (2, 3, 1, 0):
            sib_copy(d, j).start()
    for j in order:
        give[j, 0] = summed(1 if j < half else 2, j).astype(bf16)
        give[j, 1] = summed(3, j).astype(bf16)
        near_copy(j).start()
    for j in order:
        passed = summed(2 if j < half else 1, j)
        kept = summed(0, j)
        near_copy(j).wait_recv()
        give_far[j] = (passed + got[j, 1].astype(f32)).astype(bf16)
        far_copy(j).start()
        total[j] = kept + got[j, 0].astype(f32)
    for j in order:
        far_copy(j).wait_recv()
        total[j] = total[j] + got_far[j].astype(f32)
        out_copy(j).start()
    for j in order:
        out_copy(j).wait()
        near_copy(j).wait_send()
        far_copy(j).wait_send()
        for d in range(4):
            sib_copy(d, j).wait_send()


def plane_gather(x, call, chunks=4):
    width = lax.axis_size(R)
    if width != 8:
        return lax.all_gather(x, R, axis=0, tiled=True)
    out = pl.pallas_call(
        functools.partial(gather_kernel, chunks),
        out_shape=jax.ShapeDtypeStruct((width,) + x.shape, x.dtype),
        in_specs=[ANY],
        out_specs=ANY,
        scratch_shapes=[DMA] + [DMA((chunks,))] * 6 + [DMA((4, chunks))] * 2,
        compiler_params=pltpu.CompilerParams(collective_id=call, has_side_effects=True),
    )(x)
    return out.reshape((width * x.shape[0],) + x.shape[1:])


def plane_scatter(x, call, chunks=4):
    width = lax.axis_size(R)
    if width != 8:
        return lax.psum_scatter(x, R, scatter_dimension=0, tiled=True).astype(jnp.float32)
    rows, columns = x.shape[0] // width, x.shape[1]
    size = rows // chunks
    bf16 = jnp.bfloat16
    return pl.pallas_call(
        functools.partial(scatter_kernel, chunks),
        out_shape=jax.ShapeDtypeStruct((rows, columns), jnp.float32),
        in_specs=[ANY],
        out_specs=ANY,
        scratch_shapes=[
            pltpu.VMEM((4, chunks, size, columns), bf16),
            pltpu.VMEM((4, chunks, size, columns), bf16),
            pltpu.VMEM((chunks, 2, size, columns), bf16),
            pltpu.VMEM((chunks, 2, size, columns), bf16),
            pltpu.VMEM((chunks, size, columns), bf16),
            pltpu.VMEM((chunks, size, columns), bf16),
            pltpu.VMEM((chunks, size, columns), jnp.float32),
            DMA((4, chunks)),
            DMA((chunks,)),
            DMA((4, chunks)),
            DMA((4, chunks)),
        ]
        + [DMA((chunks,))] * 4,
        compiler_params=pltpu.CompilerParams(
            collective_id=call, has_side_effects=True, vmem_limit_bytes=32 << 20
        ),
    )(x)


def line_gather(x):
    return lax.all_gather(x, F, axis=0, tiled=True)


def line_scatter(x):
    return lax.psum_scatter(x, F, scatter_dimension=0, tiled=True)


def per_device(
    tokens,
    segment_ids,
    attention_gain,
    query_weight,
    key_weight,
    value_weight,
    output_weight,
    feed_gain,
    gate_weight,
    up_weight,
    down_weight,
    cotangent,
):
    f32, bf16 = jnp.float32, jnp.bfloat16
    planes, width = lax.axis_size(F), lax.axis_size(R)
    r, z = lax.axis_index(R), lax.axis_index(F)
    tok, model = tokens.shape
    length = segment_ids.shape[1]
    all_tok = width * tok
    heads = HEADS // width
    group = HEADS // KV_HEADS
    qw = heads * HEAD_DIM
    kv = (r * heads) // group
    feed = gate_weight.shape[1]
    piece = feed // (width * planes)
    hidden_units = piece * planes
    scale = HEAD_DIM ** (-0.5)

    def cols(weight, first, count):
        return lax.dynamic_slice_in_dim(weight, first, count, 1)

    def feed_cols(weight):
        return [cols(weight, p * (feed // planes) + r * piece, piece) for p in range(planes)]

    w_qkv = line_gather(
        jnp.concatenate(
            [
                cols(query_weight, r * qw, qw),
                cols(key_weight, kv * HEAD_DIM, HEAD_DIM),
                cols(value_weight, kv * HEAD_DIM, HEAD_DIM),
            ],
            axis=1,
        )
    )
    w_out = lax.all_to_all(
        line_gather(cols(output_weight, r * (model // width), model // width)),
        R,
        split_axis=0,
        concat_axis=1,
        tiled=True,
    )
    w_feed = line_gather(jnp.concatenate(feed_cols(gate_weight) + feed_cols(up_weight), axis=1))
    w_gate, w_up = w_feed[:, :hidden_units], w_feed[:, hidden_units:]
    w_down = line_gather(lax.dynamic_slice_in_dim(down_weight, r * piece, piece, 0))
    gains = lax.all_gather(jnp.stack([attention_gain, feed_gain]), F, axis=1, tiled=True)
    gain_in, gain_mid = gains[0].astype(f32), gains[1].astype(f32)

    ids = lax.all_gather(segment_ids, R, axis=0, tiled=True)
    places = jnp.arange(length, dtype=jnp.int32)
    fresh = jnp.concatenate(
        [jnp.ones((width, 1), dtype=jnp.bool_), ids[:, 1:] != ids[:, :-1]], axis=1
    )
    positions = places[None] - lax.cummax(jnp.where(fresh, places[None], 0), axis=1)
    own_ids = lax.dynamic_slice_in_dim(ids, z * tok, tok, 1)
    own_positions = lax.dynamic_slice_in_dim(positions, z * tok, tok, 1).reshape(all_tok)
    own_places = z * tok + jnp.arange(tok, dtype=jnp.int32)
    allowed = (own_ids[:, :, None] == ids[:, None, :]) & (
        places[None, None, :] <= own_places[None, :, None]
    )
    cosine, sine = rope_tables(own_positions)

    tok_float = tokens.astype(f32)
    scale_in = inverse_rms(tok_float)
    normed_in = tok_float * scale_in
    hidden_in = plane_gather((normed_in * gain_in).astype(bf16), 0)
    qkv = dot(hidden_in, w_qkv)
    query = rotate(qkv[:, :qw].reshape(all_tok, heads, HEAD_DIM), cosine, sine, 1.0).astype(bf16)
    key = rotate(qkv[:, None, qw : qw + HEAD_DIM], cosine, sine, 1.0).astype(bf16)[:, 0]
    value = qkv[:, qw + HEAD_DIM :].astype(bf16)
    kv_rows = (
        lax.all_gather(jnp.concatenate([key, value], axis=1), F, axis=0, tiled=False)
        .reshape(planes, width, tok, 2 * HEAD_DIM)
        .transpose(1, 0, 2, 3)
        .reshape(width, length, 2 * HEAD_DIM)
    )
    key_rows, value_rows = kv_rows[..., :HEAD_DIM], kv_rows[..., HEAD_DIM:]
    query_rows = query.reshape(width, tok, heads, HEAD_DIM)

    def one_forward(items):
        q, k, v, mask = items
        raw = jnp.einsum("qhd,kd->hqk", q, k, preferred_element_type=f32) * scale
        masked = jnp.where(mask, raw, NEGATIVE)
        top = jnp.max(masked, axis=-1, keepdims=True)
        total = jnp.sum(jnp.where(mask, jnp.exp(masked - top), 0.0), axis=-1, keepdims=True)
        log_total = top + jnp.log(total)
        probs = jnp.where(mask, jnp.exp(masked - log_total), 0.0).astype(bf16)
        return jnp.einsum("hqk,kd->qhd", probs, v, preferred_element_type=f32), log_total

    mixed, log_totals = lax.map(one_forward, (query_rows, key_rows, value_rows, allowed))
    mixed = mixed.reshape(all_tok, qw).astype(bf16)
    branch = plane_scatter(dot(mixed, w_out).astype(bf16), 1)
    middle = tok_float + branch
    scale_mid = inverse_rms(middle)
    normed_mid = middle * scale_mid

    hidden_mid = plane_gather((normed_mid * gain_mid).astype(bf16), 2)
    cot_all = plane_gather(cotangent, 3)
    gate_acc = dot(hidden_mid, w_gate)
    up_acc = dot(hidden_mid, w_up)
    gate_sig = jax.nn.sigmoid(gate_acc)
    gate_silu = gate_acc * gate_sig
    inner_act = (gate_silu * up_acc).astype(bf16)
    feed_out = plane_scatter(dot(inner_act, w_down).astype(bf16), 4)
    activations = (middle + feed_out).astype(bf16)
    grad_inner = dot(cot_all, w_down, 1, 1)
    grad_gate = (grad_inner * up_acc * gate_sig * (1.0 + gate_acc * (1.0 - gate_sig))).astype(bf16)
    grad_up = (grad_inner * gate_silu).astype(bf16)
    grad_hidden_mid = plane_scatter(
        (dot(grad_gate, w_gate, 1, 1) + dot(grad_up, w_up, 1, 1)).astype(bf16), 5
    )
    feed_rows = line_scatter(
        jnp.concatenate([dot(hidden_mid, grad_gate, 0, 0), dot(hidden_mid, grad_up, 0, 0)], axis=1)
        .astype(bf16)
    )
    down_rows = line_scatter(dot(inner_act, cot_all, 0, 0).astype(bf16))
    gain_mid_term = jnp.sum(grad_hidden_mid * normed_mid, axis=0)
    grad_normed_mid = grad_hidden_mid * gain_mid
    grad_middle = cotangent.astype(f32) + scale_mid * (
        grad_normed_mid - normed_mid * jnp.mean(grad_normed_mid * normed_mid, axis=1, keepdims=True)
    )

    grad_branch = plane_gather(grad_middle.astype(bf16), 6)
    grad_mixed = dot(grad_branch, w_out, 1, 1).astype(bf16)
    out_part = dot(mixed, grad_branch, 0, 0).astype(bf16)
    out_rows = line_scatter(
        lax.all_to_all(out_part, R, split_axis=1, concat_axis=0, tiled=True)
    )

    def one_backward(items):
        q, k, v, g, mask, log_total = items
        raw = jnp.einsum("qhd,kd->hqk", q, k, preferred_element_type=f32) * scale
        probs = jnp.where(mask, jnp.exp(jnp.where(mask, raw, NEGATIVE) - log_total), 0.0)
        probs_low = probs.astype(bf16)
        grad_probs = jnp.einsum("qhd,kd->hqk", g, v, preferred_element_type=f32)
        delta = jnp.sum(grad_probs * probs, axis=-1, keepdims=True)
        grad_scores = (probs * (grad_probs - delta)).astype(bf16)
        gq = jnp.einsum("hqk,kd->qhd", grad_scores, k, preferred_element_type=f32) * scale
        gk = jnp.einsum("hqk,qhd->kd", grad_scores, q, preferred_element_type=f32) * scale
        gv = jnp.einsum("hqk,qhd->kd", probs_low, g, preferred_element_type=f32)
        return gq, jnp.concatenate([gk, gv], axis=-1).astype(bf16)

    gq, gkv = lax.map(
        one_backward,
        (
            query_rows,
            key_rows,
            value_rows,
            grad_mixed.reshape(width, tok, heads, HEAD_DIM),
            allowed,
            log_totals,
        ),
    )
    gkv = gkv.reshape(width, planes, tok, 2 * HEAD_DIM).transpose(1, 0, 2, 3)
    gkv = line_scatter(gkv.reshape(planes * all_tok, 2 * HEAD_DIM)).astype(f32)
    grad_qkv = jnp.concatenate(
        [
            rotate(gq.reshape(all_tok, heads, HEAD_DIM), cosine, sine, -1.0).reshape(all_tok, qw),
            rotate(gkv[:, None, :HEAD_DIM], cosine, sine, -1.0)[:, 0],
            gkv[:, HEAD_DIM:],
        ],
        axis=1,
    ).astype(bf16)
    grad_hidden_in = plane_scatter(dot(grad_qkv, w_qkv, 1, 1).astype(bf16), 7)
    qkv_rows = line_scatter(dot(hidden_in, grad_qkv, 0, 0).astype(bf16))
    gain_in_term = jnp.sum(grad_hidden_in * normed_in, axis=0)
    grad_normed_in = grad_hidden_in * gain_in
    input_grad = (
        grad_middle
        + scale_in
        * (
            grad_normed_in
            - normed_in * jnp.mean(grad_normed_in * normed_in, axis=1, keepdims=True)
        )
    ).astype(bf16)

    gain_terms = lax.psum(
        lax.psum_scatter(
            jnp.stack([gain_in_term, gain_mid_term]), F, scatter_dimension=1, tiled=True
        ),
        R,
    )
    rows = model // planes

    def spread(x, call):
        x = plane_gather(x, call, 2)
        return x.reshape(width, x.shape[0] // width, x.shape[1])

    down_grad = spread(down_rows, 8).reshape(feed // planes, model).astype(f32)
    feed_all = spread(feed_rows, 9).reshape(width, rows, 2, planes, piece)
    feed_all = feed_all.transpose(2, 1, 3, 0, 4).reshape(2, rows, feed).astype(f32)
    out_grad = spread(out_rows, 10).transpose(1, 0, 2).reshape(output_weight.shape).astype(f32)
    qkv_all = spread(qkv_rows, 11)
    query_grad = qkv_all[..., :qw].transpose(1, 0, 2).reshape(query_weight.shape).astype(f32)
    kv_all = qkv_all[..., qw:].astype(f32).reshape(KV_HEADS, width // KV_HEADS, rows, 2, HEAD_DIM)
    kv_all = kv_all.sum(axis=1).transpose(2, 1, 0, 3).reshape(2, rows, KV_HEADS * HEAD_DIM)
    return (
        activations,
        input_grad,
        gain_terms[0],
        query_grad,
        kv_all[0],
        kv_all[1],
        out_grad,
        gain_terms[1],
        feed_all[0],
        feed_all[1],
        down_grad,
    )


def solution(mesh):
    tok = P((R, F), None)
    row = P(F, None)
    in_specs = (tok, P(R, None), P(F), row, row, row, row, P(F), row, row, row, tok)
    out_specs = (tok, tok, P(F), row, row, row, row, P(F), row, row, row)
    return jax.shard_map(
        per_device, mesh=mesh, in_specs=in_specs, out_specs=out_specs, check_vma=False
    )
```

```python
import functools
import math

import jax
import jax.numpy as jnp
from jax import lax
from jax.experimental import pallas as pl
from jax.experimental.pallas import tpu as pltpu
from jax.sharding import PartitionSpec as P

HEADS = 32
KV_HEADS = 4
HEAD_DIM = 64
EPSILON = 1e-05
NEGATIVE = -1e30
R = "replica"
F = "fsdp"
MESH = pl.DeviceIdType.MESH
DMA = pltpu.SemaphoreType.DMA
ANY = pl.BlockSpec(memory_space=pl.ANY)
KEY_BLOCK = 256
QUERY_BLOCK = 128
PARTS = 2


def inverse_rms(values):
    return lax.rsqrt(jnp.mean(values * values, axis=1, keepdims=True) + EPSILON)


def rope_tables(positions):
    half_dim = HEAD_DIM // 2
    freq_rates = jnp.exp(jnp.arange(half_dim, dtype=jnp.float32) * (-math.log(10000.0) / half_dim))
    angles = positions.astype(jnp.float32)[:, None] * freq_rates[None, :]
    return (jnp.cos(angles), jnp.sin(angles))


def rotate(tensor, cosine_table, sine_table, sign):
    half_dim = HEAD_DIM // 2
    low, up = tensor[..., :half_dim], tensor[..., half_dim:]
    cos_part = cosine_table[:, None, :]
    sin_part = sine_table[:, None, :] * sign
    return jnp.concatenate(
        [low * cos_part - up * sin_part, up * cos_part + low * sin_part], axis=-1
    )


def dot(a, b, ca=1, cb=0):
    return lax.dot_general(a, b, (((ca,), (cb,)), ((), ())), preferred_element_type=jnp.float32)


def remote(src, dst, sems, index, device):
    return pltpu.make_async_remote_copy(
        src_ref=src,
        dst_ref=dst,
        send_sem=sems[0].at[index],
        recv_sem=sems[1].at[index],
        device_id={R: device},
        device_id_type=MESH,
    )


def greet(*devices):
    barrier = pltpu.get_barrier_semaphore()
    for device in devices:
        pl.semaphore_signal(barrier, inc=1, device_id={R: device}, device_id_type=MESH)
    pl.semaphore_wait(barrier, len(devices))


class Gather:
    @staticmethod
    def scratch(count):
        return [DMA((count,))] * 6 + [DMA((4, count))] * 2

    def __init__(self, items, sems):
        self.items, self.count = items, len(items)
        self.half = self.count // 2
        self.me = lax.axis_index(R)
        self.sibling, self.x, self.y = self.me + 1 - 2 * lax.rem(self.me, 2), self.me ^ 2, self.me ^ 4
        self.across = self.me ^ 6
        self.sems = sems
        self.copies = {}

    def send(self, kind, i, owner, device):
        own, slot = self.items[i]
        sems = self.sems[2 * min(kind, 3) : 2 * min(kind, 3) + 2]
        index = i if kind < 3 else (kind - 3, i)
        src = own if owner is self.me else slot(owner)
        copy = remote(src, slot(owner), sems, index, device)
        copy.start()
        self.copies[kind, i] = copy

    def start(self):
        for i in range(self.count):
            self.send(0, i, self.me, self.x)
            j = (i + self.half) % self.count
            self.send(1, j, self.me, self.y)
        for i in range(self.count):
            self.send(3, i, self.me, self.sibling)

    def relay(self, i):
        j = (i + self.half) % self.count
        self.copies[0, i].wait_recv()
        if i < self.half:
            self.send(2, i, self.x, self.y)
        self.send(4, i, self.x, self.sibling)
        self.copies[1, j].wait_recv()
        if j >= self.half:
            self.send(2, j, self.y, self.x)
        self.send(5, j, self.y, self.sibling)

    def finish(self):
        for i in range(self.half):
            for j in (i, self.half + i):
                if j < self.count and (2, j) in self.copies and (6, j) not in self.copies:
                    self.copies[2, j].wait_recv()
                    self.send(6, j, self.across, self.sibling)
        for i in range(self.count):
            if (6, i) not in self.copies:
                self.copies[2, i].wait_recv()
                self.send(6, i, self.across, self.sibling)
        for (kind, _), copy in self.copies.items():
            if kind < 3:
                copy.wait_send()
            else:
                copy.wait()


def row_items(x, out, chunks):
    size = x.shape[0] // chunks

    def item(i):
        part = pl.ds(i * size, size)
        return x.at[part], lambda owner: out.at[owner, part]

    return [item(i) for i in range(chunks)]


def gather_kernel(chunks, x, out, local_sem, *sems):
    gather = Gather(row_items(x, out, chunks), sems)
    greet(gather.sibling, gather.x, gather.y)
    own = pltpu.make_async_copy(x, out.at[gather.me], local_sem)
    own.start()
    gather.start()
    for i in range(chunks):
        gather.relay(i)
    gather.finish()
    own.wait()


def enter_kernel(chunks, tokens, gains, ids, hidden, all_gains, all_ids, own, own_sem, to_z, at_z, *sems):
    f32 = jnp.float32
    planes = all_gains.shape[0]
    z = lax.axis_index(F)
    items = row_items(own, hidden, chunks) + [(ids, lambda owner: all_ids.at[owner])]
    gather = Gather(items, sems)
    others = [lax.rem(z + i, planes) for i in range(1, planes)]
    barrier = pltpu.get_barrier_semaphore()
    for other in others:
        pl.semaphore_signal(barrier, inc=1, device_id={F: other}, device_id_type=MESH)
    for device in (gather.sibling, gather.x, gather.y):
        pl.semaphore_signal(barrier, inc=1, device_id={R: device}, device_id_type=MESH)
    pl.semaphore_wait(barrier, planes + 2)
    copies = [
        pltpu.make_async_remote_copy(
            src_ref=gains,
            dst_ref=all_gains.at[z],
            send_sem=to_z.at[i],
            recv_sem=at_z.at[i],
            device_id={F: other},
            device_id_type=MESH,
        )
        for i, other in enumerate(others)
    ]
    for copy in copies:
        copy.start()
    all_gains[z] = gains[...]
    all_ids[gather.me] = ids[...]
    size = tokens.shape[0] // chunks
    scales = [
        inverse_rms(tokens[i * size : (i + 1) * size, :].astype(f32)) for i in range(chunks)
    ]
    for copy in copies:
        copy.wait()
    gain = jnp.concatenate([all_gains[p, 0:1] for p in range(planes)], axis=1)
    for i in range(chunks):
        part = slice(i * size, (i + 1) * size)
        own[part, :] = (tokens[part, :].astype(f32) * scales[i] * gain).astype(jnp.bfloat16)
    kept = pltpu.make_async_copy(own, hidden.at[gather.me], own_sem)
    kept.start()
    gather.start()
    for i in range(gather.count):
        gather.relay(i)
    gather.finish()
    kept.wait()


def turn(x, cosine, sine):
    half_dim = HEAD_DIM // 2
    low = lax.rem(lax.broadcasted_iota(jnp.int32, x.shape, 1), HEAD_DIM) < half_dim
    swapped = jnp.where(low, pltpu.roll(x, 2 * HEAD_DIM - half_dim, 1), pltpu.roll(x, half_dim, 1))
    return x * cosine + swapped * sine


def turn_keys(x, cosine, sine):
    is_key = lax.broadcasted_iota(jnp.int32, x.shape, 1) < HEAD_DIM
    return jnp.where(is_key, turn(x, cosine, sine), x)


def along_line(src, dst, sems, index, plane):
    return pltpu.make_async_remote_copy(
        src_ref=src,
        dst_ref=dst,
        send_sem=sems[0].at[index],
        recv_sem=sems[1].at[index],
        device_id={F: plane},
        device_id_type=MESH,
    )


def project_kernel(
    chunks, hidden, weight, cosine, sine, cotangent, query, kv, cot_all,
    own, own_sem, cot_sem, to_line, at_line, to_sib, at_sib, *sems,
):
    bf16 = jnp.bfloat16
    planes = kv.shape[1]
    z = lax.axis_index(F)
    tok = cotangent.shape[0]
    width = kv.shape[0]
    count = width // 2
    gather = Gather(row_items(cotangent, cot_all, chunks), sems)
    core = lax.rem(gather.me, 2)
    mine = pl.ds(core * count, count)
    above, below = lax.rem(z + 1, planes), lax.rem(z + planes - 1, planes)
    barrier = pltpu.get_barrier_semaphore()
    for other in (above, below):
        pl.semaphore_signal(barrier, inc=1, device_id={F: other}, device_id_type=MESH)
    for device in (gather.sibling, gather.x, gather.y):
        pl.semaphore_signal(barrier, inc=1, device_id={R: device}, device_id_type=MESH)
    pl.semaphore_wait(barrier, 5)
    kept_cot = pltpu.make_async_copy(cotangent, cot_all.at[gather.me], cot_sem)
    kept_cot.start()
    gather.start()

    def tile(i, carry):
        s = lax.rem(core * count + i, width)
        rows = pl.ds(pl.multiple_of(s * tok, tok), tok)
        acc = dot(hidden[rows, :], weight[...])
        c, n = cosine[rows, :], sine[rows, :]
        columns = acc.shape[1] - 2 * HEAD_DIM
        for first in range(0, columns, 2 * HEAD_DIM):
            part = slice(first, first + 2 * HEAD_DIM)
            query[rows, part] = turn(acc[:, part], c, n).astype(bf16)
        own[s] = turn_keys(acc[:, columns:], c, n).astype(bf16)
        return carry

    def up(step):
        slot = z - step
        src = own.at[mine] if step == 0 else kv.at[mine, slot]
        return along_line(src, kv.at[mine, slot], (to_line, at_line), step, above)

    def came(step):
        slot = z - step
        return along_line(kv.at[mine, slot], kv.at[mine, slot], (to_line, at_line), step - 1, above)

    def across(step):
        slot = z - step
        return remote(kv.at[mine, slot], kv.at[mine, slot], (to_sib, at_sib), step, gather.sibling)

    lax.fori_loop(0, count, tile, 0)

    @pl.when(z < planes - 1)
    def _():
        up(0).start()

    lax.fori_loop(count, width, tile, 0)
    kept = pltpu.make_async_copy(own, kv.at[:, z], own_sem)
    kept.start()
    done = 0
    for step in range(1, planes):

        @pl.when(z >= step)
        def _():
            came(step).wait_recv()

            @pl.when(z < planes - 1)
            def _():
                up(step).start()

            across(step).start()

        while done < chunks * step // planes:
            gather.relay(done)
            done += 1
    for i in range(done, chunks):
        gather.relay(i)
    gather.finish()
    for step in range(planes):

        @pl.when((z >= step) & (z < planes - 1))
        def _():
            up(step).wait_send()

        if step:

            @pl.when(z >= step)
            def _():
                across(step).wait()

    kept.wait()
    kept_cot.wait()


def return_kernel(
    grad_kv, grad_q, cosine, sine, grad_qkv,
    own, from_sib, inbox, outbox, own_sem, to_sib, at_sib, to_line, at_line,
):
    f32, bf16 = jnp.float32, jnp.bfloat16
    planes, count, tok = inbox.shape[0], inbox.shape[1], inbox.shape[2]
    z, me = lax.axis_index(F), lax.axis_index(R)
    core = lax.rem(me, 2)
    sibling = me + 1 - 2 * core
    above, below = lax.rem(z + 1, planes), lax.rem(z + planes - 1, planes)
    columns = grad_q.shape[1]
    barrier = pltpu.get_barrier_semaphore()
    for other in (above, below):
        pl.semaphore_signal(barrier, inc=1, device_id={F: other}, device_id_type=MESH)
    pl.semaphore_signal(barrier, inc=1, device_id={R: sibling}, device_id_type=MESH)

    def block(half, b):
        return grad_kv.at[pl.ds(half * count, count), pl.ds(b * tok, tok)]

    def load(b):
        return pltpu.make_async_copy(block(core, b), own.at[b], own_sem.at[b])

    def trade(b):
        return remote(block(1 - core, b), from_sib.at[b], (to_sib, at_sib), b, sibling)

    def down(b):
        return along_line(outbox.at[b], inbox.at[b], (to_line, at_line), b, below)

    for b in range(planes):

        @pl.when(b <= z)
        def _():
            load(b).start()

    pl.semaphore_wait(barrier, 3)
    for b in range(planes):

        @pl.when(b <= z)
        def _():
            trade(b).start()

    def queries(s, carry):
        rows = pl.ds(pl.multiple_of(s * tok, tok), tok)
        c, n = cosine[rows, :], -sine[rows, :]
        for first in range(0, columns, 2 * HEAD_DIM):
            part = slice(first, first + 2 * HEAD_DIM)
            grad_qkv[rows, part] = turn(grad_q[rows, part], c, n).astype(bf16)
        grad_qkv[rows, columns:] = jnp.zeros((tok, 2 * HEAD_DIM), bf16)
        return carry

    for b in range(planes):

        @pl.when(b <= z)
        def _():
            load(b).wait()
            trade(b).wait_recv()

            @pl.when(z < planes - 1)
            def _():
                down(b).wait_recv()

        @pl.when((b < z) & (z < planes - 1))
        def _():
            outbox[b] = (
                own[b].astype(f32) + from_sib[b].astype(f32) + inbox[b].astype(f32)
            ).astype(bf16)

        @pl.when((b < z) & (z == planes - 1))
        def _():
            outbox[b] = (own[b].astype(f32) + from_sib[b].astype(f32)).astype(bf16)

        @pl.when(b < z)
        def _():
            down(b).start()

        if b == 0:
            lax.fori_loop(0, 2 * count, queries, 0)

    def keys(i, carry):
        s = core * count + i
        rows = pl.ds(pl.multiple_of(s * tok, tok), tok)
        total = own[z, i].astype(f32) + from_sib[z, i].astype(f32)
        total = total + jnp.where(z < planes - 1, inbox[z, i].astype(f32), 0.0)
        grad_qkv[rows, columns:] = turn_keys(total, cosine[rows, :], -sine[rows, :]).astype(bf16)
        return carry

    lax.fori_loop(0, count, keys, 0)
    for b in range(planes):

        @pl.when(b <= z)
        def _():
            trade(b).wait_send()

        @pl.when(b < z)
        def _():
            down(b).wait_send()


class Scatter:
    @staticmethod
    def scratch(rows, columns, chunks):
        bf16, size = jnp.bfloat16, rows // chunks
        return [
            pltpu.VMEM((5, rows, columns), bf16),
            pltpu.VMEM((4, rows, columns), bf16),
            pltpu.VMEM((chunks, 2, size, columns), bf16),
            pltpu.VMEM((chunks, size, columns), bf16),
            pltpu.VMEM((chunks, size, columns), jnp.float32),
            DMA((4,)),
            DMA((4,)),
            DMA((chunks, 2)),
            DMA((chunks, 2)),
            DMA((chunks,)),
            DMA((chunks,)),
            DMA((chunks,)),
        ]

    def __init__(self, out, chunks, refs):
        self.out, self.chunks, self.half = out, chunks, chunks // 2
        self.own, self.sib, self.got, self.got_far, self.total = refs[:5]
        self.sib_sems, self.near_sems, self.far_sems = refs[5:7], refs[7:9], refs[9:11]
        self.out_sem = refs[11]
        self.me = lax.axis_index(R)
        self.sibling, self.x, self.y = self.me + 1 - 2 * lax.rem(self.me, 2), self.me ^ 2, self.me ^ 4
        self.size = out.shape[0] // chunks

    def owner(self, i):
        return (self.me ^ (6 - 2 * (i // 2))) ^ (1 - lax.rem(i, 2))

    def trade(self, d):
        return remote(self.own.at[4], self.sib.at[d], self.sib_sems, d, self.sibling)

    def put(self, i, value):
        d = 3 - i // 2
        for_sibling = lax.rem(i, 2) == 0

        @pl.when(for_sibling & (i >= 2))
        def _():
            self.trade(d + 1).wait_send()

        self.own[jnp.where(for_sibling, 4, d)] = value

        @pl.when(for_sibling)
        def _():
            self.trade(d).start()

    def arrived(self, d):
        self.trade(d).wait_recv()

    def part(self, j):
        return pl.ds(j * self.size, self.size)

    def summed(self, d, j):
        part = self.part(j)
        return self.own[d, part].astype(jnp.float32) + self.sib[d, part].astype(jnp.float32)

    def near_copies(self, j):
        device, d = (self.x, 1) if j < self.half else (self.y, 2)
        return [
            remote(self.own.at[e, self.part(j)], self.got.at[j, n], self.near_sems, (j, n), device)
            for n, e in enumerate((d, 3))
        ]

    def far_copy(self, j):
        device, d = (self.y, 2) if j < self.half else (self.x, 1)
        return remote(self.own.at[d, self.part(j)], self.got_far.at[j], self.far_sems, j, device)

    def out_copy(self, j):
        return pltpu.make_async_copy(self.total.at[j], self.out.at[self.part(j)], self.out_sem.at[j])

    def near(self, j):
        for e in (1 if j < self.half else 2, 3):
            self.own[e, self.part(j)] = self.summed(e, j).astype(jnp.bfloat16)
        for copy in self.near_copies(j):
            copy.start()

    def far(self, j):
        for copy in self.near_copies(j):
            copy.wait_recv()
        d = 2 if j < self.half else 1
        passed = self.summed(d, j) + self.got[j, 1].astype(jnp.float32)
        self.own[d, self.part(j)] = passed.astype(jnp.bfloat16)
        self.far_copy(j).start()
        self.total[j] = self.summed(0, j) + self.got[j, 0].astype(jnp.float32)

    def last(self, j):
        self.far_copy(j).wait_recv()
        self.total[j] = self.total[j] + self.got_far[j].astype(jnp.float32)
        self.out_copy(j).start()

    def finish(self):
        self.trade(0).wait_send()
        for j in range(self.chunks):
            self.out_copy(j).wait()
            self.far_copy(j).wait_send()
            for copy in self.near_copies(j):
                copy.wait_send()


def feed_kernel(
    chunks, hidden, cotangent, w_feed, w_down, out_part, grad_hidden, feed_part, down_part,
    hidden_in, cot_in, grads, inner_turned, out_stage, column_in, feed_stage, down_stage,
    in_sems, out_sem, column_sems, feed_sem, down_sem, *refs,
):
    f32, bf16 = jnp.float32, jnp.bfloat16
    width, tok, model = hidden.shape
    units = w_down.shape[0]
    scatter = Scatter(grad_hidden, chunks, refs)
    half = chunks // 2

    def loads(i):
        slot, owner = lax.rem(i, 2), scatter.owner(i)
        return [
            pltpu.make_async_copy(hidden.at[owner], hidden_in.at[slot], in_sems.at[0, slot]),
            pltpu.make_async_copy(cotangent.at[owner], cot_in.at[slot], in_sems.at[1, slot]),
        ]

    def out_copy(i):
        return pltpu.make_async_copy(out_stage, out_part.at[scatter.owner(i)], out_sem)

    for i in (0, 1):
        for copy in loads(i):
            copy.start()
    greet(scatter.sibling, scatter.x, scatter.y)

    def block(i, carry):
        slot = lax.rem(i, 2)
        rows = pl.ds(pl.multiple_of(i * tok, tok), tok)
        for copy in loads(i):
            copy.wait()
        acc = dot(hidden_in[slot], w_feed[...])
        gate, up = acc[:, :units], acc[:, units:]
        gate_sig = 1.0 / (1.0 + jnp.exp(-gate))
        gate_silu = gate * gate_sig
        inner = (gate_silu * up).astype(bf16)
        inner_turned[i] = inner.T
        grad_inner = dot(cot_in[slot], w_down[...], 1, 1)
        grad_gate = grad_inner * up * gate_sig * (1.0 + gate * (1.0 - gate_sig))
        both = jnp.concatenate([grad_gate, grad_inner * gate_silu], axis=1).astype(bf16)
        grads[rows, :] = both
        scatter.put(i, dot(both, w_feed[...], 1, 1).astype(bf16))

        @pl.when(i >= 1)
        def _():
            out_copy(i - 1).wait()

        out_stage[...] = dot(inner, w_down[...]).astype(bf16)
        out_copy(i).start()

        @pl.when(i + 2 < width)
        def _():
            for copy in loads(i + 2):
                copy.start()

        @pl.when(i == 4)
        def _():
            scatter.arrived(3)
            scatter.arrived(2)
            for j in range(half, chunks):
                scatter.near(j)

        @pl.when(i == 6)
        def _():
            scatter.arrived(1)
            for j in range(half):
                scatter.near(j)

        return carry

    tiles = model // tok

    def column_loads(n, source, tile):
        slot = lax.rem(n, 2)
        part = pl.ds(pl.multiple_of(tile * tok, tok), tok)
        return [
            pltpu.make_async_copy(
                source.at[scatter.owner(i), :, part],
                column_in.at[slot, pl.ds(i * tok, tok)],
                column_sems.at[slot, i],
            )
            for i in range(width)
        ]

    def start_columns(n):
        @pl.when(n < tiles)
        def _():
            for copy in column_loads(n, hidden, n):
                copy.start()

        @pl.when((n >= tiles) & (n < 2 * tiles))
        def _():
            for copy in column_loads(n, cotangent, n - tiles):
                copy.start()

    def feed_copy(n):
        rows = pl.ds(pl.multiple_of(n * tok, tok), tok)
        slot = lax.rem(n, 2)
        return pltpu.make_async_copy(feed_stage.at[slot], feed_part.at[rows], feed_sem.at[slot])

    def down_copy(n):
        part = pl.ds(pl.multiple_of((n - tiles) * tok, tok), tok)
        slot = lax.rem(n, 2)
        return pltpu.make_async_copy(down_stage.at[slot], down_part.at[:, part], down_sem.at[slot])

    def feed_tile(n, carry):
        slot = lax.rem(n, 2)
        for copy in column_loads(n, hidden, n):
            copy.wait()

        @pl.when(n >= 2)
        def _():
            feed_copy(n - 2).wait()

        feed_stage[slot] = dot(column_in[slot], grads[...], 0, 0).astype(bf16)
        feed_copy(n).start()
        start_columns(n + 2)

        @pl.when(n == 1)
        def _():
            for j in range(half, chunks):
                scatter.far(j)

        @pl.when(n == 4)
        def _():
            for j in range(half):
                scatter.far(j)

        return carry

    def down_tile(n, carry):
        slot = lax.rem(n, 2)
        for copy in column_loads(n, cotangent, n - tiles):
            copy.wait()

        @pl.when(n >= tiles + 2)
        def _():
            down_copy(n - 2).wait()

        acc = dot(inner_turned[0], column_in[slot, :tok])
        for i in range(1, width):
            acc = acc + dot(inner_turned[i], column_in[slot, i * tok : (i + 1) * tok])
        down_stage[slot] = acc.astype(bf16)
        down_copy(n).start()
        start_columns(n + 2)
        return carry

    for n in (0, 1):
        for copy in column_loads(n, hidden, n):
            copy.start()
    lax.fori_loop(0, width, block, 0)
    scatter.arrived(0)
    lax.fori_loop(0, tiles, feed_tile, 0)
    for j in range(half, chunks):
        scatter.last(j)
    lax.fori_loop(tiles, 2 * tiles, down_tile, 0)
    for j in range(half):
        scatter.last(j)
    scatter.finish()
    out_copy(width - 1).wait()
    for n in (tiles - 2, tiles - 1):
        feed_copy(n).wait()
        down_copy(n + tiles).wait()


def feed_forward(hidden, cotangent, w_feed, w_down, call, chunks=4):
    width, tok, model = hidden.shape
    units = w_down.shape[0]
    bf16 = jnp.bfloat16
    vmem = pl.BlockSpec(memory_space=pltpu.VMEM)
    return pl.pallas_call(
        functools.partial(feed_kernel, chunks),
        out_shape=[
            jax.ShapeDtypeStruct((width, tok, model), bf16),
            jax.ShapeDtypeStruct((tok, model), jnp.float32),
            jax.ShapeDtypeStruct((model, 2 * units), bf16),
            jax.ShapeDtypeStruct((units, model), bf16),
        ],
        in_specs=[ANY, ANY, vmem, vmem],
        out_specs=[ANY] * 4,
        scratch_shapes=[
            pltpu.VMEM((2, tok, model), bf16),
            pltpu.VMEM((2, tok, model), bf16),
            pltpu.VMEM((width * tok, 2 * units), bf16),
            pltpu.VMEM((width, units, tok), bf16),
            pltpu.VMEM((tok, model), bf16),
            pltpu.VMEM((2, width * tok, tok), bf16),
            pltpu.VMEM((2, tok, 2 * units), bf16),
            pltpu.VMEM((2, units, tok), bf16),
            DMA((2, 2)),
            DMA,
            DMA((2, width)),
            DMA((2,)),
            DMA((2,)),
        ]
        + Scatter.scratch(tok, model, chunks),
        compiler_params=pltpu.CompilerParams(
            collective_id=call, has_side_effects=True, vmem_limit_bytes=60 << 20
        ),
    )(hidden, cotangent, w_feed, w_down)


def enter(tokens, gains, ids, call, chunks=4):
    planes, rows = lax.axis_size(F), lax.axis_size(R)
    tok, model = tokens.shape
    vmem = pl.BlockSpec(memory_space=pltpu.VMEM)
    return pl.pallas_call(
        functools.partial(enter_kernel, chunks),
        out_shape=[
            jax.ShapeDtypeStruct((rows, tok, model), jnp.bfloat16),
            jax.ShapeDtypeStruct((planes,) + gains.shape, jnp.float32),
            jax.ShapeDtypeStruct((rows,) + ids.shape, jnp.int32),
        ],
        in_specs=[vmem] * 3,
        out_specs=[ANY, vmem, vmem],
        scratch_shapes=[pltpu.VMEM((tok, model), jnp.bfloat16), DMA]
        + [DMA((planes - 1,))] * 2
        + Gather.scratch(chunks + 1),
        compiler_params=pltpu.CompilerParams(
            collective_id=call, has_side_effects=True, vmem_limit_bytes=32 << 20
        ),
    )(tokens, gains, ids)


def project(hidden, weight, cosine, sine, cotangent, call, chunks=4):
    planes, width = lax.axis_size(F), lax.axis_size(R)
    tok, model = cotangent.shape
    bf16 = jnp.bfloat16
    vmem = pl.BlockSpec(memory_space=pltpu.VMEM)
    return pl.pallas_call(
        functools.partial(project_kernel, chunks),
        out_shape=[
            jax.ShapeDtypeStruct((width * tok, weight.shape[1] - 2 * HEAD_DIM), bf16),
            jax.ShapeDtypeStruct((width, planes, tok, 2 * HEAD_DIM), bf16),
            jax.ShapeDtypeStruct((width, tok, model), bf16),
        ],
        in_specs=[vmem] * 4 + [ANY],
        out_specs=[vmem, ANY, ANY],
        scratch_shapes=[pltpu.VMEM((width, tok, 2 * HEAD_DIM), bf16), DMA, DMA]
        + [DMA((planes,))] * 4
        + Gather.scratch(chunks),
        compiler_params=pltpu.CompilerParams(
            collective_id=call, has_side_effects=True, vmem_limit_bytes=40 << 20
        ),
    )(hidden, weight, cosine, sine, cotangent)


def return_keys(grad_kv, grad_q, cosine, sine, call):
    planes, width = lax.axis_size(F), lax.axis_size(R)
    bf16 = jnp.bfloat16
    tok = grad_kv.shape[1] // planes
    vmem = pl.BlockSpec(memory_space=pltpu.VMEM)
    blocks = pltpu.VMEM((planes, width // 2, tok, 2 * HEAD_DIM), bf16)
    return pl.pallas_call(
        return_kernel,
        out_shape=jax.ShapeDtypeStruct((grad_q.shape[0], grad_q.shape[1] + 2 * HEAD_DIM), bf16),
        in_specs=[ANY] + [vmem] * 3,
        out_specs=vmem,
        scratch_shapes=[blocks] * 4 + [DMA((planes,))] * 5,
        compiler_params=pltpu.CompilerParams(
            collective_id=call, has_side_effects=True, vmem_limit_bytes=40 << 20
        ),
    )(grad_kv, grad_q, cosine, sine)


def scatter_kernel(
    chunks, part, out, own, from_sib, give, got, give_far, got_far, total,
    own_sem, out_sem, to_sib, at_sib, to_near, at_near, to_far, at_far,
):
    f32, bf16 = jnp.float32, jnp.bfloat16
    me = lax.axis_index(R)
    flip = 1 - 2 * lax.rem(me, 2)
    sibling, beside_x, beside_y = me + flip, me ^ 2, me ^ 4
    rows = out.shape[0]
    size = rows // chunks
    half = chunks // 2
    owners = [me, beside_x, beside_y, me ^ 6]
    order = [c for j in range(half) for c in (j, half + j)]

    def rows_of(device, j):
        return part.at[pl.ds(pl.multiple_of(device * rows + j * size, 16), size)]

    def own_copy(d, j):
        return pltpu.make_async_copy(rows_of(owners[d], j), own.at[d, j], own_sem.at[d, j])

    def sib_copy(d, j):
        return remote(rows_of(owners[d] + flip, j), from_sib.at[d, j], (to_sib, at_sib), (d, j), sibling)

    def near_copy(j):
        device = beside_x if j < half else beside_y
        return remote(give.at[j], got.at[j], (to_near, at_near), j, device)

    def far_copy(j):
        device = beside_y if j < half else beside_x
        return remote(give_far.at[j], got_far.at[j], (to_far, at_far), j, device)

    def out_copy(j):
        return pltpu.make_async_copy(total.at[j], out.at[pl.ds(j * size, size)], out_sem.at[j])

    def summed(d, j):
        own_copy(d, j).wait()
        sib_copy(d, j).wait_recv()
        return own[d, j].astype(f32) + from_sib[d, j].astype(f32)

    for j in order:
        for d in (1, 2, 3, 0):
            own_copy(d, j).start()
    greet(sibling, beside_x, beside_y)
    for j in order:
        for d in (1, 3, 2, 0) if j < half else (2, 3, 1, 0):
            sib_copy(d, j).start()
    for j in order:
        give[j, 0] = summed(1 if j < half else 2, j).astype(bf16)
        give[j, 1] = summed(3, j).astype(bf16)
        near_copy(j).start()
    for j in order:
        passed = summed(2 if j < half else 1, j)
        kept = summed(0, j)
        near_copy(j).wait_recv()
        give_far[j] = (passed + got[j, 1].astype(f32)).astype(bf16)
        far_copy(j).start()
        total[j] = kept + got[j, 0].astype(f32)
    for j in order:
        far_copy(j).wait_recv()
        total[j] = total[j] + got_far[j].astype(f32)
        out_copy(j).start()
    for j in order:
        out_copy(j).wait()
        near_copy(j).wait_send()
        far_copy(j).wait_send()
        for d in range(4):
            sib_copy(d, j).wait_send()


def plane_gather(x, call, chunks=4):
    width = lax.axis_size(R)
    if width != 8:
        return lax.all_gather(x, R, axis=0, tiled=True)
    out = pl.pallas_call(
        functools.partial(gather_kernel, chunks),
        out_shape=jax.ShapeDtypeStruct((width,) + x.shape, x.dtype),
        in_specs=[ANY],
        out_specs=ANY,
        scratch_shapes=[DMA] + Gather.scratch(chunks),
        compiler_params=pltpu.CompilerParams(collective_id=call, has_side_effects=True),
    )(x)
    return out.reshape((width * x.shape[0],) + x.shape[1:])


def plane_scatter(x, call, chunks=4):
    width = lax.axis_size(R)
    if width != 8:
        return lax.psum_scatter(x, R, scatter_dimension=0, tiled=True).astype(jnp.float32)
    rows, columns = x.shape[0] // width, x.shape[1]
    size = rows // chunks
    bf16 = jnp.bfloat16
    return pl.pallas_call(
        functools.partial(scatter_kernel, chunks),
        out_shape=jax.ShapeDtypeStruct((rows, columns), jnp.float32),
        in_specs=[ANY],
        out_specs=ANY,
        scratch_shapes=[
            pltpu.VMEM((4, chunks, size, columns), bf16),
            pltpu.VMEM((4, chunks, size, columns), bf16),
            pltpu.VMEM((chunks, 2, size, columns), bf16),
            pltpu.VMEM((chunks, 2, size, columns), bf16),
            pltpu.VMEM((chunks, size, columns), bf16),
            pltpu.VMEM((chunks, size, columns), bf16),
            pltpu.VMEM((chunks, size, columns), jnp.float32),
            DMA((4, chunks)),
            DMA((chunks,)),
            DMA((4, chunks)),
            DMA((4, chunks)),
        ]
        + [DMA((chunks,))] * 4,
        compiler_params=pltpu.CompilerParams(
            collective_id=call, has_side_effects=True, vmem_limit_bytes=32 << 20
        ),
    )(x)


def line_gather(x):
    return lax.all_gather(x, F, axis=0, tiled=True)


def line_scatter(x):
    return lax.psum_scatter(x, F, scatter_dimension=0, tiled=True)


def heads_to_rows(block, heads):
    parts = [block[:, h * HEAD_DIM : (h + 1) * HEAD_DIM] for h in range(heads)]
    rows = jnp.concatenate(parts, axis=0)
    return jnp.concatenate([rows, jnp.zeros_like(rows)], axis=1)


def rows_to_heads(columns, heads):
    count = columns.shape[1] // heads
    return jnp.concatenate([columns[:, h * count : (h + 1) * count].T for h in range(heads)], axis=1)


def visible(block_index, starts, places):
    keys = block_index * KEY_BLOCK + lax.broadcasted_iota(jnp.int32, (KEY_BLOCK, starts.shape[1]), 0)
    return (keys >= starts) & (keys <= places)


def attention_kernel(heads, low, high, q, kv, starts, places, mixed, log_total):
    f32, bf16 = jnp.float32, jnp.bfloat16
    step = pl.program_id(0) * pl.num_programs(1) + pl.program_id(1)
    queries = heads_to_rows(q[...] * bf16(HEAD_DIM**-0.5), heads)
    first = jnp.concatenate([starts[0]] * heads, axis=1)
    place = jnp.concatenate([places[0]] * heads, axis=1)
    columns = queries.shape[0]

    def block(index, carry):
        top, total, acc = carry
        rows = kv[0, pl.ds(pl.multiple_of(index * KEY_BLOCK, KEY_BLOCK), KEY_BLOCK), :]
        scores = jnp.where(visible(index, first, place), dot(rows, queries, 1, 1), NEGATIVE)
        new_top = jnp.maximum(top, jnp.max(scores, axis=0, keepdims=True))
        weights = jnp.exp(scores - new_top)
        fade = jnp.exp(top - new_top)
        total = total * fade + jnp.sum(weights, axis=0, keepdims=True)
        acc = acc * fade + dot(rows, weights.astype(bf16), 0, 0)
        return new_top, total, acc

    top, total, acc = lax.fori_loop(
        low[step],
        high[step],
        block,
        (
            jnp.full((1, columns), NEGATIVE, f32),
            jnp.zeros((1, columns), f32),
            jnp.zeros((2 * HEAD_DIM, columns), f32),
        ),
    )
    mixed[...] = rows_to_heads(acc[HEAD_DIM:] / total, heads).astype(bf16)
    log_total[0] = top + jnp.log(total)


def attention_back_kernel(
    heads, low, high, q, kv, starts, places, grad, mixed, log_total, grad_q, grad_kv, sums
):
    f32, bf16 = jnp.float32, jnp.bfloat16
    step = pl.program_id(0) * pl.num_programs(1) + pl.program_id(1)
    queries = heads_to_rows(q[...] * bf16(HEAD_DIM**-0.5), heads)
    grads = heads_to_rows(grad[...], heads)
    first = jnp.concatenate([starts[0]] * heads, axis=1)
    place = jnp.concatenate([places[0]] * heads, axis=1)
    columns = queries.shape[0]
    products = grads.astype(f32) * heads_to_rows(mixed[...], heads).astype(f32)
    delta = lax.dot_general(
        jnp.ones((8, 2 * HEAD_DIM), f32),
        products,
        (((1,), (1,)), ((), ())),
        precision=lax.Precision.HIGHEST,
        preferred_element_type=f32,
    )[:1]
    level = log_total[0]
    upper = pltpu.roll(grads.astype(f32), HEAD_DIM, 1).astype(bf16)

    @pl.when(pl.program_id(1) == 0)
    def _():
        sums[...] = jnp.zeros_like(sums)

    def block(index, acc):
        part = pl.ds(pl.multiple_of(index * KEY_BLOCK, KEY_BLOCK), KEY_BLOCK)
        rows = kv[0, part, :]
        scores = dot(rows, queries, 1, 1)
        probs = jnp.where(visible(index, first, place), jnp.exp(scores - level), 0.0)
        grad_probs = dot(rows, upper, 1, 1)
        grad_scores = (probs * (grad_probs - delta)).astype(bf16)
        sums[part, :] += dot(grad_scores, queries) + dot(probs.astype(bf16), upper)
        return acc + dot(rows, grad_scores, 0, 0)

    acc = lax.fori_loop(low[step], high[step], block, jnp.zeros((2 * HEAD_DIM, columns), f32))
    grad_q[...] = rows_to_heads(acc[:HEAD_DIM] * HEAD_DIM**-0.5, heads)

    @pl.when(pl.program_id(1) == PARTS - 1)
    def _():
        grad_kv[0] = sums[...].astype(bf16)


def attention_call(kernel, heads, low, high, arrays, outs, scratch=()):
    blocks = {
        "tokens": lambda shape: pl.BlockSpec((QUERY_BLOCK, shape[1]), lambda s, b, *_: (s * PARTS + b, 0)),
        "row": lambda shape: pl.BlockSpec((1,) + shape[1:], lambda s, b, *_: (s * PARTS + b, 0, 0)),
        "sequence": lambda shape: pl.BlockSpec((1,) + shape[1:], lambda s, b, *_: (s, 0, 0)),
    }
    return pl.pallas_call(
        functools.partial(kernel, heads),
        grid_spec=pltpu.PrefetchScalarGridSpec(
            num_scalar_prefetch=2,
            grid=(low.shape[0] // PARTS, PARTS),
            in_specs=[blocks[kind](x.shape) for kind, x in arrays],
            out_specs=[blocks[kind](x.shape) for kind, x in outs],
            scratch_shapes=scratch,
        ),
        out_shape=[x for _, x in outs],
        compiler_params=pltpu.CompilerParams(vmem_limit_bytes=32 << 20),
    )(low, high, *[x for _, x in arrays])


def join_feed_kernel(planes, piece, x, gate, up):
    width = x.shape[0]
    for kind, out in enumerate((gate, up)):
        for p in range(planes):
            for r in range(width):
                first = (kind * planes + p) * piece
                to = (p * width + r) * piece
                out[:, to : to + piece] = x[r, :, first : first + piece].astype(jnp.float32)


def join_attention_kernel(sharers, qkv, o, query, key, value, out):
    f32 = jnp.float32
    width, qw, ow = qkv.shape[0], qkv.shape[2] - 2 * HEAD_DIM, o.shape[2]
    for r in range(width):
        query[:, r * qw : (r + 1) * qw] = qkv[r, :, :qw].astype(f32)
        out[:, r * ow : (r + 1) * ow] = o[r].astype(f32)
    for head in range(width // sharers):
        both = sum(qkv[head * sharers + i, :, qw:].astype(f32) for i in range(sharers))
        to = slice(head * HEAD_DIM, (head + 1) * HEAD_DIM)
        key[:, to] = both[:, :HEAD_DIM]
        value[:, to] = both[:, HEAD_DIM:]


def join_call(kernel, arrays, outs, block=64):
    rows = arrays[0].shape[1]
    return pl.pallas_call(
        kernel,
        grid=(rows // block,),
        in_specs=[pl.BlockSpec((x.shape[0], block, x.shape[2]), lambda i: (0, i, 0)) for x in arrays],
        out_specs=[pl.BlockSpec((block, columns), lambda i: (i, 0)) for columns in outs],
        out_shape=[jax.ShapeDtypeStruct((rows, columns), jnp.float32) for columns in outs],
        compiler_params=pltpu.CompilerParams(vmem_limit_bytes=32 << 20),
    )(*arrays)


def per_device(
    tokens,
    segment_ids,
    attention_gain,
    query_weight,
    key_weight,
    value_weight,
    output_weight,
    feed_gain,
    gate_weight,
    up_weight,
    down_weight,
    cotangent,
):
    f32, bf16 = jnp.float32, jnp.bfloat16
    planes, width = lax.axis_size(F), lax.axis_size(R)
    r, z = lax.axis_index(R), lax.axis_index(F)
    tok, model = tokens.shape
    length = segment_ids.shape[1]
    all_tok = width * tok
    plane_kernels = width == 8
    heads = HEADS // width
    group = HEADS // KV_HEADS
    qw = heads * HEAD_DIM
    kv = (r * heads) // group
    feed = gate_weight.shape[1]
    piece = feed // (width * planes)
    hidden_units = piece * planes

    def cols(weight, first, count):
        return lax.dynamic_slice_in_dim(weight, first, count, 1)

    def feed_cols(weight):
        return [cols(weight, p * (feed // planes) + r * piece, piece) for p in range(planes)]

    w_qkv = line_gather(
        jnp.concatenate(
            [
                cols(query_weight, r * qw, qw),
                cols(key_weight, kv * HEAD_DIM, HEAD_DIM),
                cols(value_weight, kv * HEAD_DIM, HEAD_DIM),
            ],
            axis=1,
        )
    )
    w_out = lax.all_to_all(
        line_gather(cols(output_weight, r * (model // width), model // width)),
        R,
        split_axis=0,
        concat_axis=1,
        tiled=True,
    )
    w_feed = line_gather(jnp.concatenate(feed_cols(gate_weight) + feed_cols(up_weight), axis=1))
    w_down = line_gather(lax.dynamic_slice_in_dim(down_weight, r * piece, piece, 0))
    own_gains = jnp.stack([attention_gain, feed_gain]).astype(f32)
    tok_float = tokens.astype(f32)
    scale_in = inverse_rms(tok_float)
    normed_in = tok_float * scale_in
    if plane_kernels:
        hidden_in, gains, ids = enter(
            tokens, jnp.pad(own_gains, ((0, 6), (0, 0))), segment_ids.reshape(8, length // 8), 0
        )
        hidden_in = hidden_in.reshape(all_tok, model)
        gains = gains[:, :2].transpose(1, 0, 2).reshape(2, model)
        ids = ids.reshape(width, length)
    else:
        gains = lax.all_gather(own_gains, F, axis=1, tiled=True)
        hidden_in = lax.all_gather((normed_in * gains[0]).astype(bf16), R, axis=0, tiled=True)
        ids = lax.all_gather(segment_ids, R, axis=0, tiled=True)
    gain_in, gain_mid = gains[0], gains[1]

    places = jnp.arange(length, dtype=jnp.int32)
    fresh = jnp.concatenate(
        [jnp.ones((width, 1), dtype=jnp.bool_), ids[:, 1:] != ids[:, :-1]], axis=1
    )
    positions = places[None] - lax.cummax(jnp.where(fresh, places[None], 0), axis=1)
    own_positions = lax.dynamic_slice_in_dim(positions, z * tok, tok, 1).reshape(all_tok)
    own_places = z * tok + jnp.arange(all_tok, dtype=jnp.int32) % tok
    own_starts = own_places - own_positions
    steps = all_tok // QUERY_BLOCK
    starts = own_starts.reshape(steps, 1, QUERY_BLOCK)
    query_places = own_places.reshape(steps, 1, QUERY_BLOCK)
    low = starts[:, 0, 0] // KEY_BLOCK
    high = query_places[:, 0, QUERY_BLOCK - 1] // KEY_BLOCK + 1
    cosine, sine = rope_tables(own_positions)

    if plane_kernels:
        wide_cosine = jnp.concatenate([cosine] * 4, axis=1)
        wide_sine = jnp.concatenate([-sine, sine] * 2, axis=1)
        query, kv_rows, cot_all = project(hidden_in, w_qkv, wide_cosine, wide_sine, cotangent, 3)
        kv_rows = kv_rows.reshape(width, length, 2 * HEAD_DIM)
        cot_all = cot_all.reshape(all_tok, model)
    else:
        qkv = dot(hidden_in, w_qkv)
        query = rotate(qkv[:, :qw].reshape(all_tok, heads, HEAD_DIM), cosine, sine, 1.0)
        query = query.astype(bf16).reshape(all_tok, qw)
        key = rotate(qkv[:, None, qw : qw + HEAD_DIM], cosine, sine, 1.0).astype(bf16)[:, 0]
        value = qkv[:, qw + HEAD_DIM :].astype(bf16)
        kv_rows = (
            lax.all_gather(jnp.concatenate([key, value], axis=1), F, axis=0, tiled=False)
            .reshape(planes, width, tok, 2 * HEAD_DIM)
            .transpose(1, 0, 2, 3)
            .reshape(width, length, 2 * HEAD_DIM)
        )
        cot_all = lax.all_gather(cotangent, R, axis=0, tiled=True)
    common = [("tokens", query), ("sequence", kv_rows), ("row", starts), ("row", query_places)]
    mixed, log_totals = attention_call(
        attention_kernel,
        heads,
        low,
        high,
        common,
        [
            ("tokens", jax.ShapeDtypeStruct((all_tok, qw), bf16)),
            ("row", jax.ShapeDtypeStruct((steps, 1, heads * QUERY_BLOCK), f32)),
        ],
    )
    branch = plane_scatter(dot(mixed, w_out).astype(bf16), 1)
    middle = tok_float + branch
    scale_mid = inverse_rms(middle)
    normed_mid = middle * scale_mid

    hidden_mid = plane_gather((normed_mid * gain_mid).astype(bf16), 2)
    if plane_kernels:
        out_part, grad_hidden_mid, feed_part, down_part = feed_forward(
            hidden_mid.reshape(width, tok, model),
            cot_all.reshape(width, tok, model),
            w_feed,
            w_down,
            5,
        )
        out_part = out_part.reshape(all_tok, model)
    else:
        w_gate, w_up = w_feed[:, :hidden_units], w_feed[:, hidden_units:]
        gate_acc = dot(hidden_mid, w_gate)
        up_acc = dot(hidden_mid, w_up)
        gate_sig = jax.nn.sigmoid(gate_acc)
        gate_silu = gate_acc * gate_sig
        inner_act = (gate_silu * up_acc).astype(bf16)
        out_part = dot(inner_act, w_down).astype(bf16)
        grad_inner = dot(cot_all, w_down, 1, 1)
        grad_gate = grad_inner * up_acc * gate_sig * (1.0 + gate_acc * (1.0 - gate_sig))
        grad_gate = grad_gate.astype(bf16)
        grad_up = (grad_inner * gate_silu).astype(bf16)
        feed_part = jnp.concatenate(
            [dot(hidden_mid, grad_gate, 0, 0), dot(hidden_mid, grad_up, 0, 0)], axis=1
        ).astype(bf16)
        down_part = dot(inner_act, cot_all, 0, 0).astype(bf16)
        grad_hidden_part = dot(grad_gate, w_gate, 1, 1) + dot(grad_up, w_up, 1, 1)
        grad_hidden_mid = plane_scatter(grad_hidden_part.astype(bf16), 5)
    feed_out = plane_scatter(out_part, 4)
    activations = (middle + feed_out).astype(bf16)
    feed_rows = line_scatter(feed_part)
    down_rows = line_scatter(down_part)
    gain_mid_term = jnp.sum(grad_hidden_mid * normed_mid, axis=0)
    grad_normed_mid = grad_hidden_mid * gain_mid
    grad_middle = cotangent.astype(f32) + scale_mid * (
        grad_normed_mid - normed_mid * jnp.mean(grad_normed_mid * normed_mid, axis=1, keepdims=True)
    )

    grad_branch = plane_gather(grad_middle.astype(bf16), 6)
    grad_mixed = dot(grad_branch, w_out, 1, 1).astype(bf16)
    out_part = dot(mixed, grad_branch, 0, 0).astype(bf16)
    out_rows = line_scatter(
        lax.all_to_all(out_part, R, split_axis=1, concat_axis=0, tiled=True)
    )

    grad_mixed, feed_rows = lax.optimization_barrier((grad_mixed, feed_rows))
    gq, gkv = attention_call(
        attention_back_kernel,
        heads,
        low,
        high,
        common + [("tokens", grad_mixed), ("tokens", mixed), ("row", log_totals)],
        [
            ("tokens", jax.ShapeDtypeStruct((all_tok, qw), f32)),
            ("sequence", jax.ShapeDtypeStruct((width, length, 2 * HEAD_DIM), bf16)),
        ],
        [pltpu.VMEM((length, 2 * HEAD_DIM), f32)],
    )
    if plane_kernels:
        grad_qkv = return_keys(gkv, gq, wide_cosine, wide_sine, 10)
    else:
        gkv = gkv.reshape(width, planes, tok, 2 * HEAD_DIM).transpose(1, 0, 2, 3)
        gkv = line_scatter(gkv.reshape(planes * all_tok, 2 * HEAD_DIM)).astype(f32)
        gq = rotate(gq.reshape(all_tok, heads, HEAD_DIM), cosine, sine, -1.0)
        gk = rotate(gkv[:, None, :HEAD_DIM], cosine, sine, -1.0)[:, 0]
        grad_qkv = jnp.concatenate([gq.reshape(all_tok, qw), gk, gkv[:, HEAD_DIM:]], axis=1)
        grad_qkv = grad_qkv.astype(bf16)
    hidden_part = dot(grad_qkv, w_qkv, 1, 1).astype(bf16)
    hidden_part, down_rows = lax.optimization_barrier((hidden_part, down_rows))
    grad_hidden_in = plane_scatter(hidden_part, 7)
    qkv_rows = line_scatter(dot(hidden_in, grad_qkv, 0, 0).astype(bf16))
    gain_in_term = jnp.sum(grad_hidden_in * normed_in, axis=0)
    grad_normed_in = grad_hidden_in * gain_in
    input_grad = (
        grad_middle
        + scale_in
        * (
            grad_normed_in
            - normed_in * jnp.mean(grad_normed_in * normed_in, axis=1, keepdims=True)
        )
    ).astype(bf16)

    gain_terms = lax.psum(
        lax.psum_scatter(
            jnp.stack([gain_in_term, gain_mid_term]), F, scatter_dimension=1, tiled=True
        ),
        R,
    )
    rows = model // planes

    def spread(x, call=None):
        x = lax.all_gather(x, R, axis=0, tiled=True) if call is None else plane_gather(x, call, 2)
        return x.reshape(width, x.shape[0] // width, x.shape[1])

    down_grad = spread(down_rows).reshape(feed // planes, model).astype(f32)
    gate_grad, up_grad = join_call(
        functools.partial(join_feed_kernel, planes, piece), [spread(feed_rows)], [feed, feed]
    )
    query_grad, key_grad, value_grad, out_grad = join_call(
        functools.partial(join_attention_kernel, width // KV_HEADS),
        [spread(qkv_rows, 9), spread(out_rows, 8)],
        [width * qw, KV_HEADS * HEAD_DIM, KV_HEADS * HEAD_DIM, model],
    )
    return (
        activations,
        input_grad,
        gain_terms[0],
        query_grad,
        key_grad,
        value_grad,
        out_grad,
        gain_terms[1],
        gate_grad,
        up_grad,
        down_grad,
    )


def solution(mesh):
    tok = P((R, F), None)
    row = P(F, None)
    in_specs = (tok, P(R, None), P(F), row, row, row, row, P(F), row, row, row, tok)
    out_specs = (tok, tok, P(F), row, row, row, row, P(F), row, row, row)
    return jax.shard_map(
        per_device, mesh=mesh, in_specs=in_specs, out_specs=out_specs, check_vma=False
    )
```

```python
import functools
import math

import jax
import jax.numpy as jnp
from jax import lax
from jax.experimental import pallas as pl
from jax.experimental.pallas import tpu as pltpu
from jax.sharding import PartitionSpec as P

HEADS = 32
KV_HEADS = 4
HEAD_DIM = 64
EPSILON = 1e-05
NEGATIVE = -1e30
R = "replica"
F = "fsdp"
MESH = pl.DeviceIdType.MESH
DMA = pltpu.SemaphoreType.DMA
ANY = pl.BlockSpec(memory_space=pl.ANY)
KEY_BLOCK = 256
QUERY_BLOCK = 128
PARTS = 2
FIRST_DOC = 800


def inverse_rms(values):
    return lax.rsqrt(jnp.mean(values * values, axis=1, keepdims=True) + EPSILON)


def rope_tables(positions, repeats=1):
    half_dim = HEAD_DIM // 2
    places = jnp.arange(repeats * half_dim, dtype=jnp.int32) % half_dim
    freq_rates = jnp.exp(places.astype(jnp.float32) * (-math.log(10000.0) / half_dim))
    angles = positions.astype(jnp.float32)[:, None] * freq_rates[None, :]
    return (jnp.cos(angles), jnp.sin(angles))


def rotate(tensor, cosine_table, sine_table, sign):
    half_dim = HEAD_DIM // 2
    low, up = tensor[..., :half_dim], tensor[..., half_dim:]
    cos_part = cosine_table[:, None, :]
    sin_part = sine_table[:, None, :] * sign
    return jnp.concatenate(
        [low * cos_part - up * sin_part, up * cos_part + low * sin_part], axis=-1
    )


def dot(a, b, ca=1, cb=0):
    return lax.dot_general(a, b, (((ca,), (cb,)), ((), ())), preferred_element_type=jnp.float32)


def remote(src, dst, sems, index, device):
    return pltpu.make_async_remote_copy(
        src_ref=src,
        dst_ref=dst,
        send_sem=sems[0].at[index],
        recv_sem=sems[1].at[index],
        device_id={R: device},
        device_id_type=MESH,
    )


def greet(*devices):
    barrier = pltpu.get_barrier_semaphore()
    for device in devices:
        pl.semaphore_signal(barrier, inc=1, device_id={R: device}, device_id_type=MESH)
    pl.semaphore_wait(barrier, len(devices))


class Gather:
    @staticmethod
    def scratch(count):
        return [DMA((count,))] * 6 + [DMA((4, count))] * 2

    def __init__(self, items, sems):
        self.items, self.count = items, len(items)
        self.half = self.count // 2
        self.me = lax.axis_index(R)
        self.sibling, self.x, self.y = self.me + 1 - 2 * lax.rem(self.me, 2), self.me ^ 2, self.me ^ 4
        self.across = self.me ^ 6
        self.sems = sems
        self.copies = {}

    def send(self, kind, i, owner, device):
        own, slot = self.items[i]
        sems = self.sems[2 * min(kind, 3) : 2 * min(kind, 3) + 2]
        index = i if kind < 3 else (kind - 3, i)
        src = own if owner is self.me else slot(owner)
        copy = remote(src, slot(owner), sems, index, device)
        copy.start()
        self.copies[kind, i] = copy

    def start(self, kept=()):
        ready = [i for i in range(self.count) if i not in kept]
        for i in ready:
            self.send(0, i, self.me, self.x)
            self.send(1, ready[(ready.index(i) + self.half) % len(ready)], self.me, self.y)
        for i in ready:
            self.send(3, i, self.me, self.sibling)

    def start_kept(self, kept):
        for i in kept:
            self.send(0, i, self.me, self.x)
            self.send(1, i, self.me, self.y)
            self.send(3, i, self.me, self.sibling)

    def relay(self, i):
        j = (i + self.half) % self.count
        self.copies[0, i].wait_recv()
        if i < self.half:
            self.send(2, i, self.x, self.y)
        self.send(4, i, self.x, self.sibling)
        self.copies[1, j].wait_recv()
        if j >= self.half:
            self.send(2, j, self.y, self.x)
        self.send(5, j, self.y, self.sibling)

    def finish(self):
        for i in range(self.half):
            for j in (i, self.half + i):
                if j < self.count and (2, j) in self.copies and (6, j) not in self.copies:
                    self.copies[2, j].wait_recv()
                    self.send(6, j, self.across, self.sibling)
        for i in range(self.count):
            if (6, i) not in self.copies:
                self.copies[2, i].wait_recv()
                self.send(6, i, self.across, self.sibling)
        for (kind, _), copy in self.copies.items():
            if kind < 3:
                copy.wait_send()
            else:
                copy.wait()


def row_items(x, out, chunks):
    size = x.shape[0] // chunks

    def item(i):
        part = pl.ds(i * size, size)
        return x.at[part], lambda owner: out.at[owner, part]

    return [item(i) for i in range(chunks)]


def gather_kernel(chunks, x, out, local_sem, *sems):
    gather = Gather(row_items(x, out, chunks), sems)
    greet(gather.sibling, gather.x, gather.y)
    own = pltpu.make_async_copy(x, out.at[gather.me], local_sem)
    own.start()
    gather.start()
    for i in range(chunks):
        gather.relay(i)
    gather.finish()
    own.wait()


def enter_kernel(chunks, tokens, gains, ids, hidden, all_gains, all_ids, own, own_sem, to_z, at_z, *sems):
    f32 = jnp.float32
    planes = all_gains.shape[0]
    z = lax.axis_index(F)
    items = row_items(own, hidden, chunks) + [(ids, lambda owner: all_ids.at[owner])]
    gather = Gather(items, sems)
    others = [lax.rem(z + i, planes) for i in range(1, planes)]
    barrier = pltpu.get_barrier_semaphore()
    for other in others:
        pl.semaphore_signal(barrier, inc=1, device_id={F: other}, device_id_type=MESH)
    for device in (gather.sibling, gather.x, gather.y):
        pl.semaphore_signal(barrier, inc=1, device_id={R: device}, device_id_type=MESH)
    pl.semaphore_wait(barrier, planes + 2)
    copies = [
        pltpu.make_async_remote_copy(
            src_ref=gains,
            dst_ref=all_gains.at[z],
            send_sem=to_z.at[i],
            recv_sem=at_z.at[i],
            device_id={F: other},
            device_id_type=MESH,
        )
        for i, other in enumerate(others)
    ]
    for copy in copies:
        copy.start()
    all_gains[z] = gains[...]
    all_ids[gather.me] = ids[...]
    size = tokens.shape[0] // chunks
    scales = [
        inverse_rms(tokens[i * size : (i + 1) * size, :].astype(f32)) for i in range(chunks)
    ]
    for copy in copies:
        copy.wait()
    gain = jnp.concatenate([all_gains[p, 0:1] for p in range(planes)], axis=1)
    for i in range(chunks):
        part = slice(i * size, (i + 1) * size)
        own[part, :] = (tokens[part, :].astype(f32) * scales[i] * gain).astype(jnp.bfloat16)
    kept = pltpu.make_async_copy(own, hidden.at[gather.me], own_sem)
    kept.start()
    gather.start()
    for i in range(gather.count):
        gather.relay(i)
    gather.finish()
    kept.wait()


def turn(x, cosine, sine):
    half_dim = HEAD_DIM // 2
    low = lax.rem(lax.broadcasted_iota(jnp.int32, x.shape, 1), HEAD_DIM) < half_dim
    swapped = jnp.where(low, pltpu.roll(x, 2 * HEAD_DIM - half_dim, 1), pltpu.roll(x, half_dim, 1))
    return x * cosine + swapped * sine


def turn_keys(x, cosine, sine):
    is_key = lax.broadcasted_iota(jnp.int32, x.shape, 1) < HEAD_DIM
    return jnp.where(is_key, turn(x, cosine, sine), x)


def along_line(src, dst, sems, index, plane):
    return pltpu.make_async_remote_copy(
        src_ref=src,
        dst_ref=dst,
        send_sem=sems[0].at[index],
        recv_sem=sems[1].at[index],
        device_id={F: plane},
        device_id_type=MESH,
    )


def project_kernel(
    chunks, hidden, weight, cosine, sine, cotangent, query, kv, cot_all,
    own, own_sem, cot_sem, to_line, at_line, to_sib, at_sib, *sems,
):
    bf16 = jnp.bfloat16
    planes = kv.shape[1]
    z = lax.axis_index(F)
    tok = cotangent.shape[0]
    width = kv.shape[0]
    count = width // 2
    gather = Gather(row_items(cotangent, cot_all, chunks), sems)
    core = lax.rem(gather.me, 2)
    mine = pl.ds(core * count, count)
    above, below = lax.rem(z + 1, planes), lax.rem(z + planes - 1, planes)
    barrier = pltpu.get_barrier_semaphore()
    for other in (above, below):
        pl.semaphore_signal(barrier, inc=1, device_id={F: other}, device_id_type=MESH)
    for device in (gather.sibling, gather.x, gather.y):
        pl.semaphore_signal(barrier, inc=1, device_id={R: device}, device_id_type=MESH)
    pl.semaphore_wait(barrier, 5)
    kept_cot = pltpu.make_async_copy(cotangent, cot_all.at[gather.me], cot_sem)
    kept_cot.start()
    gather.start()

    def tile(i, carry):
        s = lax.rem(core * count + i, width)
        rows = pl.ds(pl.multiple_of(s * tok, tok), tok)
        acc = dot(hidden[rows, :], weight[...])
        c, n = cosine[rows, :], sine[rows, :]
        columns = acc.shape[1] - 2 * HEAD_DIM
        for first in range(0, columns, 2 * HEAD_DIM):
            part = slice(first, first + 2 * HEAD_DIM)
            query[rows, part] = turn(acc[:, part], c, n).astype(bf16)
        own[s] = turn_keys(acc[:, columns:], c, n).astype(bf16)
        return carry

    class Group:
        def __init__(self, make):
            self.each = [make(i) for i in range(count)]

        def __getattr__(self, name):
            def call():
                for copy in self.each:
                    getattr(copy, name)()

            return call

    def up(step):
        slot = z - step

        def make(i):
            dst = kv.at[core * count + i, slot]
            src = own.at[core * count + i] if step == 0 else dst
            return along_line(src, dst, (to_line, at_line), (step, i), above)

        return Group(make)

    def came(step):
        def make(i):
            dst = kv.at[core * count + i, z - step]
            return along_line(dst, dst, (to_line, at_line), (step - 1, i), above)

        return Group(make)

    def across(step):
        slot = z - step
        return remote(kv.at[mine, slot], kv.at[mine, slot], (to_sib, at_sib), step, gather.sibling)

    lax.fori_loop(0, count, tile, 0)

    @pl.when(z < planes - 1)
    def _():
        up(0).start()

    lax.fori_loop(count, width, tile, 0)
    kept = pltpu.make_async_copy(own, kv.at[:, z], own_sem)
    kept.start()
    done = 0
    for step in range(1, planes):

        @pl.when(z >= step)
        def _():
            came(step).wait_recv()

            @pl.when(z < planes - 1)
            def _():
                up(step).start()

            across(step).start()

        while done < chunks * step // planes:
            gather.relay(done)
            done += 1
    for i in range(done, chunks):
        gather.relay(i)
    gather.finish()
    for step in range(planes):

        @pl.when((z >= step) & (z < planes - 1))
        def _():
            up(step).wait_send()

        if step:

            @pl.when(z >= step)
            def _():
                across(step).wait()

    kept.wait()
    kept_cot.wait()


def finish_kernel(
    qkv, out_rows, terms, all_qkv, all_out, gains, own_gain, all_gains,
    at_planes, own_sems, to_z, at_z, *sems,
):
    planes = terms.shape[0]
    z = lax.axis_index(F)
    chunks = [x for pair in zip(row_items(qkv, all_qkv, 2), row_items(out_rows, all_out, 2)) for x in pair]
    gather = Gather(chunks + [(own_gain, lambda owner: all_gains.at[owner])], sems)
    me, last = gather.me, gather.count - 1
    others = [lax.rem(z + i, planes) for i in range(1, planes)]
    barrier = pltpu.get_barrier_semaphore()
    for other in others:
        pl.semaphore_signal(barrier, inc=1, device_id={F: other}, device_id_type=MESH)
    for device in (gather.sibling, gather.x, gather.y):
        pl.semaphore_signal(barrier, inc=1, device_id={R: device}, device_id_type=MESH)
    pl.semaphore_wait(barrier, planes + 2)
    copies = [
        along_line(terms.at[other], at_planes.at[i], (to_z, at_z), i, other)
        for i, other in enumerate(others)
    ]
    for copy in copies:
        copy.start()
    kept = [
        pltpu.make_async_copy(qkv, all_qkv.at[me], own_sems.at[0]),
        pltpu.make_async_copy(out_rows, all_out.at[me], own_sems.at[1]),
    ]
    for copy in kept:
        copy.start()
    gather.start((last,))
    total = terms[z]
    for i, copy in enumerate(copies):
        copy.wait()
        total = total + at_planes[i]
    own_gain[...] = total
    all_gains[me] = total
    gather.start_kept((last,))
    for i in range(gather.count):
        gather.relay(i)
    gather.finish()
    total = all_gains[0]
    for device in range(1, all_gains.shape[0]):
        total = total + all_gains[device]
    gains[...] = total
    for copy in kept:
        copy.wait()


def finish(qkv, out_rows, terms, call):
    planes, width = lax.axis_size(F), lax.axis_size(R)
    f32, bf16 = jnp.float32, jnp.bfloat16
    vmem = pl.BlockSpec(memory_space=pltpu.VMEM)
    block = terms.shape[1:]
    return pl.pallas_call(
        finish_kernel,
        out_shape=[
            jax.ShapeDtypeStruct((width,) + qkv.shape, bf16),
            jax.ShapeDtypeStruct((width,) + out_rows.shape, bf16),
            jax.ShapeDtypeStruct(block, f32),
        ],
        in_specs=[ANY, ANY, vmem],
        out_specs=[ANY, ANY, vmem],
        scratch_shapes=[
            pltpu.VMEM(block, f32),
            pltpu.VMEM((width,) + block, f32),
            pltpu.VMEM((planes - 1,) + block, f32),
            DMA((2,)),
            DMA((planes - 1,)),
            DMA((planes - 1,)),
        ]
        + Gather.scratch(5),
        compiler_params=pltpu.CompilerParams(collective_id=call, has_side_effects=True),
    )(qkv, out_rows, terms)


class Scatter:
    @staticmethod
    def scratch(rows, columns, chunks):
        bf16, size = jnp.bfloat16, rows // chunks
        return [
            pltpu.VMEM((5, rows, columns), bf16),
            pltpu.VMEM((4, rows, columns), bf16),
            pltpu.VMEM((chunks, 2, size, columns), bf16),
            pltpu.VMEM((chunks, size, columns), bf16),
            pltpu.VMEM((2, size, columns), jnp.float32),
            DMA((4,)),
            DMA((4,)),
            DMA((chunks, 2)),
            DMA((chunks, 2)),
            DMA((chunks,)),
            DMA((chunks,)),
            DMA((2,)),
        ]

    def __init__(self, out, chunks, refs):
        self.out, self.chunks, self.half = out, chunks, chunks // 2
        self.own, self.sib, self.got, self.got_far, self.total = refs[:5]
        self.sib_sems, self.near_sems, self.far_sems = refs[5:7], refs[7:9], refs[9:11]
        self.out_sem = refs[11]
        self.me = lax.axis_index(R)
        self.sibling, self.x, self.y = self.me + 1 - 2 * lax.rem(self.me, 2), self.me ^ 2, self.me ^ 4
        self.size = out.shape[0] // chunks
        self.order = [*range(self.half, chunks), *range(self.half)]
        self.trades = None

    def owner(self, i):
        return (self.me ^ (6 - 2 * (i // 2))) ^ (1 - lax.rem(i, 2))

    def trade(self, d):
        return remote(self.own.at[4], self.sib.at[d], self.sib_sems, d, self.sibling)

    def put(self, i, value):
        d = 3 - i // 2
        for_sibling = lax.rem(i, 2) == 0

        @pl.when(for_sibling & (i >= 2))
        def _():
            self.trade(d + 1).wait_send()

        self.own[jnp.where(for_sibling, 4, d)] = value

        @pl.when(for_sibling)
        def _():
            self.trade(d).start()

    def take(self, part, sems):
        self.loads, self.trades = {}, {}
        for d in (3, 2, 1, 0):
            self.loads[d] = pltpu.make_async_copy(part.at[self.me ^ (2 * d)], self.own.at[d], sems.at[d])
            self.loads[d].start()
        for d in (3, 2, 1, 0):
            self.trades[d] = remote(
                part.at[self.sibling ^ (2 * d)], self.sib.at[d], self.sib_sems, d, self.sibling
            )
            self.trades[d].start()

    def taken(self, d):
        self.loads[d].wait()
        self.trades[d].wait_recv()

    def arrived(self, d):
        self.trade(d).wait_recv()

    def part(self, j):
        return pl.ds(j * self.size, self.size)

    def summed(self, d, j):
        part = self.part(j)
        return self.own[d, part].astype(jnp.float32) + self.sib[d, part].astype(jnp.float32)

    def near_copies(self, j):
        device, d = (self.x, 1) if j < self.half else (self.y, 2)
        return [
            remote(self.own.at[e, self.part(j)], self.got.at[j, n], self.near_sems, (j, n), device)
            for n, e in enumerate((d, 3))
        ]

    def far_copy(self, j):
        device, d = (self.y, 2) if j < self.half else (self.x, 1)
        return remote(self.own.at[d, self.part(j)], self.got_far.at[j], self.far_sems, j, device)

    def out_copy(self, j):
        slot = self.order.index(j) % 2
        return pltpu.make_async_copy(
            self.total.at[slot], self.out.at[self.part(j)], self.out_sem.at[slot]
        )

    def near(self, j):
        for e in (1 if j < self.half else 2, 3):
            self.own[e, self.part(j)] = self.summed(e, j).astype(jnp.bfloat16)
        for copy in self.near_copies(j):
            copy.start()

    def far(self, j):
        for copy in self.near_copies(j):
            copy.wait_recv()
        d = 2 if j < self.half else 1
        passed = self.summed(d, j) + self.got[j, 1].astype(jnp.float32)
        self.own[d, self.part(j)] = passed.astype(jnp.bfloat16)
        self.far_copy(j).start()

    def last(self, j):
        self.far_copy(j).wait_recv()
        turn = self.order.index(j)
        if turn >= 2:
            self.out_copy(self.order[turn - 2]).wait()
        self.total[turn % 2] = (
            self.summed(0, j)
            + self.got[j, 0].astype(jnp.float32)
            + self.got_far[j].astype(jnp.float32)
        )
        self.out_copy(j).start()

    def finish(self):
        if self.trades is None:
            self.trade(0).wait_send()
        else:
            for copy in self.trades.values():
                copy.wait_send()
        for j in self.order[-2:]:
            self.out_copy(j).wait()
        for j in range(self.chunks):
            self.far_copy(j).wait_send()
            for copy in self.near_copies(j):
                copy.wait_send()


def feed_in_kernel(hidden, cotangent, w_feed, acts, down_part, inner_turned):
    width, _, tok = inner_turned.shape
    units = w_feed.shape[1] // 2
    i = pl.program_id(0)

    @pl.when(i < width)
    def _():
        acc = dot(hidden[0], w_feed[...])
        acts[0] = acc
        gate, up = acc[:, :units], acc[:, units:]
        inner_turned[i] = (gate / (1.0 + jnp.exp(-gate)) * up).astype(jnp.bfloat16).T

    @pl.when(i >= width)
    def _():
        acc = dot(inner_turned[0], cotangent[0])
        for s in range(1, width):
            acc = acc + dot(inner_turned[s], cotangent[s])
        down_part[...] = acc.astype(jnp.bfloat16)


def feed_in(hidden, cotangent, w_feed):
    width, tok, model = hidden.shape
    units = w_feed.shape[1] // 2
    tiles = model // tok
    return pl.pallas_call(
        feed_in_kernel,
        grid=(width + tiles,),
        out_shape=[
            jax.ShapeDtypeStruct((width, tok, 2 * units), jnp.float32),
            jax.ShapeDtypeStruct((units, model), jnp.bfloat16),
        ],
        in_specs=[
            pl.BlockSpec((1, tok, model), lambda i: (jnp.minimum(i, width - 1), 0, 0)),
            pl.BlockSpec((width, tok, tok), lambda i: (0, 0, jnp.maximum(i - width, 0))),
            pl.BlockSpec(memory_space=pltpu.VMEM),
        ],
        out_specs=[
            pl.BlockSpec((1, tok, 2 * units), lambda i: (jnp.minimum(i, width - 1), 0, 0)),
            pl.BlockSpec((units, tok), lambda i: (0, jnp.maximum(i - width, 0))),
        ],
        scratch_shapes=[pltpu.VMEM((width, units, tok), jnp.bfloat16)],
        compiler_params=pltpu.CompilerParams(vmem_limit_bytes=48 << 20),
    )(hidden, cotangent, w_feed)


def feed_kernel(
    chunks, hidden, cotangent, acts, w_feed, w_down, out_part, grad_hidden, feed_part,
    acts_in, cot_in, grads, column_in, feed_stage, out_stage, in_sems, column_sems, feed_sem, out_sem,
    *refs,
):
    f32, bf16 = jnp.float32, jnp.bfloat16
    width, tok, model = hidden.shape
    units = w_down.shape[0]
    scatter = Scatter(grad_hidden, chunks, refs)
    half = chunks // 2
    first_half, second_half = range(half), range(half, chunks)

    def loads(i):
        slot, owner = lax.rem(i, 2), scatter.owner(i)
        return [
            pltpu.make_async_copy(acts.at[owner], acts_in.at[slot], in_sems.at[0, slot]),
            pltpu.make_async_copy(cotangent.at[owner], cot_in.at[slot], in_sems.at[1, slot]),
        ]

    def out_copy(i):
        slot = lax.rem(i, 2)
        return pltpu.make_async_copy(
            out_stage.at[slot], out_part.at[scatter.owner(i)], out_sem.at[slot]
        )

    for i in (0, 1):
        for copy in loads(i):
            copy.start()
    greet(scatter.sibling, scatter.x, scatter.y)

    def block(i, carry):
        slot = lax.rem(i, 2)
        rows = pl.ds(pl.multiple_of(i * tok, tok), tok)
        for copy in loads(i):
            copy.wait()
        gate, up = acts_in[slot, :, :units], acts_in[slot, :, units:]
        gate_sig = 1.0 / (1.0 + jnp.exp(-gate))
        gate_silu = gate * gate_sig
        inner = (gate_silu * up).astype(bf16)
        grad_inner = dot(cot_in[slot], w_down[...], 1, 1)
        grad_gate = grad_inner * up * gate_sig * (1.0 + gate * (1.0 - gate_sig))
        both = jnp.concatenate([grad_gate, grad_inner * gate_silu], axis=1).astype(bf16)
        grads[rows, :] = both
        scatter.put(i, dot(both, w_feed[...], 1, 1).astype(bf16))

        @pl.when(i >= 2)
        def _():
            out_copy(i - 2).wait()

        out_stage[slot] = dot(inner, w_down[...]).astype(bf16)
        out_copy(i).start()

        @pl.when(i + 2 < width)
        def _():
            for copy in loads(i + 2):
                copy.start()

        @pl.when(i == 4)
        def _():
            scatter.arrived(3)
            scatter.arrived(2)
            for j in second_half:
                scatter.near(j)

        @pl.when(i == 6)
        def _():
            scatter.arrived(1)
            for j in first_half:
                scatter.near(j)

        return carry

    tiles = model // tok

    def column_loads(n):
        slot = lax.rem(n, 2)
        part = pl.ds(pl.multiple_of(n * tok, tok), tok)
        return [
            pltpu.make_async_copy(
                hidden.at[scatter.owner(i), :, part],
                column_in.at[slot, pl.ds(i * tok, tok)],
                column_sems.at[slot, i],
            )
            for i in range(width)
        ]

    def feed_copy(n):
        rows = pl.ds(pl.multiple_of(n * tok, tok), tok)
        slot = lax.rem(n, 2)
        return pltpu.make_async_copy(feed_stage.at[slot], feed_part.at[rows], feed_sem.at[slot])

    def feed_tile(n, carry):
        slot = lax.rem(n, 2)
        for copy in column_loads(n):
            copy.wait()

        @pl.when(n >= 2)
        def _():
            feed_copy(n - 2).wait()

        feed_stage[slot] = dot(column_in[slot], grads[...], 0, 0).astype(bf16)
        feed_copy(n).start()

        @pl.when(n + 2 < tiles)
        def _():
            for copy in column_loads(n + 2):
                copy.start()

        @pl.when(n == 2)
        def _():
            for j in second_half:
                scatter.far(j)

        @pl.when(n == 5)
        def _():
            for j in first_half:
                scatter.far(j)

        return carry

    for n in (0, 1):
        for copy in column_loads(n):
            copy.start()
    lax.fori_loop(0, width, block, 0)
    scatter.arrived(0)
    lax.fori_loop(0, tiles, feed_tile, 0)
    for j in scatter.order:
        scatter.last(j)
    scatter.finish()
    for i in (width - 2, width - 1):
        out_copy(i).wait()
    for n in (tiles - 2, tiles - 1):
        feed_copy(n).wait()


def feed_forward(hidden, cotangent, acts, w_feed, w_down, call, chunks=4):
    width, tok, model = hidden.shape
    units = w_down.shape[0]
    bf16 = jnp.bfloat16
    vmem = pl.BlockSpec(memory_space=pltpu.VMEM)
    return pl.pallas_call(
        functools.partial(feed_kernel, chunks),
        out_shape=[
            jax.ShapeDtypeStruct((width, tok, model), bf16),
            jax.ShapeDtypeStruct((tok, model), jnp.float32),
            jax.ShapeDtypeStruct((model, 2 * units), bf16),
        ],
        in_specs=[ANY, ANY, ANY, vmem, vmem],
        out_specs=[ANY] * 3,
        scratch_shapes=[
            pltpu.VMEM((2, tok, 2 * units), jnp.float32),
            pltpu.VMEM((2, tok, model), bf16),
            pltpu.VMEM((width * tok, 2 * units), bf16),
            pltpu.VMEM((2, width * tok, tok), bf16),
            pltpu.VMEM((2, tok, 2 * units), bf16),
            pltpu.VMEM((2, tok, model), bf16),
            DMA((2, 2)),
            DMA((2, width)),
            DMA((2,)),
            DMA((2,)),
        ]
        + Scatter.scratch(tok, model, chunks),
        compiler_params=pltpu.CompilerParams(
            collective_id=call, has_side_effects=True, vmem_limit_bytes=62 << 20
        ),
    )(hidden, cotangent, acts, w_feed, w_down)


def back_kernel(
    chunks, heads, q, kv, starts, places, grad, mixed, log_total, cosine, sine, out_part, down_rows, w_part,
    grad_qkv, feed_out, all_down, w_rows,
    sums, grad_kv, from_sib, inbox, outbox, to_sib, at_sib, to_line, at_line, down_sem, w_sem,
    to_all, at_all, load_sems, *refs,
):
    f32, bf16 = jnp.float32, jnp.bfloat16
    planes, count, tok = inbox.shape[0], inbox.shape[1], inbox.shape[2]
    width = 2 * count
    columns = heads * HEAD_DIM
    z, me = lax.axis_index(F), lax.axis_index(R)
    core = lax.rem(me, 2)
    above, below = lax.rem(z + 1, planes), lax.rem(z + planes - 1, planes)
    scatter = Scatter(feed_out, chunks, refs[:12])
    gather = Gather([(down_rows, lambda owner: all_down.at[owner])] * 1, refs[12:])
    half = chunks // 2
    barrier = pltpu.get_barrier_semaphore()
    for other in (above, below):
        pl.semaphore_signal(barrier, inc=1, device_id={F: other}, device_id_type=MESH)
    peers = [me ^ distance for distance in range(1, width)]
    for device in peers:
        pl.semaphore_signal(barrier, inc=1, device_id={R: device}, device_id_type=MESH)
    pl.semaphore_wait(barrier, 1 + width)
    share = w_part.shape[1] // width

    def share_of(device):
        return w_part.at[:, pl.ds(pl.multiple_of(device * share, share), share)]

    w_copies = [
        remote(share_of(device), w_rows.at[me], (to_all, at_all), i, device)
        for i, device in enumerate(peers)
    ]
    w_kept = pltpu.make_async_copy(share_of(me), w_rows.at[me], w_sem)
    for copy in [w_kept] + w_copies:
        copy.start()
    scatter.take(out_part, load_sems)
    kept = pltpu.make_async_copy(down_rows, all_down.at[me], down_sem)
    kept.start()
    parts = tok // QUERY_BLOCK

    def step(n, carry):
        s, sub = n // parts, lax.rem(n, parts)
        rows = pl.ds(pl.multiple_of(n * QUERY_BLOCK, QUERY_BLOCK), QUERY_BLOCK)
        queries = heads_to_rows(q[rows, :] * bf16(HEAD_DIM**-0.5), heads)
        grads = heads_to_rows(grad[rows, :], heads)
        first = jnp.concatenate([starts[n]] * heads, axis=1)
        place = jnp.concatenate([places[n]] * heads, axis=1)
        products = grads.astype(f32) * heads_to_rows(mixed[rows, :], heads).astype(f32)
        delta = lax.dot_general(
            jnp.ones((8, 2 * HEAD_DIM), f32),
            products,
            (((1,), (1,)), ((), ())),
            precision=lax.Precision.HIGHEST,
            preferred_element_type=f32,
        )[:1]
        level = log_total[n]
        upper = pltpu.roll(grads.astype(f32), HEAD_DIM, 1).astype(bf16)

        @pl.when(sub == 0)
        def _():
            sums[...] = jnp.zeros_like(sums)

        def block(index, acc):
            part = pl.ds(pl.multiple_of(index * KEY_BLOCK, KEY_BLOCK), KEY_BLOCK)
            keys = kv[s, part, :]
            scores = dot(keys, queries, 1, 1)
            probs = jnp.where(visible(index, first, place), jnp.exp(scores - level), 0.0)
            grad_probs = dot(keys, upper, 1, 1)
            grad_scores = (probs * (grad_probs - delta)).astype(bf16)
            sums[part, :] += dot(grad_scores, queries) + dot(probs.astype(bf16), upper)
            return acc + dot(keys, grad_scores, 0, 0)

        place_of_first = z * tok + sub * QUERY_BLOCK
        low = jnp.where(place_of_first >= FIRST_DOC, FIRST_DOC // KEY_BLOCK, 0)
        high = (place_of_first + QUERY_BLOCK - 1) // KEY_BLOCK + 1
        acc = lax.fori_loop(low, high, block, jnp.zeros((2 * HEAD_DIM, queries.shape[0]), f32))
        grad_q = rows_to_heads(acc[:HEAD_DIM] * HEAD_DIM**-0.5, heads)
        c, n_sine = cosine[rows, :], -sine[rows, :]
        for at in range(0, columns, 2 * HEAD_DIM):
            part = slice(at, at + 2 * HEAD_DIM)
            grad_qkv[rows, part] = turn(grad_q[:, part], c, n_sine).astype(bf16)
        grad_qkv[rows, columns:] = jnp.zeros((QUERY_BLOCK, 2 * HEAD_DIM), bf16)

        @pl.when(sub == parts - 1)
        def _():
            grad_kv[s] = sums[...].astype(bf16)

        return carry

    lax.fori_loop(0, width // 2, step, 0)
    for d in (3, 2):
        scatter.taken(d)
    for j in range(half, chunks):
        scatter.near(j)
    scatter.taken(1)
    for j in range(half):
        scatter.near(j)
    gather.start()
    lax.fori_loop(width // 2, width * parts, step, 0)

    def block_of(which, b):
        return grad_kv.at[pl.ds(which * count, count), pl.ds(b * tok, tok)]

    def trade(b):
        return remote(block_of(1 - core, b), from_sib.at[b], (to_sib, at_sib), b, scatter.sibling)

    def down(b):
        return along_line(outbox.at[b], inbox.at[b], (to_line, at_line), b, below)

    def own(b):
        part = pl.ds(b * tok, tok)
        return grad_kv[pl.ds(core * count, count), part, :].astype(f32) + from_sib[b].astype(f32)

    for b in range(planes):

        @pl.when(b <= z)
        def _():
            trade(b).start()

    scatter.taken(0)
    for b in range(planes):

        @pl.when(b <= z)
        def _():
            trade(b).wait_recv()

            @pl.when(z < planes - 1)
            def _():
                down(b).wait_recv()

        @pl.when((b < z) & (z < planes - 1))
        def _():
            outbox[b] = (own(b) + inbox[b].astype(f32)).astype(bf16)

        @pl.when((b < z) & (z == planes - 1))
        def _():
            outbox[b] = own(b).astype(bf16)

        @pl.when(b < z)
        def _():
            down(b).start()

        if b == 0:
            for j in range(half, chunks):
                scatter.far(j)
        if b == 1:
            gather.relay(0)
            for j in range(half):
                scatter.far(j)

    def keys(i, carry):
        rows = pl.ds(pl.multiple_of((core * count + i) * tok, tok), tok)
        part = pl.ds(pl.multiple_of(z * tok, tok), tok)
        total = grad_kv[core * count + i, part, :].astype(f32) + from_sib[z, i].astype(f32)
        total = total + jnp.where(z < planes - 1, inbox[z, i].astype(f32), 0.0)
        grad_qkv[rows, columns:] = turn_keys(total, cosine[rows, :], -sine[rows, :]).astype(bf16)
        return carry

    lax.fori_loop(0, count, keys, 0)
    for j in scatter.order:
        scatter.last(j)
    gather.finish()
    scatter.finish()
    for b in range(planes):

        @pl.when(b <= z)
        def _():
            trade(b).wait_send()

        @pl.when(b < z)
        def _():
            down(b).wait_send()

    for copy in [kept, w_kept] + w_copies:
        copy.wait()


def attention_back(
    heads, q, kv, starts, places, grad, mixed, log_total, cosine, sine, out_part, down_rows, w_part, call,
    chunks=4,
):
    planes, width = lax.axis_size(F), lax.axis_size(R)
    f32, bf16 = jnp.float32, jnp.bfloat16
    tok, model = out_part.shape[1:]
    length = kv.shape[1]
    vmem = pl.BlockSpec(memory_space=pltpu.VMEM)
    blocks = pltpu.VMEM((planes, width // 2, tok, 2 * HEAD_DIM), bf16)
    return pl.pallas_call(
        functools.partial(back_kernel, chunks, heads),
        out_shape=[
            jax.ShapeDtypeStruct((q.shape[0], q.shape[1] + 2 * HEAD_DIM), bf16),
            jax.ShapeDtypeStruct((tok, model), f32),
            jax.ShapeDtypeStruct((width,) + down_rows.shape, bf16),
            jax.ShapeDtypeStruct((width, w_part.shape[0], w_part.shape[1] // width), bf16),
        ],
        in_specs=[vmem] * 9 + [ANY] * 3,
        out_specs=[vmem] + [ANY] * 3,
        scratch_shapes=[
            pltpu.VMEM((length, 2 * HEAD_DIM), f32),
            pltpu.VMEM((width, length, 2 * HEAD_DIM), bf16),
            blocks,
            blocks,
            blocks,
        ]
        + [DMA((planes,))] * 4
        + [DMA, DMA, DMA((width - 1,)), DMA((width - 1,)), DMA((4,))]
        + Scatter.scratch(tok, model, chunks)
        + Gather.scratch(1),
        compiler_params=pltpu.CompilerParams(
            collective_id=call, has_side_effects=True, vmem_limit_bytes=60 << 20
        ),
    )(q, kv, starts, places, grad, mixed, log_total, cosine, sine, out_part, down_rows, w_part)


def enter(tokens, gains, ids, call, chunks=4):
    planes, rows = lax.axis_size(F), lax.axis_size(R)
    tok, model = tokens.shape
    vmem = pl.BlockSpec(memory_space=pltpu.VMEM)
    return pl.pallas_call(
        functools.partial(enter_kernel, chunks),
        out_shape=[
            jax.ShapeDtypeStruct((rows, tok, model), jnp.bfloat16),
            jax.ShapeDtypeStruct((planes,) + gains.shape, jnp.float32),
            jax.ShapeDtypeStruct((rows,) + ids.shape, jnp.int32),
        ],
        in_specs=[vmem] * 3,
        out_specs=[ANY, vmem, vmem],
        scratch_shapes=[pltpu.VMEM((tok, model), jnp.bfloat16), DMA]
        + [DMA((planes - 1,))] * 2
        + Gather.scratch(chunks + 1),
        compiler_params=pltpu.CompilerParams(
            collective_id=call, has_side_effects=True, vmem_limit_bytes=32 << 20
        ),
    )(tokens, gains, ids)


def project(hidden, weight, cosine, sine, cotangent, call, chunks=4):
    planes, width = lax.axis_size(F), lax.axis_size(R)
    tok, model = cotangent.shape
    bf16 = jnp.bfloat16
    vmem = pl.BlockSpec(memory_space=pltpu.VMEM)
    return pl.pallas_call(
        functools.partial(project_kernel, chunks),
        out_shape=[
            jax.ShapeDtypeStruct((width * tok, weight.shape[1] - 2 * HEAD_DIM), bf16),
            jax.ShapeDtypeStruct((width, planes, tok, 2 * HEAD_DIM), bf16),
            jax.ShapeDtypeStruct((width, tok, model), bf16),
        ],
        in_specs=[vmem] * 4 + [ANY],
        out_specs=[vmem, ANY, ANY],
        scratch_shapes=[pltpu.VMEM((width, tok, 2 * HEAD_DIM), bf16), DMA, DMA]
        + [DMA((planes, width // 2))] * 2
        + [DMA((planes,))] * 2
        + Gather.scratch(chunks),
        compiler_params=pltpu.CompilerParams(
            collective_id=call, has_side_effects=True, vmem_limit_bytes=40 << 20
        ),
    )(hidden, weight, cosine, sine, cotangent)


def scatter_kernel(
    chunks, part, out, own, from_sib, give, got, give_far, got_far, total,
    own_sem, out_sem, to_sib, at_sib, to_near, at_near, to_far, at_far,
):
    f32, bf16 = jnp.float32, jnp.bfloat16
    me = lax.axis_index(R)
    flip = 1 - 2 * lax.rem(me, 2)
    sibling, beside_x, beside_y = me + flip, me ^ 2, me ^ 4
    rows = out.shape[0]
    size = rows // chunks
    half = chunks // 2
    owners = [me, beside_x, beside_y, me ^ 6]
    order = [c for j in range(half) for c in (j, half + j)]

    def rows_of(device, j):
        return part.at[pl.ds(pl.multiple_of(device * rows + j * size, 16), size)]

    def own_copy(d, j):
        return pltpu.make_async_copy(rows_of(owners[d], j), own.at[d, j], own_sem.at[d, j])

    def sib_copy(d, j):
        return remote(rows_of(owners[d] + flip, j), from_sib.at[d, j], (to_sib, at_sib), (d, j), sibling)

    def near_copy(j):
        device = beside_x if j < half else beside_y
        return remote(give.at[j], got.at[j], (to_near, at_near), j, device)

    def far_copy(j):
        device = beside_y if j < half else beside_x
        return remote(give_far.at[j], got_far.at[j], (to_far, at_far), j, device)

    def out_copy(j):
        return pltpu.make_async_copy(total.at[j], out.at[pl.ds(j * size, size)], out_sem.at[j])

    def summed(d, j):
        own_copy(d, j).wait()
        sib_copy(d, j).wait_recv()
        return own[d, j].astype(f32) + from_sib[d, j].astype(f32)

    for j in order:
        for d in (1, 2, 3, 0):
            own_copy(d, j).start()
    greet(sibling, beside_x, beside_y)
    for j in order:
        for d in (1, 3, 2, 0) if j < half else (2, 3, 1, 0):
            sib_copy(d, j).start()
    for j in order:
        give[j, 0] = summed(1 if j < half else 2, j).astype(bf16)
        give[j, 1] = summed(3, j).astype(bf16)
        near_copy(j).start()
    for j in order:
        passed = summed(2 if j < half else 1, j)
        kept = summed(0, j)
        near_copy(j).wait_recv()
        give_far[j] = (passed + got[j, 1].astype(f32)).astype(bf16)
        far_copy(j).start()
        total[j] = kept + got[j, 0].astype(f32)
    for j in order:
        far_copy(j).wait_recv()
        total[j] = total[j] + got_far[j].astype(f32)
        out_copy(j).start()
    for j in order:
        out_copy(j).wait()
        near_copy(j).wait_send()
        far_copy(j).wait_send()
        for d in range(4):
            sib_copy(d, j).wait_send()


def plane_gather(x, call, chunks=4):
    width = lax.axis_size(R)
    if width != 8:
        return lax.all_gather(x, R, axis=0, tiled=True)
    out = pl.pallas_call(
        functools.partial(gather_kernel, chunks),
        out_shape=jax.ShapeDtypeStruct((width,) + x.shape, x.dtype),
        in_specs=[ANY],
        out_specs=ANY,
        scratch_shapes=[DMA] + Gather.scratch(chunks),
        compiler_params=pltpu.CompilerParams(collective_id=call, has_side_effects=True),
    )(x)
    return out.reshape((width * x.shape[0],) + x.shape[1:])


def plane_scatter(x, call, chunks=4):
    width = lax.axis_size(R)
    if width != 8:
        return lax.psum_scatter(x, R, scatter_dimension=0, tiled=True).astype(jnp.float32)
    rows, columns = x.shape[0] // width, x.shape[1]
    size = rows // chunks
    bf16 = jnp.bfloat16
    return pl.pallas_call(
        functools.partial(scatter_kernel, chunks),
        out_shape=jax.ShapeDtypeStruct((rows, columns), jnp.float32),
        in_specs=[ANY],
        out_specs=ANY,
        scratch_shapes=[
            pltpu.VMEM((4, chunks, size, columns), bf16),
            pltpu.VMEM((4, chunks, size, columns), bf16),
            pltpu.VMEM((chunks, 2, size, columns), bf16),
            pltpu.VMEM((chunks, 2, size, columns), bf16),
            pltpu.VMEM((chunks, size, columns), bf16),
            pltpu.VMEM((chunks, size, columns), bf16),
            pltpu.VMEM((chunks, size, columns), jnp.float32),
            DMA((4, chunks)),
            DMA((chunks,)),
            DMA((4, chunks)),
            DMA((4, chunks)),
        ]
        + [DMA((chunks,))] * 4,
        compiler_params=pltpu.CompilerParams(
            collective_id=call, has_side_effects=True, vmem_limit_bytes=32 << 20
        ),
    )(x)


def line_gather(x):
    return lax.all_gather(x, F, axis=0, tiled=True)


def line_scatter(x):
    return lax.psum_scatter(x, F, scatter_dimension=0, tiled=True)


def heads_to_rows(block, heads):
    parts = [block[:, h * HEAD_DIM : (h + 1) * HEAD_DIM] for h in range(heads)]
    rows = jnp.concatenate(parts, axis=0)
    return jnp.concatenate([rows, jnp.zeros_like(rows)], axis=1)


def rows_to_heads(columns, heads):
    count = columns.shape[1] // heads
    return jnp.concatenate([columns[:, h * count : (h + 1) * count].T for h in range(heads)], axis=1)


def visible(block_index, starts, places):
    keys = block_index * KEY_BLOCK + lax.broadcasted_iota(jnp.int32, (KEY_BLOCK, starts.shape[1]), 0)
    return (keys >= starts) & (keys <= places)


def attention_kernel(heads, low, high, q, kv, starts, places, mixed, log_total):
    f32, bf16 = jnp.float32, jnp.bfloat16
    step = pl.program_id(0) * pl.num_programs(1) + pl.program_id(1)
    queries = heads_to_rows(q[...] * bf16(HEAD_DIM**-0.5), heads)
    first = jnp.concatenate([starts[0]] * heads, axis=1)
    place = jnp.concatenate([places[0]] * heads, axis=1)
    columns = queries.shape[0]

    def block(index, carry):
        top, total, acc = carry
        rows = kv[0, pl.ds(pl.multiple_of(index * KEY_BLOCK, KEY_BLOCK), KEY_BLOCK), :]
        scores = jnp.where(visible(index, first, place), dot(rows, queries, 1, 1), NEGATIVE)
        new_top = jnp.maximum(top, jnp.max(scores, axis=0, keepdims=True))
        weights = jnp.exp(scores - new_top)
        fade = jnp.exp(top - new_top)
        total = total * fade + jnp.sum(weights, axis=0, keepdims=True)
        acc = acc * fade + dot(rows, weights.astype(bf16), 0, 0)
        return new_top, total, acc

    top, total, acc = lax.fori_loop(
        low[step],
        high[step],
        block,
        (
            jnp.full((1, columns), NEGATIVE, f32),
            jnp.zeros((1, columns), f32),
            jnp.zeros((2 * HEAD_DIM, columns), f32),
        ),
    )
    mixed[...] = rows_to_heads(acc[HEAD_DIM:] / total, heads).astype(bf16)
    log_total[0] = top + jnp.log(total)


def attention_back_kernel(
    heads, low, high, q, kv, starts, places, grad, mixed, log_total, grad_q, grad_kv, sums
):
    f32, bf16 = jnp.float32, jnp.bfloat16
    step = pl.program_id(0) * pl.num_programs(1) + pl.program_id(1)
    queries = heads_to_rows(q[...] * bf16(HEAD_DIM**-0.5), heads)
    grads = heads_to_rows(grad[...], heads)
    first = jnp.concatenate([starts[0]] * heads, axis=1)
    place = jnp.concatenate([places[0]] * heads, axis=1)
    columns = queries.shape[0]
    products = grads.astype(f32) * heads_to_rows(mixed[...], heads).astype(f32)
    delta = lax.dot_general(
        jnp.ones((8, 2 * HEAD_DIM), f32),
        products,
        (((1,), (1,)), ((), ())),
        precision=lax.Precision.HIGHEST,
        preferred_element_type=f32,
    )[:1]
    level = log_total[0]
    upper = pltpu.roll(grads.astype(f32), HEAD_DIM, 1).astype(bf16)

    @pl.when(pl.program_id(1) == 0)
    def _():
        sums[...] = jnp.zeros_like(sums)

    def block(index, acc):
        part = pl.ds(pl.multiple_of(index * KEY_BLOCK, KEY_BLOCK), KEY_BLOCK)
        rows = kv[0, part, :]
        scores = dot(rows, queries, 1, 1)
        probs = jnp.where(visible(index, first, place), jnp.exp(scores - level), 0.0)
        grad_probs = dot(rows, upper, 1, 1)
        grad_scores = (probs * (grad_probs - delta)).astype(bf16)
        sums[part, :] += dot(grad_scores, queries) + dot(probs.astype(bf16), upper)
        return acc + dot(rows, grad_scores, 0, 0)

    acc = lax.fori_loop(low[step], high[step], block, jnp.zeros((2 * HEAD_DIM, columns), f32))
    grad_q[...] = rows_to_heads(acc[:HEAD_DIM] * HEAD_DIM**-0.5, heads)

    @pl.when(pl.program_id(1) == PARTS - 1)
    def _():
        grad_kv[0] = sums[...].astype(bf16)


def attention_call(kernel, heads, low, high, arrays, outs, scratch=()):
    blocks = {
        "tokens": lambda shape: pl.BlockSpec((QUERY_BLOCK, shape[1]), lambda s, b, *_: (s * PARTS + b, 0)),
        "row": lambda shape: pl.BlockSpec((1,) + shape[1:], lambda s, b, *_: (s * PARTS + b, 0, 0)),
        "sequence": lambda shape: pl.BlockSpec((1,) + shape[1:], lambda s, b, *_: (s, 0, 0)),
    }
    return pl.pallas_call(
        functools.partial(kernel, heads),
        grid_spec=pltpu.PrefetchScalarGridSpec(
            num_scalar_prefetch=2,
            grid=(low.shape[0] // PARTS, PARTS),
            in_specs=[blocks[kind](x.shape) for kind, x in arrays],
            out_specs=[blocks[kind](x.shape) for kind, x in outs],
            scratch_shapes=scratch,
        ),
        out_shape=[x for _, x in outs],
        compiler_params=pltpu.CompilerParams(vmem_limit_bytes=32 << 20),
    )(low, high, *[x for _, x in arrays])


def join_feed_kernel(planes, piece, x, gate, up):
    width = x.shape[0]
    for kind, out in enumerate((gate, up)):
        for p in range(planes):
            for r in range(width):
                first = (kind * planes + p) * piece
                to = (p * width + r) * piece
                out[:, to : to + piece] = x[r, :, first : first + piece].astype(jnp.float32)


def join_attention_kernel(sharers, qkv, o, query, key, value, out):
    f32 = jnp.float32
    width, qw, ow = qkv.shape[0], qkv.shape[2] - 2 * HEAD_DIM, o.shape[2]
    for r in range(width):
        query[:, r * qw : (r + 1) * qw] = qkv[r, :, :qw].astype(f32)
        out[:, r * ow : (r + 1) * ow] = o[r].astype(f32)
    for head in range(width // sharers):
        both = sum(qkv[head * sharers + i, :, qw:].astype(f32) for i in range(sharers))
        to = slice(head * HEAD_DIM, (head + 1) * HEAD_DIM)
        key[:, to] = both[:, :HEAD_DIM]
        value[:, to] = both[:, HEAD_DIM:]


def join_call(kernel, arrays, outs, block=64):
    rows = arrays[0].shape[1]
    return pl.pallas_call(
        kernel,
        grid=(rows // block,),
        in_specs=[pl.BlockSpec((x.shape[0], block, x.shape[2]), lambda i: (0, i, 0)) for x in arrays],
        out_specs=[pl.BlockSpec((block, columns), lambda i: (i, 0)) for columns in outs],
        out_shape=[jax.ShapeDtypeStruct((rows, columns), jnp.float32) for columns in outs],
        compiler_params=pltpu.CompilerParams(vmem_limit_bytes=32 << 20),
    )(*arrays)


def per_device(
    tokens,
    segment_ids,
    attention_gain,
    query_weight,
    key_weight,
    value_weight,
    output_weight,
    feed_gain,
    gate_weight,
    up_weight,
    down_weight,
    cotangent,
):
    f32, bf16 = jnp.float32, jnp.bfloat16
    planes, width = lax.axis_size(F), lax.axis_size(R)
    r, z = lax.axis_index(R), lax.axis_index(F)
    tok, model = tokens.shape
    length = segment_ids.shape[1]
    all_tok = width * tok
    plane_kernels = width == 8
    heads = HEADS // width
    group = HEADS // KV_HEADS
    qw = heads * HEAD_DIM
    kv = (r * heads) // group
    feed = gate_weight.shape[1]
    piece = feed // (width * planes)
    hidden_units = piece * planes

    def cols(weight, first, count):
        return lax.dynamic_slice_in_dim(weight, first, count, 1)

    def feed_cols(weight):
        return [cols(weight, p * (feed // planes) + r * piece, piece) for p in range(planes)]

    w_attention = line_gather(
        jnp.concatenate(
            [
                cols(query_weight, r * qw, qw),
                cols(key_weight, kv * HEAD_DIM, HEAD_DIM),
                cols(value_weight, kv * HEAD_DIM, HEAD_DIM),
                cols(output_weight, r * (model // width), model // width),
            ],
            axis=1,
        )
    )
    w_qkv = w_attention[:, : qw + 2 * HEAD_DIM]
    w_out = lax.all_to_all(
        w_attention[:, qw + 2 * HEAD_DIM :], R, split_axis=0, concat_axis=1, tiled=True
    )
    own_gains = jnp.stack([attention_gain, feed_gain]).astype(f32)
    tok_float = tokens.astype(f32)
    scale_in = inverse_rms(tok_float)
    normed_in = tok_float * scale_in
    if plane_kernels:
        hidden_in, gains, ids = enter(
            tokens, jnp.pad(own_gains, ((0, 6), (0, 0))), segment_ids.reshape(8, length // 8), 0
        )
        hidden_in = hidden_in.reshape(all_tok, model)
        gains = gains[:, :2].transpose(1, 0, 2).reshape(2, model)
        ids = ids.reshape(width, length)
    else:
        gains = lax.all_gather(own_gains, F, axis=1, tiled=True)
        hidden_in = lax.all_gather((normed_in * gains[0]).astype(bf16), R, axis=0, tiled=True)
        ids = lax.all_gather(segment_ids, R, axis=0, tiled=True)
    gain_in, gain_mid = gains[0], gains[1]
    gate_weight, up_weight, down_weight, ids = lax.optimization_barrier(
        (gate_weight, up_weight, down_weight, ids)
    )
    w_feed = line_gather(jnp.concatenate(feed_cols(gate_weight) + feed_cols(up_weight), axis=1))
    w_down = line_gather(lax.dynamic_slice_in_dim(down_weight, r * piece, piece, 0))

    places = jnp.arange(length, dtype=jnp.int32)
    fresh = jnp.concatenate(
        [jnp.ones((width, 1), dtype=jnp.bool_), ids[:, 1:] != ids[:, :-1]], axis=1
    )
    positions = places[None] - lax.cummax(jnp.where(fresh, places[None], 0), axis=1)
    own_positions = lax.dynamic_slice_in_dim(positions, z * tok, tok, 1).reshape(all_tok)
    own_places = z * tok + jnp.arange(all_tok, dtype=jnp.int32) % tok
    own_starts = own_places - own_positions
    steps = all_tok // QUERY_BLOCK
    starts = own_starts.reshape(steps, 1, QUERY_BLOCK)
    query_places = own_places.reshape(steps, 1, QUERY_BLOCK)
    low = starts[:, 0, 0] // KEY_BLOCK
    high = query_places[:, 0, QUERY_BLOCK - 1] // KEY_BLOCK + 1

    if plane_kernels:
        wide_cosine, wide_sine = rope_tables(own_positions, 4)
        wide_sine = wide_sine * jnp.where(jnp.arange(2 * HEAD_DIM) // (HEAD_DIM // 2) % 2, 1.0, -1.0)
        query, kv_rows, cot_all = project(hidden_in, w_qkv, wide_cosine, wide_sine, cotangent, 3)
        kv_rows = kv_rows.reshape(width, length, 2 * HEAD_DIM)
        cot_all = cot_all.reshape(all_tok, model)
    else:
        cosine, sine = rope_tables(own_positions)
        qkv = dot(hidden_in, w_qkv)
        query = rotate(qkv[:, :qw].reshape(all_tok, heads, HEAD_DIM), cosine, sine, 1.0)
        query = query.astype(bf16).reshape(all_tok, qw)
        key = rotate(qkv[:, None, qw : qw + HEAD_DIM], cosine, sine, 1.0).astype(bf16)[:, 0]
        value = qkv[:, qw + HEAD_DIM :].astype(bf16)
        kv_rows = (
            lax.all_gather(jnp.concatenate([key, value], axis=1), F, axis=0, tiled=False)
            .reshape(planes, width, tok, 2 * HEAD_DIM)
            .transpose(1, 0, 2, 3)
            .reshape(width, length, 2 * HEAD_DIM)
        )
        cot_all = lax.all_gather(cotangent, R, axis=0, tiled=True)
    common = [("tokens", query), ("sequence", kv_rows), ("row", starts), ("row", query_places)]
    mixed, log_totals = attention_call(
        attention_kernel,
        heads,
        low,
        high,
        common,
        [
            ("tokens", jax.ShapeDtypeStruct((all_tok, qw), bf16)),
            ("row", jax.ShapeDtypeStruct((steps, 1, heads * QUERY_BLOCK), f32)),
        ],
    )
    branch = plane_scatter(dot(mixed, w_out).astype(bf16), 1)
    middle = tok_float + branch
    scale_mid = inverse_rms(middle)
    normed_mid = middle * scale_mid

    hidden_mid = plane_gather((normed_mid * gain_mid).astype(bf16), 2)
    if plane_kernels:
        hidden_blocks = hidden_mid.reshape(width, tok, model)
        cot_blocks = cot_all.reshape(width, tok, model)
        acts, down_part = feed_in(hidden_blocks, cot_blocks, w_feed)
        out_part, grad_hidden_mid, feed_part = feed_forward(
            hidden_blocks, cot_blocks, acts, w_feed, w_down, 5
        )
    else:
        w_gate, w_up = w_feed[:, :hidden_units], w_feed[:, hidden_units:]
        gate_acc = dot(hidden_mid, w_gate)
        up_acc = dot(hidden_mid, w_up)
        gate_sig = jax.nn.sigmoid(gate_acc)
        gate_silu = gate_acc * gate_sig
        inner_act = (gate_silu * up_acc).astype(bf16)
        out_part = dot(inner_act, w_down).astype(bf16)
        grad_inner = dot(cot_all, w_down, 1, 1)
        grad_gate = grad_inner * up_acc * gate_sig * (1.0 + gate_acc * (1.0 - gate_sig))
        grad_gate = grad_gate.astype(bf16)
        grad_up = (grad_inner * gate_silu).astype(bf16)
        feed_part = jnp.concatenate(
            [dot(hidden_mid, grad_gate, 0, 0), dot(hidden_mid, grad_up, 0, 0)], axis=1
        ).astype(bf16)
        down_part = dot(inner_act, cot_all, 0, 0).astype(bf16)
        grad_hidden_part = dot(grad_gate, w_gate, 1, 1) + dot(grad_up, w_up, 1, 1)
        grad_hidden_mid = plane_scatter(grad_hidden_part.astype(bf16), 5)
        feed_out = plane_scatter(out_part, 4)
    down_rows = line_scatter(down_part)
    feed_rows = line_scatter(feed_part)
    gain_mid_term = jnp.sum(grad_hidden_mid * normed_mid, axis=0)
    grad_normed_mid = grad_hidden_mid * gain_mid
    grad_middle = cotangent.astype(f32) + scale_mid * (
        grad_normed_mid - normed_mid * jnp.mean(grad_normed_mid * normed_mid, axis=1, keepdims=True)
    )

    grad_branch = plane_gather(grad_middle.astype(bf16), 6)
    grad_mixed = dot(grad_branch, w_out, 1, 1).astype(bf16)
    w_out_part = dot(mixed, grad_branch, 0, 0).astype(bf16)

    if plane_kernels:
        grad_qkv, feed_out, down_all, w_out_part = attention_back(
            heads,
            query,
            kv_rows,
            starts,
            query_places,
            grad_mixed,
            mixed,
            log_totals,
            wide_cosine,
            wide_sine,
            out_part,
            down_rows,
            w_out_part,
            10,
        )
        w_out_part = w_out_part.reshape(width * qw, model // width)
    else:
        gq, gkv = attention_call(
            attention_back_kernel,
            heads,
            low,
            high,
            common + [("tokens", grad_mixed), ("tokens", mixed), ("row", log_totals)],
            [
                ("tokens", jax.ShapeDtypeStruct((all_tok, qw), f32)),
                ("sequence", jax.ShapeDtypeStruct((width, length, 2 * HEAD_DIM), bf16)),
            ],
            [pltpu.VMEM((length, 2 * HEAD_DIM), f32)],
        )
        gkv = gkv.reshape(width, planes, tok, 2 * HEAD_DIM).transpose(1, 0, 2, 3)
        gkv = line_scatter(gkv.reshape(planes * all_tok, 2 * HEAD_DIM)).astype(f32)
        gq = rotate(gq.reshape(all_tok, heads, HEAD_DIM), cosine, sine, -1.0)
        gk = rotate(gkv[:, None, :HEAD_DIM], cosine, sine, -1.0)[:, 0]
        grad_qkv = jnp.concatenate([gq.reshape(all_tok, qw), gk, gkv[:, HEAD_DIM:]], axis=1)
        grad_qkv = grad_qkv.astype(bf16)
        down_all = lax.all_gather(down_rows, R, axis=0, tiled=True)
        w_out_part = lax.all_to_all(w_out_part, R, split_axis=1, concat_axis=0, tiled=True)
    out_rows = line_scatter(w_out_part)
    activations = (middle + feed_out).astype(bf16)
    hidden_part = dot(grad_qkv, w_qkv, 1, 1).astype(bf16)
    qkv_part = dot(hidden_in, grad_qkv, 0, 0).astype(bf16)
    hidden_part, qkv_part, feed_rows = lax.optimization_barrier((hidden_part, qkv_part, feed_rows))
    qkv_rows = line_scatter(qkv_part)
    grad_hidden_in = plane_scatter(hidden_part, 7)
    gain_in_term = jnp.sum(grad_hidden_in * normed_in, axis=0)
    grad_normed_in = grad_hidden_in * gain_in
    input_grad = (
        grad_middle
        + scale_in
        * (
            grad_normed_in
            - normed_in * jnp.mean(grad_normed_in * normed_in, axis=1, keepdims=True)
        )
    ).astype(bf16)

    rows = model // planes
    feed_all = plane_gather(feed_rows, 4, 2).reshape((width,) + feed_rows.shape)
    terms = jnp.stack([gain_in_term, gain_mid_term])
    if plane_kernels:
        terms = jnp.pad(terms.reshape(2, planes, rows).transpose(1, 0, 2), ((0, 0), (0, 6), (0, 0)))
        qkv_all, out_all, gain_terms = finish(qkv_rows, out_rows, terms, 9)
    else:
        qkv_all = lax.all_gather(qkv_rows, R, axis=0, tiled=False)
        out_all = lax.all_gather(out_rows, R, axis=0, tiled=False)
        gain_terms = lax.psum(lax.psum_scatter(terms, F, scatter_dimension=1, tiled=True), R)
    down_grad = down_all.reshape(feed // planes, model).astype(f32)
    gate_grad, up_grad = join_call(
        functools.partial(join_feed_kernel, planes, piece), [feed_all], [feed, feed]
    )
    query_grad, key_grad, value_grad, out_grad = join_call(
        functools.partial(join_attention_kernel, width // KV_HEADS),
        [qkv_all, out_all],
        [width * qw, KV_HEADS * HEAD_DIM, KV_HEADS * HEAD_DIM, model],
    )
    return (
        activations,
        input_grad,
        gain_terms[0],
        query_grad,
        key_grad,
        value_grad,
        out_grad,
        gain_terms[1],
        gate_grad,
        up_grad,
        down_grad,
    )


def solution(mesh):
    tok = P((R, F), None)
    row = P(F, None)
    in_specs = (tok, P(R, None), P(F), row, row, row, row, P(F), row, row, row, tok)
    out_specs = (tok, tok, P(F), row, row, row, row, P(F), row, row, row)
    return jax.shard_map(
        per_device, mesh=mesh, in_specs=in_specs, out_specs=out_specs, check_vma=False
    )
```

```python
import functools
import math

import jax
import jax.numpy as jnp
from jax import lax
from jax.experimental import pallas as pl
from jax.experimental.pallas import tpu as pltpu
from jax.sharding import PartitionSpec as P

HEADS = 32
KV_HEADS = 4
HEAD_DIM = 64
EPSILON = 1e-05
NEGATIVE = -1e30
R = "replica"
F = "fsdp"
MESH = pl.DeviceIdType.MESH
DMA = pltpu.SemaphoreType.DMA
ANY = pl.BlockSpec(memory_space=pl.ANY)
KEY_BLOCK = 256
QUERY_BLOCK = 128
PARTS = 2
FIRST_DOC = 800


def inverse_rms(values):
    return lax.rsqrt(jnp.mean(values * values, axis=1, keepdims=True) + EPSILON)


def rope_tables(positions, repeats=1):
    half_dim = HEAD_DIM // 2
    places = jnp.arange(repeats * half_dim, dtype=jnp.int32) % half_dim
    freq_rates = jnp.exp(places.astype(jnp.float32) * (-math.log(10000.0) / half_dim))
    angles = positions.astype(jnp.float32)[:, None] * freq_rates[None, :]
    return (jnp.cos(angles), jnp.sin(angles))


def rotate(tensor, cosine_table, sine_table, sign):
    half_dim = HEAD_DIM // 2
    low, up = tensor[..., :half_dim], tensor[..., half_dim:]
    cos_part = cosine_table[:, None, :]
    sin_part = sine_table[:, None, :] * sign
    return jnp.concatenate(
        [low * cos_part - up * sin_part, up * cos_part + low * sin_part], axis=-1
    )


def dot(a, b, ca=1, cb=0):
    return lax.dot_general(a, b, (((ca,), (cb,)), ((), ())), preferred_element_type=jnp.float32)


def remote(src, dst, sems, index, device):
    return pltpu.make_async_remote_copy(
        src_ref=src,
        dst_ref=dst,
        send_sem=sems[0].at[index],
        recv_sem=sems[1].at[index],
        device_id={R: device},
        device_id_type=MESH,
    )


def greet(*devices):
    barrier = pltpu.get_barrier_semaphore()
    for device in devices:
        pl.semaphore_signal(barrier, inc=1, device_id={R: device}, device_id_type=MESH)
    pl.semaphore_wait(barrier, len(devices))


class Gather:
    @staticmethod
    def scratch(count):
        return [DMA((count,))] * 6 + [DMA((4, count))] * 2

    def __init__(self, items, sems):
        self.items, self.count = items, len(items)
        self.half = self.count // 2
        self.me = lax.axis_index(R)
        self.sibling, self.x, self.y = self.me + 1 - 2 * lax.rem(self.me, 2), self.me ^ 2, self.me ^ 4
        self.sems = sems

    def copy(self, kind, i):
        first = i < self.half
        owner, device = {
            0: (self.me, self.x),
            1: (self.me, self.y),
            2: (self.x, self.y) if first else (self.y, self.x),
            3: (self.me, self.sibling),
            4: (self.x, self.sibling),
            5: (self.y, self.sibling),
            6: (self.me ^ 6, self.sibling),
        }[kind]
        own, slot = self.items[i]
        sems = self.sems[2 * min(kind, 3) : 2 * min(kind, 3) + 2]
        src = own if kind in (0, 1, 3) else slot(owner)
        return remote(src, slot(owner), sems, i if kind < 3 else (kind - 3, i), device)

    def start(self, kept=()):
        ready = [i for i in range(self.count) if i not in kept]
        for n, i in enumerate(ready):
            self.copy(0, i).start()
            self.copy(1, ready[(n + self.half) % len(ready)]).start()
        for i in ready:
            self.copy(3, i).start()

    def start_items(self, items):
        for i in items:
            for kind in (0, 1, 3):
                self.copy(kind, i).start()

    def pass_on(self, kind, i):
        self.copy(kind, i).wait_recv()
        if kind < 2 and (i < self.half) == (kind == 0):
            self.copy(2, i).start()
        self.copy(kind + 4, i).start()

    def relay(self, i):
        self.pass_on(0, i)
        self.pass_on(1, (i + self.half) % self.count)

    def far(self):
        for i in range(self.half):
            self.pass_on(2, i)
            self.pass_on(2, self.half + i)
        for i in range(2 * self.half, self.count):
            self.pass_on(2, i)

    def from_sibling(self, kind):
        for i in range(self.count):
            self.copy(kind, i).wait_recv()

    def wait_sends(self):
        for i in range(self.count):
            for kind in range(7):
                self.copy(kind, i).wait_send()

    def finish(self):
        self.far()
        for kind in range(3, 7):
            self.from_sibling(kind)
        self.wait_sends()


def row_items(x, out, chunks):
    size = x.shape[0] // chunks

    def item(i):
        part = pl.ds(i * size, size)
        return x.at[part], lambda owner: out.at[owner, part]

    return [item(i) for i in range(chunks)]


def gather_kernel(chunks, x, out, local_sem, *sems):
    gather = Gather(row_items(x, out, chunks), sems)
    greet(gather.sibling, gather.x, gather.y)
    own = pltpu.make_async_copy(x, out.at[gather.me], local_sem)
    own.start()
    gather.start()
    for i in range(chunks):
        gather.relay(i)
    gather.finish()
    own.wait()


def enter_kernel(chunks, tokens, gains, ids, hidden, all_gains, all_ids, own, own_sem, to_z, at_z, *sems):
    f32 = jnp.float32
    planes = all_gains.shape[0]
    z = lax.axis_index(F)
    items = row_items(own, hidden, chunks) + [(ids, lambda owner: all_ids.at[owner])]
    gather = Gather(items, sems)
    others = [lax.rem(z + i, planes) for i in range(1, planes)]
    barrier = pltpu.get_barrier_semaphore()
    for other in others:
        pl.semaphore_signal(barrier, inc=1, device_id={F: other}, device_id_type=MESH)
    for device in (gather.sibling, gather.x, gather.y):
        pl.semaphore_signal(barrier, inc=1, device_id={R: device}, device_id_type=MESH)
    pl.semaphore_wait(barrier, planes + 2)
    copies = [
        pltpu.make_async_remote_copy(
            src_ref=gains,
            dst_ref=all_gains.at[z],
            send_sem=to_z.at[i],
            recv_sem=at_z.at[i],
            device_id={F: other},
            device_id_type=MESH,
        )
        for i, other in enumerate(others)
    ]
    for copy in copies:
        copy.start()
    all_gains[z] = gains[...]
    all_ids[gather.me] = ids[...]
    size = tokens.shape[0] // chunks
    scales = [
        inverse_rms(tokens[i * size : (i + 1) * size, :].astype(f32)) for i in range(chunks)
    ]
    for copy in copies:
        copy.wait()
    gain = jnp.concatenate([all_gains[p, 0:1] for p in range(planes)], axis=1)
    for i in range(chunks):
        part = slice(i * size, (i + 1) * size)
        own[part, :] = (tokens[part, :].astype(f32) * scales[i] * gain).astype(jnp.bfloat16)
    kept = pltpu.make_async_copy(own, hidden.at[gather.me], own_sem)
    kept.start()
    gather.start()
    for i in range(gather.count):
        gather.relay(i)
    gather.finish()
    kept.wait()


def turn(x, cosine, sine):
    half_dim = HEAD_DIM // 2
    low = lax.rem(lax.broadcasted_iota(jnp.int32, x.shape, 1), HEAD_DIM) < half_dim
    swapped = jnp.where(low, pltpu.roll(x, 2 * HEAD_DIM - half_dim, 1), pltpu.roll(x, half_dim, 1))
    return x * cosine + swapped * sine


def turn_keys(x, cosine, sine):
    is_key = lax.broadcasted_iota(jnp.int32, x.shape, 1) < HEAD_DIM
    return jnp.where(is_key, turn(x, cosine, sine), x)


def along_line(src, dst, sems, index, plane):
    return pltpu.make_async_remote_copy(
        src_ref=src,
        dst_ref=dst,
        send_sem=sems[0].at[index],
        recv_sem=sems[1].at[index],
        device_id={F: plane},
        device_id_type=MESH,
    )


def project_kernel(
    chunks, hidden, weight, cosine, sine, cotangent, query, kv, cot_all,
    own, own_sem, cot_sem, to_line, at_line, to_sib, at_sib, *sems,
):
    bf16 = jnp.bfloat16
    planes = kv.shape[1]
    z = lax.axis_index(F)
    tok = cotangent.shape[0]
    width = kv.shape[0]
    count = width // 2
    gather = Gather(row_items(cotangent, cot_all, chunks), sems)
    core = lax.rem(gather.me, 2)
    mine = pl.ds(core * count, count)
    above, below = lax.rem(z + 1, planes), lax.rem(z + planes - 1, planes)
    barrier = pltpu.get_barrier_semaphore()
    for other in (above, below):
        pl.semaphore_signal(barrier, inc=1, device_id={F: other}, device_id_type=MESH)
    for device in (gather.sibling, gather.x, gather.y):
        pl.semaphore_signal(barrier, inc=1, device_id={R: device}, device_id_type=MESH)
    pl.semaphore_wait(barrier, 5)
    kept_cot = pltpu.make_async_copy(cotangent, cot_all.at[gather.me], cot_sem)
    kept_cot.start()
    gather.start()

    def tile(i, carry):
        s = lax.rem(core * count + i, width)
        rows = pl.ds(pl.multiple_of(s * tok, tok), tok)
        acc = dot(hidden[rows, :], weight[...])
        c, n = cosine[rows, :], sine[rows, :]
        columns = acc.shape[1] - 2 * HEAD_DIM
        for first in range(0, columns, 2 * HEAD_DIM):
            part = slice(first, first + 2 * HEAD_DIM)
            query[rows, part] = turn(acc[:, part], c, n).astype(bf16)
        own[s] = turn_keys(acc[:, columns:], c, n).astype(bf16)
        return carry

    class Group:
        def __init__(self, make):
            self.each = [make(i) for i in range(count)]

        def __getattr__(self, name):
            def call():
                for copy in self.each:
                    getattr(copy, name)()

            return call

    def up(step):
        slot = z - step

        def make(i):
            dst = kv.at[core * count + i, slot]
            src = own.at[core * count + i] if step == 0 else dst
            return along_line(src, dst, (to_line, at_line), (step, i), above)

        return Group(make)

    def came(step):
        def make(i):
            dst = kv.at[core * count + i, z - step]
            return along_line(dst, dst, (to_line, at_line), (step - 1, i), above)

        return Group(make)

    def across(step):
        slot = z - step
        return remote(kv.at[mine, slot], kv.at[mine, slot], (to_sib, at_sib), step, gather.sibling)

    lax.fori_loop(0, count, tile, 0)

    @pl.when(z < planes - 1)
    def _():
        up(0).start()

    lax.fori_loop(count, width, tile, 0)
    kept = pltpu.make_async_copy(own, kv.at[:, z], own_sem)
    kept.start()
    done = 0
    for step in range(1, planes):

        @pl.when(z >= step)
        def _():
            arriving, leaving = came(step), up(step)
            for i in range(count):
                arriving.each[i].wait_recv()

                @pl.when(z < planes - 1)
                def _():
                    leaving.each[i].start()

            across(step).start()

        while done < chunks * step // planes:
            gather.relay(done)
            done += 1
    for i in range(done, chunks):
        gather.relay(i)
    gather.finish()
    for step in range(planes):

        @pl.when((z >= step) & (z < planes - 1))
        def _():
            up(step).wait_send()

        if step:

            @pl.when(z >= step)
            def _():
                across(step).wait()

    kept.wait()
    kept_cot.wait()


def finish_kernel(
    qkv, out_rows, terms, all_qkv, all_out, gains, own_gain, all_gains,
    at_planes, own_sems, to_z, at_z, *sems,
):
    planes = terms.shape[0]
    z = lax.axis_index(F)
    chunks = [x for pair in zip(row_items(qkv, all_qkv, 2), row_items(out_rows, all_out, 2)) for x in pair]
    gather = Gather(chunks + [(own_gain, lambda owner: all_gains.at[owner])], sems)
    me, last = gather.me, gather.count - 1
    others = [lax.rem(z + i, planes) for i in range(1, planes)]
    barrier = pltpu.get_barrier_semaphore()
    for other in others:
        pl.semaphore_signal(barrier, inc=1, device_id={F: other}, device_id_type=MESH)
    for device in (gather.sibling, gather.x, gather.y):
        pl.semaphore_signal(barrier, inc=1, device_id={R: device}, device_id_type=MESH)
    pl.semaphore_wait(barrier, planes + 2)
    copies = [
        along_line(terms.at[other], at_planes.at[i], (to_z, at_z), i, other)
        for i, other in enumerate(others)
    ]
    for copy in copies:
        copy.start()
    kept = [
        pltpu.make_async_copy(qkv, all_qkv.at[me], own_sems.at[0]),
        pltpu.make_async_copy(out_rows, all_out.at[me], own_sems.at[1]),
    ]
    for copy in kept:
        copy.start()
    gather.start((last,))
    total = terms[z]
    for i, copy in enumerate(copies):
        copy.wait()
        total = total + at_planes[i]
    own_gain[...] = total
    all_gains[me] = total
    gather.start_items((last,))
    for i in range(gather.count):
        gather.relay(i)
    gather.finish()
    total = all_gains[0]
    for device in range(1, all_gains.shape[0]):
        total = total + all_gains[device]
    gains[...] = total
    for copy in kept:
        copy.wait()


def finish(qkv, out_rows, terms, call):
    planes, width = lax.axis_size(F), lax.axis_size(R)
    f32, bf16 = jnp.float32, jnp.bfloat16
    vmem = pl.BlockSpec(memory_space=pltpu.VMEM)
    block = terms.shape[1:]
    return pl.pallas_call(
        finish_kernel,
        out_shape=[
            jax.ShapeDtypeStruct((width,) + qkv.shape, bf16),
            jax.ShapeDtypeStruct((width,) + out_rows.shape, bf16),
            jax.ShapeDtypeStruct(block, f32),
        ],
        in_specs=[ANY, ANY, vmem],
        out_specs=[ANY, ANY, vmem],
        scratch_shapes=[
            pltpu.VMEM(block, f32),
            pltpu.VMEM((width,) + block, f32),
            pltpu.VMEM((planes - 1,) + block, f32),
            DMA((2,)),
            DMA((planes - 1,)),
            DMA((planes - 1,)),
        ]
        + Gather.scratch(5),
        compiler_params=pltpu.CompilerParams(collective_id=call, has_side_effects=True),
    )(qkv, out_rows, terms)


class Scatter:
    @staticmethod
    def scratch(rows, columns, chunks):
        bf16, size = jnp.bfloat16, rows // chunks
        return [
            pltpu.VMEM((5, rows, columns), bf16),
            pltpu.VMEM((4, rows, columns), bf16),
            pltpu.VMEM((chunks, 2, size, columns), bf16),
            pltpu.VMEM((chunks, size, columns), bf16),
            pltpu.VMEM((2, size, columns), jnp.float32),
            DMA((4,)),
            DMA((4,)),
            DMA((chunks, 2)),
            DMA((chunks, 2)),
            DMA((chunks,)),
            DMA((chunks,)),
            DMA((2,)),
        ]

    def __init__(self, out, chunks, refs):
        self.out, self.chunks, self.half = out, chunks, chunks // 2
        self.own, self.sib, self.got, self.got_far, self.total = refs[:5]
        self.sib_sems, self.near_sems, self.far_sems = refs[5:7], refs[7:9], refs[9:11]
        self.out_sem = refs[11]
        self.me = lax.axis_index(R)
        self.sibling, self.x, self.y = self.me + 1 - 2 * lax.rem(self.me, 2), self.me ^ 2, self.me ^ 4
        self.size = out.shape[0] // chunks
        self.order = [*range(self.half, chunks), *range(self.half)]
        self.trades = None

    def owner(self, i):
        return (self.me ^ (6 - 2 * (i // 2))) ^ (1 - lax.rem(i, 2))

    def trade(self, d):
        return remote(self.own.at[4], self.sib.at[d], self.sib_sems, d, self.sibling)

    def put(self, i, value):
        d = 3 - i // 2
        for_sibling = lax.rem(i, 2) == 0

        @pl.when(for_sibling & (i >= 2))
        def _():
            self.trade(d + 1).wait_send()

        self.own[jnp.where(for_sibling, 4, d)] = value

        @pl.when(for_sibling)
        def _():
            self.trade(d).start()

    def take(self, part, sems):
        self.loads, self.trades = {}, {}
        for d in (3, 2, 1, 0):
            self.loads[d] = pltpu.make_async_copy(part.at[self.me ^ (2 * d)], self.own.at[d], sems.at[d])
            self.loads[d].start()
        for d in (3, 2, 1, 0):
            self.trades[d] = remote(
                part.at[self.sibling ^ (2 * d)], self.sib.at[d], self.sib_sems, d, self.sibling
            )
            self.trades[d].start()

    def taken(self, d):
        self.loads[d].wait()
        self.trades[d].wait_recv()

    def arrived(self, d):
        self.trade(d).wait_recv()

    def part(self, j):
        return pl.ds(j * self.size, self.size)

    def summed(self, d, j):
        part = self.part(j)
        return self.own[d, part].astype(jnp.float32) + self.sib[d, part].astype(jnp.float32)

    def near_copy(self, j, n):
        device, d = (self.x, 1) if j < self.half else (self.y, 2)
        src = self.own.at[3 if n else d, self.part(j)]
        return remote(src, self.got.at[j, n], self.near_sems, (j, n), device)

    def far_copy(self, j):
        device, d = (self.y, 2) if j < self.half else (self.x, 1)
        return remote(self.own.at[d, self.part(j)], self.got_far.at[j], self.far_sems, j, device)

    def out_copy(self, j):
        slot = self.order.index(j) % 2
        return pltpu.make_async_copy(
            self.total.at[slot], self.out.at[self.part(j)], self.out_sem.at[slot]
        )

    def near(self, j, n):
        e = 3 if n else (1 if j < self.half else 2)
        self.own[e, self.part(j)] = self.summed(e, j).astype(jnp.bfloat16)
        self.near_copy(j, n).start()

    def progress(self, i):
        @pl.when(i == 2)
        def _():
            self.arrived(3)
            for j in self.order:
                self.near(j, 1)

        @pl.when(i == 4)
        def _():
            self.arrived(2)
            for j in range(self.half, self.chunks):
                self.near(j, 0)

        @pl.when(i == 6)
        def _():
            self.arrived(1)
            for j in range(self.half):
                self.near(j, 0)

    def far(self, j):
        for n in (0, 1):
            self.near_copy(j, n).wait_recv()
        d = 2 if j < self.half else 1
        passed = self.summed(d, j) + self.got[j, 1].astype(jnp.float32)
        self.own[d, self.part(j)] = passed.astype(jnp.bfloat16)
        self.far_copy(j).start()

    def result(self, j):
        self.far_copy(j).wait_recv()
        return (
            self.summed(0, j)
            + self.got[j, 0].astype(jnp.float32)
            + self.got_far[j].astype(jnp.float32)
        )

    def last(self, j):
        total = self.result(j)
        turn = self.order.index(j)
        if turn >= 2:
            self.out_copy(self.order[turn - 2]).wait()
        self.total[turn % 2] = total
        self.out_copy(j).start()

    def finish(self, written=True):
        if self.trades is None:
            self.trade(0).wait_send()
        else:
            for copy in self.trades.values():
                copy.wait_send()
        if written:
            for j in self.order[-2:]:
                self.out_copy(j).wait()
        for j in range(self.chunks):
            self.far_copy(j).wait_send()
            for n in (0, 1):
                self.near_copy(j, n).wait_send()


def middle_kernel(
    chunks, mixed, w_out, tokens, gain, w_feed, cotangent, middle, hidden, acts, down_part,
    blocks, act_stage, inner_turned, column_in, down_stage, out_sems, act_sems, column_sems, down_sem, *refs,
):
    f32, bf16 = jnp.float32, jnp.bfloat16
    width, tok, _ = blocks.shape
    scatter = Scatter(middle, chunks, refs[:12])
    me = scatter.me
    size = tok // chunks

    def item(j):
        part = pl.ds(j * size, size)
        return blocks.at[me, part], lambda owner: blocks.at[owner, part]

    gather = Gather([item(j) for j in range(chunks)], refs[12:])
    greet(scatter.sibling, scatter.x, scatter.y)

    def branch(i, carry):
        rows = pl.ds(pl.multiple_of(scatter.owner(i) * tok, tok), tok)
        scatter.put(i, dot(mixed[rows, :], w_out[...]).astype(bf16))
        scatter.progress(i)
        return carry

    lax.fori_loop(0, width, branch, 0)
    scatter.arrived(0)
    for j in scatter.order:
        scatter.far(j)
    for j in scatter.order:
        part = pl.ds(j * size, size)
        total = tokens[part, :].astype(f32) + scatter.result(j)
        middle[part, :] = total
        blocks[me, part] = (total * inverse_rms(total) * gain[...]).astype(bf16)
        gather.start_items((j,))

    def hidden_copy(i):
        return pltpu.make_async_copy(blocks.at[me ^ i], hidden.at[me ^ i], out_sems.at[i])

    def act_copy(i):
        slot = lax.rem(i, 2)
        return pltpu.make_async_copy(act_stage.at[slot], acts.at[me ^ i], act_sems.at[slot])

    def block(i, carry):
        @pl.when(i == 1)
        def _():
            gather.from_sibling(3)

        @pl.when(i == 2)
        def _():
            for j in scatter.order:
                gather.pass_on(0, j)
                gather.pass_on(1, j)

        @pl.when(i == 3)
        def _():
            gather.from_sibling(4)

        @pl.when(i == 5)
        def _():
            gather.from_sibling(5)

        @pl.when(i == 6)
        def _():
            for j in scatter.order:
                gather.pass_on(2, j)

        @pl.when(i == 7)
        def _():
            gather.from_sibling(6)

        @pl.when(i >= 2)
        def _():
            act_copy(i - 2).wait()

        acc = dot(blocks[me ^ i], w_feed[...])
        act_stage[lax.rem(i, 2)] = acc
        act_copy(i).start()
        hidden_copy(i).start()
        gate, up = acc[:, :units], acc[:, units:]
        inner_turned[i] = (gate / (1.0 + jnp.exp(-gate)) * up).astype(bf16).T
        return carry

    units = w_feed.shape[1] // 2
    tiles = tokens.shape[1] // tok

    def column_loads(n):
        slot = lax.rem(n, 2)
        part = pl.ds(pl.multiple_of(n * tok, tok), tok)
        return [
            pltpu.make_async_copy(
                cotangent.at[me ^ i, :, part],
                column_in.at[slot, pl.ds(i * tok, tok)],
                column_sems.at[slot, i],
            )
            for i in range(width)
        ]

    def down_copy(n):
        part = pl.ds(pl.multiple_of(n * tok, tok), tok)
        slot = lax.rem(n, 2)
        return pltpu.make_async_copy(down_stage.at[slot], down_part.at[:, part], down_sem.at[slot])

    def down_tile(n, carry):
        slot = lax.rem(n, 2)
        for copy in column_loads(n):
            copy.wait()

        @pl.when(n >= 2)
        def _():
            down_copy(n - 2).wait()

        acc = dot(inner_turned[0], column_in[slot, :tok])
        for i in range(1, width):
            acc = acc + dot(inner_turned[i], column_in[slot, i * tok : (i + 1) * tok])
        down_stage[slot] = acc.astype(bf16)
        down_copy(n).start()

        @pl.when(n + 2 < tiles)
        def _():
            for copy in column_loads(n + 2):
                copy.start()

        return carry

    for n in (0, 1):
        for copy in column_loads(n):
            copy.start()
    lax.fori_loop(0, width, block, 0)
    lax.fori_loop(0, tiles, down_tile, 0)
    for n in (tiles - 2, tiles - 1):
        down_copy(n).wait()
    gather.wait_sends()
    scatter.finish(False)
    for i in (width - 2, width - 1):
        act_copy(i).wait()
    for i in range(width):
        hidden_copy(i).wait()


def middle_layer(mixed, w_out, tokens, gain, w_feed, cotangent, call, chunks=4):
    width = lax.axis_size(R)
    tok, model = tokens.shape
    bf16, f32 = jnp.bfloat16, jnp.float32
    units = w_feed.shape[1] // 2
    vmem = pl.BlockSpec(memory_space=pltpu.VMEM)
    return pl.pallas_call(
        functools.partial(middle_kernel, chunks),
        out_shape=[
            jax.ShapeDtypeStruct((tok, model), f32),
            jax.ShapeDtypeStruct((width, tok, model), bf16),
            jax.ShapeDtypeStruct((width, tok, 2 * units), f32),
            jax.ShapeDtypeStruct((units, model), bf16),
        ],
        in_specs=[vmem] * 5 + [ANY],
        out_specs=[vmem, ANY, ANY, ANY],
        scratch_shapes=[
            pltpu.VMEM((width, tok, model), bf16),
            pltpu.VMEM((2, tok, 2 * units), f32),
            pltpu.VMEM((width, units, tok), bf16),
            pltpu.VMEM((2, width * tok, tok), bf16),
            pltpu.VMEM((2, units, tok), bf16),
            DMA((width,)),
            DMA((2,)),
            DMA((2, width)),
            DMA((2,)),
        ]
        + Scatter.scratch(tok, model, chunks)
        + Gather.scratch(chunks),
        compiler_params=pltpu.CompilerParams(
            collective_id=call, has_side_effects=True, vmem_limit_bytes=56 << 20
        ),
    )(mixed, w_out, tokens, gain, w_feed, cotangent)


def feed_kernel(
    chunks, hidden, cotangent, acts, w_feed, w_down, out_part, grad_hidden, feed_part,
    acts_in, cot_in, grads, column_in, feed_stage, out_stage, in_sems, column_sems, feed_sem, out_sem,
    *refs,
):
    f32, bf16 = jnp.float32, jnp.bfloat16
    width, tok, model = hidden.shape
    units = w_down.shape[0]
    scatter = Scatter(grad_hidden, chunks, refs)
    half = chunks // 2
    first_half, second_half = range(half), range(half, chunks)

    def loads(i):
        slot, owner = lax.rem(i, 2), scatter.owner(i)
        return [
            pltpu.make_async_copy(acts.at[owner], acts_in.at[slot], in_sems.at[0, slot]),
            pltpu.make_async_copy(cotangent.at[owner], cot_in.at[slot], in_sems.at[1, slot]),
        ]

    def out_copy(i):
        slot = lax.rem(i, 2)
        return pltpu.make_async_copy(
            out_stage.at[slot], out_part.at[scatter.owner(i)], out_sem.at[slot]
        )

    for i in (0, 1):
        for copy in loads(i):
            copy.start()
    greet(scatter.sibling, scatter.x, scatter.y)

    def block(i, carry):
        slot = lax.rem(i, 2)
        rows = pl.ds(pl.multiple_of(i * tok, tok), tok)
        for copy in loads(i):
            copy.wait()
        gate, up = acts_in[slot, :, :units], acts_in[slot, :, units:]
        gate_sig = 1.0 / (1.0 + jnp.exp(-gate))
        gate_silu = gate * gate_sig
        inner = (gate_silu * up).astype(bf16)
        grad_inner = dot(cot_in[slot], w_down[...], 1, 1)
        grad_gate = grad_inner * up * gate_sig * (1.0 + gate * (1.0 - gate_sig))
        both = jnp.concatenate([grad_gate, grad_inner * gate_silu], axis=1).astype(bf16)
        grads[rows, :] = both
        scatter.put(i, dot(both, w_feed[...], 1, 1).astype(bf16))

        @pl.when(i >= 2)
        def _():
            out_copy(i - 2).wait()

        out_stage[slot] = dot(inner, w_down[...]).astype(bf16)
        out_copy(i).start()

        @pl.when(i + 2 < width)
        def _():
            for copy in loads(i + 2):
                copy.start()

        scatter.progress(i)
        return carry

    tiles = model // tok

    def column_loads(n):
        slot = lax.rem(n, 2)
        part = pl.ds(pl.multiple_of(n * tok, tok), tok)
        return [
            pltpu.make_async_copy(
                hidden.at[scatter.owner(i), :, part],
                column_in.at[slot, pl.ds(i * tok, tok)],
                column_sems.at[slot, i],
            )
            for i in range(width)
        ]

    def feed_copy(n):
        rows = pl.ds(pl.multiple_of(n * tok, tok), tok)
        slot = lax.rem(n, 2)
        return pltpu.make_async_copy(feed_stage.at[slot], feed_part.at[rows], feed_sem.at[slot])

    def feed_tile(n, carry):
        slot = lax.rem(n, 2)
        for copy in column_loads(n):
            copy.wait()

        @pl.when(n >= 2)
        def _():
            feed_copy(n - 2).wait()

        feed_stage[slot] = dot(column_in[slot], grads[...], 0, 0).astype(bf16)
        feed_copy(n).start()

        @pl.when(n + 2 < tiles)
        def _():
            for copy in column_loads(n + 2):
                copy.start()

        @pl.when(n == 2)
        def _():
            for j in second_half:
                scatter.far(j)

        @pl.when(n == 5)
        def _():
            for j in first_half:
                scatter.far(j)

        return carry

    for n in (0, 1):
        for copy in column_loads(n):
            copy.start()
    lax.fori_loop(0, width, block, 0)
    scatter.arrived(0)
    lax.fori_loop(0, tiles, feed_tile, 0)
    for j in scatter.order:
        scatter.last(j)
    scatter.finish()
    for i in (width - 2, width - 1):
        out_copy(i).wait()
    for n in (tiles - 2, tiles - 1):
        feed_copy(n).wait()


def feed_forward(hidden, cotangent, acts, w_feed, w_down, call, chunks=4):
    width, tok, model = hidden.shape
    units = w_down.shape[0]
    bf16 = jnp.bfloat16
    vmem = pl.BlockSpec(memory_space=pltpu.VMEM)
    return pl.pallas_call(
        functools.partial(feed_kernel, chunks),
        out_shape=[
            jax.ShapeDtypeStruct((width, tok, model), bf16),
            jax.ShapeDtypeStruct((tok, model), jnp.float32),
            jax.ShapeDtypeStruct((model, 2 * units), bf16),
        ],
        in_specs=[ANY, ANY, ANY, vmem, vmem],
        out_specs=[ANY] * 3,
        scratch_shapes=[
            pltpu.VMEM((2, tok, 2 * units), jnp.float32),
            pltpu.VMEM((2, tok, model), bf16),
            pltpu.VMEM((width * tok, 2 * units), bf16),
            pltpu.VMEM((2, width * tok, tok), bf16),
            pltpu.VMEM((2, tok, 2 * units), bf16),
            pltpu.VMEM((2, tok, model), bf16),
            DMA((2, 2)),
            DMA((2, width)),
            DMA((2,)),
            DMA((2,)),
        ]
        + Scatter.scratch(tok, model, chunks),
        compiler_params=pltpu.CompilerParams(
            collective_id=call, has_side_effects=True, vmem_limit_bytes=62 << 20
        ),
    )(hidden, cotangent, acts, w_feed, w_down)


def back_kernel(
    chunks, heads, q, kv, starts, places, grad, mixed, log_total, cosine, sine, out_part, down_rows, w_part,
    grad_qkv, feed_out, all_down, w_rows,
    sums, grad_kv, from_sib, inbox, outbox, to_sib, at_sib, to_line, at_line, down_sem, w_sem,
    to_all, at_all, load_sems, *refs,
):
    f32, bf16 = jnp.float32, jnp.bfloat16
    planes, count, tok = inbox.shape[0], inbox.shape[1], inbox.shape[2]
    width = 2 * count
    columns = heads * HEAD_DIM
    z, me = lax.axis_index(F), lax.axis_index(R)
    core = lax.rem(me, 2)
    above, below = lax.rem(z + 1, planes), lax.rem(z + planes - 1, planes)
    scatter = Scatter(feed_out, chunks, refs[:12])
    gather = Gather([(down_rows, lambda owner: all_down.at[owner])] * 1, refs[12:])
    half = chunks // 2
    barrier = pltpu.get_barrier_semaphore()
    for other in (above, below):
        pl.semaphore_signal(barrier, inc=1, device_id={F: other}, device_id_type=MESH)
    peers = [me ^ distance for distance in range(1, width)]
    for device in peers:
        pl.semaphore_signal(barrier, inc=1, device_id={R: device}, device_id_type=MESH)
    pl.semaphore_wait(barrier, 1 + width)
    share = w_part.shape[1] // width

    def share_of(device):
        return w_part.at[:, pl.ds(pl.multiple_of(device * share, share), share)]

    w_copies = [
        remote(share_of(device), w_rows.at[me], (to_all, at_all), i, device)
        for i, device in enumerate(peers)
    ]
    w_kept = pltpu.make_async_copy(share_of(me), w_rows.at[me], w_sem)
    for copy in [w_kept] + w_copies:
        copy.start()
    scatter.take(out_part, load_sems)
    kept = pltpu.make_async_copy(down_rows, all_down.at[me], down_sem)
    kept.start()
    parts = tok // QUERY_BLOCK

    def step(n, carry):
        s, sub = n // parts, lax.rem(n, parts)
        rows = pl.ds(pl.multiple_of(n * QUERY_BLOCK, QUERY_BLOCK), QUERY_BLOCK)
        queries = heads_to_rows(q[rows, :] * bf16(HEAD_DIM**-0.5), heads)
        grads = heads_to_rows(grad[rows, :], heads)
        first = jnp.concatenate([starts[n]] * heads, axis=1)
        place = jnp.concatenate([places[n]] * heads, axis=1)
        products = grads.astype(f32) * heads_to_rows(mixed[rows, :], heads).astype(f32)
        delta = lax.dot_general(
            jnp.ones((8, 2 * HEAD_DIM), f32),
            products,
            (((1,), (1,)), ((), ())),
            precision=lax.Precision.HIGHEST,
            preferred_element_type=f32,
        )[:1]
        level = log_total[n]
        upper = pltpu.roll(grads.astype(f32), HEAD_DIM, 1).astype(bf16)

        @pl.when(sub == 0)
        def _():
            sums[...] = jnp.zeros_like(sums)

        def block(index, acc):
            part = pl.ds(pl.multiple_of(index * KEY_BLOCK, KEY_BLOCK), KEY_BLOCK)
            keys = kv[s, part, :]
            scores = dot(keys, queries, 1, 1)
            probs = jnp.where(visible(index, first, place), jnp.exp(scores - level), 0.0)
            grad_probs = dot(keys, upper, 1, 1)
            grad_scores = (probs * (grad_probs - delta)).astype(bf16)
            sums[part, :] += dot(grad_scores, queries) + dot(probs.astype(bf16), upper)
            return acc + dot(keys, grad_scores, 0, 0)

        place_of_first = z * tok + sub * QUERY_BLOCK
        low = jnp.where(place_of_first >= FIRST_DOC, FIRST_DOC // KEY_BLOCK, 0)
        high = (place_of_first + QUERY_BLOCK - 1) // KEY_BLOCK + 1
        acc = lax.fori_loop(low, high, block, jnp.zeros((2 * HEAD_DIM, queries.shape[0]), f32))
        grad_q = rows_to_heads(acc[:HEAD_DIM] * HEAD_DIM**-0.5, heads)
        c, n_sine = cosine[rows, :], -sine[rows, :]
        for at in range(0, columns, 2 * HEAD_DIM):
            part = slice(at, at + 2 * HEAD_DIM)
            grad_qkv[rows, part] = turn(grad_q[:, part], c, n_sine).astype(bf16)
        grad_qkv[rows, columns:] = jnp.zeros((QUERY_BLOCK, 2 * HEAD_DIM), bf16)

        @pl.when(sub == parts - 1)
        def _():
            grad_kv[s] = sums[...].astype(bf16)

        return carry

    lax.fori_loop(0, width // 2, step, 0)
    scatter.taken(3)
    for j in scatter.order:
        scatter.near(j, 1)
    scatter.taken(2)
    for j in range(half, chunks):
        scatter.near(j, 0)
    scatter.taken(1)
    for j in range(half):
        scatter.near(j, 0)
    gather.start()
    lax.fori_loop(width // 2, width * parts, step, 0)

    def block_of(which, b):
        return grad_kv.at[pl.ds(which * count, count), pl.ds(b * tok, tok)]

    def trade(b):
        return remote(block_of(1 - core, b), from_sib.at[b], (to_sib, at_sib), b, scatter.sibling)

    def down(b):
        return along_line(outbox.at[b], inbox.at[b], (to_line, at_line), b, below)

    def own(b):
        part = pl.ds(b * tok, tok)
        return grad_kv[pl.ds(core * count, count), part, :].astype(f32) + from_sib[b].astype(f32)

    for b in range(planes):

        @pl.when(b <= z)
        def _():
            trade(b).start()

    scatter.taken(0)
    for b in range(planes):

        @pl.when(b <= z)
        def _():
            trade(b).wait_recv()

            @pl.when(z < planes - 1)
            def _():
                down(b).wait_recv()

        @pl.when((b < z) & (z < planes - 1))
        def _():
            outbox[b] = (own(b) + inbox[b].astype(f32)).astype(bf16)

        @pl.when((b < z) & (z == planes - 1))
        def _():
            outbox[b] = own(b).astype(bf16)

        @pl.when(b < z)
        def _():
            down(b).start()

        if b == 0:
            for j in range(half, chunks):
                scatter.far(j)
        if b == 1:
            gather.relay(0)
            for j in range(half):
                scatter.far(j)

    def keys(i, carry):
        rows = pl.ds(pl.multiple_of((core * count + i) * tok, tok), tok)
        part = pl.ds(pl.multiple_of(z * tok, tok), tok)
        total = grad_kv[core * count + i, part, :].astype(f32) + from_sib[z, i].astype(f32)
        total = total + jnp.where(z < planes - 1, inbox[z, i].astype(f32), 0.0)
        grad_qkv[rows, columns:] = turn_keys(total, cosine[rows, :], -sine[rows, :]).astype(bf16)
        return carry

    lax.fori_loop(0, count, keys, 0)
    for j in scatter.order:
        scatter.last(j)
    gather.finish()
    scatter.finish()
    for b in range(planes):

        @pl.when(b <= z)
        def _():
            trade(b).wait_send()

        @pl.when(b < z)
        def _():
            down(b).wait_send()

    for copy in [kept, w_kept] + w_copies:
        copy.wait()


def attention_back(
    heads, q, kv, starts, places, grad, mixed, log_total, cosine, sine, out_part, down_rows, w_part, call,
    chunks=4,
):
    planes, width = lax.axis_size(F), lax.axis_size(R)
    f32, bf16 = jnp.float32, jnp.bfloat16
    tok, model = out_part.shape[1:]
    length = kv.shape[1]
    vmem = pl.BlockSpec(memory_space=pltpu.VMEM)
    blocks = pltpu.VMEM((planes, width // 2, tok, 2 * HEAD_DIM), bf16)
    return pl.pallas_call(
        functools.partial(back_kernel, chunks, heads),
        out_shape=[
            jax.ShapeDtypeStruct((q.shape[0], q.shape[1] + 2 * HEAD_DIM), bf16),
            jax.ShapeDtypeStruct((tok, model), f32),
            jax.ShapeDtypeStruct((width,) + down_rows.shape, bf16),
            jax.ShapeDtypeStruct((width, w_part.shape[0], w_part.shape[1] // width), bf16),
        ],
        in_specs=[vmem] * 9 + [ANY] * 3,
        out_specs=[vmem] + [ANY] * 3,
        scratch_shapes=[
            pltpu.VMEM((length, 2 * HEAD_DIM), f32),
            pltpu.VMEM((width, length, 2 * HEAD_DIM), bf16),
            blocks,
            blocks,
            blocks,
        ]
        + [DMA((planes,))] * 4
        + [DMA, DMA, DMA((width - 1,)), DMA((width - 1,)), DMA((4,))]
        + Scatter.scratch(tok, model, chunks)
        + Gather.scratch(1),
        compiler_params=pltpu.CompilerParams(
            collective_id=call, has_side_effects=True, vmem_limit_bytes=60 << 20
        ),
    )(q, kv, starts, places, grad, mixed, log_total, cosine, sine, out_part, down_rows, w_part)


def hidden_kernel(chunks, grad_qkv, weight, feed_rows, grad_hidden, all_feed, feed_sem, *refs):
    bf16 = jnp.bfloat16
    scatter = Scatter(grad_hidden, chunks, refs[:12])
    gather = Gather(row_items(feed_rows, all_feed, chunks), refs[12:])
    tok = grad_hidden.shape[0]
    columns = grad_qkv.shape[1]
    greet(scatter.sibling, scatter.x, scatter.y)
    kept = pltpu.make_async_copy(feed_rows, all_feed.at[scatter.me], feed_sem)
    kept.start()
    gather.start()

    def block(i, carry):
        rows = pl.ds(pl.multiple_of(scatter.owner(i) * tok, tok), tok)
        scatter.put(i, dot(grad_qkv[rows, :], weight[:, :columns], 1, 1).astype(bf16))
        scatter.progress(i)
        return carry

    lax.fori_loop(0, grad_qkv.shape[0] // tok, block, 0)
    scatter.arrived(0)
    for i in range(chunks):
        gather.relay(i)
    for j in scatter.order:
        scatter.far(j)
    gather.finish()
    for j in scatter.order:
        scatter.last(j)
    scatter.finish()
    kept.wait()


def scatter_hidden(grad_qkv, weight, feed_rows, tok, call, chunks=4):
    width, model = lax.axis_size(R), weight.shape[0]
    vmem = pl.BlockSpec(memory_space=pltpu.VMEM)
    return pl.pallas_call(
        functools.partial(hidden_kernel, chunks),
        out_shape=[
            jax.ShapeDtypeStruct((tok, model), jnp.float32),
            jax.ShapeDtypeStruct((width,) + feed_rows.shape, jnp.bfloat16),
        ],
        in_specs=[vmem, vmem, ANY],
        out_specs=[ANY, ANY],
        scratch_shapes=[DMA] + Scatter.scratch(tok, model, chunks) + Gather.scratch(chunks),
        compiler_params=pltpu.CompilerParams(
            collective_id=call, has_side_effects=True, vmem_limit_bytes=40 << 20
        ),
    )(grad_qkv, weight, feed_rows)


def enter(tokens, gains, ids, call, chunks=4):
    planes, rows = lax.axis_size(F), lax.axis_size(R)
    tok, model = tokens.shape
    vmem = pl.BlockSpec(memory_space=pltpu.VMEM)
    return pl.pallas_call(
        functools.partial(enter_kernel, chunks),
        out_shape=[
            jax.ShapeDtypeStruct((rows, tok, model), jnp.bfloat16),
            jax.ShapeDtypeStruct((planes,) + gains.shape, jnp.float32),
            jax.ShapeDtypeStruct((rows,) + ids.shape, jnp.int32),
        ],
        in_specs=[vmem] * 3,
        out_specs=[ANY, vmem, vmem],
        scratch_shapes=[pltpu.VMEM((tok, model), jnp.bfloat16), DMA]
        + [DMA((planes - 1,))] * 2
        + Gather.scratch(chunks + 1),
        compiler_params=pltpu.CompilerParams(
            collective_id=call, has_side_effects=True, vmem_limit_bytes=32 << 20
        ),
    )(tokens, gains, ids)


def project(hidden, weight, cosine, sine, cotangent, call, chunks=4):
    planes, width = lax.axis_size(F), lax.axis_size(R)
    tok, model = cotangent.shape
    bf16 = jnp.bfloat16
    vmem = pl.BlockSpec(memory_space=pltpu.VMEM)
    return pl.pallas_call(
        functools.partial(project_kernel, chunks),
        out_shape=[
            jax.ShapeDtypeStruct((width * tok, weight.shape[1] - 2 * HEAD_DIM), bf16),
            jax.ShapeDtypeStruct((width, planes, tok, 2 * HEAD_DIM), bf16),
            jax.ShapeDtypeStruct((width, tok, model), bf16),
        ],
        in_specs=[vmem] * 4 + [ANY],
        out_specs=[vmem, ANY, ANY],
        scratch_shapes=[pltpu.VMEM((width, tok, 2 * HEAD_DIM), bf16), DMA, DMA]
        + [DMA((planes, width // 2))] * 2
        + [DMA((planes,))] * 2
        + Gather.scratch(chunks),
        compiler_params=pltpu.CompilerParams(
            collective_id=call, has_side_effects=True, vmem_limit_bytes=40 << 20
        ),
    )(hidden, weight, cosine, sine, cotangent)


def scatter_kernel(
    chunks, part, out, own, from_sib, give, got, give_far, got_far, total,
    own_sem, out_sem, to_sib, at_sib, to_near, at_near, to_far, at_far,
):
    f32, bf16 = jnp.float32, jnp.bfloat16
    me = lax.axis_index(R)
    flip = 1 - 2 * lax.rem(me, 2)
    sibling, beside_x, beside_y = me + flip, me ^ 2, me ^ 4
    rows = out.shape[0]
    size = rows // chunks
    half = chunks // 2
    owners = [me, beside_x, beside_y, me ^ 6]
    order = [c for j in range(half) for c in (j, half + j)]

    def rows_of(device, j):
        return part.at[pl.ds(pl.multiple_of(device * rows + j * size, 16), size)]

    def own_copy(d, j):
        return pltpu.make_async_copy(rows_of(owners[d], j), own.at[d, j], own_sem.at[d, j])

    def sib_copy(d, j):
        return remote(rows_of(owners[d] + flip, j), from_sib.at[d, j], (to_sib, at_sib), (d, j), sibling)

    def near_copy(j):
        device = beside_x if j < half else beside_y
        return remote(give.at[j], got.at[j], (to_near, at_near), j, device)

    def far_copy(j):
        device = beside_y if j < half else beside_x
        return remote(give_far.at[j], got_far.at[j], (to_far, at_far), j, device)

    def out_copy(j):
        return pltpu.make_async_copy(total.at[j], out.at[pl.ds(j * size, size)], out_sem.at[j])

    def summed(d, j):
        own_copy(d, j).wait()
        sib_copy(d, j).wait_recv()
        return own[d, j].astype(f32) + from_sib[d, j].astype(f32)

    for j in order:
        for d in (1, 2, 3, 0):
            own_copy(d, j).start()
    greet(sibling, beside_x, beside_y)
    for j in order:
        for d in (1, 3, 2, 0) if j < half else (2, 3, 1, 0):
            sib_copy(d, j).start()
    for j in order:
        give[j, 0] = summed(1 if j < half else 2, j).astype(bf16)
        give[j, 1] = summed(3, j).astype(bf16)
        near_copy(j).start()
    for j in order:
        passed = summed(2 if j < half else 1, j)
        kept = summed(0, j)
        near_copy(j).wait_recv()
        give_far[j] = (passed + got[j, 1].astype(f32)).astype(bf16)
        far_copy(j).start()
        total[j] = kept + got[j, 0].astype(f32)
    for j in order:
        far_copy(j).wait_recv()
        total[j] = total[j] + got_far[j].astype(f32)
        out_copy(j).start()
    for j in order:
        out_copy(j).wait()
        near_copy(j).wait_send()
        far_copy(j).wait_send()
        for d in range(4):
            sib_copy(d, j).wait_send()


def plane_gather(x, call, chunks=4):
    width = lax.axis_size(R)
    if width != 8:
        return lax.all_gather(x, R, axis=0, tiled=True)
    out = pl.pallas_call(
        functools.partial(gather_kernel, chunks),
        out_shape=jax.ShapeDtypeStruct((width,) + x.shape, x.dtype),
        in_specs=[ANY],
        out_specs=ANY,
        scratch_shapes=[DMA] + Gather.scratch(chunks),
        compiler_params=pltpu.CompilerParams(collective_id=call, has_side_effects=True),
    )(x)
    return out.reshape((width * x.shape[0],) + x.shape[1:])


def plane_scatter(x, call, chunks=4):
    width = lax.axis_size(R)
    if width != 8:
        return lax.psum_scatter(x, R, scatter_dimension=0, tiled=True).astype(jnp.float32)
    rows, columns = x.shape[0] // width, x.shape[1]
    size = rows // chunks
    bf16 = jnp.bfloat16
    return pl.pallas_call(
        functools.partial(scatter_kernel, chunks),
        out_shape=jax.ShapeDtypeStruct((rows, columns), jnp.float32),
        in_specs=[ANY],
        out_specs=ANY,
        scratch_shapes=[
            pltpu.VMEM((4, chunks, size, columns), bf16),
            pltpu.VMEM((4, chunks, size, columns), bf16),
            pltpu.VMEM((chunks, 2, size, columns), bf16),
            pltpu.VMEM((chunks, 2, size, columns), bf16),
            pltpu.VMEM((chunks, size, columns), bf16),
            pltpu.VMEM((chunks, size, columns), bf16),
            pltpu.VMEM((chunks, size, columns), jnp.float32),
            DMA((4, chunks)),
            DMA((chunks,)),
            DMA((4, chunks)),
            DMA((4, chunks)),
        ]
        + [DMA((chunks,))] * 4,
        compiler_params=pltpu.CompilerParams(
            collective_id=call, has_side_effects=True, vmem_limit_bytes=32 << 20
        ),
    )(x)


def line_gather(x):
    return lax.all_gather(x, F, axis=0, tiled=True)


def line_scatter(x):
    return lax.psum_scatter(x, F, scatter_dimension=0, tiled=True)


def heads_to_rows(block, heads):
    parts = [block[:, h * HEAD_DIM : (h + 1) * HEAD_DIM] for h in range(heads)]
    rows = jnp.concatenate(parts, axis=0)
    return jnp.concatenate([rows, jnp.zeros_like(rows)], axis=1)


def rows_to_heads(columns, heads):
    count = columns.shape[1] // heads
    return jnp.concatenate([columns[:, h * count : (h + 1) * count].T for h in range(heads)], axis=1)


def visible(block_index, starts, places):
    keys = block_index * KEY_BLOCK + lax.broadcasted_iota(jnp.int32, (KEY_BLOCK, starts.shape[1]), 0)
    return (keys >= starts) & (keys <= places)


def attention_kernel(heads, low, high, q, kv, starts, places, mixed, log_total):
    f32, bf16 = jnp.float32, jnp.bfloat16
    step = pl.program_id(0) * pl.num_programs(1) + pl.program_id(1)
    queries = heads_to_rows(q[...] * bf16(HEAD_DIM**-0.5), heads)
    first = jnp.concatenate([starts[0]] * heads, axis=1)
    place = jnp.concatenate([places[0]] * heads, axis=1)
    columns = queries.shape[0]

    def block(index, carry):
        top, total, acc = carry
        rows = kv[0, pl.ds(pl.multiple_of(index * KEY_BLOCK, KEY_BLOCK), KEY_BLOCK), :]
        scores = jnp.where(visible(index, first, place), dot(rows, queries, 1, 1), NEGATIVE)
        new_top = jnp.maximum(top, jnp.max(scores, axis=0, keepdims=True))
        weights = jnp.exp(scores - new_top)
        fade = jnp.exp(top - new_top)
        total = total * fade + jnp.sum(weights, axis=0, keepdims=True)
        acc = acc * fade + dot(rows, weights.astype(bf16), 0, 0)
        return new_top, total, acc

    top, total, acc = lax.fori_loop(
        low[step],
        high[step],
        block,
        (
            jnp.full((1, columns), NEGATIVE, f32),
            jnp.zeros((1, columns), f32),
            jnp.zeros((2 * HEAD_DIM, columns), f32),
        ),
    )
    mixed[...] = rows_to_heads(acc[HEAD_DIM:] / total, heads).astype(bf16)
    log_total[0] = top + jnp.log(total)


def attention_back_kernel(
    heads, low, high, q, kv, starts, places, grad, mixed, log_total, grad_q, grad_kv, sums
):
    f32, bf16 = jnp.float32, jnp.bfloat16
    step = pl.program_id(0) * pl.num_programs(1) + pl.program_id(1)
    queries = heads_to_rows(q[...] * bf16(HEAD_DIM**-0.5), heads)
    grads = heads_to_rows(grad[...], heads)
    first = jnp.concatenate([starts[0]] * heads, axis=1)
    place = jnp.concatenate([places[0]] * heads, axis=1)
    columns = queries.shape[0]
    products = grads.astype(f32) * heads_to_rows(mixed[...], heads).astype(f32)
    delta = lax.dot_general(
        jnp.ones((8, 2 * HEAD_DIM), f32),
        products,
        (((1,), (1,)), ((), ())),
        precision=lax.Precision.HIGHEST,
        preferred_element_type=f32,
    )[:1]
    level = log_total[0]
    upper = pltpu.roll(grads.astype(f32), HEAD_DIM, 1).astype(bf16)

    @pl.when(pl.program_id(1) == 0)
    def _():
        sums[...] = jnp.zeros_like(sums)

    def block(index, acc):
        part = pl.ds(pl.multiple_of(index * KEY_BLOCK, KEY_BLOCK), KEY_BLOCK)
        rows = kv[0, part, :]
        scores = dot(rows, queries, 1, 1)
        probs = jnp.where(visible(index, first, place), jnp.exp(scores - level), 0.0)
        grad_probs = dot(rows, upper, 1, 1)
        grad_scores = (probs * (grad_probs - delta)).astype(bf16)
        sums[part, :] += dot(grad_scores, queries) + dot(probs.astype(bf16), upper)
        return acc + dot(rows, grad_scores, 0, 0)

    acc = lax.fori_loop(low[step], high[step], block, jnp.zeros((2 * HEAD_DIM, columns), f32))
    grad_q[...] = rows_to_heads(acc[:HEAD_DIM] * HEAD_DIM**-0.5, heads)

    @pl.when(pl.program_id(1) == PARTS - 1)
    def _():
        grad_kv[0] = sums[...].astype(bf16)


def attention_call(kernel, heads, low, high, arrays, outs, scratch=()):
    blocks = {
        "tokens": lambda shape: pl.BlockSpec((QUERY_BLOCK, shape[1]), lambda s, b, *_: (s * PARTS + b, 0)),
        "row": lambda shape: pl.BlockSpec((1,) + shape[1:], lambda s, b, *_: (s * PARTS + b, 0, 0)),
        "sequence": lambda shape: pl.BlockSpec((1,) + shape[1:], lambda s, b, *_: (s, 0, 0)),
    }
    return pl.pallas_call(
        functools.partial(kernel, heads),
        grid_spec=pltpu.PrefetchScalarGridSpec(
            num_scalar_prefetch=2,
            grid=(low.shape[0] // PARTS, PARTS),
            in_specs=[blocks[kind](x.shape) for kind, x in arrays],
            out_specs=[blocks[kind](x.shape) for kind, x in outs],
            scratch_shapes=scratch,
        ),
        out_shape=[x for _, x in outs],
        compiler_params=pltpu.CompilerParams(vmem_limit_bytes=32 << 20),
    )(low, high, *[x for _, x in arrays])


def join_feed_kernel(planes, piece, x, gate, up):
    width = x.shape[0]
    for kind, out in enumerate((gate, up)):
        for p in range(planes):
            for r in range(width):
                first = (kind * planes + p) * piece
                to = (p * width + r) * piece
                out[:, to : to + piece] = x[r, :, first : first + piece].astype(jnp.float32)


def join_attention_kernel(sharers, qkv, o, query, key, value, out):
    f32 = jnp.float32
    width, qw, ow = qkv.shape[0], qkv.shape[2] - 2 * HEAD_DIM, o.shape[2]
    for r in range(width):
        query[:, r * qw : (r + 1) * qw] = qkv[r, :, :qw].astype(f32)
        out[:, r * ow : (r + 1) * ow] = o[r].astype(f32)
    for head in range(width // sharers):
        both = sum(qkv[head * sharers + i, :, qw:].astype(f32) for i in range(sharers))
        to = slice(head * HEAD_DIM, (head + 1) * HEAD_DIM)
        key[:, to] = both[:, :HEAD_DIM]
        value[:, to] = both[:, HEAD_DIM:]


def join_call(kernel, arrays, outs, block=64):
    rows = arrays[0].shape[1]
    return pl.pallas_call(
        kernel,
        grid=(rows // block,),
        in_specs=[pl.BlockSpec((x.shape[0], block, x.shape[2]), lambda i: (0, i, 0)) for x in arrays],
        out_specs=[pl.BlockSpec((block, columns), lambda i: (i, 0)) for columns in outs],
        out_shape=[jax.ShapeDtypeStruct((rows, columns), jnp.float32) for columns in outs],
        compiler_params=pltpu.CompilerParams(vmem_limit_bytes=32 << 20),
    )(*arrays)


def per_device(
    tokens,
    segment_ids,
    attention_gain,
    query_weight,
    key_weight,
    value_weight,
    output_weight,
    feed_gain,
    gate_weight,
    up_weight,
    down_weight,
    cotangent,
):
    f32, bf16 = jnp.float32, jnp.bfloat16
    planes, width = lax.axis_size(F), lax.axis_size(R)
    r, z = lax.axis_index(R), lax.axis_index(F)
    tok, model = tokens.shape
    length = segment_ids.shape[1]
    all_tok = width * tok
    plane_kernels = width == 8
    heads = HEADS // width
    group = HEADS // KV_HEADS
    qw = heads * HEAD_DIM
    kv = (r * heads) // group
    feed = gate_weight.shape[1]
    piece = feed // (width * planes)
    hidden_units = piece * planes

    def cols(weight, first, count):
        return lax.dynamic_slice_in_dim(weight, first, count, 1)

    def feed_cols(weight):
        return [cols(weight, p * (feed // planes) + r * piece, piece) for p in range(planes)]

    w_attention = line_gather(
        jnp.concatenate(
            [
                cols(query_weight, r * qw, qw),
                cols(key_weight, kv * HEAD_DIM, HEAD_DIM),
                cols(value_weight, kv * HEAD_DIM, HEAD_DIM),
                cols(output_weight, r * (model // width), model // width),
            ],
            axis=1,
        )
    )
    w_qkv = w_attention[:, : qw + 2 * HEAD_DIM]
    w_out = lax.all_to_all(
        w_attention[:, qw + 2 * HEAD_DIM :], R, split_axis=0, concat_axis=1, tiled=True
    )
    own_gains = jnp.stack([attention_gain, feed_gain]).astype(f32)
    tok_float = tokens.astype(f32)
    scale_in = inverse_rms(tok_float)
    normed_in = tok_float * scale_in
    if plane_kernels:
        hidden_in, gains, ids = enter(
            tokens, jnp.pad(own_gains, ((0, 6), (0, 0))), segment_ids.reshape(8, length // 8), 0
        )
        hidden_in = hidden_in.reshape(all_tok, model)
        gains = gains[:, :2].transpose(1, 0, 2).reshape(2, model)
        ids = ids.reshape(width, length)
    else:
        gains = lax.all_gather(own_gains, F, axis=1, tiled=True)
        hidden_in = lax.all_gather((normed_in * gains[0]).astype(bf16), R, axis=0, tiled=True)
        ids = lax.all_gather(segment_ids, R, axis=0, tiled=True)
    gain_in, gain_mid = gains[0], gains[1]
    gate_weight, up_weight, down_weight, ids = lax.optimization_barrier(
        (gate_weight, up_weight, down_weight, ids)
    )
    w_feed = line_gather(jnp.concatenate(feed_cols(gate_weight) + feed_cols(up_weight), axis=1))
    w_down = line_gather(lax.dynamic_slice_in_dim(down_weight, r * piece, piece, 0))

    places = jnp.arange(length, dtype=jnp.int32)
    fresh = jnp.concatenate(
        [jnp.ones((width, 1), dtype=jnp.bool_), ids[:, 1:] != ids[:, :-1]], axis=1
    )
    positions = places[None] - lax.cummax(jnp.where(fresh, places[None], 0), axis=1)
    own_positions = lax.dynamic_slice_in_dim(positions, z * tok, tok, 1).reshape(all_tok)
    own_places = z * tok + jnp.arange(all_tok, dtype=jnp.int32) % tok
    own_starts = own_places - own_positions
    steps = all_tok // QUERY_BLOCK
    starts = own_starts.reshape(steps, 1, QUERY_BLOCK)
    query_places = own_places.reshape(steps, 1, QUERY_BLOCK)
    low = starts[:, 0, 0] // KEY_BLOCK
    high = query_places[:, 0, QUERY_BLOCK - 1] // KEY_BLOCK + 1

    if plane_kernels:
        wide_cosine, wide_sine = rope_tables(own_positions, 4)
        wide_sine = wide_sine * jnp.where(jnp.arange(2 * HEAD_DIM) // (HEAD_DIM // 2) % 2, 1.0, -1.0)
        query, kv_rows, cot_all = project(hidden_in, w_qkv, wide_cosine, wide_sine, cotangent, 3)
        kv_rows = kv_rows.reshape(width, length, 2 * HEAD_DIM)
        cot_all = cot_all.reshape(all_tok, model)
    else:
        cosine, sine = rope_tables(own_positions)
        qkv = dot(hidden_in, w_qkv)
        query = rotate(qkv[:, :qw].reshape(all_tok, heads, HEAD_DIM), cosine, sine, 1.0)
        query = query.astype(bf16).reshape(all_tok, qw)
        key = rotate(qkv[:, None, qw : qw + HEAD_DIM], cosine, sine, 1.0).astype(bf16)[:, 0]
        value = qkv[:, qw + HEAD_DIM :].astype(bf16)
        kv_rows = (
            lax.all_gather(jnp.concatenate([key, value], axis=1), F, axis=0, tiled=False)
            .reshape(planes, width, tok, 2 * HEAD_DIM)
            .transpose(1, 0, 2, 3)
            .reshape(width, length, 2 * HEAD_DIM)
        )
        cot_all = lax.all_gather(cotangent, R, axis=0, tiled=True)
    common = [("tokens", query), ("sequence", kv_rows), ("row", starts), ("row", query_places)]
    mixed, log_totals = attention_call(
        attention_kernel,
        heads,
        low,
        high,
        common,
        [
            ("tokens", jax.ShapeDtypeStruct((all_tok, qw), bf16)),
            ("row", jax.ShapeDtypeStruct((steps, 1, heads * QUERY_BLOCK), f32)),
        ],
    )
    if plane_kernels:
        cot_blocks = cot_all.reshape(width, tok, model)
        middle, hidden_blocks, acts, down_part = middle_layer(
            mixed, w_out, tokens, gain_mid[None], w_feed, cot_blocks, 1
        )
    else:
        middle = tok_float + plane_scatter(dot(mixed, w_out).astype(bf16), 1)
    scale_mid = inverse_rms(middle)
    normed_mid = middle * scale_mid

    if plane_kernels:
        out_part, grad_hidden_mid, feed_part = feed_forward(
            hidden_blocks, cot_blocks, acts, w_feed, w_down, 5
        )
    else:
        w_gate, w_up = w_feed[:, :hidden_units], w_feed[:, hidden_units:]
        hidden_mid = plane_gather((normed_mid * gain_mid).astype(bf16), 2)
        gate_acc = dot(hidden_mid, w_gate)
        up_acc = dot(hidden_mid, w_up)
        gate_sig = jax.nn.sigmoid(gate_acc)
        gate_silu = gate_acc * gate_sig
        inner_act = (gate_silu * up_acc).astype(bf16)
        out_part = dot(inner_act, w_down).astype(bf16)
        grad_inner = dot(cot_all, w_down, 1, 1)
        grad_gate = grad_inner * up_acc * gate_sig * (1.0 + gate_acc * (1.0 - gate_sig))
        grad_gate = grad_gate.astype(bf16)
        grad_up = (grad_inner * gate_silu).astype(bf16)
        feed_part = jnp.concatenate(
            [dot(hidden_mid, grad_gate, 0, 0), dot(hidden_mid, grad_up, 0, 0)], axis=1
        ).astype(bf16)
        down_part = dot(inner_act, cot_all, 0, 0).astype(bf16)
        grad_hidden_part = dot(grad_gate, w_gate, 1, 1) + dot(grad_up, w_up, 1, 1)
        grad_hidden_mid = plane_scatter(grad_hidden_part.astype(bf16), 5)
        feed_out = plane_scatter(out_part, 4)
    down_rows = line_scatter(down_part)
    feed_rows = line_scatter(feed_part)
    gain_mid_term = jnp.sum(grad_hidden_mid * normed_mid, axis=0)
    grad_normed_mid = grad_hidden_mid * gain_mid
    grad_middle = cotangent.astype(f32) + scale_mid * (
        grad_normed_mid - normed_mid * jnp.mean(grad_normed_mid * normed_mid, axis=1, keepdims=True)
    )

    grad_branch = plane_gather(grad_middle.astype(bf16), 6)
    grad_mixed = dot(grad_branch, w_out, 1, 1).astype(bf16)
    w_out_part = dot(mixed, grad_branch, 0, 0).astype(bf16)

    if plane_kernels:
        grad_qkv, feed_out, down_all, w_out_part = attention_back(
            heads,
            query,
            kv_rows,
            starts,
            query_places,
            grad_mixed,
            mixed,
            log_totals,
            wide_cosine,
            wide_sine,
            out_part,
            down_rows,
            w_out_part,
            10,
        )
        w_out_part = w_out_part.reshape(width * qw, model // width)
    else:
        gq, gkv = attention_call(
            attention_back_kernel,
            heads,
            low,
            high,
            common + [("tokens", grad_mixed), ("tokens", mixed), ("row", log_totals)],
            [
                ("tokens", jax.ShapeDtypeStruct((all_tok, qw), f32)),
                ("sequence", jax.ShapeDtypeStruct((width, length, 2 * HEAD_DIM), bf16)),
            ],
            [pltpu.VMEM((length, 2 * HEAD_DIM), f32)],
        )
        gkv = gkv.reshape(width, planes, tok, 2 * HEAD_DIM).transpose(1, 0, 2, 3)
        gkv = line_scatter(gkv.reshape(planes * all_tok, 2 * HEAD_DIM)).astype(f32)
        gq = rotate(gq.reshape(all_tok, heads, HEAD_DIM), cosine, sine, -1.0)
        gk = rotate(gkv[:, None, :HEAD_DIM], cosine, sine, -1.0)[:, 0]
        grad_qkv = jnp.concatenate([gq.reshape(all_tok, qw), gk, gkv[:, HEAD_DIM:]], axis=1)
        grad_qkv = grad_qkv.astype(bf16)
        down_all = lax.all_gather(down_rows, R, axis=0, tiled=True)
        w_out_part = lax.all_to_all(w_out_part, R, split_axis=1, concat_axis=0, tiled=True)
    out_rows = line_scatter(w_out_part)
    activations = (middle + feed_out).astype(bf16)
    qkv_part = dot(hidden_in, grad_qkv, 0, 0).astype(bf16)
    grad_qkv, qkv_part, feed_rows = lax.optimization_barrier((grad_qkv, qkv_part, feed_rows))
    qkv_rows = line_scatter(qkv_part)
    if plane_kernels:
        grad_hidden_in, feed_all = scatter_hidden(grad_qkv, w_attention, feed_rows, tok, 7)
    else:
        grad_hidden_in = plane_scatter(dot(grad_qkv, w_qkv, 1, 1).astype(bf16), 7)
        feed_all = lax.all_gather(feed_rows, R, axis=0, tiled=False)
    gain_in_term = jnp.sum(grad_hidden_in * normed_in, axis=0)
    grad_normed_in = grad_hidden_in * gain_in
    input_grad = (
        grad_middle
        + scale_in
        * (
            grad_normed_in
            - normed_in * jnp.mean(grad_normed_in * normed_in, axis=1, keepdims=True)
        )
    ).astype(bf16)

    rows = model // planes
    terms = jnp.stack([gain_in_term, gain_mid_term])
    if plane_kernels:
        terms = jnp.pad(terms.reshape(2, planes, rows).transpose(1, 0, 2), ((0, 0), (0, 6), (0, 0)))
        qkv_all, out_all, gain_terms = finish(qkv_rows, out_rows, terms, 9)
    else:
        qkv_all = lax.all_gather(qkv_rows, R, axis=0, tiled=False)
        out_all = lax.all_gather(out_rows, R, axis=0, tiled=False)
        gain_terms = lax.psum(lax.psum_scatter(terms, F, scatter_dimension=1, tiled=True), R)
    down_grad = down_all.reshape(feed // planes, model).astype(f32)
    gate_grad, up_grad = join_call(
        functools.partial(join_feed_kernel, planes, piece), [feed_all], [feed, feed]
    )
    query_grad, key_grad, value_grad, out_grad = join_call(
        functools.partial(join_attention_kernel, width // KV_HEADS),
        [qkv_all, out_all],
        [width * qw, KV_HEADS * HEAD_DIM, KV_HEADS * HEAD_DIM, model],
    )
    return (
        activations,
        input_grad,
        gain_terms[0],
        query_grad,
        key_grad,
        value_grad,
        out_grad,
        gain_terms[1],
        gate_grad,
        up_grad,
        down_grad,
    )


def solution(mesh):
    tok = P((R, F), None)
    row = P(F, None)
    in_specs = (tok, P(R, None), P(F), row, row, row, row, P(F), row, row, row, tok)
    out_specs = (tok, tok, P(F), row, row, row, row, P(F), row, row, row)
    return jax.shard_map(
        per_device, mesh=mesh, in_specs=in_specs, out_specs=out_specs, check_vma=False
    )
```

```python
import functools
import math

import jax
import jax.numpy as jnp
from jax import lax
from jax.experimental import pallas as pl
from jax.experimental.pallas import tpu as pltpu
from jax.sharding import PartitionSpec as P

HEADS = 32
KV_HEADS = 4
HEAD_DIM = 64
EPSILON = 1e-05
NEGATIVE = -1e30
R = "replica"
F = "fsdp"
MESH = pl.DeviceIdType.MESH
DMA = pltpu.SemaphoreType.DMA
ANY = pl.BlockSpec(memory_space=pl.ANY)
KEY_BLOCK = 256
QUERY_BLOCK = 128
PARTS = 2
FIRST_DOC = 800


def inverse_rms(values):
    return lax.rsqrt(jnp.mean(values * values, axis=1, keepdims=True) + EPSILON)


def rope_tables(positions, repeats=1):
    half_dim = HEAD_DIM // 2
    places = jnp.arange(repeats * half_dim, dtype=jnp.int32) % half_dim
    freq_rates = jnp.exp(places.astype(jnp.float32) * (-math.log(10000.0) / half_dim))
    angles = positions.astype(jnp.float32)[:, None] * freq_rates[None, :]
    return (jnp.cos(angles), jnp.sin(angles))


def rotate(tensor, cosine_table, sine_table, sign):
    half_dim = HEAD_DIM // 2
    low, up = tensor[..., :half_dim], tensor[..., half_dim:]
    cos_part = cosine_table[:, None, :]
    sin_part = sine_table[:, None, :] * sign
    return jnp.concatenate(
        [low * cos_part - up * sin_part, up * cos_part + low * sin_part], axis=-1
    )


def dot(a, b, ca=1, cb=0):
    return lax.dot_general(a, b, (((ca,), (cb,)), ((), ())), preferred_element_type=jnp.float32)


def remote(src, dst, sems, index, device):
    return pltpu.make_async_remote_copy(
        src_ref=src,
        dst_ref=dst,
        send_sem=sems[0].at[index],
        recv_sem=sems[1].at[index],
        device_id={R: device},
        device_id_type=MESH,
    )


def greet(*devices):
    barrier = pltpu.get_barrier_semaphore()
    for device in devices:
        pl.semaphore_signal(barrier, inc=1, device_id={R: device}, device_id_type=MESH)
    pl.semaphore_wait(barrier, len(devices))


class Gather:
    @staticmethod
    def scratch(count):
        return [DMA((count,))] * 6 + [DMA((4, count))] * 2

    def __init__(self, items, sems):
        self.items, self.count = items, len(items)
        self.half = self.count // 2
        self.me = lax.axis_index(R)
        self.sibling, self.x, self.y = self.me + 1 - 2 * lax.rem(self.me, 2), self.me ^ 2, self.me ^ 4
        self.sems = sems

    def copy(self, kind, i):
        first = i < self.half
        owner, device = {
            0: (self.me, self.x),
            1: (self.me, self.y),
            2: (self.x, self.y) if first else (self.y, self.x),
            3: (self.me, self.sibling),
            4: (self.x, self.sibling),
            5: (self.y, self.sibling),
            6: (self.me ^ 6, self.sibling),
        }[kind]
        own, slot = self.items[i]
        sems = self.sems[2 * min(kind, 3) : 2 * min(kind, 3) + 2]
        src = own if kind in (0, 1, 3) else slot(owner)
        return remote(src, slot(owner), sems, i if kind < 3 else (kind - 3, i), device)

    def start(self, kept=()):
        ready = [i for i in range(self.count) if i not in kept]
        for n, i in enumerate(ready):
            self.copy(0, i).start()
            self.copy(1, ready[(n + self.half) % len(ready)]).start()
        for i in ready:
            self.copy(3, i).start()

    def start_items(self, items):
        for i in items:
            for kind in (0, 1, 3):
                self.copy(kind, i).start()

    def pass_on(self, kind, i):
        self.copy(kind, i).wait_recv()
        if kind < 2 and (i < self.half) == (kind == 0):
            self.copy(2, i).start()
        self.copy(kind + 4, i).start()

    def relay(self, i):
        self.pass_on(0, i)
        self.pass_on(1, (i + self.half) % self.count)

    def far(self):
        for i in range(self.half):
            self.pass_on(2, i)
            self.pass_on(2, self.half + i)
        for i in range(2 * self.half, self.count):
            self.pass_on(2, i)

    def from_sibling(self, kind):
        for i in range(self.count):
            self.copy(kind, i).wait_recv()

    def wait_sends(self):
        for i in range(self.count):
            for kind in range(7):
                self.copy(kind, i).wait_send()

    def finish(self):
        self.far()
        for kind in range(3, 7):
            self.from_sibling(kind)
        self.wait_sends()


def row_items(x, out, chunks):
    size = x.shape[0] // chunks

    def item(i):
        part = pl.ds(i * size, size)
        return x.at[part], lambda owner: out.at[owner, part]

    return [item(i) for i in range(chunks)]


def gather_kernel(chunks, x, out, local_sem, *sems):
    gather = Gather(row_items(x, out, chunks), sems)
    greet(gather.sibling, gather.x, gather.y)
    own = pltpu.make_async_copy(x, out.at[gather.me], local_sem)
    own.start()
    gather.start()
    for i in range(chunks):
        gather.relay(i)
    gather.finish()
    own.wait()


def enter_kernel(chunks, tokens, gains, ids, hidden, all_gains, all_ids, own, own_sem, to_z, at_z, *sems):
    f32 = jnp.float32
    planes = all_gains.shape[0]
    z = lax.axis_index(F)
    items = row_items(own, hidden, chunks) + [(ids, lambda owner: all_ids.at[owner])]
    gather = Gather(items, sems)
    others = [lax.rem(z + i, planes) for i in range(1, planes)]
    barrier = pltpu.get_barrier_semaphore()
    for other in others:
        pl.semaphore_signal(barrier, inc=1, device_id={F: other}, device_id_type=MESH)
    for device in (gather.sibling, gather.x, gather.y):
        pl.semaphore_signal(barrier, inc=1, device_id={R: device}, device_id_type=MESH)
    pl.semaphore_wait(barrier, planes + 2)
    copies = [
        pltpu.make_async_remote_copy(
            src_ref=gains,
            dst_ref=all_gains.at[z],
            send_sem=to_z.at[i],
            recv_sem=at_z.at[i],
            device_id={F: other},
            device_id_type=MESH,
        )
        for i, other in enumerate(others)
    ]
    for copy in copies:
        copy.start()
    all_gains[z] = gains[...]
    all_ids[gather.me] = ids[...]
    size = tokens.shape[0] // chunks
    scales = [
        inverse_rms(tokens[i * size : (i + 1) * size, :].astype(f32)) for i in range(chunks)
    ]
    for copy in copies:
        copy.wait()
    gain = jnp.concatenate([all_gains[p, 0:1] for p in range(planes)], axis=1)
    for i in range(chunks):
        part = slice(i * size, (i + 1) * size)
        own[part, :] = (tokens[part, :].astype(f32) * scales[i] * gain).astype(jnp.bfloat16)
    kept = pltpu.make_async_copy(own, hidden.at[gather.me], own_sem)
    kept.start()
    gather.start()
    for i in range(gather.count):
        gather.relay(i)
    gather.finish()
    kept.wait()


def turn(x, cosine, sine):
    half_dim = HEAD_DIM // 2
    low = lax.rem(lax.broadcasted_iota(jnp.int32, x.shape, 1), HEAD_DIM) < half_dim
    swapped = jnp.where(low, pltpu.roll(x, 2 * HEAD_DIM - half_dim, 1), pltpu.roll(x, half_dim, 1))
    return x * cosine + swapped * sine


def turn_keys(x, cosine, sine):
    is_key = lax.broadcasted_iota(jnp.int32, x.shape, 1) < HEAD_DIM
    return jnp.where(is_key, turn(x, cosine, sine), x)


def along_line(src, dst, sems, index, plane):
    return pltpu.make_async_remote_copy(
        src_ref=src,
        dst_ref=dst,
        send_sem=sems[0].at[index],
        recv_sem=sems[1].at[index],
        device_id={F: plane},
        device_id_type=MESH,
    )


def project_kernel(
    chunks, hidden, weight, cosine, sine, cotangent, w_cols, query, kv, cot_all, w_out,
    own, hidden_in, hidden_sems, own_sem, cot_sem, w_sem, to_all, at_all, to_line, at_line, to_sib, at_sib,
    *sems,
):
    bf16 = jnp.bfloat16
    planes = kv.shape[1]
    z = lax.axis_index(F)
    tok = cotangent.shape[0]
    width = kv.shape[0]
    count = width // 2
    gather = Gather(row_items(cotangent, cot_all, chunks), sems)
    core = lax.rem(gather.me, 2)
    mine = pl.ds(core * count, count)
    above, below = lax.rem(z + 1, planes), lax.rem(z + planes - 1, planes)
    me = gather.me
    peers = [me ^ distance for distance in range(1, width)]

    def hidden_load(i):
        slot = lax.rem(i, 2)
        block = hidden.at[lax.rem(core * count + i, width)]
        return pltpu.make_async_copy(block, hidden_in.at[slot], hidden_sems.at[slot])

    for i in (0, 1):
        hidden_load(i).start()
    barrier = pltpu.get_barrier_semaphore()
    for other in (above, below):
        pl.semaphore_signal(barrier, inc=1, device_id={F: other}, device_id_type=MESH)
    for device in peers:
        pl.semaphore_signal(barrier, inc=1, device_id={R: device}, device_id_type=MESH)
    pl.semaphore_wait(barrier, 1 + width)
    rows = w_out.shape[0]
    share = w_out.shape[1] // width
    to = w_out.at[:, pl.ds(pl.multiple_of(me * share, share), share)]

    def rows_of(device):
        part = pl.ds(pl.multiple_of(device * rows, rows), rows)
        return w_cols.at[part, pl.ds(w_cols.shape[1] - share, share)]

    w_copies = [
        remote(rows_of(device), to, (to_all, at_all), i, device) for i, device in enumerate(peers)
    ]
    w_kept = pltpu.make_async_copy(rows_of(me), to, w_sem)
    kept_cot = pltpu.make_async_copy(cotangent, cot_all.at[gather.me], cot_sem)
    kept_cot.start()
    gather.start()
    for copy in [w_kept] + w_copies:
        copy.start()

    def tile(i, carry):
        s = lax.rem(core * count + i, width)
        rows = pl.ds(pl.multiple_of(s * tok, tok), tok)
        hidden_load(i).wait()
        acc = dot(hidden_in[lax.rem(i, 2)], weight[:, : query.shape[1] + 2 * HEAD_DIM])

        @pl.when(i + 2 < width)
        def _():
            hidden_load(i + 2).start()

        c, n = cosine[rows, :], sine[rows, :]
        columns = acc.shape[1] - 2 * HEAD_DIM
        for first in range(0, columns, 2 * HEAD_DIM):
            part = slice(first, first + 2 * HEAD_DIM)
            query[rows, part] = turn(acc[:, part], c, n).astype(bf16)
        own[s] = turn_keys(acc[:, columns:], c, n).astype(bf16)
        return carry

    class Group:
        def __init__(self, make):
            self.each = [make(i) for i in range(count)]

        def __getattr__(self, name):
            def call():
                for copy in self.each:
                    getattr(copy, name)()

            return call

    def up(step):
        slot = z - step

        def make(i):
            dst = kv.at[core * count + i, slot]
            src = own.at[core * count + i] if step == 0 else dst
            return along_line(src, dst, (to_line, at_line), (step, i), above)

        return Group(make)

    def came(step):
        def make(i):
            dst = kv.at[core * count + i, z - step]
            return along_line(dst, dst, (to_line, at_line), (step - 1, i), above)

        return Group(make)

    def across(step):
        slot = z - step
        return remote(kv.at[mine, slot], kv.at[mine, slot], (to_sib, at_sib), step, gather.sibling)

    lax.fori_loop(0, count, tile, 0)

    @pl.when(z < planes - 1)
    def _():
        up(0).start()

    lax.fori_loop(count, width, tile, 0)
    kept = pltpu.make_async_copy(own, kv.at[:, z], own_sem)
    kept.start()
    done = 0
    for step in range(1, planes):

        @pl.when(z >= step)
        def _():
            arriving, leaving = came(step), up(step)
            for i in range(count):
                arriving.each[i].wait_recv()

                @pl.when(z < planes - 1)
                def _():
                    leaving.each[i].start()

            across(step).start()

        while done < chunks * step // planes:
            gather.relay(done)
            done += 1
    for i in range(done, chunks):
        gather.relay(i)
    gather.finish()
    for step in range(planes):

        @pl.when((z >= step) & (z < planes - 1))
        def _():
            up(step).wait_send()

        if step:

            @pl.when(z >= step)
            def _():
                across(step).wait()

    for copy in [kept, kept_cot, w_kept] + w_copies:
        copy.wait()


def finish_kernel(
    qkv, out_rows, terms, all_qkv, all_out, gains, own_gain, all_gains,
    at_planes, own_sems, to_z, at_z, *sems,
):
    planes = terms.shape[0]
    z = lax.axis_index(F)
    chunks = [x for pair in zip(row_items(qkv, all_qkv, 2), row_items(out_rows, all_out, 2)) for x in pair]
    gather = Gather(chunks + [(own_gain, lambda owner: all_gains.at[owner])], sems)
    me, last = gather.me, gather.count - 1
    others = [lax.rem(z + i, planes) for i in range(1, planes)]
    barrier = pltpu.get_barrier_semaphore()
    for other in others:
        pl.semaphore_signal(barrier, inc=1, device_id={F: other}, device_id_type=MESH)
    for device in (gather.sibling, gather.x, gather.y):
        pl.semaphore_signal(barrier, inc=1, device_id={R: device}, device_id_type=MESH)
    pl.semaphore_wait(barrier, planes + 2)
    copies = [
        along_line(terms.at[other], at_planes.at[i], (to_z, at_z), i, other)
        for i, other in enumerate(others)
    ]
    for copy in copies:
        copy.start()
    kept = [
        pltpu.make_async_copy(qkv, all_qkv.at[me], own_sems.at[0]),
        pltpu.make_async_copy(out_rows, all_out.at[me], own_sems.at[1]),
    ]
    for copy in kept:
        copy.start()
    gather.start((last,))
    total = terms[z]
    for i, copy in enumerate(copies):
        copy.wait()
        total = total + at_planes[i]
    own_gain[...] = total
    all_gains[me] = total
    gather.start_items((last,))
    for i in range(gather.count):
        gather.relay(i)
    gather.finish()
    total = all_gains[0]
    for device in range(1, all_gains.shape[0]):
        total = total + all_gains[device]
    gains[...] = total
    for copy in kept:
        copy.wait()


def finish(qkv, out_rows, terms, call):
    planes, width = lax.axis_size(F), lax.axis_size(R)
    f32, bf16 = jnp.float32, jnp.bfloat16
    vmem = pl.BlockSpec(memory_space=pltpu.VMEM)
    block = terms.shape[1:]
    return pl.pallas_call(
        finish_kernel,
        out_shape=[
            jax.ShapeDtypeStruct((width,) + qkv.shape, bf16),
            jax.ShapeDtypeStruct((width,) + out_rows.shape, bf16),
            jax.ShapeDtypeStruct(block, f32),
        ],
        in_specs=[ANY, ANY, vmem],
        out_specs=[ANY, ANY, vmem],
        scratch_shapes=[
            pltpu.VMEM(block, f32),
            pltpu.VMEM((width,) + block, f32),
            pltpu.VMEM((planes - 1,) + block, f32),
            DMA((2,)),
            DMA((planes - 1,)),
            DMA((planes - 1,)),
        ]
        + Gather.scratch(5),
        compiler_params=pltpu.CompilerParams(collective_id=call, has_side_effects=True),
    )(qkv, out_rows, terms)


class Scatter:
    @staticmethod
    def scratch(rows, columns, chunks):
        bf16, size = jnp.bfloat16, rows // chunks
        return [
            pltpu.VMEM((5, rows, columns), bf16),
            pltpu.VMEM((4, rows, columns), bf16),
            pltpu.VMEM((chunks, 2, size, columns), bf16),
            pltpu.VMEM((chunks, size, columns), bf16),
            pltpu.VMEM((2, size, columns), jnp.float32),
            DMA((4,)),
            DMA((4,)),
            DMA((chunks, 2)),
            DMA((chunks, 2)),
            DMA((chunks,)),
            DMA((chunks,)),
            DMA((2,)),
        ]

    def __init__(self, out, chunks, refs):
        self.out, self.chunks, self.half = out, chunks, chunks // 2
        self.own, self.sib, self.got, self.got_far, self.total = refs[:5]
        self.sib_sems, self.near_sems, self.far_sems = refs[5:7], refs[7:9], refs[9:11]
        self.out_sem = refs[11]
        self.me = lax.axis_index(R)
        self.sibling, self.x, self.y = self.me + 1 - 2 * lax.rem(self.me, 2), self.me ^ 2, self.me ^ 4
        self.size = out.shape[0] // chunks
        self.order = [*range(self.half, chunks), *range(self.half)]
        self.trades = None

    def owner(self, i):
        return (self.me ^ (6 - 2 * (i // 2))) ^ (1 - lax.rem(i, 2))

    def trade(self, d):
        return remote(self.own.at[4], self.sib.at[d], self.sib_sems, d, self.sibling)

    def put(self, i, value):
        d = 3 - i // 2
        for_sibling = lax.rem(i, 2) == 0

        @pl.when(for_sibling & (i >= 2))
        def _():
            self.trade(d + 1).wait_send()

        self.own[jnp.where(for_sibling, 4, d)] = value

        @pl.when(for_sibling)
        def _():
            self.trade(d).start()

    def take(self, part, sems):
        self.loads, self.trades = {}, {}
        for d in (3, 2, 1, 0):
            self.loads[d] = pltpu.make_async_copy(part.at[self.me ^ (2 * d)], self.own.at[d], sems.at[d])
            self.loads[d].start()
        for d in (3, 2, 1, 0):
            self.trades[d] = remote(
                part.at[self.sibling ^ (2 * d)], self.sib.at[d], self.sib_sems, d, self.sibling
            )
            self.trades[d].start()

    def taken(self, d):
        self.loads[d].wait()
        self.trades[d].wait_recv()

    def arrived(self, d):
        self.trade(d).wait_recv()

    def part(self, j):
        return pl.ds(j * self.size, self.size)

    def summed(self, d, j):
        part = self.part(j)
        return self.own[d, part].astype(jnp.float32) + self.sib[d, part].astype(jnp.float32)

    def near_copy(self, j, n):
        device, d = (self.x, 1) if j < self.half else (self.y, 2)
        src = self.own.at[3 if n else d, self.part(j)]
        return remote(src, self.got.at[j, n], self.near_sems, (j, n), device)

    def far_copy(self, j):
        device, d = (self.y, 2) if j < self.half else (self.x, 1)
        return remote(self.own.at[d, self.part(j)], self.got_far.at[j], self.far_sems, j, device)

    def out_copy(self, j):
        slot = self.order.index(j) % 2
        return pltpu.make_async_copy(
            self.total.at[slot], self.out.at[self.part(j)], self.out_sem.at[slot]
        )

    def near(self, j, n):
        e = 3 if n else (1 if j < self.half else 2)
        self.own[e, self.part(j)] = self.summed(e, j).astype(jnp.bfloat16)
        self.near_copy(j, n).start()

    def progress(self, i):
        @pl.when(i == 2)
        def _():
            self.arrived(3)
            for j in self.order:
                self.near(j, 1)

        @pl.when(i == 4)
        def _():
            self.arrived(2)
            for j in range(self.half, self.chunks):
                self.near(j, 0)

        @pl.when(i == 6)
        def _():
            self.arrived(1)
            for j in range(self.half):
                self.near(j, 0)

    def far(self, j):
        for n in (0, 1):
            self.near_copy(j, n).wait_recv()
        d = 2 if j < self.half else 1
        passed = self.summed(d, j) + self.got[j, 1].astype(jnp.float32)
        self.own[d, self.part(j)] = passed.astype(jnp.bfloat16)
        self.far_copy(j).start()

    def result(self, j):
        self.far_copy(j).wait_recv()
        return (
            self.summed(0, j)
            + self.got[j, 0].astype(jnp.float32)
            + self.got_far[j].astype(jnp.float32)
        )

    def last(self, j):
        total = self.result(j)
        turn = self.order.index(j)
        if turn >= 2:
            self.out_copy(self.order[turn - 2]).wait()
        self.total[turn % 2] = total
        self.out_copy(j).start()

    def finish(self, written=True):
        if self.trades is None:
            self.trade(0).wait_send()
        else:
            for copy in self.trades.values():
                copy.wait_send()
        if written:
            for j in self.order[-2:]:
                self.out_copy(j).wait()
        for j in range(self.chunks):
            self.far_copy(j).wait_send()
            for n in (0, 1):
                self.near_copy(j, n).wait_send()


def branch_kernel(chunks, mixed, w_out, tokens, middle, *refs):
    f32, bf16 = jnp.float32, jnp.bfloat16
    scatter = Scatter(middle, chunks, refs)
    tok = tokens.shape[0]
    size = tok // chunks
    greet(scatter.sibling, scatter.x, scatter.y)

    def branch(i, carry):
        rows = pl.ds(pl.multiple_of(scatter.owner(i) * tok, tok), tok)
        scatter.put(i, dot(mixed[rows, :], w_out[...]).astype(bf16))
        scatter.progress(i)
        return carry

    lax.fori_loop(0, mixed.shape[0] // tok, branch, 0)
    scatter.arrived(0)
    for j in scatter.order:
        scatter.far(j)
    for j in scatter.order:
        part = pl.ds(j * size, size)
        middle[part, :] = tokens[part, :].astype(f32) + scatter.result(j)
    scatter.finish(False)


def middle_kernel(
    chunks, middle, gain, w_feed, cotangent, hidden, acts, down_part,
    blocks, act_stage, inner_turned, column_in, down_stage, out_sems, act_sems, column_sems, down_sem, *sems,
):
    f32, bf16 = jnp.float32, jnp.bfloat16
    width, tok, _ = blocks.shape
    me = lax.axis_index(R)
    size = tok // chunks

    def item(j):
        part = pl.ds(j * size, size)
        return blocks.at[me, part], lambda owner: blocks.at[owner, part]

    gather = Gather([item(j) for j in range(chunks)], sems)
    units = w_feed.shape[1] // 2
    tiles = middle.shape[1] // tok
    order = [*range(chunks // 2, chunks), *range(chunks // 2)]

    def column_loads(n):
        slot = lax.rem(n, 2)
        part = pl.ds(pl.multiple_of(n * tok, tok), tok)
        return [
            pltpu.make_async_copy(
                cotangent.at[me ^ i, :, part],
                column_in.at[slot, pl.ds(i * tok, tok)],
                column_sems.at[slot, i],
            )
            for i in range(width)
        ]

    for n in (0, 1):
        for copy in column_loads(n):
            copy.start()
    greet(gather.sibling, gather.x, gather.y)
    for j in order:
        part = pl.ds(j * size, size)
        total = middle[part, :]
        blocks[me, part] = (total * inverse_rms(total) * gain[...]).astype(bf16)
        gather.start_items((j,))

    def hidden_copy(i):
        return pltpu.make_async_copy(blocks.at[me ^ i], hidden.at[me ^ i], out_sems.at[i])

    def act_copy(i):
        slot = lax.rem(i, 2)
        return pltpu.make_async_copy(act_stage.at[slot], acts.at[me ^ i], act_sems.at[slot])

    def block(i, carry):
        @pl.when(i == 1)
        def _():
            gather.from_sibling(3)

        @pl.when(i == 2)
        def _():
            for j in order:
                gather.pass_on(0, j)
                gather.pass_on(1, j)

        @pl.when(i == 3)
        def _():
            gather.from_sibling(4)

        @pl.when(i == 5)
        def _():
            gather.from_sibling(5)

        @pl.when(i == 6)
        def _():
            for j in order:
                gather.pass_on(2, j)

        @pl.when(i == 7)
        def _():
            gather.from_sibling(6)

        @pl.when(i >= 2)
        def _():
            act_copy(i - 2).wait()

        acc = dot(blocks[me ^ i], w_feed[...])
        act_stage[lax.rem(i, 2)] = acc
        act_copy(i).start()
        hidden_copy(i).start()
        gate, up = acc[:, :units], acc[:, units:]
        inner_turned[i] = (gate / (1.0 + jnp.exp(-gate)) * up).astype(bf16).T
        return carry

    def down_copy(n):
        part = pl.ds(pl.multiple_of(n * tok, tok), tok)
        slot = lax.rem(n, 2)
        return pltpu.make_async_copy(down_stage.at[slot], down_part.at[:, part], down_sem.at[slot])

    def down_tile(n, carry):
        slot = lax.rem(n, 2)
        for copy in column_loads(n):
            copy.wait()

        @pl.when(n >= 2)
        def _():
            down_copy(n - 2).wait()

        acc = dot(inner_turned[0], column_in[slot, :tok])
        for i in range(1, width):
            acc = acc + dot(inner_turned[i], column_in[slot, i * tok : (i + 1) * tok])
        down_stage[slot] = acc.astype(bf16)
        down_copy(n).start()

        @pl.when(n + 2 < tiles)
        def _():
            for copy in column_loads(n + 2):
                copy.start()

        return carry

    lax.fori_loop(0, width, block, 0)
    lax.fori_loop(0, tiles, down_tile, 0)
    for n in (tiles - 2, tiles - 1):
        down_copy(n).wait()
    gather.wait_sends()
    for i in (width - 2, width - 1):
        act_copy(i).wait()
    for i in range(width):
        hidden_copy(i).wait()


def branch_layer(mixed, w_out, tokens, call, chunks=4):
    vmem = pl.BlockSpec(memory_space=pltpu.VMEM)
    return pl.pallas_call(
        functools.partial(branch_kernel, chunks),
        out_shape=jax.ShapeDtypeStruct(tokens.shape, jnp.float32),
        in_specs=[vmem] * 3,
        out_specs=vmem,
        scratch_shapes=Scatter.scratch(*tokens.shape, chunks),
        compiler_params=pltpu.CompilerParams(
            collective_id=call, has_side_effects=True, vmem_limit_bytes=40 << 20
        ),
    )(mixed, w_out, tokens)


def middle_layer(middle, gain, w_feed, cotangent, call, chunks=4):
    width = lax.axis_size(R)
    tok, model = middle.shape
    bf16, f32 = jnp.bfloat16, jnp.float32
    units = w_feed.shape[1] // 2
    vmem = pl.BlockSpec(memory_space=pltpu.VMEM)
    return pl.pallas_call(
        functools.partial(middle_kernel, chunks),
        out_shape=[
            jax.ShapeDtypeStruct((width, tok, model), bf16),
            jax.ShapeDtypeStruct((width, tok, 2 * units), f32),
            jax.ShapeDtypeStruct((units, model), bf16),
        ],
        in_specs=[vmem] * 3 + [ANY],
        out_specs=[ANY] * 3,
        scratch_shapes=[
            pltpu.VMEM((width, tok, model), bf16),
            pltpu.VMEM((2, tok, 2 * units), f32),
            pltpu.VMEM((width, units, tok), bf16),
            pltpu.VMEM((2, width * tok, tok), bf16),
            pltpu.VMEM((2, units, tok), bf16),
            DMA((width,)),
            DMA((2,)),
            DMA((2, width)),
            DMA((2,)),
        ]
        + Gather.scratch(chunks),
        compiler_params=pltpu.CompilerParams(
            collective_id=call, has_side_effects=True, vmem_limit_bytes=56 << 20
        ),
    )(middle, gain, w_feed, cotangent)


def feed_kernel(
    chunks, hidden, cotangent, acts, w_feed, w_down, out_part, grad_hidden, feed_part,
    acts_in, cot_in, grads, column_in, feed_stage, out_stage, in_sems, column_sems, feed_sem, out_sem,
    *refs,
):
    f32, bf16 = jnp.float32, jnp.bfloat16
    width, tok, model = hidden.shape
    units = w_down.shape[0]
    scatter = Scatter(grad_hidden, chunks, refs)
    half = chunks // 2
    first_half, second_half = range(half), range(half, chunks)

    def loads(i):
        slot, owner = lax.rem(i, 2), scatter.owner(i)
        return [
            pltpu.make_async_copy(acts.at[owner], acts_in.at[slot], in_sems.at[0, slot]),
            pltpu.make_async_copy(cotangent.at[owner], cot_in.at[slot], in_sems.at[1, slot]),
        ]

    def out_copy(i):
        slot = lax.rem(i, 2)
        return pltpu.make_async_copy(
            out_stage.at[slot], out_part.at[scatter.owner(i)], out_sem.at[slot]
        )

    for i in (0, 1):
        for copy in loads(i):
            copy.start()
    greet(scatter.sibling, scatter.x, scatter.y)

    def block(i, carry):
        slot = lax.rem(i, 2)
        rows = pl.ds(pl.multiple_of(i * tok, tok), tok)
        for copy in loads(i):
            copy.wait()
        gate, up = acts_in[slot, :, :units], acts_in[slot, :, units:]
        gate_sig = 1.0 / (1.0 + jnp.exp(-gate))
        gate_silu = gate * gate_sig
        inner = (gate_silu * up).astype(bf16)
        grad_inner = dot(cot_in[slot], w_down[...], 1, 1)
        grad_gate = grad_inner * up * gate_sig * (1.0 + gate * (1.0 - gate_sig))
        both = jnp.concatenate([grad_gate, grad_inner * gate_silu], axis=1).astype(bf16)
        grads[rows, :] = both
        scatter.put(i, dot(both, w_feed[...], 1, 1).astype(bf16))

        @pl.when(i >= 2)
        def _():
            out_copy(i - 2).wait()

        out_stage[slot] = dot(inner, w_down[...]).astype(bf16)
        out_copy(i).start()

        @pl.when(i + 2 < width)
        def _():
            for copy in loads(i + 2):
                copy.start()

        scatter.progress(i)
        return carry

    tiles = model // tok

    def column_loads(n):
        slot = lax.rem(n, 2)
        part = pl.ds(pl.multiple_of(n * tok, tok), tok)
        return [
            pltpu.make_async_copy(
                hidden.at[scatter.owner(i), :, part],
                column_in.at[slot, pl.ds(i * tok, tok)],
                column_sems.at[slot, i],
            )
            for i in range(width)
        ]

    def feed_copy(n):
        rows = pl.ds(pl.multiple_of(n * tok, tok), tok)
        slot = lax.rem(n, 2)
        return pltpu.make_async_copy(feed_stage.at[slot], feed_part.at[rows], feed_sem.at[slot])

    def feed_tile(n, carry):
        slot = lax.rem(n, 2)
        for copy in column_loads(n):
            copy.wait()

        @pl.when(n >= 2)
        def _():
            feed_copy(n - 2).wait()

        feed_stage[slot] = dot(column_in[slot], grads[...], 0, 0).astype(bf16)
        feed_copy(n).start()

        @pl.when(n + 2 < tiles)
        def _():
            for copy in column_loads(n + 2):
                copy.start()

        @pl.when(n == 2)
        def _():
            for j in second_half:
                scatter.far(j)

        @pl.when(n == 5)
        def _():
            for j in first_half:
                scatter.far(j)

        return carry

    for n in (0, 1):
        for copy in column_loads(n):
            copy.start()
    lax.fori_loop(0, width, block, 0)
    scatter.arrived(0)
    lax.fori_loop(0, tiles, feed_tile, 0)
    for j in scatter.order:
        scatter.last(j)
    scatter.finish()
    for i in (width - 2, width - 1):
        out_copy(i).wait()
    for n in (tiles - 2, tiles - 1):
        feed_copy(n).wait()


def feed_forward(hidden, cotangent, acts, w_feed, w_down, call, chunks=4):
    width, tok, model = hidden.shape
    units = w_down.shape[0]
    bf16 = jnp.bfloat16
    vmem = pl.BlockSpec(memory_space=pltpu.VMEM)
    return pl.pallas_call(
        functools.partial(feed_kernel, chunks),
        out_shape=[
            jax.ShapeDtypeStruct((width, tok, model), bf16),
            jax.ShapeDtypeStruct((tok, model), jnp.float32),
            jax.ShapeDtypeStruct((model, 2 * units), bf16),
        ],
        in_specs=[ANY, ANY, ANY, vmem, vmem],
        out_specs=[ANY] * 3,
        scratch_shapes=[
            pltpu.VMEM((2, tok, 2 * units), jnp.float32),
            pltpu.VMEM((2, tok, model), bf16),
            pltpu.VMEM((width * tok, 2 * units), bf16),
            pltpu.VMEM((2, width * tok, tok), bf16),
            pltpu.VMEM((2, tok, 2 * units), bf16),
            pltpu.VMEM((2, tok, model), bf16),
            DMA((2, 2)),
            DMA((2, width)),
            DMA((2,)),
            DMA((2,)),
        ]
        + Scatter.scratch(tok, model, chunks),
        compiler_params=pltpu.CompilerParams(
            collective_id=call, has_side_effects=True, vmem_limit_bytes=62 << 20
        ),
    )(hidden, cotangent, acts, w_feed, w_down)


def back_kernel(
    chunks, heads, q, kv, starts, places, grad, mixed, log_total, cosine, sine, hidden, out_part, down_rows, w_part,
    grad_qkv, weight_part, feed_out, all_down, w_rows,
    sums, grad_kv, from_sib, inbox, outbox, to_sib, at_sib, to_line, at_line, down_sem, w_sem,
    to_all, at_all, column_in, weight_stage, column_sems, weight_sem, load_sems, *refs,
):
    f32, bf16 = jnp.float32, jnp.bfloat16
    planes, count, tok = inbox.shape[0], inbox.shape[1], inbox.shape[2]
    width = 2 * count
    columns = heads * HEAD_DIM
    z, me = lax.axis_index(F), lax.axis_index(R)
    core = lax.rem(me, 2)
    above, below = lax.rem(z + 1, planes), lax.rem(z + planes - 1, planes)
    scatter = Scatter(feed_out, chunks, refs[:12])
    gather = Gather(row_items(down_rows, all_down, 1), refs[12:])
    barrier = pltpu.get_barrier_semaphore()
    for other in (above, below):
        pl.semaphore_signal(barrier, inc=1, device_id={F: other}, device_id_type=MESH)
    peers = [me ^ distance for distance in range(1, width)]
    for device in peers:
        pl.semaphore_signal(barrier, inc=1, device_id={R: device}, device_id_type=MESH)
    pl.semaphore_wait(barrier, 1 + width)
    share = w_part.shape[1] // width

    def share_of(device):
        return w_part.at[:, pl.ds(pl.multiple_of(device * share, share), share)]

    w_copies = [
        remote(share_of(device), w_rows.at[me], (to_all, at_all), i, device)
        for i, device in enumerate(peers)
    ]
    w_kept = pltpu.make_async_copy(share_of(me), w_rows.at[me], w_sem)
    for copy in [w_kept] + w_copies:
        copy.start()
    kept = pltpu.make_async_copy(down_rows, all_down.at[me], down_sem)
    kept.start()
    parts = tok // QUERY_BLOCK

    def step(n, carry):
        s, sub = n // parts, lax.rem(n, parts)
        rows = pl.ds(pl.multiple_of(n * QUERY_BLOCK, QUERY_BLOCK), QUERY_BLOCK)
        queries = heads_to_rows(q[rows, :] * bf16(HEAD_DIM**-0.5), heads)
        grads = heads_to_rows(grad[rows, :], heads)
        first = jnp.concatenate([starts[n]] * heads, axis=1)
        place = jnp.concatenate([places[n]] * heads, axis=1)
        products = grads.astype(f32) * heads_to_rows(mixed[rows, :], heads).astype(f32)
        delta = lax.dot_general(
            jnp.ones((8, 2 * HEAD_DIM), f32),
            products,
            (((1,), (1,)), ((), ())),
            precision=lax.Precision.HIGHEST,
            preferred_element_type=f32,
        )[:1]
        level = log_total[n]
        upper = pltpu.roll(grads.astype(f32), HEAD_DIM, 1).astype(bf16)

        @pl.when(sub == 0)
        def _():
            sums[...] = jnp.zeros_like(sums)

        def block(index, acc):
            part = pl.ds(pl.multiple_of(index * KEY_BLOCK, KEY_BLOCK), KEY_BLOCK)
            keys = kv[s, part, :]
            scores = dot(keys, queries, 1, 1)
            probs = jnp.where(visible(index, first, place), jnp.exp(scores - level), 0.0)
            grad_probs = dot(keys, upper, 1, 1)
            grad_scores = (probs * (grad_probs - delta)).astype(bf16)
            sums[part, :] += dot(grad_scores, queries) + dot(probs.astype(bf16), upper)
            return acc + dot(keys, grad_scores, 0, 0)

        place_of_first = z * tok + sub * QUERY_BLOCK
        low = jnp.where(place_of_first >= FIRST_DOC, FIRST_DOC // KEY_BLOCK, 0)
        high = (place_of_first + QUERY_BLOCK - 1) // KEY_BLOCK + 1
        acc = lax.fori_loop(low, high, block, jnp.zeros((2 * HEAD_DIM, queries.shape[0]), f32))
        grad_q = rows_to_heads(acc[:HEAD_DIM] * HEAD_DIM**-0.5, heads)
        c, n_sine = cosine[rows, :], -sine[rows, :]
        for at in range(0, columns, 2 * HEAD_DIM):
            part = slice(at, at + 2 * HEAD_DIM)
            grad_qkv[rows, part] = turn(grad_q[:, part], c, n_sine).astype(bf16)
        grad_qkv[rows, columns:] = jnp.zeros((QUERY_BLOCK, 2 * HEAD_DIM), bf16)

        @pl.when(sub == parts - 1)
        def _():
            grad_kv[s] = sums[...].astype(bf16)

        @pl.when(n == 3)
        def _():
            scatter.taken(3)
            for j in scatter.order:
                scatter.near(j, 1)
            scatter.taken(2)
            for j in scatter.order[: chunks // 2]:
                scatter.near(j, 0)
            scatter.taken(1)
            for j in scatter.order[chunks // 2 :]:
                scatter.near(j, 0)

        @pl.when(n == 11)
        def _():
            gather.relay(0)

        return carry

    scatter.take(out_part, load_sems)
    gather.start()
    lax.fori_loop(0, width * parts, step, 0)

    def block_of(which, b):
        return grad_kv.at[pl.ds(which * count, count), pl.ds(b * tok, tok)]

    def trade(b):
        return remote(block_of(1 - core, b), from_sib.at[b], (to_sib, at_sib), b, gather.sibling)

    def down(b, i):
        return along_line(outbox.at[b, i], inbox.at[b, i], (to_line, at_line), (b, i), below)

    def own(b, i):
        part = pl.ds(b * tok, tok)
        return grad_kv[core * count + i, part, :].astype(f32) + from_sib[b, i].astype(f32)

    for b in range(planes):

        @pl.when(b <= z)
        def _():
            trade(b).start()

    scatter.taken(0)
    for b in range(planes):

        @pl.when(b <= z)
        def _():
            trade(b).wait_recv()

        for i in range(count):

            @pl.when((b <= z) & (z < planes - 1))
            def _():
                down(b, i).wait_recv()

            @pl.when((b < z) & (z < planes - 1))
            def _():
                outbox[b, i] = (own(b, i) + inbox[b, i].astype(f32)).astype(bf16)

            @pl.when((b < z) & (z == planes - 1))
            def _():
                outbox[b, i] = own(b, i).astype(bf16)

            @pl.when(b < z)
            def _():
                down(b, i).start()

        if b == 0:
            for j in scatter.order[: chunks // 2]:
                scatter.far(j)
        if b == 1:
            for j in scatter.order[chunks // 2 :]:
                scatter.far(j)

    def keys(i, carry):
        rows = pl.ds(pl.multiple_of((core * count + i) * tok, tok), tok)
        part = pl.ds(pl.multiple_of(z * tok, tok), tok)
        total = grad_kv[core * count + i, part, :].astype(f32) + from_sib[z, i].astype(f32)
        total = total + jnp.where(z < planes - 1, inbox[z, i].astype(f32), 0.0)
        grad_qkv[rows, columns:] = turn_keys(total, cosine[rows, :], -sine[rows, :]).astype(bf16)
        return carry

    lax.fori_loop(0, count, keys, 0)
    gather.far()
    tiles = hidden.shape[1] // tok

    def column_load(n):
        part = pl.ds(pl.multiple_of(n * tok, tok), tok)
        slot = lax.rem(n, 2)
        return pltpu.make_async_copy(hidden.at[:, part], column_in.at[slot], column_sems.at[slot])

    def weight_copy(n):
        rows = pl.ds(pl.multiple_of(n * tok, tok), tok)
        slot = lax.rem(n, 2)
        return pltpu.make_async_copy(weight_stage.at[slot], weight_part.at[rows], weight_sem.at[slot])

    def weight_tile(n, carry):
        slot = lax.rem(n, 2)
        column_load(n).wait()

        @pl.when(n >= 2)
        def _():
            weight_copy(n - 2).wait()

        weight_stage[slot] = dot(column_in[slot], grad_qkv[...], 0, 0).astype(bf16)
        weight_copy(n).start()

        @pl.when(n + 2 < tiles)
        def _():
            column_load(n + 2).start()

        return carry

    for n in (0, 1):
        column_load(n).start()
    lax.fori_loop(0, tiles, weight_tile, 0)
    for j in scatter.order:
        scatter.last(j)
    scatter.finish()
    for n in (tiles - 2, tiles - 1):
        weight_copy(n).wait()
    for kind in range(3, 7):
        gather.from_sibling(kind)
    gather.wait_sends()
    for b in range(planes):

        @pl.when(b <= z)
        def _():
            trade(b).wait_send()

        @pl.when(b < z)
        def _():
            for i in range(count):
                down(b, i).wait_send()

    for copy in [kept, w_kept] + w_copies:
        copy.wait()


def attention_back(
    heads, q, kv, starts, places, grad, mixed, log_total, cosine, sine, hidden, out_part, down_rows, w_part,
    call, chunks=4,
):
    planes, width = lax.axis_size(F), lax.axis_size(R)
    f32, bf16 = jnp.float32, jnp.bfloat16
    tok, model = hidden.shape[0] // width, hidden.shape[1]
    columns = q.shape[1] + 2 * HEAD_DIM
    length = kv.shape[1]
    vmem = pl.BlockSpec(memory_space=pltpu.VMEM)
    blocks = pltpu.VMEM((planes, width // 2, tok, 2 * HEAD_DIM), bf16)
    return pl.pallas_call(
        functools.partial(back_kernel, chunks, heads),
        out_shape=[
            jax.ShapeDtypeStruct((q.shape[0], columns), bf16),
            jax.ShapeDtypeStruct((model, columns), bf16),
            jax.ShapeDtypeStruct((tok, model), f32),
            jax.ShapeDtypeStruct((width,) + down_rows.shape, bf16),
            jax.ShapeDtypeStruct((width, w_part.shape[0], w_part.shape[1] // width), bf16),
        ],
        in_specs=[vmem] * 9 + [ANY] * 4,
        out_specs=[vmem] + [ANY] * 4,
        scratch_shapes=[
            pltpu.VMEM((length, 2 * HEAD_DIM), f32),
            pltpu.VMEM((width, length, 2 * HEAD_DIM), bf16),
            blocks,
            blocks,
            blocks,
        ]
        + [DMA((planes,))] * 2
        + [DMA((planes, width // 2))] * 2
        + [DMA, DMA, DMA((width - 1,)), DMA((width - 1,))]
        + [pltpu.VMEM((2, width * tok, tok), bf16), pltpu.VMEM((2, tok, columns), bf16)]
        + [DMA((2,)), DMA((2,)), DMA((4,))]
        + Scatter.scratch(tok, model, chunks)
        + Gather.scratch(1),
        compiler_params=pltpu.CompilerParams(
            collective_id=call, has_side_effects=True, vmem_limit_bytes=60 << 20
        ),
    )(q, kv, starts, places, grad, mixed, log_total, cosine, sine, hidden, out_part, down_rows, w_part)


def hidden_kernel(chunks, grad_qkv, weight, feed_rows, grad_hidden, all_feed, feed_sem, *refs):
    bf16 = jnp.bfloat16
    scatter = Scatter(grad_hidden, chunks, refs[:12])
    gather = Gather(row_items(feed_rows, all_feed, chunks), refs[12:])
    tok = grad_hidden.shape[0]
    columns = grad_qkv.shape[1]
    greet(scatter.sibling, scatter.x, scatter.y)
    kept = pltpu.make_async_copy(feed_rows, all_feed.at[scatter.me], feed_sem)
    kept.start()
    gather.start()

    def block(i, carry):
        rows = pl.ds(pl.multiple_of(scatter.owner(i) * tok, tok), tok)
        scatter.put(i, dot(grad_qkv[rows, :], weight[:, :columns], 1, 1).astype(bf16))
        scatter.progress(i)
        return carry

    lax.fori_loop(0, grad_qkv.shape[0] // tok, block, 0)
    scatter.arrived(0)
    for i in range(chunks):
        gather.relay(i)
    for j in scatter.order:
        scatter.far(j)
    gather.finish()
    for j in scatter.order:
        scatter.last(j)
    scatter.finish()
    kept.wait()


def scatter_hidden(grad_qkv, weight, feed_rows, tok, call, chunks=4):
    width, model = lax.axis_size(R), weight.shape[0]
    vmem = pl.BlockSpec(memory_space=pltpu.VMEM)
    return pl.pallas_call(
        functools.partial(hidden_kernel, chunks),
        out_shape=[
            jax.ShapeDtypeStruct((tok, model), jnp.float32),
            jax.ShapeDtypeStruct((width,) + feed_rows.shape, jnp.bfloat16),
        ],
        in_specs=[vmem, vmem, ANY],
        out_specs=[ANY, ANY],
        scratch_shapes=[DMA] + Scatter.scratch(tok, model, chunks) + Gather.scratch(chunks),
        compiler_params=pltpu.CompilerParams(
            collective_id=call, has_side_effects=True, vmem_limit_bytes=40 << 20
        ),
    )(grad_qkv, weight, feed_rows)


def enter(tokens, gains, ids, call, chunks=4):
    planes, rows = lax.axis_size(F), lax.axis_size(R)
    tok, model = tokens.shape
    vmem = pl.BlockSpec(memory_space=pltpu.VMEM)
    return pl.pallas_call(
        functools.partial(enter_kernel, chunks),
        out_shape=[
            jax.ShapeDtypeStruct((rows, tok, model), jnp.bfloat16),
            jax.ShapeDtypeStruct((planes,) + gains.shape, jnp.float32),
            jax.ShapeDtypeStruct((rows,) + ids.shape, jnp.int32),
        ],
        in_specs=[vmem] * 3,
        out_specs=[ANY, vmem, vmem],
        scratch_shapes=[pltpu.VMEM((tok, model), jnp.bfloat16), DMA]
        + [DMA((planes - 1,))] * 2
        + Gather.scratch(chunks + 1),
        compiler_params=pltpu.CompilerParams(
            collective_id=call, has_side_effects=True, vmem_limit_bytes=32 << 20
        ),
    )(tokens, gains, ids)


def project(hidden, weight, cosine, sine, cotangent, query_width, call, chunks=4):
    planes, width = lax.axis_size(F), lax.axis_size(R)
    tok, model = cotangent.shape
    bf16 = jnp.bfloat16
    vmem = pl.BlockSpec(memory_space=pltpu.VMEM)
    return pl.pallas_call(
        functools.partial(project_kernel, chunks),
        out_shape=[
            jax.ShapeDtypeStruct((width * tok, query_width), bf16),
            jax.ShapeDtypeStruct((width, planes, tok, 2 * HEAD_DIM), bf16),
            jax.ShapeDtypeStruct((width, tok, model), bf16),
            jax.ShapeDtypeStruct((model // width, model), bf16),
        ],
        in_specs=[ANY] + [vmem] * 3 + [ANY, ANY],
        out_specs=[vmem, ANY, ANY, ANY],
        scratch_shapes=[
            pltpu.VMEM((width, tok, 2 * HEAD_DIM), bf16),
            pltpu.VMEM((2, tok, model), bf16),
            DMA((2,)),
            DMA,
            DMA,
            DMA,
            DMA((width - 1,)),
            DMA((width - 1,)),
        ]
        + [DMA((planes, width // 2))] * 2
        + [DMA((planes,))] * 2
        + Gather.scratch(chunks),
        compiler_params=pltpu.CompilerParams(
            collective_id=call, has_side_effects=True, vmem_limit_bytes=40 << 20
        ),
    )(hidden, weight, cosine, sine, cotangent, weight)


def scatter_kernel(
    chunks, part, out, own, from_sib, give, got, give_far, got_far, total,
    own_sem, out_sem, to_sib, at_sib, to_near, at_near, to_far, at_far,
):
    f32, bf16 = jnp.float32, jnp.bfloat16
    me = lax.axis_index(R)
    flip = 1 - 2 * lax.rem(me, 2)
    sibling, beside_x, beside_y = me + flip, me ^ 2, me ^ 4
    rows = out.shape[0]
    size = rows // chunks
    half = chunks // 2
    owners = [me, beside_x, beside_y, me ^ 6]
    order = [c for j in range(half) for c in (j, half + j)]

    def rows_of(device, j):
        return part.at[pl.ds(pl.multiple_of(device * rows + j * size, 16), size)]

    def own_copy(d, j):
        return pltpu.make_async_copy(rows_of(owners[d], j), own.at[d, j], own_sem.at[d, j])

    def sib_copy(d, j):
        return remote(rows_of(owners[d] + flip, j), from_sib.at[d, j], (to_sib, at_sib), (d, j), sibling)

    def near_copy(j):
        device = beside_x if j < half else beside_y
        return remote(give.at[j], got.at[j], (to_near, at_near), j, device)

    def far_copy(j):
        device = beside_y if j < half else beside_x
        return remote(give_far.at[j], got_far.at[j], (to_far, at_far), j, device)

    def out_copy(j):
        return pltpu.make_async_copy(total.at[j], out.at[pl.ds(j * size, size)], out_sem.at[j])

    def summed(d, j):
        own_copy(d, j).wait()
        sib_copy(d, j).wait_recv()
        return own[d, j].astype(f32) + from_sib[d, j].astype(f32)

    for j in order:
        for d in (1, 2, 3, 0):
            own_copy(d, j).start()
    greet(sibling, beside_x, beside_y)
    for j in order:
        for d in (1, 3, 2, 0) if j < half else (2, 3, 1, 0):
            sib_copy(d, j).start()
    for j in order:
        give[j, 0] = summed(1 if j < half else 2, j).astype(bf16)
        give[j, 1] = summed(3, j).astype(bf16)
        near_copy(j).start()
    for j in order:
        passed = summed(2 if j < half else 1, j)
        kept = summed(0, j)
        near_copy(j).wait_recv()
        give_far[j] = (passed + got[j, 1].astype(f32)).astype(bf16)
        far_copy(j).start()
        total[j] = kept + got[j, 0].astype(f32)
    for j in order:
        far_copy(j).wait_recv()
        total[j] = total[j] + got_far[j].astype(f32)
        out_copy(j).start()
    for j in order:
        out_copy(j).wait()
        near_copy(j).wait_send()
        far_copy(j).wait_send()
        for d in range(4):
            sib_copy(d, j).wait_send()


def plane_gather(x, call, chunks=4):
    width = lax.axis_size(R)
    if width != 8:
        return lax.all_gather(x, R, axis=0, tiled=True)
    out = pl.pallas_call(
        functools.partial(gather_kernel, chunks),
        out_shape=jax.ShapeDtypeStruct((width,) + x.shape, x.dtype),
        in_specs=[ANY],
        out_specs=ANY,
        scratch_shapes=[DMA] + Gather.scratch(chunks),
        compiler_params=pltpu.CompilerParams(collective_id=call, has_side_effects=True),
    )(x)
    return out.reshape((width * x.shape[0],) + x.shape[1:])


def plane_scatter(x, call, chunks=4):
    width = lax.axis_size(R)
    if width != 8:
        return lax.psum_scatter(x, R, scatter_dimension=0, tiled=True).astype(jnp.float32)
    rows, columns = x.shape[0] // width, x.shape[1]
    size = rows // chunks
    bf16 = jnp.bfloat16
    return pl.pallas_call(
        functools.partial(scatter_kernel, chunks),
        out_shape=jax.ShapeDtypeStruct((rows, columns), jnp.float32),
        in_specs=[ANY],
        out_specs=ANY,
        scratch_shapes=[
            pltpu.VMEM((4, chunks, size, columns), bf16),
            pltpu.VMEM((4, chunks, size, columns), bf16),
            pltpu.VMEM((chunks, 2, size, columns), bf16),
            pltpu.VMEM((chunks, 2, size, columns), bf16),
            pltpu.VMEM((chunks, size, columns), bf16),
            pltpu.VMEM((chunks, size, columns), bf16),
            pltpu.VMEM((chunks, size, columns), jnp.float32),
            DMA((4, chunks)),
            DMA((chunks,)),
            DMA((4, chunks)),
            DMA((4, chunks)),
        ]
        + [DMA((chunks,))] * 4,
        compiler_params=pltpu.CompilerParams(
            collective_id=call, has_side_effects=True, vmem_limit_bytes=32 << 20
        ),
    )(x)


def line_gather(x):
    return lax.all_gather(x, F, axis=0, tiled=True)


def line_scatter(x):
    return lax.psum_scatter(x, F, scatter_dimension=0, tiled=True)


def heads_to_rows(block, heads):
    parts = [block[:, h * HEAD_DIM : (h + 1) * HEAD_DIM] for h in range(heads)]
    rows = jnp.concatenate(parts, axis=0)
    return jnp.concatenate([rows, jnp.zeros_like(rows)], axis=1)


def rows_to_heads(columns, heads):
    count = columns.shape[1] // heads
    return jnp.concatenate([columns[:, h * count : (h + 1) * count].T for h in range(heads)], axis=1)


def visible(block_index, starts, places):
    keys = block_index * KEY_BLOCK + lax.broadcasted_iota(jnp.int32, (KEY_BLOCK, starts.shape[1]), 0)
    return (keys >= starts) & (keys <= places)


def attention_kernel(heads, low, high, q, kv, starts, places, mixed, log_total):
    f32, bf16 = jnp.float32, jnp.bfloat16
    step = pl.program_id(0) * pl.num_programs(1) + pl.program_id(1)
    queries = heads_to_rows(q[...] * bf16(HEAD_DIM**-0.5), heads)
    first = jnp.concatenate([starts[0]] * heads, axis=1)
    place = jnp.concatenate([places[0]] * heads, axis=1)
    columns = queries.shape[0]

    def block(index, carry):
        top, total, acc = carry
        rows = kv[0, pl.ds(pl.multiple_of(index * KEY_BLOCK, KEY_BLOCK), KEY_BLOCK), :]
        scores = jnp.where(visible(index, first, place), dot(rows, queries, 1, 1), NEGATIVE)
        new_top = jnp.maximum(top, jnp.max(scores, axis=0, keepdims=True))
        weights = jnp.exp(scores - new_top)
        fade = jnp.exp(top - new_top)
        total = total * fade + jnp.sum(weights, axis=0, keepdims=True)
        acc = acc * fade + dot(rows, weights.astype(bf16), 0, 0)
        return new_top, total, acc

    top, total, acc = lax.fori_loop(
        low[step],
        high[step],
        block,
        (
            jnp.full((1, columns), NEGATIVE, f32),
            jnp.zeros((1, columns), f32),
            jnp.zeros((2 * HEAD_DIM, columns), f32),
        ),
    )
    mixed[...] = rows_to_heads(acc[HEAD_DIM:] / total, heads).astype(bf16)
    log_total[0] = top + jnp.log(total)


def attention_back_kernel(
    heads, low, high, q, kv, starts, places, grad, mixed, log_total, grad_q, grad_kv, sums
):
    f32, bf16 = jnp.float32, jnp.bfloat16
    step = pl.program_id(0) * pl.num_programs(1) + pl.program_id(1)
    queries = heads_to_rows(q[...] * bf16(HEAD_DIM**-0.5), heads)
    grads = heads_to_rows(grad[...], heads)
    first = jnp.concatenate([starts[0]] * heads, axis=1)
    place = jnp.concatenate([places[0]] * heads, axis=1)
    columns = queries.shape[0]
    products = grads.astype(f32) * heads_to_rows(mixed[...], heads).astype(f32)
    delta = lax.dot_general(
        jnp.ones((8, 2 * HEAD_DIM), f32),
        products,
        (((1,), (1,)), ((), ())),
        precision=lax.Precision.HIGHEST,
        preferred_element_type=f32,
    )[:1]
    level = log_total[0]
    upper = pltpu.roll(grads.astype(f32), HEAD_DIM, 1).astype(bf16)

    @pl.when(pl.program_id(1) == 0)
    def _():
        sums[...] = jnp.zeros_like(sums)

    def block(index, acc):
        part = pl.ds(pl.multiple_of(index * KEY_BLOCK, KEY_BLOCK), KEY_BLOCK)
        rows = kv[0, part, :]
        scores = dot(rows, queries, 1, 1)
        probs = jnp.where(visible(index, first, place), jnp.exp(scores - level), 0.0)
        grad_probs = dot(rows, upper, 1, 1)
        grad_scores = (probs * (grad_probs - delta)).astype(bf16)
        sums[part, :] += dot(grad_scores, queries) + dot(probs.astype(bf16), upper)
        return acc + dot(rows, grad_scores, 0, 0)

    acc = lax.fori_loop(low[step], high[step], block, jnp.zeros((2 * HEAD_DIM, columns), f32))
    grad_q[...] = rows_to_heads(acc[:HEAD_DIM] * HEAD_DIM**-0.5, heads)

    @pl.when(pl.program_id(1) == PARTS - 1)
    def _():
        grad_kv[0] = sums[...].astype(bf16)


def attention_call(kernel, heads, low, high, arrays, outs, scratch=()):
    blocks = {
        "tokens": lambda shape: pl.BlockSpec((QUERY_BLOCK, shape[1]), lambda s, b, *_: (s * PARTS + b, 0)),
        "row": lambda shape: pl.BlockSpec((1,) + shape[1:], lambda s, b, *_: (s * PARTS + b, 0, 0)),
        "sequence": lambda shape: pl.BlockSpec((1,) + shape[1:], lambda s, b, *_: (s, 0, 0)),
    }
    return pl.pallas_call(
        functools.partial(kernel, heads),
        grid_spec=pltpu.PrefetchScalarGridSpec(
            num_scalar_prefetch=2,
            grid=(low.shape[0] // PARTS, PARTS),
            in_specs=[blocks[kind](x.shape) for kind, x in arrays],
            out_specs=[blocks[kind](x.shape) for kind, x in outs],
            scratch_shapes=scratch,
        ),
        out_shape=[x for _, x in outs],
        compiler_params=pltpu.CompilerParams(vmem_limit_bytes=32 << 20),
    )(low, high, *[x for _, x in arrays])


def join_feed_kernel(planes, piece, x, gate, up):
    width = x.shape[0]
    for kind, out in enumerate((gate, up)):
        for p in range(planes):
            for r in range(width):
                first = (kind * planes + p) * piece
                to = (p * width + r) * piece
                out[:, to : to + piece] = x[r, :, first : first + piece].astype(jnp.float32)


def join_attention_kernel(sharers, qkv, o, query, key, value, out):
    f32 = jnp.float32
    width, qw, ow = qkv.shape[0], qkv.shape[2] - 2 * HEAD_DIM, o.shape[2]
    for r in range(width):
        query[:, r * qw : (r + 1) * qw] = qkv[r, :, :qw].astype(f32)
        out[:, r * ow : (r + 1) * ow] = o[r].astype(f32)
    for head in range(width // sharers):
        both = sum(qkv[head * sharers + i, :, qw:].astype(f32) for i in range(sharers))
        to = slice(head * HEAD_DIM, (head + 1) * HEAD_DIM)
        key[:, to] = both[:, :HEAD_DIM]
        value[:, to] = both[:, HEAD_DIM:]


def join_call(kernel, arrays, outs, block=64):
    rows = arrays[0].shape[1]
    return pl.pallas_call(
        kernel,
        grid=(rows // block,),
        in_specs=[pl.BlockSpec((x.shape[0], block, x.shape[2]), lambda i: (0, i, 0)) for x in arrays],
        out_specs=[pl.BlockSpec((block, columns), lambda i: (i, 0)) for columns in outs],
        out_shape=[jax.ShapeDtypeStruct((rows, columns), jnp.float32) for columns in outs],
        compiler_params=pltpu.CompilerParams(vmem_limit_bytes=32 << 20),
    )(*arrays)


def per_device(
    tokens,
    segment_ids,
    attention_gain,
    query_weight,
    key_weight,
    value_weight,
    output_weight,
    feed_gain,
    gate_weight,
    up_weight,
    down_weight,
    cotangent,
):
    f32, bf16 = jnp.float32, jnp.bfloat16
    planes, width = lax.axis_size(F), lax.axis_size(R)
    r, z = lax.axis_index(R), lax.axis_index(F)
    tok, model = tokens.shape
    length = segment_ids.shape[1]
    all_tok = width * tok
    plane_kernels = width == 8
    heads = HEADS // width
    group = HEADS // KV_HEADS
    qw = heads * HEAD_DIM
    kv = (r * heads) // group
    feed = gate_weight.shape[1]
    piece = feed // (width * planes)
    hidden_units = piece * planes

    def cols(weight, first, count):
        return lax.dynamic_slice_in_dim(weight, first, count, 1)

    def feed_cols(weight):
        return [cols(weight, p * (feed // planes) + r * piece, piece) for p in range(planes)]

    w_attention = line_gather(
        jnp.concatenate(
            [
                cols(query_weight, r * qw, qw),
                cols(key_weight, kv * HEAD_DIM, HEAD_DIM),
                cols(value_weight, kv * HEAD_DIM, HEAD_DIM),
                cols(output_weight, r * (model // width), model // width),
            ],
            axis=1,
        )
    )
    w_qkv = w_attention[:, : qw + 2 * HEAD_DIM]
    own_gains = jnp.stack([attention_gain, feed_gain]).astype(f32)
    tok_float = tokens.astype(f32)
    scale_in = inverse_rms(tok_float)
    normed_in = tok_float * scale_in
    if plane_kernels:
        hidden_in, gains, ids = enter(
            tokens, jnp.pad(own_gains, ((0, 6), (0, 0))), segment_ids.reshape(8, length // 8), 0
        )
        hidden_in = hidden_in.reshape(all_tok, model)
        gains = gains[:, :2].transpose(1, 0, 2).reshape(2, model)
        ids = ids.reshape(width, length)
    else:
        gains = lax.all_gather(own_gains, F, axis=1, tiled=True)
        hidden_in = lax.all_gather((normed_in * gains[0]).astype(bf16), R, axis=0, tiled=True)
        ids = lax.all_gather(segment_ids, R, axis=0, tiled=True)
    gain_in, gain_mid = gains[0], gains[1]
    gate_weight, up_weight, down_weight, ids = lax.optimization_barrier(
        (gate_weight, up_weight, down_weight, ids)
    )
    w_feed = line_gather(jnp.concatenate(feed_cols(gate_weight) + feed_cols(up_weight), axis=1))
    w_down = line_gather(lax.dynamic_slice_in_dim(down_weight, r * piece, piece, 0))

    places = jnp.arange(length, dtype=jnp.int32)
    fresh = jnp.concatenate(
        [jnp.ones((width, 1), dtype=jnp.bool_), ids[:, 1:] != ids[:, :-1]], axis=1
    )
    positions = places[None] - lax.cummax(jnp.where(fresh, places[None], 0), axis=1)
    own_positions = lax.dynamic_slice_in_dim(positions, z * tok, tok, 1).reshape(all_tok)
    own_places = z * tok + jnp.arange(all_tok, dtype=jnp.int32) % tok
    own_starts = own_places - own_positions
    steps = all_tok // QUERY_BLOCK
    starts = own_starts.reshape(steps, 1, QUERY_BLOCK)
    query_places = own_places.reshape(steps, 1, QUERY_BLOCK)
    low = starts[:, 0, 0] // KEY_BLOCK
    high = query_places[:, 0, QUERY_BLOCK - 1] // KEY_BLOCK + 1

    if plane_kernels:
        wide_cosine, wide_sine = rope_tables(own_positions, 4)
        wide_sine = wide_sine * jnp.where(jnp.arange(2 * HEAD_DIM) // (HEAD_DIM // 2) % 2, 1.0, -1.0)
        query, kv_rows, cot_all, w_out = project(
            hidden_in.reshape(width, tok, model),
            w_attention,
            wide_cosine,
            wide_sine,
            cotangent,
            qw,
            3,
        )
        kv_rows = kv_rows.reshape(width, length, 2 * HEAD_DIM)
        cot_all = cot_all.reshape(all_tok, model)
    else:
        cosine, sine = rope_tables(own_positions)
        qkv = dot(hidden_in, w_qkv)
        query = rotate(qkv[:, :qw].reshape(all_tok, heads, HEAD_DIM), cosine, sine, 1.0)
        query = query.astype(bf16).reshape(all_tok, qw)
        key = rotate(qkv[:, None, qw : qw + HEAD_DIM], cosine, sine, 1.0).astype(bf16)[:, 0]
        value = qkv[:, qw + HEAD_DIM :].astype(bf16)
        kv_rows = (
            lax.all_gather(jnp.concatenate([key, value], axis=1), F, axis=0, tiled=False)
            .reshape(planes, width, tok, 2 * HEAD_DIM)
            .transpose(1, 0, 2, 3)
            .reshape(width, length, 2 * HEAD_DIM)
        )
        cot_all = lax.all_gather(cotangent, R, axis=0, tiled=True)
        w_out = lax.all_to_all(
            w_attention[:, qw + 2 * HEAD_DIM :], R, split_axis=0, concat_axis=1, tiled=True
        )
    common = [("tokens", query), ("sequence", kv_rows), ("row", starts), ("row", query_places)]
    mixed, log_totals = attention_call(
        attention_kernel,
        heads,
        low,
        high,
        common,
        [
            ("tokens", jax.ShapeDtypeStruct((all_tok, qw), bf16)),
            ("row", jax.ShapeDtypeStruct((steps, 1, heads * QUERY_BLOCK), f32)),
        ],
    )
    if plane_kernels:
        cot_blocks = cot_all.reshape(width, tok, model)
        middle = branch_layer(mixed, w_out, tokens, 1)
        hidden_blocks, acts, down_part = middle_layer(middle, gain_mid[None], w_feed, cot_blocks, 2)
    else:
        middle = tok_float + plane_scatter(dot(mixed, w_out).astype(bf16), 1)
    scale_mid = inverse_rms(middle)
    normed_mid = middle * scale_mid

    if plane_kernels:
        out_part, grad_hidden_mid, feed_part = feed_forward(
            hidden_blocks, cot_blocks, acts, w_feed, w_down, 5
        )
    else:
        w_gate, w_up = w_feed[:, :hidden_units], w_feed[:, hidden_units:]
        hidden_mid = plane_gather((normed_mid * gain_mid).astype(bf16), 2)
        gate_acc = dot(hidden_mid, w_gate)
        up_acc = dot(hidden_mid, w_up)
        gate_sig = jax.nn.sigmoid(gate_acc)
        gate_silu = gate_acc * gate_sig
        inner_act = (gate_silu * up_acc).astype(bf16)
        out_part = dot(inner_act, w_down).astype(bf16)
        grad_inner = dot(cot_all, w_down, 1, 1)
        grad_gate = grad_inner * up_acc * gate_sig * (1.0 + gate_acc * (1.0 - gate_sig))
        grad_gate = grad_gate.astype(bf16)
        grad_up = (grad_inner * gate_silu).astype(bf16)
        feed_part = jnp.concatenate(
            [dot(hidden_mid, grad_gate, 0, 0), dot(hidden_mid, grad_up, 0, 0)], axis=1
        ).astype(bf16)
        down_part = dot(inner_act, cot_all, 0, 0).astype(bf16)
        grad_hidden_part = dot(grad_gate, w_gate, 1, 1) + dot(grad_up, w_up, 1, 1)
        grad_hidden_mid = plane_scatter(grad_hidden_part.astype(bf16), 5)
        feed_out = plane_scatter(out_part, 4)
    down_rows = line_scatter(down_part)
    feed_rows = line_scatter(feed_part)
    gain_mid_term = jnp.sum(grad_hidden_mid * normed_mid, axis=0)
    grad_normed_mid = grad_hidden_mid * gain_mid
    grad_middle = cotangent.astype(f32) + scale_mid * (
        grad_normed_mid - normed_mid * jnp.mean(grad_normed_mid * normed_mid, axis=1, keepdims=True)
    )

    grad_branch = plane_gather(grad_middle.astype(bf16), 6)
    grad_mixed = dot(grad_branch, w_out, 1, 1).astype(bf16)
    w_out_part = dot(mixed, grad_branch, 0, 0).astype(bf16)

    if plane_kernels:
        grad_qkv, qkv_part, feed_out, down_all, w_out_part = attention_back(
            heads,
            query,
            kv_rows,
            starts,
            query_places,
            grad_mixed,
            mixed,
            log_totals,
            wide_cosine,
            wide_sine,
            hidden_in,
            out_part,
            down_rows,
            w_out_part,
            10,
        )
        w_out_part = w_out_part.reshape(width * qw, model // width)
    else:
        gq, gkv = attention_call(
            attention_back_kernel,
            heads,
            low,
            high,
            common + [("tokens", grad_mixed), ("tokens", mixed), ("row", log_totals)],
            [
                ("tokens", jax.ShapeDtypeStruct((all_tok, qw), f32)),
                ("sequence", jax.ShapeDtypeStruct((width, length, 2 * HEAD_DIM), bf16)),
            ],
            [pltpu.VMEM((length, 2 * HEAD_DIM), f32)],
        )
        gkv = gkv.reshape(width, planes, tok, 2 * HEAD_DIM).transpose(1, 0, 2, 3)
        gkv = line_scatter(gkv.reshape(planes * all_tok, 2 * HEAD_DIM)).astype(f32)
        gq = rotate(gq.reshape(all_tok, heads, HEAD_DIM), cosine, sine, -1.0)
        gk = rotate(gkv[:, None, :HEAD_DIM], cosine, sine, -1.0)[:, 0]
        grad_qkv = jnp.concatenate([gq.reshape(all_tok, qw), gk, gkv[:, HEAD_DIM:]], axis=1)
        grad_qkv = grad_qkv.astype(bf16)
        qkv_part = dot(hidden_in, grad_qkv, 0, 0).astype(bf16)
        down_all = lax.all_gather(down_rows, R, axis=0, tiled=True)
        w_out_part = lax.all_to_all(w_out_part, R, split_axis=1, concat_axis=0, tiled=True)
    out_rows = line_scatter(w_out_part)
    activations = (middle + feed_out).astype(bf16)
    grad_qkv, qkv_part, feed_rows = lax.optimization_barrier((grad_qkv, qkv_part, feed_rows))
    qkv_rows = line_scatter(qkv_part)
    if plane_kernels:
        grad_hidden_in, feed_all = scatter_hidden(grad_qkv, w_attention, feed_rows, tok, 7)
    else:
        grad_hidden_in = plane_scatter(dot(grad_qkv, w_qkv, 1, 1).astype(bf16), 7)
        feed_all = lax.all_gather(feed_rows, R, axis=0, tiled=False)
    gain_in_term = jnp.sum(grad_hidden_in * normed_in, axis=0)
    grad_normed_in = grad_hidden_in * gain_in
    input_grad = (
        grad_middle
        + scale_in
        * (
            grad_normed_in
            - normed_in * jnp.mean(grad_normed_in * normed_in, axis=1, keepdims=True)
        )
    ).astype(bf16)

    rows = model // planes
    terms = jnp.stack([gain_in_term, gain_mid_term])
    if plane_kernels:
        terms = jnp.pad(terms.reshape(2, planes, rows).transpose(1, 0, 2), ((0, 0), (0, 6), (0, 0)))
        qkv_all, out_all, gain_terms = finish(qkv_rows, out_rows, terms, 9)
    else:
        qkv_all = lax.all_gather(qkv_rows, R, axis=0, tiled=False)
        out_all = lax.all_gather(out_rows, R, axis=0, tiled=False)
        gain_terms = lax.psum(lax.psum_scatter(terms, F, scatter_dimension=1, tiled=True), R)
    down_grad = down_all.reshape(feed // planes, model).astype(f32)
    gate_grad, up_grad = join_call(
        functools.partial(join_feed_kernel, planes, piece), [feed_all], [feed, feed]
    )
    query_grad, key_grad, value_grad, out_grad = join_call(
        functools.partial(join_attention_kernel, width // KV_HEADS),
        [qkv_all, out_all],
        [width * qw, KV_HEADS * HEAD_DIM, KV_HEADS * HEAD_DIM, model],
    )
    return (
        activations,
        input_grad,
        gain_terms[0],
        query_grad,
        key_grad,
        value_grad,
        out_grad,
        gain_terms[1],
        gate_grad,
        up_grad,
        down_grad,
    )


def solution(mesh):
    tok = P((R, F), None)
    row = P(F, None)
    in_specs = (tok, P(R, None), P(F), row, row, row, row, P(F), row, row, row, tok)
    out_specs = (tok, tok, P(F), row, row, row, row, P(F), row, row, row)
    return jax.shard_map(
        per_device, mesh=mesh, in_specs=in_specs, out_specs=out_specs, check_vma=False
    )
```

```python
import functools
import math

import jax
import jax.numpy as jnp
from jax import lax
from jax.experimental import pallas as pl
from jax.experimental.pallas import tpu as pltpu
from jax.sharding import PartitionSpec as P

HEADS = 32
KV_HEADS = 4
HEAD_DIM = 64
EPSILON = 1e-05
NEGATIVE = -1e30
R = "replica"
F = "fsdp"
MESH = pl.DeviceIdType.MESH
DMA = pltpu.SemaphoreType.DMA
ANY = pl.BlockSpec(memory_space=pl.ANY)
KEY_BLOCK = 256
QUERY_BLOCK = 128
PARTS = 2
FIRST_DOC = 800


def inverse_rms(values):
    return lax.rsqrt(jnp.mean(values * values, axis=1, keepdims=True) + EPSILON)


def rope_tables(positions, repeats=1):
    half_dim = HEAD_DIM // 2
    places = jnp.arange(repeats * half_dim, dtype=jnp.int32) % half_dim
    freq_rates = jnp.exp(places.astype(jnp.float32) * (-math.log(10000.0) / half_dim))
    angles = positions.astype(jnp.float32)[:, None] * freq_rates[None, :]
    return (jnp.cos(angles), jnp.sin(angles))


def rotate(tensor, cosine_table, sine_table, sign):
    half_dim = HEAD_DIM // 2
    low, up = tensor[..., :half_dim], tensor[..., half_dim:]
    cos_part = cosine_table[:, None, :]
    sin_part = sine_table[:, None, :] * sign
    return jnp.concatenate(
        [low * cos_part - up * sin_part, up * cos_part + low * sin_part], axis=-1
    )


def dot(a, b, ca=1, cb=0):
    return lax.dot_general(a, b, (((ca,), (cb,)), ((), ())), preferred_element_type=jnp.float32)


def remote(src, dst, sems, index, device):
    return pltpu.make_async_remote_copy(
        src_ref=src,
        dst_ref=dst,
        send_sem=sems[0].at[index],
        recv_sem=sems[1].at[index],
        device_id={R: device},
        device_id_type=MESH,
    )


def greet(*devices):
    barrier = pltpu.get_barrier_semaphore()
    for device in devices:
        pl.semaphore_signal(barrier, inc=1, device_id={R: device}, device_id_type=MESH)
    pl.semaphore_wait(barrier, len(devices))


class Gather:
    @staticmethod
    def scratch(count):
        return [DMA((count,))] * 6 + [DMA((4, count))] * 2

    def __init__(self, items, sems):
        self.items, self.count = items, len(items)
        self.half = self.count // 2
        self.me = lax.axis_index(R)
        self.sibling, self.x, self.y = self.me + 1 - 2 * lax.rem(self.me, 2), self.me ^ 2, self.me ^ 4
        self.sems = sems

    def copy(self, kind, i):
        first = i < self.half
        owner, device = {
            0: (self.me, self.x),
            1: (self.me, self.y),
            2: (self.x, self.y) if first else (self.y, self.x),
            3: (self.me, self.sibling),
            4: (self.x, self.sibling),
            5: (self.y, self.sibling),
            6: (self.me ^ 6, self.sibling),
        }[kind]
        own, slot = self.items[i]
        sems = self.sems[2 * min(kind, 3) : 2 * min(kind, 3) + 2]
        src = own if kind in (0, 1, 3) else slot(owner)
        return remote(src, slot(owner), sems, i if kind < 3 else (kind - 3, i), device)

    def start(self, kept=()):
        ready = [i for i in range(self.count) if i not in kept]
        for n, i in enumerate(ready):
            self.copy(0, i).start()
            self.copy(1, ready[(n + self.half) % len(ready)]).start()
        for i in ready:
            self.copy(3, i).start()

    def start_items(self, items):
        for i in items:
            for kind in (0, 1, 3):
                self.copy(kind, i).start()

    def pass_on(self, kind, i):
        self.copy(kind, i).wait_recv()
        if kind < 2 and (i < self.half) == (kind == 0):
            self.copy(2, i).start()
        self.copy(kind + 4, i).start()

    def relay(self, i):
        self.pass_on(0, i)
        self.pass_on(1, (i + self.half) % self.count)

    def far(self):
        for i in range(self.half):
            self.pass_on(2, i)
            self.pass_on(2, self.half + i)
        for i in range(2 * self.half, self.count):
            self.pass_on(2, i)

    def from_sibling(self, kind):
        for i in range(self.count):
            self.copy(kind, i).wait_recv()

    def wait_sends(self):
        for i in range(self.count):
            for kind in range(7):
                self.copy(kind, i).wait_send()

    def finish(self):
        self.far()
        for kind in range(3, 7):
            self.from_sibling(kind)
        self.wait_sends()


def row_items(x, out, chunks):
    size = x.shape[0] // chunks

    def item(i):
        part = pl.ds(i * size, size)
        return x.at[part], lambda owner: out.at[owner, part]

    return [item(i) for i in range(chunks)]


def gather_kernel(chunks, x, out, local_sem, *sems):
    gather = Gather(row_items(x, out, chunks), sems)
    greet(gather.sibling, gather.x, gather.y)
    own = pltpu.make_async_copy(x, out.at[gather.me], local_sem)
    own.start()
    gather.start()
    for i in range(chunks):
        gather.relay(i)
    gather.finish()
    own.wait()


def enter_kernel(chunks, tokens, gains, ids, hidden, all_gains, all_ids, own, own_sem, to_z, at_z, *sems):
    f32 = jnp.float32
    planes = all_gains.shape[0]
    z = lax.axis_index(F)
    items = row_items(own, hidden, chunks) + [(ids, lambda owner: all_ids.at[owner])]
    gather = Gather(items, sems)
    others = [lax.rem(z + i, planes) for i in range(1, planes)]
    barrier = pltpu.get_barrier_semaphore()
    for other in others:
        pl.semaphore_signal(barrier, inc=1, device_id={F: other}, device_id_type=MESH)
    for device in (gather.sibling, gather.x, gather.y):
        pl.semaphore_signal(barrier, inc=1, device_id={R: device}, device_id_type=MESH)
    pl.semaphore_wait(barrier, planes + 2)
    copies = [
        pltpu.make_async_remote_copy(
            src_ref=gains,
            dst_ref=all_gains.at[z],
            send_sem=to_z.at[i],
            recv_sem=at_z.at[i],
            device_id={F: other},
            device_id_type=MESH,
        )
        for i, other in enumerate(others)
    ]
    for copy in copies:
        copy.start()
    all_gains[z] = gains[...]
    all_ids[gather.me] = ids[...]
    size = tokens.shape[0] // chunks
    scales = [
        inverse_rms(tokens[i * size : (i + 1) * size, :].astype(f32)) for i in range(chunks)
    ]
    for copy in copies:
        copy.wait()
    gain = jnp.concatenate([all_gains[p, 0:1] for p in range(planes)], axis=1)
    for i in range(chunks):
        part = slice(i * size, (i + 1) * size)
        own[part, :] = (tokens[part, :].astype(f32) * scales[i] * gain).astype(jnp.bfloat16)
    kept = pltpu.make_async_copy(own, hidden.at[gather.me], own_sem)
    kept.start()
    gather.start()
    for i in range(gather.count):
        gather.relay(i)
    gather.finish()
    kept.wait()


def turn(x, cosine, sine):
    half_dim = HEAD_DIM // 2
    low = lax.rem(lax.broadcasted_iota(jnp.int32, x.shape, 1), HEAD_DIM) < half_dim
    swapped = jnp.where(low, pltpu.roll(x, 2 * HEAD_DIM - half_dim, 1), pltpu.roll(x, half_dim, 1))
    return x * cosine + swapped * sine


def turn_keys(x, cosine, sine):
    is_key = lax.broadcasted_iota(jnp.int32, x.shape, 1) < HEAD_DIM
    return jnp.where(is_key, turn(x, cosine, sine), x)


def along_line(src, dst, sems, index, plane):
    return pltpu.make_async_remote_copy(
        src_ref=src,
        dst_ref=dst,
        send_sem=sems[0].at[index],
        recv_sem=sems[1].at[index],
        device_id={F: plane},
        device_id_type=MESH,
    )


def project_kernel(
    chunks, hidden, weight, cosine, sine, cotangent, w_cols, query, kv, cot_all, w_out,
    own, hidden_in, hidden_sems, own_sem, cot_sem, w_sem, to_all, at_all, to_line, at_line, to_sib, at_sib,
    *sems,
):
    bf16 = jnp.bfloat16
    planes = kv.shape[1]
    z = lax.axis_index(F)
    tok = cotangent.shape[0]
    width = kv.shape[0]
    count = width // 2
    gather = Gather(row_items(cotangent, cot_all, chunks), sems)
    core = lax.rem(gather.me, 2)
    mine = pl.ds(core * count, count)
    above, below = lax.rem(z + 1, planes), lax.rem(z + planes - 1, planes)
    me = gather.me
    peers = [me ^ distance for distance in range(1, width)]

    def hidden_load(i):
        slot = lax.rem(i, 2)
        block = hidden.at[lax.rem(core * count + i, width)]
        return pltpu.make_async_copy(block, hidden_in.at[slot], hidden_sems.at[slot])

    for i in (0, 1):
        hidden_load(i).start()
    barrier = pltpu.get_barrier_semaphore()
    for other in (above, below):
        pl.semaphore_signal(barrier, inc=1, device_id={F: other}, device_id_type=MESH)
    for device in peers:
        pl.semaphore_signal(barrier, inc=1, device_id={R: device}, device_id_type=MESH)
    pl.semaphore_wait(barrier, 1 + width)
    rows = w_out.shape[0]
    share = w_out.shape[1] // width
    to = w_out.at[:, pl.ds(pl.multiple_of(me * share, share), share)]

    def rows_of(device):
        part = pl.ds(pl.multiple_of(device * rows, rows), rows)
        return w_cols.at[part, pl.ds(w_cols.shape[1] - share, share)]

    w_copies = [
        remote(rows_of(device), to, (to_all, at_all), i, device) for i, device in enumerate(peers)
    ]
    w_kept = pltpu.make_async_copy(rows_of(me), to, w_sem)
    kept_cot = pltpu.make_async_copy(cotangent, cot_all.at[gather.me], cot_sem)
    kept_cot.start()
    gather.start()
    for copy in [w_kept] + w_copies:
        copy.start()

    def tile(i, carry):
        s = lax.rem(core * count + i, width)
        rows = pl.ds(pl.multiple_of(s * tok, tok), tok)
        hidden_load(i).wait()
        acc = dot(hidden_in[lax.rem(i, 2)], weight[:, : query.shape[1] + 2 * HEAD_DIM])

        @pl.when(i + 2 < width)
        def _():
            hidden_load(i + 2).start()

        c, n = cosine[rows, :], sine[rows, :]
        columns = acc.shape[1] - 2 * HEAD_DIM
        for first in range(0, columns, 2 * HEAD_DIM):
            part = slice(first, first + 2 * HEAD_DIM)
            query[rows, part] = turn(acc[:, part], c, n).astype(bf16)
        own[s] = turn_keys(acc[:, columns:], c, n).astype(bf16)
        return carry

    class Group:
        def __init__(self, make):
            self.each = [make(i) for i in range(count)]

        def __getattr__(self, name):
            def call():
                for copy in self.each:
                    getattr(copy, name)()

            return call

    def up(step):
        slot = z - step

        def make(i):
            dst = kv.at[core * count + i, slot]
            src = own.at[core * count + i] if step == 0 else dst
            return along_line(src, dst, (to_line, at_line), (step, i), above)

        return Group(make)

    def came(step):
        def make(i):
            dst = kv.at[core * count + i, z - step]
            return along_line(dst, dst, (to_line, at_line), (step - 1, i), above)

        return Group(make)

    def across(step):
        slot = z - step
        return remote(kv.at[mine, slot], kv.at[mine, slot], (to_sib, at_sib), step, gather.sibling)

    lax.fori_loop(0, count, tile, 0)

    @pl.when(z < planes - 1)
    def _():
        up(0).start()

    lax.fori_loop(count, width, tile, 0)
    kept = pltpu.make_async_copy(own, kv.at[:, z], own_sem)
    kept.start()
    done = 0
    for step in range(1, planes):

        @pl.when(z >= step)
        def _():
            arriving, leaving = came(step), up(step)
            for i in range(count):
                arriving.each[i].wait_recv()

                @pl.when(z < planes - 1)
                def _():
                    leaving.each[i].start()

            across(step).start()

        while done < chunks * step // planes:
            gather.relay(done)
            done += 1
    for i in range(done, chunks):
        gather.relay(i)
    gather.finish()
    for step in range(planes):

        @pl.when((z >= step) & (z < planes - 1))
        def _():
            up(step).wait_send()

        if step:

            @pl.when(z >= step)
            def _():
                across(step).wait()

    for copy in [kept, kept_cot, w_kept] + w_copies:
        copy.wait()


def finish_kernel(
    qkv, out_rows, terms, all_qkv, all_out, gains, own_gain, all_gains,
    at_planes, own_sems, to_z, at_z, *sems,
):
    planes = terms.shape[0]
    z = lax.axis_index(F)
    chunks = [x for pair in zip(row_items(qkv, all_qkv, 2), row_items(out_rows, all_out, 2)) for x in pair]
    gather = Gather(chunks + [(own_gain, lambda owner: all_gains.at[owner])], sems)
    me, last = gather.me, gather.count - 1
    others = [lax.rem(z + i, planes) for i in range(1, planes)]
    barrier = pltpu.get_barrier_semaphore()
    for other in others:
        pl.semaphore_signal(barrier, inc=1, device_id={F: other}, device_id_type=MESH)
    for device in (gather.sibling, gather.x, gather.y):
        pl.semaphore_signal(barrier, inc=1, device_id={R: device}, device_id_type=MESH)
    pl.semaphore_wait(barrier, planes + 2)
    copies = [
        along_line(terms.at[other], at_planes.at[i], (to_z, at_z), i, other)
        for i, other in enumerate(others)
    ]
    for copy in copies:
        copy.start()
    kept = [
        pltpu.make_async_copy(qkv, all_qkv.at[me], own_sems.at[0]),
        pltpu.make_async_copy(out_rows, all_out.at[me], own_sems.at[1]),
    ]
    for copy in kept:
        copy.start()
    gather.start((last,))
    total = terms[z]
    for i, copy in enumerate(copies):
        copy.wait()
        total = total + at_planes[i]
    own_gain[...] = total
    all_gains[me] = total
    gather.start_items((last,))
    for i in range(gather.count):
        gather.relay(i)
    gather.finish()
    total = all_gains[0]
    for device in range(1, all_gains.shape[0]):
        total = total + all_gains[device]
    gains[...] = total
    for copy in kept:
        copy.wait()


def finish(qkv, out_rows, terms, call):
    planes, width = lax.axis_size(F), lax.axis_size(R)
    f32, bf16 = jnp.float32, jnp.bfloat16
    vmem = pl.BlockSpec(memory_space=pltpu.VMEM)
    block = terms.shape[1:]
    return pl.pallas_call(
        finish_kernel,
        out_shape=[
            jax.ShapeDtypeStruct((width,) + qkv.shape, bf16),
            jax.ShapeDtypeStruct((width,) + out_rows.shape, bf16),
            jax.ShapeDtypeStruct(block, f32),
        ],
        in_specs=[ANY, ANY, vmem],
        out_specs=[ANY, ANY, vmem],
        scratch_shapes=[
            pltpu.VMEM(block, f32),
            pltpu.VMEM((width,) + block, f32),
            pltpu.VMEM((planes - 1,) + block, f32),
            DMA((2,)),
            DMA((planes - 1,)),
            DMA((planes - 1,)),
        ]
        + Gather.scratch(5),
        compiler_params=pltpu.CompilerParams(collective_id=call, has_side_effects=True),
    )(qkv, out_rows, terms)


class Scatter:
    @staticmethod
    def scratch(rows, columns, chunks):
        bf16, size = jnp.bfloat16, rows // chunks
        return [
            pltpu.VMEM((5, rows, columns), bf16),
            pltpu.VMEM((4, rows, columns), bf16),
            pltpu.VMEM((chunks, 2, size, columns), bf16),
            pltpu.VMEM((chunks, size, columns), bf16),
            pltpu.VMEM((2, size, columns), jnp.float32),
            DMA((4,)),
            DMA((4,)),
            DMA((chunks, 2)),
            DMA((chunks, 2)),
            DMA((chunks,)),
            DMA((chunks,)),
            DMA((2,)),
        ]

    def __init__(self, out, chunks, refs):
        self.out, self.chunks, self.half = out, chunks, chunks // 2
        self.own, self.sib, self.got, self.got_far, self.total = refs[:5]
        self.sib_sems, self.near_sems, self.far_sems = refs[5:7], refs[7:9], refs[9:11]
        self.out_sem = refs[11]
        self.me = lax.axis_index(R)
        self.sibling, self.x, self.y = self.me + 1 - 2 * lax.rem(self.me, 2), self.me ^ 2, self.me ^ 4
        self.size = out.shape[0] // chunks
        self.order = [*range(self.half, chunks), *range(self.half)]
        self.trades = None

    def owner(self, i):
        return (self.me ^ (6 - 2 * (i // 2))) ^ (1 - lax.rem(i, 2))

    def trade(self, d):
        return remote(self.own.at[4], self.sib.at[d], self.sib_sems, d, self.sibling)

    def put(self, i, value):
        d = 3 - i // 2
        for_sibling = lax.rem(i, 2) == 0

        @pl.when(for_sibling & (i >= 2))
        def _():
            self.trade(d + 1).wait_send()

        self.own[jnp.where(for_sibling, 4, d)] = value

        @pl.when(for_sibling)
        def _():
            self.trade(d).start()

    def take(self, part, sems):
        self.loads, self.trades = {}, {}
        for d in (3, 2, 1, 0):
            self.loads[d] = pltpu.make_async_copy(part.at[self.me ^ (2 * d)], self.own.at[d], sems.at[d])
            self.loads[d].start()
        for d in (3, 2, 1, 0):
            self.trades[d] = remote(
                part.at[self.sibling ^ (2 * d)], self.sib.at[d], self.sib_sems, d, self.sibling
            )
            self.trades[d].start()

    def taken(self, d):
        self.loads[d].wait()
        self.trades[d].wait_recv()

    def arrived(self, d):
        self.trade(d).wait_recv()

    def part(self, j):
        return pl.ds(j * self.size, self.size)

    def summed(self, d, j):
        part = self.part(j)
        return self.own[d, part].astype(jnp.float32) + self.sib[d, part].astype(jnp.float32)

    def near_copy(self, j, n):
        device, d = (self.x, 1) if j < self.half else (self.y, 2)
        src = self.own.at[3 if n else d, self.part(j)]
        return remote(src, self.got.at[j, n], self.near_sems, (j, n), device)

    def far_copy(self, j):
        device, d = (self.y, 2) if j < self.half else (self.x, 1)
        return remote(self.own.at[d, self.part(j)], self.got_far.at[j], self.far_sems, j, device)

    def out_copy(self, j):
        slot = self.order.index(j) % 2
        return pltpu.make_async_copy(
            self.total.at[slot], self.out.at[self.part(j)], self.out_sem.at[slot]
        )

    def near(self, j, n):
        e = 3 if n else (1 if j < self.half else 2)
        self.own[e, self.part(j)] = self.summed(e, j).astype(jnp.bfloat16)
        self.near_copy(j, n).start()

    def progress(self, i):
        @pl.when(i == 2)
        def _():
            self.arrived(3)
            for j in self.order:
                self.near(j, 1)

        @pl.when(i == 4)
        def _():
            self.arrived(2)
            for j in range(self.half, self.chunks):
                self.near(j, 0)

        @pl.when(i == 6)
        def _():
            self.arrived(1)
            for j in range(self.half):
                self.near(j, 0)

    def far(self, j):
        for n in (0, 1):
            self.near_copy(j, n).wait_recv()
        d = 2 if j < self.half else 1
        passed = self.summed(d, j) + self.got[j, 1].astype(jnp.float32)
        self.own[d, self.part(j)] = passed.astype(jnp.bfloat16)
        self.far_copy(j).start()

    def result(self, j):
        self.far_copy(j).wait_recv()
        return (
            self.summed(0, j)
            + self.got[j, 0].astype(jnp.float32)
            + self.got_far[j].astype(jnp.float32)
        )

    def last(self, j):
        total = self.result(j)
        turn = self.order.index(j)
        if turn >= 2:
            self.out_copy(self.order[turn - 2]).wait()
        self.total[turn % 2] = total
        self.out_copy(j).start()

    def finish(self, written=True):
        if self.trades is None:
            self.trade(0).wait_send()
        else:
            for copy in self.trades.values():
                copy.wait_send()
        if written:
            for j in self.order[-2:]:
                self.out_copy(j).wait()
        for j in range(self.chunks):
            self.far_copy(j).wait_send()
            for n in (0, 1):
                self.near_copy(j, n).wait_send()


def branch_kernel(chunks, mixed, w_out, tokens, middle, *refs):
    f32, bf16 = jnp.float32, jnp.bfloat16
    scatter = Scatter(middle, chunks, refs)
    tok = tokens.shape[0]
    size = tok // chunks
    greet(scatter.sibling, scatter.x, scatter.y)

    def branch(i, carry):
        rows = pl.ds(pl.multiple_of(scatter.owner(i) * tok, tok), tok)
        scatter.put(i, dot(mixed[rows, :], w_out[...]).astype(bf16))
        scatter.progress(i)
        return carry

    lax.fori_loop(0, mixed.shape[0] // tok, branch, 0)
    scatter.arrived(0)
    for j in scatter.order:
        scatter.far(j)
    for j in scatter.order:
        part = pl.ds(j * size, size)
        middle[part, :] = tokens[part, :].astype(f32) + scatter.result(j)
    scatter.finish(False)


def middle_kernel(
    chunks, middle, gain, w_feed, cotangent, hidden, acts, down_part,
    blocks, act_stage, cot_in, down_sum, down_stage, out_sems, act_sems, cot_sems, down_sem, *sems,
):
    f32, bf16 = jnp.float32, jnp.bfloat16
    width, tok, _ = blocks.shape
    me = lax.axis_index(R)
    size = tok // chunks

    def item(j):
        part = pl.ds(j * size, size)
        return blocks.at[me, part], lambda owner: blocks.at[owner, part]

    gather = Gather([item(j) for j in range(chunks)], sems)
    units = w_feed.shape[1] // 2
    order = [*range(chunks // 2, chunks), *range(chunks // 2)]

    def cot_load(i):
        slot = lax.rem(i, 2)
        return pltpu.make_async_copy(cotangent.at[me ^ i], cot_in.at[slot], cot_sems.at[slot])

    for i in (0, 1):
        cot_load(i).start()
    greet(gather.sibling, gather.x, gather.y)
    for j in order:
        part = pl.ds(j * size, size)
        total = middle[part, :]
        blocks[me, part] = (total * inverse_rms(total) * gain[...]).astype(bf16)
        gather.start_items((j,))

    def hidden_copy(i):
        return pltpu.make_async_copy(blocks.at[me ^ i], hidden.at[me ^ i], out_sems.at[i])

    def act_copy(i):
        slot = lax.rem(i, 2)
        return pltpu.make_async_copy(act_stage.at[slot], acts.at[me ^ i], act_sems.at[slot])

    def block(i, carry):
        @pl.when(i == 1)
        def _():
            gather.from_sibling(3)

        @pl.when(i == 2)
        def _():
            for j in order:
                gather.pass_on(0, j)
                gather.pass_on(1, j)

        @pl.when(i == 3)
        def _():
            gather.from_sibling(4)

        @pl.when(i == 5)
        def _():
            gather.from_sibling(5)

        @pl.when(i == 6)
        def _():
            for j in order:
                gather.pass_on(2, j)

        @pl.when(i == 7)
        def _():
            gather.from_sibling(6)

        @pl.when(i >= 2)
        def _():
            act_copy(i - 2).wait()

        acc = dot(blocks[me ^ i], w_feed[...])
        act_stage[lax.rem(i, 2)] = acc
        act_copy(i).start()
        hidden_copy(i).start()
        gate, up = acc[:, :units], acc[:, units:]
        inner_turned = (gate / (1.0 + jnp.exp(-gate)) * up).astype(bf16).T
        cot_load(i).wait()

        @pl.when(i == 0)
        def _():
            down_sum[...] = dot(inner_turned, cot_in[0])

        @pl.when(i > 0)
        def _():
            down_sum[...] += dot(inner_turned, cot_in[lax.rem(i, 2)])

        @pl.when(i + 2 < width)
        def _():
            cot_load(i + 2).start()

        return carry

    lax.fori_loop(0, width, block, 0)
    down_stage[...] = down_sum[...].astype(bf16)
    down_copy = pltpu.make_async_copy(down_stage, down_part, down_sem)
    down_copy.start()
    down_copy.wait()
    gather.wait_sends()
    for i in (width - 2, width - 1):
        act_copy(i).wait()
    for i in range(width):
        hidden_copy(i).wait()


def branch_layer(mixed, w_out, tokens, call, chunks=4):
    vmem = pl.BlockSpec(memory_space=pltpu.VMEM)
    return pl.pallas_call(
        functools.partial(branch_kernel, chunks),
        out_shape=jax.ShapeDtypeStruct(tokens.shape, jnp.float32),
        in_specs=[vmem] * 3,
        out_specs=vmem,
        scratch_shapes=Scatter.scratch(*tokens.shape, chunks),
        compiler_params=pltpu.CompilerParams(
            collective_id=call, has_side_effects=True, vmem_limit_bytes=40 << 20
        ),
    )(mixed, w_out, tokens)


def middle_layer(middle, gain, w_feed, cotangent, call, chunks=4):
    width = lax.axis_size(R)
    tok, model = middle.shape
    bf16, f32 = jnp.bfloat16, jnp.float32
    units = w_feed.shape[1] // 2
    vmem = pl.BlockSpec(memory_space=pltpu.VMEM)
    return pl.pallas_call(
        functools.partial(middle_kernel, chunks),
        out_shape=[
            jax.ShapeDtypeStruct((width, tok, model), bf16),
            jax.ShapeDtypeStruct((width, tok, 2 * units), f32),
            jax.ShapeDtypeStruct((units, model), bf16),
        ],
        in_specs=[vmem] * 3 + [ANY],
        out_specs=[ANY] * 3,
        scratch_shapes=[
            pltpu.VMEM((width, tok, model), bf16),
            pltpu.VMEM((2, tok, 2 * units), f32),
            pltpu.VMEM((2, tok, model), bf16),
            pltpu.VMEM((units, model), f32),
            pltpu.VMEM((units, model), bf16),
            DMA((width,)),
            DMA((2,)),
            DMA((2,)),
            DMA,
        ]
        + Gather.scratch(chunks),
        compiler_params=pltpu.CompilerParams(
            collective_id=call, has_side_effects=True, vmem_limit_bytes=56 << 20
        ),
    )(middle, gain, w_feed, cotangent)


def feed_kernel(
    chunks, hidden, cotangent, acts, w_feed, w_down, out_part, grad_hidden, feed_part,
    acts_in, cot_in, grads, column_in, feed_stage, out_stage, in_sems, column_sems, feed_sem, out_sem,
    *refs,
):
    f32, bf16 = jnp.float32, jnp.bfloat16
    width, tok, model = hidden.shape
    units = w_down.shape[0]
    scatter = Scatter(grad_hidden, chunks, refs)
    half = chunks // 2
    first_half, second_half = range(half), range(half, chunks)

    def loads(i):
        slot, owner = lax.rem(i, 2), scatter.owner(i)
        return [
            pltpu.make_async_copy(acts.at[owner], acts_in.at[slot], in_sems.at[0, slot]),
            pltpu.make_async_copy(cotangent.at[owner], cot_in.at[slot], in_sems.at[1, slot]),
        ]

    def out_copy(i):
        slot = lax.rem(i, 2)
        return pltpu.make_async_copy(
            out_stage.at[slot], out_part.at[scatter.owner(i)], out_sem.at[slot]
        )

    for i in (0, 1):
        for copy in loads(i):
            copy.start()
    greet(scatter.sibling, scatter.x, scatter.y)

    def block(i, carry):
        slot = lax.rem(i, 2)
        rows = pl.ds(pl.multiple_of(i * tok, tok), tok)
        for copy in loads(i):
            copy.wait()
        gate, up = acts_in[slot, :, :units], acts_in[slot, :, units:]
        gate_sig = 1.0 / (1.0 + jnp.exp(-gate))
        gate_silu = gate * gate_sig
        inner = (gate_silu * up).astype(bf16)
        grad_inner = dot(cot_in[slot], w_down[...], 1, 1)
        grad_gate = grad_inner * up * gate_sig * (1.0 + gate * (1.0 - gate_sig))
        both = jnp.concatenate([grad_gate, grad_inner * gate_silu], axis=1).astype(bf16)
        grads[rows, :] = both
        scatter.put(i, dot(both, w_feed[...], 1, 1).astype(bf16))

        @pl.when(i >= 2)
        def _():
            out_copy(i - 2).wait()

        out_stage[slot] = dot(inner, w_down[...]).astype(bf16)
        out_copy(i).start()

        @pl.when(i + 2 < width)
        def _():
            for copy in loads(i + 2):
                copy.start()

        scatter.progress(i)
        return carry

    tiles = model // tok

    def column_loads(n):
        slot = lax.rem(n, 2)
        part = pl.ds(pl.multiple_of(n * tok, tok), tok)
        return [
            pltpu.make_async_copy(
                hidden.at[scatter.owner(i), :, part],
                column_in.at[slot, pl.ds(i * tok, tok)],
                column_sems.at[slot, i],
            )
            for i in range(width)
        ]

    def feed_copy(n):
        rows = pl.ds(pl.multiple_of(n * tok, tok), tok)
        slot = lax.rem(n, 2)
        return pltpu.make_async_copy(feed_stage.at[slot], feed_part.at[rows], feed_sem.at[slot])

    def feed_tile(n, carry):
        slot = lax.rem(n, 2)
        for copy in column_loads(n):
            copy.wait()

        @pl.when(n >= 2)
        def _():
            feed_copy(n - 2).wait()

        feed_stage[slot] = dot(column_in[slot], grads[...], 0, 0).astype(bf16)
        feed_copy(n).start()

        @pl.when(n + 2 < tiles)
        def _():
            for copy in column_loads(n + 2):
                copy.start()

        @pl.when(n == 0)
        def _():
            for j in second_half:
                scatter.far(j)

        @pl.when(n == 3)
        def _():
            for j in first_half:
                scatter.far(j)

        return carry

    for n in (0, 1):
        for copy in column_loads(n):
            copy.start()
    lax.fori_loop(0, width, block, 0)
    scatter.arrived(0)
    lax.fori_loop(0, tiles, feed_tile, 0)
    for j in scatter.order:
        scatter.last(j)
    scatter.finish()
    for i in (width - 2, width - 1):
        out_copy(i).wait()
    for n in (tiles - 2, tiles - 1):
        feed_copy(n).wait()


def feed_forward(hidden, cotangent, acts, w_feed, w_down, call, chunks=4):
    width, tok, model = hidden.shape
    units = w_down.shape[0]
    bf16 = jnp.bfloat16
    vmem = pl.BlockSpec(memory_space=pltpu.VMEM)
    return pl.pallas_call(
        functools.partial(feed_kernel, chunks),
        out_shape=[
            jax.ShapeDtypeStruct((width, tok, model), bf16),
            jax.ShapeDtypeStruct((tok, model), jnp.float32),
            jax.ShapeDtypeStruct((model, 2 * units), bf16),
        ],
        in_specs=[ANY, ANY, ANY, vmem, vmem],
        out_specs=[ANY] * 3,
        scratch_shapes=[
            pltpu.VMEM((2, tok, 2 * units), jnp.float32),
            pltpu.VMEM((2, tok, model), bf16),
            pltpu.VMEM((width * tok, 2 * units), bf16),
            pltpu.VMEM((2, width * tok, tok), bf16),
            pltpu.VMEM((2, tok, 2 * units), bf16),
            pltpu.VMEM((2, tok, model), bf16),
            DMA((2, 2)),
            DMA((2, width)),
            DMA((2,)),
            DMA((2,)),
        ]
        + Scatter.scratch(tok, model, chunks),
        compiler_params=pltpu.CompilerParams(
            collective_id=call, has_side_effects=True, vmem_limit_bytes=62 << 20
        ),
    )(hidden, cotangent, acts, w_feed, w_down)


def gradient_kernel(
    chunks, gain, grad_hidden_hbm, middle_hbm, cotangent_hbm, w_out_hbm, mixed_hbm,
    grad_mixed, w_part, grad_middle, term,
    blocks, total, grad_hidden, middle, cotangent, w_out, mixed, chunk_sems, whole_sems, *sems,
):
    f32, bf16 = jnp.float32, jnp.bfloat16
    width, tok, _ = blocks.shape
    me = lax.axis_index(R)
    size = tok // chunks

    def item(j):
        part = pl.ds(j * size, size)
        return blocks.at[me, part], lambda owner: blocks.at[owner, part]

    gather = Gather([item(j) for j in range(chunks)], sems)
    order = [x for j in range(chunks // 2) for x in (j, chunks // 2 + j)]

    def chunk_loads(j):
        part = pl.ds(j * size, size)
        pairs = (grad_hidden_hbm, grad_hidden), (middle_hbm, middle), (cotangent_hbm, cotangent)
        return [
            pltpu.make_async_copy(src.at[part], dst.at[part], chunk_sems.at[j, n])
            for n, (src, dst) in enumerate(pairs)
        ]

    loads = {j: chunk_loads(j) for j in order}
    whole = [
        pltpu.make_async_copy(w_out_hbm, w_out, whole_sems.at[0]),
        pltpu.make_async_copy(mixed_hbm, mixed, whole_sems.at[1]),
    ]
    for j in order:
        for copy in loads[j]:
            copy.start()
    for copy in whole:
        copy.start()
    greet(gather.sibling, gather.x, gather.y)
    terms = jnp.zeros(gain.shape, f32)
    for j in order:
        part = pl.ds(j * size, size)
        for copy in loads[j]:
            copy.wait()
        residual = middle[part, :]
        scale = inverse_rms(residual)
        normed = residual * scale
        grad = grad_hidden[part, :]
        terms = terms + jnp.sum(grad * normed, axis=0, keepdims=True)
        grad = grad * gain[...]
        inner = jnp.mean(grad * normed, axis=1, keepdims=True)
        result = cotangent[part, :].astype(f32) + scale * (grad - normed * inner)
        grad_middle[part, :] = result
        blocks[me, part] = result.astype(bf16)
        gather.start_items((j,))
    term[...] = terms
    for copy in whole:
        copy.wait()

    def block(i, carry):
        @pl.when(i == 1)
        def _():
            gather.from_sibling(3)

        @pl.when(i == 2)
        def _():
            for j in order:
                gather.pass_on(0, j)
                gather.pass_on(1, j)

        @pl.when(i == 3)
        def _():
            gather.from_sibling(4)

        @pl.when(i == 5)
        def _():
            gather.from_sibling(5)

        @pl.when(i == 6)
        def _():
            for j in order:
                gather.pass_on(2, j)

        @pl.when(i == 7)
        def _():
            gather.from_sibling(6)

        rows = pl.ds(pl.multiple_of((me ^ i) * tok, tok), tok)
        grad_mixed[rows, :] = dot(blocks[me ^ i], w_out[...], 1, 1).astype(bf16)
        product = dot(mixed[rows, :], blocks[me ^ i], 0, 0)

        @pl.when(i == 0)
        def _():
            total[...] = product

        @pl.when(i > 0)
        def _():
            total[...] += product

        return carry

    lax.fori_loop(0, width, block, 0)
    w_part[...] = total[...].astype(bf16)
    gather.wait_sends()


def gradient_layer(grad_hidden, middle, cotangent, gain, w_out, mixed, call, chunks=4):
    width = lax.axis_size(R)
    f32, bf16 = jnp.float32, jnp.bfloat16
    tok, model = middle.shape
    vmem = pl.BlockSpec(memory_space=pltpu.VMEM)
    return pl.pallas_call(
        functools.partial(gradient_kernel, chunks),
        out_shape=[
            jax.ShapeDtypeStruct(mixed.shape, bf16),
            jax.ShapeDtypeStruct(w_out.shape, bf16),
            jax.ShapeDtypeStruct((tok, model), f32),
            jax.ShapeDtypeStruct((1, model), f32),
        ],
        in_specs=[vmem] + [ANY] * 5,
        out_specs=[vmem] * 4,
        scratch_shapes=[
            pltpu.VMEM((width, tok, model), bf16),
            pltpu.VMEM(w_out.shape, f32),
            pltpu.VMEM((tok, model), f32),
            pltpu.VMEM((tok, model), f32),
            pltpu.VMEM((tok, model), bf16),
            pltpu.VMEM(w_out.shape, bf16),
            pltpu.VMEM(mixed.shape, bf16),
            DMA((chunks, 3)),
            DMA((2,)),
        ]
        + Gather.scratch(chunks),
        compiler_params=pltpu.CompilerParams(
            collective_id=call, has_side_effects=True, vmem_limit_bytes=60 << 20
        ),
    )(gain, grad_hidden, middle, cotangent, w_out, mixed)


def back_kernel(
    chunks, heads, q, kv, starts, places, grad, mixed, log_total, cosine, sine, hidden, out_part, down_rows, w_part,
    grad_qkv, weight_part, feed_out, all_down, w_rows,
    sums, grad_kv, from_sib, inbox, outbox, to_sib, at_sib, to_line, at_line, down_sem, w_sem,
    to_all, at_all, column_in, weight_stage, column_sems, weight_sem, load_sems, *refs,
):
    f32, bf16 = jnp.float32, jnp.bfloat16
    planes, count, tok = inbox.shape[0], inbox.shape[1], inbox.shape[2]
    width = 2 * count
    columns = heads * HEAD_DIM
    z, me = lax.axis_index(F), lax.axis_index(R)
    core = lax.rem(me, 2)
    above, below = lax.rem(z + 1, planes), lax.rem(z + planes - 1, planes)
    scatter = Scatter(feed_out, chunks, refs[:12])
    gather = Gather(row_items(down_rows, all_down, 1), refs[12:])
    barrier = pltpu.get_barrier_semaphore()
    for other in (above, below):
        pl.semaphore_signal(barrier, inc=1, device_id={F: other}, device_id_type=MESH)
    peers = [me ^ distance for distance in range(1, width)]
    for device in peers:
        pl.semaphore_signal(barrier, inc=1, device_id={R: device}, device_id_type=MESH)
    pl.semaphore_wait(barrier, 1 + width)
    share = w_part.shape[1] // width

    def share_of(device):
        return w_part.at[:, pl.ds(pl.multiple_of(device * share, share), share)]

    w_copies = [
        remote(share_of(device), w_rows.at[me], (to_all, at_all), i, device)
        for i, device in enumerate(peers)
    ]
    w_kept = pltpu.make_async_copy(share_of(me), w_rows.at[me], w_sem)
    for copy in [w_kept] + w_copies:
        copy.start()
    kept = pltpu.make_async_copy(down_rows, all_down.at[me], down_sem)
    kept.start()
    parts = tok // QUERY_BLOCK

    def step(n, carry):
        s, sub = n // parts, lax.rem(n, parts)
        rows = pl.ds(pl.multiple_of(n * QUERY_BLOCK, QUERY_BLOCK), QUERY_BLOCK)
        queries = heads_to_rows(q[rows, :] * bf16(HEAD_DIM**-0.5), heads)
        grads = heads_to_rows(grad[rows, :], heads)
        first = jnp.concatenate([starts[n]] * heads, axis=1)
        place = jnp.concatenate([places[n]] * heads, axis=1)
        products = grads.astype(f32) * heads_to_rows(mixed[rows, :], heads).astype(f32)
        delta = lax.dot_general(
            jnp.ones((8, 2 * HEAD_DIM), f32),
            products,
            (((1,), (1,)), ((), ())),
            precision=lax.Precision.HIGHEST,
            preferred_element_type=f32,
        )[:1]
        level = log_total[n]
        upper = pltpu.roll(grads.astype(f32), HEAD_DIM, 1).astype(bf16)

        @pl.when(sub == 0)
        def _():
            sums[...] = jnp.zeros_like(sums)

        def block(index, acc):
            part = pl.ds(pl.multiple_of(index * KEY_BLOCK, KEY_BLOCK), KEY_BLOCK)
            keys = kv[s, part, :]
            scores = dot(keys, queries, 1, 1)
            probs = jnp.where(visible(index, first, place), jnp.exp(scores - level), 0.0)
            grad_probs = dot(keys, upper, 1, 1)
            grad_scores = (probs * (grad_probs - delta)).astype(bf16)
            sums[part, :] += dot(grad_scores, queries) + dot(probs.astype(bf16), upper)
            return acc + dot(keys, grad_scores, 0, 0)

        place_of_first = z * tok + sub * QUERY_BLOCK
        low = jnp.where(place_of_first >= FIRST_DOC, FIRST_DOC // KEY_BLOCK, 0)
        high = (place_of_first + QUERY_BLOCK - 1) // KEY_BLOCK + 1
        acc = lax.fori_loop(low, high, block, jnp.zeros((2 * HEAD_DIM, queries.shape[0]), f32))
        grad_q = rows_to_heads(acc[:HEAD_DIM] * HEAD_DIM**-0.5, heads)
        c, n_sine = cosine[rows, :], -sine[rows, :]
        for at in range(0, columns, 2 * HEAD_DIM):
            part = slice(at, at + 2 * HEAD_DIM)
            grad_qkv[rows, part] = turn(grad_q[:, part], c, n_sine).astype(bf16)
        grad_qkv[rows, columns:] = jnp.zeros((QUERY_BLOCK, 2 * HEAD_DIM), bf16)

        @pl.when(sub == parts - 1)
        def _():
            grad_kv[s] = sums[...].astype(bf16)

        @pl.when(n == 3)
        def _():
            scatter.taken(3)
            for j in scatter.order:
                scatter.near(j, 1)
            scatter.taken(2)
            for j in scatter.order[: chunks // 2]:
                scatter.near(j, 0)
            scatter.taken(1)
            for j in scatter.order[chunks // 2 :]:
                scatter.near(j, 0)

        @pl.when(n == 11)
        def _():
            gather.relay(0)

        return carry

    scatter.take(out_part, load_sems)
    gather.start()
    lax.fori_loop(0, width * parts, step, 0)

    def block_of(which, b):
        return grad_kv.at[pl.ds(which * count, count), pl.ds(b * tok, tok)]

    def trade(b):
        return remote(block_of(1 - core, b), from_sib.at[b], (to_sib, at_sib), b, gather.sibling)

    def down(b, i):
        return along_line(outbox.at[b, i], inbox.at[b, i], (to_line, at_line), (b, i), below)

    def own(b, i):
        part = pl.ds(b * tok, tok)
        return grad_kv[core * count + i, part, :].astype(f32) + from_sib[b, i].astype(f32)

    for b in range(planes):

        @pl.when(b <= z)
        def _():
            trade(b).start()

    scatter.taken(0)
    for b in range(planes):

        @pl.when(b <= z)
        def _():
            trade(b).wait_recv()

        for i in range(count):

            @pl.when((b <= z) & (z < planes - 1))
            def _():
                down(b, i).wait_recv()

            @pl.when((b < z) & (z < planes - 1))
            def _():
                outbox[b, i] = (own(b, i) + inbox[b, i].astype(f32)).astype(bf16)

            @pl.when((b < z) & (z == planes - 1))
            def _():
                outbox[b, i] = own(b, i).astype(bf16)

            @pl.when(b < z)
            def _():
                down(b, i).start()

        if b == 0:
            for j in scatter.order[: chunks // 2]:
                scatter.far(j)
        if b == 1:
            for j in scatter.order[chunks // 2 :]:
                scatter.far(j)

    def keys(i, carry):
        rows = pl.ds(pl.multiple_of((core * count + i) * tok, tok), tok)
        part = pl.ds(pl.multiple_of(z * tok, tok), tok)
        total = grad_kv[core * count + i, part, :].astype(f32) + from_sib[z, i].astype(f32)
        total = total + jnp.where(z < planes - 1, inbox[z, i].astype(f32), 0.0)
        grad_qkv[rows, columns:] = turn_keys(total, cosine[rows, :], -sine[rows, :]).astype(bf16)
        return carry

    lax.fori_loop(0, count, keys, 0)
    gather.far()
    tiles = hidden.shape[1] // tok

    def column_load(n):
        part = pl.ds(pl.multiple_of(n * tok, tok), tok)
        slot = lax.rem(n, 2)
        return pltpu.make_async_copy(hidden.at[:, part], column_in.at[slot], column_sems.at[slot])

    def weight_copy(n):
        rows = pl.ds(pl.multiple_of(n * tok, tok), tok)
        slot = lax.rem(n, 2)
        return pltpu.make_async_copy(weight_stage.at[slot], weight_part.at[rows], weight_sem.at[slot])

    def weight_tile(n, carry):
        slot = lax.rem(n, 2)
        column_load(n).wait()

        @pl.when(n >= 2)
        def _():
            weight_copy(n - 2).wait()

        weight_stage[slot] = dot(column_in[slot], grad_qkv[...], 0, 0).astype(bf16)
        weight_copy(n).start()

        @pl.when(n + 2 < tiles)
        def _():
            column_load(n + 2).start()

        return carry

    for n in (0, 1):
        column_load(n).start()
    lax.fori_loop(0, tiles, weight_tile, 0)
    for j in scatter.order:
        scatter.last(j)
    scatter.finish()
    for n in (tiles - 2, tiles - 1):
        weight_copy(n).wait()
    for kind in range(3, 7):
        gather.from_sibling(kind)
    gather.wait_sends()
    for b in range(planes):

        @pl.when(b <= z)
        def _():
            trade(b).wait_send()

        @pl.when(b < z)
        def _():
            for i in range(count):
                down(b, i).wait_send()

    for copy in [kept, w_kept] + w_copies:
        copy.wait()


def attention_back(
    heads, q, kv, starts, places, grad, mixed, log_total, cosine, sine, hidden, out_part, down_rows, w_part,
    call, chunks=4,
):
    planes, width = lax.axis_size(F), lax.axis_size(R)
    f32, bf16 = jnp.float32, jnp.bfloat16
    tok, model = hidden.shape[0] // width, hidden.shape[1]
    columns = q.shape[1] + 2 * HEAD_DIM
    length = kv.shape[1]
    vmem = pl.BlockSpec(memory_space=pltpu.VMEM)
    blocks = pltpu.VMEM((planes, width // 2, tok, 2 * HEAD_DIM), bf16)
    return pl.pallas_call(
        functools.partial(back_kernel, chunks, heads),
        out_shape=[
            jax.ShapeDtypeStruct((q.shape[0], columns), bf16),
            jax.ShapeDtypeStruct((model, columns), bf16),
            jax.ShapeDtypeStruct((tok, model), f32),
            jax.ShapeDtypeStruct((width,) + down_rows.shape, bf16),
            jax.ShapeDtypeStruct((width, w_part.shape[0], w_part.shape[1] // width), bf16),
        ],
        in_specs=[vmem] * 9 + [ANY] * 4,
        out_specs=[vmem] + [ANY] * 4,
        scratch_shapes=[
            pltpu.VMEM((length, 2 * HEAD_DIM), f32),
            pltpu.VMEM((width, length, 2 * HEAD_DIM), bf16),
            blocks,
            blocks,
            blocks,
        ]
        + [DMA((planes,))] * 2
        + [DMA((planes, width // 2))] * 2
        + [DMA, DMA, DMA((width - 1,)), DMA((width - 1,))]
        + [pltpu.VMEM((2, width * tok, tok), bf16), pltpu.VMEM((2, tok, columns), bf16)]
        + [DMA((2,)), DMA((2,)), DMA((4,))]
        + Scatter.scratch(tok, model, chunks)
        + Gather.scratch(1),
        compiler_params=pltpu.CompilerParams(
            collective_id=call, has_side_effects=True, vmem_limit_bytes=60 << 20
        ),
    )(q, kv, starts, places, grad, mixed, log_total, cosine, sine, hidden, out_part, down_rows, w_part)


def hidden_kernel(chunks, grad_qkv, weight, feed_rows, grad_hidden, all_feed, feed_sem, *refs):
    bf16 = jnp.bfloat16
    scatter = Scatter(grad_hidden, chunks, refs[:12])
    gather = Gather(row_items(feed_rows, all_feed, chunks), refs[12:])
    tok = grad_hidden.shape[0]
    columns = grad_qkv.shape[1]
    greet(scatter.sibling, scatter.x, scatter.y)
    kept = pltpu.make_async_copy(feed_rows, all_feed.at[scatter.me], feed_sem)
    kept.start()
    gather.start()

    def block(i, carry):
        rows = pl.ds(pl.multiple_of(scatter.owner(i) * tok, tok), tok)
        scatter.put(i, dot(grad_qkv[rows, :], weight[:, :columns], 1, 1).astype(bf16))
        scatter.progress(i)
        return carry

    lax.fori_loop(0, grad_qkv.shape[0] // tok, block, 0)
    scatter.arrived(0)
    for i in range(chunks):
        gather.relay(i)
    for j in scatter.order:
        scatter.far(j)
    gather.finish()
    for j in scatter.order:
        scatter.last(j)
    scatter.finish()
    kept.wait()


def scatter_hidden(grad_qkv, weight, feed_rows, tok, call, chunks=4):
    width, model = lax.axis_size(R), weight.shape[0]
    vmem = pl.BlockSpec(memory_space=pltpu.VMEM)
    return pl.pallas_call(
        functools.partial(hidden_kernel, chunks),
        out_shape=[
            jax.ShapeDtypeStruct((tok, model), jnp.float32),
            jax.ShapeDtypeStruct((width,) + feed_rows.shape, jnp.bfloat16),
        ],
        in_specs=[vmem, vmem, ANY],
        out_specs=[ANY, ANY],
        scratch_shapes=[DMA] + Scatter.scratch(tok, model, chunks) + Gather.scratch(chunks),
        compiler_params=pltpu.CompilerParams(
            collective_id=call, has_side_effects=True, vmem_limit_bytes=40 << 20
        ),
    )(grad_qkv, weight, feed_rows)


def enter(tokens, gains, ids, call, chunks=4):
    planes, rows = lax.axis_size(F), lax.axis_size(R)
    tok, model = tokens.shape
    vmem = pl.BlockSpec(memory_space=pltpu.VMEM)
    return pl.pallas_call(
        functools.partial(enter_kernel, chunks),
        out_shape=[
            jax.ShapeDtypeStruct((rows, tok, model), jnp.bfloat16),
            jax.ShapeDtypeStruct((planes,) + gains.shape, jnp.float32),
            jax.ShapeDtypeStruct((rows,) + ids.shape, jnp.int32),
        ],
        in_specs=[vmem] * 3,
        out_specs=[ANY, vmem, vmem],
        scratch_shapes=[pltpu.VMEM((tok, model), jnp.bfloat16), DMA]
        + [DMA((planes - 1,))] * 2
        + Gather.scratch(chunks + 1),
        compiler_params=pltpu.CompilerParams(
            collective_id=call, has_side_effects=True, vmem_limit_bytes=32 << 20
        ),
    )(tokens, gains, ids)


def project(hidden, weight, cosine, sine, cotangent, query_width, call, chunks=4):
    planes, width = lax.axis_size(F), lax.axis_size(R)
    tok, model = cotangent.shape
    bf16 = jnp.bfloat16
    vmem = pl.BlockSpec(memory_space=pltpu.VMEM)
    return pl.pallas_call(
        functools.partial(project_kernel, chunks),
        out_shape=[
            jax.ShapeDtypeStruct((width * tok, query_width), bf16),
            jax.ShapeDtypeStruct((width, planes, tok, 2 * HEAD_DIM), bf16),
            jax.ShapeDtypeStruct((width, tok, model), bf16),
            jax.ShapeDtypeStruct((model // width, model), bf16),
        ],
        in_specs=[ANY] + [vmem] * 3 + [ANY, ANY],
        out_specs=[vmem, ANY, ANY, ANY],
        scratch_shapes=[
            pltpu.VMEM((width, tok, 2 * HEAD_DIM), bf16),
            pltpu.VMEM((2, tok, model), bf16),
            DMA((2,)),
            DMA,
            DMA,
            DMA,
            DMA((width - 1,)),
            DMA((width - 1,)),
        ]
        + [DMA((planes, width // 2))] * 2
        + [DMA((planes,))] * 2
        + Gather.scratch(chunks),
        compiler_params=pltpu.CompilerParams(
            collective_id=call, has_side_effects=True, vmem_limit_bytes=40 << 20
        ),
    )(hidden, weight, cosine, sine, cotangent, weight)


def scatter_kernel(
    chunks, part, out, own, from_sib, give, got, give_far, got_far, total,
    own_sem, out_sem, to_sib, at_sib, to_near, at_near, to_far, at_far,
):
    f32, bf16 = jnp.float32, jnp.bfloat16
    me = lax.axis_index(R)
    flip = 1 - 2 * lax.rem(me, 2)
    sibling, beside_x, beside_y = me + flip, me ^ 2, me ^ 4
    rows = out.shape[0]
    size = rows // chunks
    half = chunks // 2
    owners = [me, beside_x, beside_y, me ^ 6]
    order = [c for j in range(half) for c in (j, half + j)]

    def rows_of(device, j):
        return part.at[pl.ds(pl.multiple_of(device * rows + j * size, 16), size)]

    def own_copy(d, j):
        return pltpu.make_async_copy(rows_of(owners[d], j), own.at[d, j], own_sem.at[d, j])

    def sib_copy(d, j):
        return remote(rows_of(owners[d] + flip, j), from_sib.at[d, j], (to_sib, at_sib), (d, j), sibling)

    def near_copy(j):
        device = beside_x if j < half else beside_y
        return remote(give.at[j], got.at[j], (to_near, at_near), j, device)

    def far_copy(j):
        device = beside_y if j < half else beside_x
        return remote(give_far.at[j], got_far.at[j], (to_far, at_far), j, device)

    def out_copy(j):
        return pltpu.make_async_copy(total.at[j], out.at[pl.ds(j * size, size)], out_sem.at[j])

    def summed(d, j):
        own_copy(d, j).wait()
        sib_copy(d, j).wait_recv()
        return own[d, j].astype(f32) + from_sib[d, j].astype(f32)

    for j in order:
        for d in (1, 2, 3, 0):
            own_copy(d, j).start()
    greet(sibling, beside_x, beside_y)
    for j in order:
        for d in (1, 3, 2, 0) if j < half else (2, 3, 1, 0):
            sib_copy(d, j).start()
    for j in order:
        give[j, 0] = summed(1 if j < half else 2, j).astype(bf16)
        give[j, 1] = summed(3, j).astype(bf16)
        near_copy(j).start()
    for j in order:
        passed = summed(2 if j < half else 1, j)
        kept = summed(0, j)
        near_copy(j).wait_recv()
        give_far[j] = (passed + got[j, 1].astype(f32)).astype(bf16)
        far_copy(j).start()
        total[j] = kept + got[j, 0].astype(f32)
    for j in order:
        far_copy(j).wait_recv()
        total[j] = total[j] + got_far[j].astype(f32)
        out_copy(j).start()
    for j in order:
        out_copy(j).wait()
        near_copy(j).wait_send()
        far_copy(j).wait_send()
        for d in range(4):
            sib_copy(d, j).wait_send()


def plane_gather(x, call, chunks=4):
    width = lax.axis_size(R)
    if width != 8:
        return lax.all_gather(x, R, axis=0, tiled=True)
    out = pl.pallas_call(
        functools.partial(gather_kernel, chunks),
        out_shape=jax.ShapeDtypeStruct((width,) + x.shape, x.dtype),
        in_specs=[ANY],
        out_specs=ANY,
        scratch_shapes=[DMA] + Gather.scratch(chunks),
        compiler_params=pltpu.CompilerParams(collective_id=call, has_side_effects=True),
    )(x)
    return out.reshape((width * x.shape[0],) + x.shape[1:])


def plane_scatter(x, call, chunks=4):
    width = lax.axis_size(R)
    if width != 8:
        return lax.psum_scatter(x, R, scatter_dimension=0, tiled=True).astype(jnp.float32)
    rows, columns = x.shape[0] // width, x.shape[1]
    size = rows // chunks
    bf16 = jnp.bfloat16
    return pl.pallas_call(
        functools.partial(scatter_kernel, chunks),
        out_shape=jax.ShapeDtypeStruct((rows, columns), jnp.float32),
        in_specs=[ANY],
        out_specs=ANY,
        scratch_shapes=[
            pltpu.VMEM((4, chunks, size, columns), bf16),
            pltpu.VMEM((4, chunks, size, columns), bf16),
            pltpu.VMEM((chunks, 2, size, columns), bf16),
            pltpu.VMEM((chunks, 2, size, columns), bf16),
            pltpu.VMEM((chunks, size, columns), bf16),
            pltpu.VMEM((chunks, size, columns), bf16),
            pltpu.VMEM((chunks, size, columns), jnp.float32),
            DMA((4, chunks)),
            DMA((chunks,)),
            DMA((4, chunks)),
            DMA((4, chunks)),
        ]
        + [DMA((chunks,))] * 4,
        compiler_params=pltpu.CompilerParams(
            collective_id=call, has_side_effects=True, vmem_limit_bytes=32 << 20
        ),
    )(x)


def line_gather(x):
    return lax.all_gather(x, F, axis=0, tiled=True)


def line_scatter(x):
    return lax.psum_scatter(x, F, scatter_dimension=0, tiled=True)


def heads_to_rows(block, heads):
    parts = [block[:, h * HEAD_DIM : (h + 1) * HEAD_DIM] for h in range(heads)]
    rows = jnp.concatenate(parts, axis=0)
    return jnp.concatenate([rows, jnp.zeros_like(rows)], axis=1)


def rows_to_heads(columns, heads):
    count = columns.shape[1] // heads
    return jnp.concatenate([columns[:, h * count : (h + 1) * count].T for h in range(heads)], axis=1)


def visible(block_index, starts, places):
    keys = block_index * KEY_BLOCK + lax.broadcasted_iota(jnp.int32, (KEY_BLOCK, starts.shape[1]), 0)
    return (keys >= starts) & (keys <= places)


def attention_kernel(heads, low, high, q, kv, starts, places, mixed, log_total):
    f32, bf16 = jnp.float32, jnp.bfloat16
    step = pl.program_id(0) * pl.num_programs(1) + pl.program_id(1)
    queries = heads_to_rows(q[...] * bf16(HEAD_DIM**-0.5), heads)
    first = jnp.concatenate([starts[0]] * heads, axis=1)
    place = jnp.concatenate([places[0]] * heads, axis=1)
    columns = queries.shape[0]

    def block(index, carry):
        top, total, acc = carry
        rows = kv[0, pl.ds(pl.multiple_of(index * KEY_BLOCK, KEY_BLOCK), KEY_BLOCK), :]
        scores = jnp.where(visible(index, first, place), dot(rows, queries, 1, 1), NEGATIVE)
        new_top = jnp.maximum(top, jnp.max(scores, axis=0, keepdims=True))
        weights = jnp.exp(scores - new_top)
        fade = jnp.exp(top - new_top)
        total = total * fade + jnp.sum(weights, axis=0, keepdims=True)
        acc = acc * fade + dot(rows, weights.astype(bf16), 0, 0)
        return new_top, total, acc

    top, total, acc = lax.fori_loop(
        low[step],
        high[step],
        block,
        (
            jnp.full((1, columns), NEGATIVE, f32),
            jnp.zeros((1, columns), f32),
            jnp.zeros((2 * HEAD_DIM, columns), f32),
        ),
    )
    mixed[...] = rows_to_heads(acc[HEAD_DIM:] / total, heads).astype(bf16)
    log_total[0] = top + jnp.log(total)


def attention_back_kernel(
    heads, low, high, q, kv, starts, places, grad, mixed, log_total, grad_q, grad_kv, sums
):
    f32, bf16 = jnp.float32, jnp.bfloat16
    step = pl.program_id(0) * pl.num_programs(1) + pl.program_id(1)
    queries = heads_to_rows(q[...] * bf16(HEAD_DIM**-0.5), heads)
    grads = heads_to_rows(grad[...], heads)
    first = jnp.concatenate([starts[0]] * heads, axis=1)
    place = jnp.concatenate([places[0]] * heads, axis=1)
    columns = queries.shape[0]
    products = grads.astype(f32) * heads_to_rows(mixed[...], heads).astype(f32)
    delta = lax.dot_general(
        jnp.ones((8, 2 * HEAD_DIM), f32),
        products,
        (((1,), (1,)), ((), ())),
        precision=lax.Precision.HIGHEST,
        preferred_element_type=f32,
    )[:1]
    level = log_total[0]
    upper = pltpu.roll(grads.astype(f32), HEAD_DIM, 1).astype(bf16)

    @pl.when(pl.program_id(1) == 0)
    def _():
        sums[...] = jnp.zeros_like(sums)

    def block(index, acc):
        part = pl.ds(pl.multiple_of(index * KEY_BLOCK, KEY_BLOCK), KEY_BLOCK)
        rows = kv[0, part, :]
        scores = dot(rows, queries, 1, 1)
        probs = jnp.where(visible(index, first, place), jnp.exp(scores - level), 0.0)
        grad_probs = dot(rows, upper, 1, 1)
        grad_scores = (probs * (grad_probs - delta)).astype(bf16)
        sums[part, :] += dot(grad_scores, queries) + dot(probs.astype(bf16), upper)
        return acc + dot(rows, grad_scores, 0, 0)

    acc = lax.fori_loop(low[step], high[step], block, jnp.zeros((2 * HEAD_DIM, columns), f32))
    grad_q[...] = rows_to_heads(acc[:HEAD_DIM] * HEAD_DIM**-0.5, heads)

    @pl.when(pl.program_id(1) == PARTS - 1)
    def _():
        grad_kv[0] = sums[...].astype(bf16)


def attention_call(kernel, heads, low, high, arrays, outs, scratch=()):
    blocks = {
        "tokens": lambda shape: pl.BlockSpec((QUERY_BLOCK, shape[1]), lambda s, b, *_: (s * PARTS + b, 0)),
        "row": lambda shape: pl.BlockSpec((1,) + shape[1:], lambda s, b, *_: (s * PARTS + b, 0, 0)),
        "sequence": lambda shape: pl.BlockSpec((1,) + shape[1:], lambda s, b, *_: (s, 0, 0)),
    }
    return pl.pallas_call(
        functools.partial(kernel, heads),
        grid_spec=pltpu.PrefetchScalarGridSpec(
            num_scalar_prefetch=2,
            grid=(low.shape[0] // PARTS, PARTS),
            in_specs=[blocks[kind](x.shape) for kind, x in arrays],
            out_specs=[blocks[kind](x.shape) for kind, x in outs],
            scratch_shapes=scratch,
        ),
        out_shape=[x for _, x in outs],
        compiler_params=pltpu.CompilerParams(vmem_limit_bytes=32 << 20),
    )(low, high, *[x for _, x in arrays])


def join_feed_kernel(planes, piece, x, gate, up):
    width = x.shape[0]
    for kind, out in enumerate((gate, up)):
        for p in range(planes):
            for r in range(width):
                first = (kind * planes + p) * piece
                to = (p * width + r) * piece
                out[:, to : to + piece] = x[r, :, first : first + piece].astype(jnp.float32)


def join_attention_kernel(sharers, qkv, o, query, key, value, out):
    f32 = jnp.float32
    width, qw, ow = qkv.shape[0], qkv.shape[2] - 2 * HEAD_DIM, o.shape[2]
    for r in range(width):
        query[:, r * qw : (r + 1) * qw] = qkv[r, :, :qw].astype(f32)
        out[:, r * ow : (r + 1) * ow] = o[r].astype(f32)
    for head in range(width // sharers):
        both = sum(qkv[head * sharers + i, :, qw:].astype(f32) for i in range(sharers))
        to = slice(head * HEAD_DIM, (head + 1) * HEAD_DIM)
        key[:, to] = both[:, :HEAD_DIM]
        value[:, to] = both[:, HEAD_DIM:]


def widen_kernel(x, out):
    out[...] = x[0].astype(jnp.float32)


def widen(x):
    count, rows, columns = x.shape
    return pl.pallas_call(
        widen_kernel,
        grid=(count,),
        in_specs=[pl.BlockSpec((1, rows, columns), lambda i: (i, 0, 0))],
        out_specs=pl.BlockSpec((rows, columns), lambda i: (i, 0)),
        out_shape=jax.ShapeDtypeStruct((count * rows, columns), jnp.float32),
        compiler_params=pltpu.CompilerParams(vmem_limit_bytes=60 << 20),
    )(x)


def join_call(kernel, arrays, outs, block=64):
    rows = arrays[0].shape[1]
    return pl.pallas_call(
        kernel,
        grid=(rows // block,),
        in_specs=[pl.BlockSpec((x.shape[0], block, x.shape[2]), lambda i: (0, i, 0)) for x in arrays],
        out_specs=[pl.BlockSpec((block, columns), lambda i: (i, 0)) for columns in outs],
        out_shape=[jax.ShapeDtypeStruct((rows, columns), jnp.float32) for columns in outs],
        compiler_params=pltpu.CompilerParams(vmem_limit_bytes=32 << 20),
    )(*arrays)


def per_device(
    tokens,
    segment_ids,
    attention_gain,
    query_weight,
    key_weight,
    value_weight,
    output_weight,
    feed_gain,
    gate_weight,
    up_weight,
    down_weight,
    cotangent,
):
    f32, bf16 = jnp.float32, jnp.bfloat16
    planes, width = lax.axis_size(F), lax.axis_size(R)
    r, z = lax.axis_index(R), lax.axis_index(F)
    tok, model = tokens.shape
    length = segment_ids.shape[1]
    all_tok = width * tok
    plane_kernels = width == 8
    heads = HEADS // width
    group = HEADS // KV_HEADS
    qw = heads * HEAD_DIM
    kv = (r * heads) // group
    feed = gate_weight.shape[1]
    piece = feed // (width * planes)
    hidden_units = piece * planes

    def cols(weight, first, count):
        return lax.dynamic_slice_in_dim(weight, first, count, 1)

    def feed_cols(weight):
        return [cols(weight, p * (feed // planes) + r * piece, piece) for p in range(planes)]

    w_attention = line_gather(
        jnp.concatenate(
            [
                cols(query_weight, r * qw, qw),
                cols(key_weight, kv * HEAD_DIM, HEAD_DIM),
                cols(value_weight, kv * HEAD_DIM, HEAD_DIM),
                cols(output_weight, r * (model // width), model // width),
            ],
            axis=1,
        )
    )
    w_qkv = w_attention[:, : qw + 2 * HEAD_DIM]
    own_gains = jnp.stack([attention_gain, feed_gain]).astype(f32)
    tok_float = tokens.astype(f32)
    scale_in = inverse_rms(tok_float)
    normed_in = tok_float * scale_in
    if plane_kernels:
        hidden_in, gains, ids = enter(
            tokens, jnp.pad(own_gains, ((0, 6), (0, 0))), segment_ids.reshape(8, length // 8), 0
        )
        hidden_in = hidden_in.reshape(all_tok, model)
        gains = gains[:, :2].transpose(1, 0, 2).reshape(2, model)
        ids = ids.reshape(width, length)
    else:
        gains = lax.all_gather(own_gains, F, axis=1, tiled=True)
        hidden_in = lax.all_gather((normed_in * gains[0]).astype(bf16), R, axis=0, tiled=True)
        ids = lax.all_gather(segment_ids, R, axis=0, tiled=True)
    gain_in, gain_mid = gains[0], gains[1]
    gate_weight, up_weight, down_weight, ids = lax.optimization_barrier(
        (gate_weight, up_weight, down_weight, ids)
    )
    w_feed = line_gather(jnp.concatenate(feed_cols(gate_weight) + feed_cols(up_weight), axis=1))
    w_down = line_gather(lax.dynamic_slice_in_dim(down_weight, r * piece, piece, 0))

    places = jnp.arange(length, dtype=jnp.int32)
    fresh = jnp.concatenate(
        [jnp.ones((width, 1), dtype=jnp.bool_), ids[:, 1:] != ids[:, :-1]], axis=1
    )
    positions = places[None] - lax.cummax(jnp.where(fresh, places[None], 0), axis=1)
    own_positions = lax.dynamic_slice_in_dim(positions, z * tok, tok, 1).reshape(all_tok)
    own_places = z * tok + jnp.arange(all_tok, dtype=jnp.int32) % tok
    own_starts = own_places - own_positions
    steps = all_tok // QUERY_BLOCK
    starts = own_starts.reshape(steps, 1, QUERY_BLOCK)
    query_places = own_places.reshape(steps, 1, QUERY_BLOCK)
    low = starts[:, 0, 0] // KEY_BLOCK
    high = query_places[:, 0, QUERY_BLOCK - 1] // KEY_BLOCK + 1

    if plane_kernels:
        wide_cosine, wide_sine = rope_tables(own_positions, 4)
        wide_sine = wide_sine * jnp.where(jnp.arange(2 * HEAD_DIM) // (HEAD_DIM // 2) % 2, 1.0, -1.0)
        query, kv_rows, cot_all, w_out = project(
            hidden_in.reshape(width, tok, model),
            w_attention,
            wide_cosine,
            wide_sine,
            cotangent,
            qw,
            3,
        )
        kv_rows = kv_rows.reshape(width, length, 2 * HEAD_DIM)
        cot_all = cot_all.reshape(all_tok, model)
    else:
        cosine, sine = rope_tables(own_positions)
        qkv = dot(hidden_in, w_qkv)
        query = rotate(qkv[:, :qw].reshape(all_tok, heads, HEAD_DIM), cosine, sine, 1.0)
        query = query.astype(bf16).reshape(all_tok, qw)
        key = rotate(qkv[:, None, qw : qw + HEAD_DIM], cosine, sine, 1.0).astype(bf16)[:, 0]
        value = qkv[:, qw + HEAD_DIM :].astype(bf16)
        kv_rows = (
            lax.all_gather(jnp.concatenate([key, value], axis=1), F, axis=0, tiled=False)
            .reshape(planes, width, tok, 2 * HEAD_DIM)
            .transpose(1, 0, 2, 3)
            .reshape(width, length, 2 * HEAD_DIM)
        )
        cot_all = lax.all_gather(cotangent, R, axis=0, tiled=True)
        w_out = lax.all_to_all(
            w_attention[:, qw + 2 * HEAD_DIM :], R, split_axis=0, concat_axis=1, tiled=True
        )
    common = [("tokens", query), ("sequence", kv_rows), ("row", starts), ("row", query_places)]
    mixed, log_totals = attention_call(
        attention_kernel,
        heads,
        low,
        high,
        common,
        [
            ("tokens", jax.ShapeDtypeStruct((all_tok, qw), bf16)),
            ("row", jax.ShapeDtypeStruct((steps, 1, heads * QUERY_BLOCK), f32)),
        ],
    )
    if plane_kernels:
        cot_blocks = cot_all.reshape(width, tok, model)
        middle = branch_layer(mixed, w_out, tokens, 1)
        hidden_blocks, acts, down_part = middle_layer(middle, gain_mid[None], w_feed, cot_blocks, 2)
    else:
        middle = tok_float + plane_scatter(dot(mixed, w_out).astype(bf16), 1)

    if plane_kernels:
        out_part, grad_hidden_mid, feed_part = feed_forward(
            hidden_blocks, cot_blocks, acts, w_feed, w_down, 5
        )
    else:
        w_gate, w_up = w_feed[:, :hidden_units], w_feed[:, hidden_units:]
        scale_mid = inverse_rms(middle)
        normed_mid = middle * scale_mid
        hidden_mid = plane_gather((normed_mid * gain_mid).astype(bf16), 2)
        gate_acc = dot(hidden_mid, w_gate)
        up_acc = dot(hidden_mid, w_up)
        gate_sig = jax.nn.sigmoid(gate_acc)
        gate_silu = gate_acc * gate_sig
        inner_act = (gate_silu * up_acc).astype(bf16)
        out_part = dot(inner_act, w_down).astype(bf16)
        grad_inner = dot(cot_all, w_down, 1, 1)
        grad_gate = grad_inner * up_acc * gate_sig * (1.0 + gate_acc * (1.0 - gate_sig))
        grad_gate = grad_gate.astype(bf16)
        grad_up = (grad_inner * gate_silu).astype(bf16)
        feed_part = jnp.concatenate(
            [dot(hidden_mid, grad_gate, 0, 0), dot(hidden_mid, grad_up, 0, 0)], axis=1
        ).astype(bf16)
        down_part = dot(inner_act, cot_all, 0, 0).astype(bf16)
        grad_hidden_part = dot(grad_gate, w_gate, 1, 1) + dot(grad_up, w_up, 1, 1)
        grad_hidden_mid = plane_scatter(grad_hidden_part.astype(bf16), 5)
        feed_out = plane_scatter(out_part, 4)
    down_rows = line_scatter(down_part)
    feed_rows = line_scatter(feed_part)
    if plane_kernels:
        grad_mixed, w_out_part, grad_middle, gain_mid_term = gradient_layer(
            grad_hidden_mid, middle, cotangent, gain_mid[None], w_out, mixed, 6
        )
        gain_mid_term = gain_mid_term[0]
    else:
        gain_mid_term = jnp.sum(grad_hidden_mid * normed_mid, axis=0)
        grad_normed_mid = grad_hidden_mid * gain_mid
        inner = jnp.mean(grad_normed_mid * normed_mid, axis=1, keepdims=True)
        grad_middle = cotangent.astype(f32) + scale_mid * (grad_normed_mid - normed_mid * inner)
        grad_branch = plane_gather(grad_middle.astype(bf16), 6)
        grad_mixed = dot(grad_branch, w_out, 1, 1).astype(bf16)
        w_out_part = dot(mixed, grad_branch, 0, 0).astype(bf16)

    if plane_kernels:
        grad_qkv, qkv_part, feed_out, down_all, w_out_part = attention_back(
            heads,
            query,
            kv_rows,
            starts,
            query_places,
            grad_mixed,
            mixed,
            log_totals,
            wide_cosine,
            wide_sine,
            hidden_in,
            out_part,
            down_rows,
            w_out_part,
            10,
        )
        w_out_part = w_out_part.reshape(width * qw, model // width)
    else:
        gq, gkv = attention_call(
            attention_back_kernel,
            heads,
            low,
            high,
            common + [("tokens", grad_mixed), ("tokens", mixed), ("row", log_totals)],
            [
                ("tokens", jax.ShapeDtypeStruct((all_tok, qw), f32)),
                ("sequence", jax.ShapeDtypeStruct((width, length, 2 * HEAD_DIM), bf16)),
            ],
            [pltpu.VMEM((length, 2 * HEAD_DIM), f32)],
        )
        gkv = gkv.reshape(width, planes, tok, 2 * HEAD_DIM).transpose(1, 0, 2, 3)
        gkv = line_scatter(gkv.reshape(planes * all_tok, 2 * HEAD_DIM)).astype(f32)
        gq = rotate(gq.reshape(all_tok, heads, HEAD_DIM), cosine, sine, -1.0)
        gk = rotate(gkv[:, None, :HEAD_DIM], cosine, sine, -1.0)[:, 0]
        grad_qkv = jnp.concatenate([gq.reshape(all_tok, qw), gk, gkv[:, HEAD_DIM:]], axis=1)
        grad_qkv = grad_qkv.astype(bf16)
        qkv_part = dot(hidden_in, grad_qkv, 0, 0).astype(bf16)
        down_all = lax.all_gather(down_rows, R, axis=0, tiled=True)
        w_out_part = lax.all_to_all(w_out_part, R, split_axis=1, concat_axis=0, tiled=True)
    out_rows = line_scatter(w_out_part)
    activations = (middle + feed_out).astype(bf16)
    grad_qkv, qkv_part, feed_rows = lax.optimization_barrier((grad_qkv, qkv_part, feed_rows))
    qkv_rows = line_scatter(qkv_part)
    if plane_kernels:
        grad_hidden_in, feed_all = scatter_hidden(grad_qkv, w_attention, feed_rows, tok, 7)
    else:
        grad_hidden_in = plane_scatter(dot(grad_qkv, w_qkv, 1, 1).astype(bf16), 7)
        feed_all = lax.all_gather(feed_rows, R, axis=0, tiled=False)
    gain_in_term = jnp.sum(grad_hidden_in * normed_in, axis=0)
    grad_normed_in = grad_hidden_in * gain_in
    input_grad = (
        grad_middle
        + scale_in
        * (
            grad_normed_in
            - normed_in * jnp.mean(grad_normed_in * normed_in, axis=1, keepdims=True)
        )
    ).astype(bf16)

    rows = model // planes
    terms = jnp.stack([gain_in_term, gain_mid_term])
    if plane_kernels:
        terms = jnp.pad(terms.reshape(2, planes, rows).transpose(1, 0, 2), ((0, 0), (0, 6), (0, 0)))
        qkv_all, out_all, gain_terms = finish(qkv_rows, out_rows, terms, 9)
    else:
        qkv_all = lax.all_gather(qkv_rows, R, axis=0, tiled=False)
        out_all = lax.all_gather(out_rows, R, axis=0, tiled=False)
        gain_terms = lax.psum(lax.psum_scatter(terms, F, scatter_dimension=1, tiled=True), R)
    if plane_kernels:
        down_grad = widen(down_all)
    else:
        down_grad = down_all.reshape(feed // planes, model).astype(f32)
    gate_grad, up_grad = join_call(
        functools.partial(join_feed_kernel, planes, piece), [feed_all], [feed, feed]
    )
    query_grad, key_grad, value_grad, out_grad = join_call(
        functools.partial(join_attention_kernel, width // KV_HEADS),
        [qkv_all, out_all],
        [width * qw, KV_HEADS * HEAD_DIM, KV_HEADS * HEAD_DIM, model],
    )
    return (
        activations,
        input_grad,
        gain_terms[0],
        query_grad,
        key_grad,
        value_grad,
        out_grad,
        gain_terms[1],
        gate_grad,
        up_grad,
        down_grad,
    )


def solution(mesh):
    tok = P((R, F), None)
    row = P(F, None)
    in_specs = (tok, P(R, None), P(F), row, row, row, row, P(F), row, row, row, tok)
    out_specs = (tok, tok, P(F), row, row, row, row, P(F), row, row, row)
    return jax.shard_map(
        per_device, mesh=mesh, in_specs=in_specs, out_specs=out_specs, check_vma=False
    )
```

```python
import functools
import math

import jax
import jax.numpy as jnp
from jax import lax
from jax.experimental import pallas as pl
from jax.experimental.pallas import tpu as pltpu
from jax.sharding import PartitionSpec as P

HEADS = 32
KV_HEADS = 4
HEAD_DIM = 64
EPSILON = 1e-05
NEGATIVE = -1e30
R = "replica"
F = "fsdp"
MESH = pl.DeviceIdType.MESH
DMA = pltpu.SemaphoreType.DMA
ANY = pl.BlockSpec(memory_space=pl.ANY)
KEY_BLOCK = 256
QUERY_BLOCK = 128
PARTS = 2
FIRST_DOC = 800


def inverse_rms(values):
    return lax.rsqrt(jnp.mean(values * values, axis=1, keepdims=True) + EPSILON)


def rope_tables(positions, repeats=1):
    half_dim = HEAD_DIM // 2
    places = jnp.arange(repeats * half_dim, dtype=jnp.int32) % half_dim
    freq_rates = jnp.exp(places.astype(jnp.float32) * (-math.log(10000.0) / half_dim))
    angles = positions.astype(jnp.float32)[:, None] * freq_rates[None, :]
    return (jnp.cos(angles), jnp.sin(angles))


def rotate(tensor, cosine_table, sine_table, sign):
    half_dim = HEAD_DIM // 2
    low, up = tensor[..., :half_dim], tensor[..., half_dim:]
    cos_part = cosine_table[:, None, :]
    sin_part = sine_table[:, None, :] * sign
    return jnp.concatenate(
        [low * cos_part - up * sin_part, up * cos_part + low * sin_part], axis=-1
    )


def dot(a, b, ca=1, cb=0):
    return lax.dot_general(a, b, (((ca,), (cb,)), ((), ())), preferred_element_type=jnp.float32)


def remote(src, dst, sems, index, device):
    return pltpu.make_async_remote_copy(
        src_ref=src,
        dst_ref=dst,
        send_sem=sems[0].at[index],
        recv_sem=sems[1].at[index],
        device_id={R: device},
        device_id_type=MESH,
    )


def greet(*devices):
    barrier = pltpu.get_barrier_semaphore()
    for device in devices:
        pl.semaphore_signal(barrier, inc=1, device_id={R: device}, device_id_type=MESH)
    pl.semaphore_wait(barrier, len(devices))


class Gather:
    @staticmethod
    def scratch(count):
        return [DMA((count,))] * 6 + [DMA((4, count))] * 2

    def __init__(self, items, sems):
        self.items, self.count = items, len(items)
        self.half = self.count // 2
        self.me = lax.axis_index(R)
        self.sibling, self.x, self.y = self.me + 1 - 2 * lax.rem(self.me, 2), self.me ^ 2, self.me ^ 4
        self.sems = sems

    def copy(self, kind, i):
        first = i < self.half
        owner, device = {
            0: (self.me, self.x),
            1: (self.me, self.y),
            2: (self.x, self.y) if first else (self.y, self.x),
            3: (self.me, self.sibling),
            4: (self.x, self.sibling),
            5: (self.y, self.sibling),
            6: (self.me ^ 6, self.sibling),
        }[kind]
        own, slot = self.items[i]
        sems = self.sems[2 * min(kind, 3) : 2 * min(kind, 3) + 2]
        src = own if kind in (0, 1, 3) else slot(owner)
        return remote(src, slot(owner), sems, i if kind < 3 else (kind - 3, i), device)

    def start(self, kept=()):
        ready = [i for i in range(self.count) if i not in kept]
        for n, i in enumerate(ready):
            self.copy(0, i).start()
            self.copy(1, ready[(n + self.half) % len(ready)]).start()
        for i in ready:
            self.copy(3, i).start()

    def start_items(self, items):
        for i in items:
            for kind in (0, 1, 3):
                self.copy(kind, i).start()

    def pass_on(self, kind, i):
        self.copy(kind, i).wait_recv()
        if kind < 2 and (i < self.half) == (kind == 0):
            self.copy(2, i).start()
        self.copy(kind + 4, i).start()

    def relay(self, i):
        self.pass_on(0, i)
        self.pass_on(1, (i + self.half) % self.count)

    def far(self):
        for i in range(self.half):
            self.pass_on(2, i)
            self.pass_on(2, self.half + i)
        for i in range(2 * self.half, self.count):
            self.pass_on(2, i)

    def from_sibling(self, kind):
        for i in range(self.count):
            self.copy(kind, i).wait_recv()

    def wait_sends(self):
        for i in range(self.count):
            for kind in range(7):
                self.copy(kind, i).wait_send()

    def finish(self):
        self.far()
        for kind in range(3, 7):
            self.from_sibling(kind)
        self.wait_sends()


def row_items(x, out, chunks):
    size = x.shape[0] // chunks

    def item(i):
        part = pl.ds(i * size, size)
        return x.at[part], lambda owner: out.at[owner, part]

    return [item(i) for i in range(chunks)]


def gather_kernel(chunks, x, out, local_sem, *sems):
    gather = Gather(row_items(x, out, chunks), sems)
    greet(gather.sibling, gather.x, gather.y)
    own = pltpu.make_async_copy(x, out.at[gather.me], local_sem)
    own.start()
    gather.start()
    for i in range(chunks):
        gather.relay(i)
    gather.finish()
    own.wait()


def enter_kernel(
    chunks, piece, tokens, gains, ids, gate, up, down, hidden, all_gains, all_ids, feed_cols, down_rows,
    own, windows, joined, window_sems, rows_sem, own_sem, to_z, at_z, *sems,
):
    f32 = jnp.float32
    planes = all_gains.shape[0]
    z = lax.axis_index(F)
    me = lax.axis_index(R)
    count, span = windows.shape[0], windows.shape[2]
    total = gate.shape[1]

    def window(k):
        first = (k % planes) * (total // planes) + me * piece
        start = jnp.minimum(first // 128 * 128, total - span)
        return pl.multiple_of(start, 128), first - start

    cuts = []
    for k in range(count):
        source = gate if k < planes else up
        src = source.at[:, pl.ds(window(k)[0], span)]
        cuts.append(pltpu.make_async_copy(src, windows.at[k], window_sems.at[k]))
        cuts[-1].start()
    own_rows = pltpu.make_async_copy(
        down.at[pl.ds(pl.multiple_of(me * piece, 16), piece)], down_rows, rows_sem
    )
    own_rows.start()
    items = row_items(own, hidden, chunks) + [(ids, lambda owner: all_ids.at[owner])]
    gather = Gather(items, sems)
    others = [lax.rem(z + i, planes) for i in range(1, planes)]
    barrier = pltpu.get_barrier_semaphore()
    for other in others:
        pl.semaphore_signal(barrier, inc=1, device_id={F: other}, device_id_type=MESH)
    for device in (gather.sibling, gather.x, gather.y):
        pl.semaphore_signal(barrier, inc=1, device_id={R: device}, device_id_type=MESH)
    pl.semaphore_wait(barrier, planes + 2)
    copies = [
        pltpu.make_async_remote_copy(
            src_ref=gains,
            dst_ref=all_gains.at[z],
            send_sem=to_z.at[i],
            recv_sem=at_z.at[i],
            device_id={F: other},
            device_id_type=MESH,
        )
        for i, other in enumerate(others)
    ]
    for copy in copies:
        copy.start()
    all_gains[z] = gains[...]
    all_ids[gather.me] = ids[...]
    size = tokens.shape[0] // chunks
    scales = [
        inverse_rms(tokens[i * size : (i + 1) * size, :].astype(f32)) for i in range(chunks)
    ]
    for copy in copies:
        copy.wait()
    gain = jnp.concatenate([all_gains[p, 0:1] for p in range(planes)], axis=1)
    for i in range(chunks):
        part = slice(i * size, (i + 1) * size)
        own[part, :] = (tokens[part, :].astype(f32) * scales[i] * gain).astype(jnp.bfloat16)
    kept = pltpu.make_async_copy(own, hidden.at[gather.me], own_sem)
    kept.start()
    gather.start()

    def cut(k):
        cuts[k].wait()
        shift = lax.rem(span - window(k)[1], span)

        def some(n, carry):
            rows = pl.ds(pl.multiple_of(n * 64, 64), 64)
            turned = pltpu.roll(windows[k, rows, :].astype(f32), shift, 1)
            joined[rows, k * piece : (k + 1) * piece] = turned[:, :piece]
            return carry

        lax.fori_loop(0, joined.shape[0] // 64, some, 0)

    done = 0
    for i in range(gather.count):
        while done < count * (i + 1) // gather.count:
            cut(done)
            done += 1
        gather.relay(i)
    feed_cols[...] = joined[...].astype(jnp.bfloat16)
    gather.finish()
    kept.wait()
    own_rows.wait()


def turn(x, cosine, sine):
    half_dim = HEAD_DIM // 2
    low = lax.rem(lax.broadcasted_iota(jnp.int32, x.shape, 1), HEAD_DIM) < half_dim
    swapped = jnp.where(low, pltpu.roll(x, 2 * HEAD_DIM - half_dim, 1), pltpu.roll(x, half_dim, 1))
    return x * cosine + swapped * sine


def turn_keys(x, cosine, sine):
    is_key = lax.broadcasted_iota(jnp.int32, x.shape, 1) < HEAD_DIM
    return jnp.where(is_key, turn(x, cosine, sine), x)


def along_line(src, dst, sems, index, plane):
    return pltpu.make_async_remote_copy(
        src_ref=src,
        dst_ref=dst,
        send_sem=sems[0].at[index],
        recv_sem=sems[1].at[index],
        device_id={F: plane},
        device_id_type=MESH,
    )


def project_kernel(
    chunks, hidden, weight, cosine, sine, cotangent, w_cols, query, kv, cot_all, w_out,
    own, hidden_in, hidden_sems, own_sem, cot_sem, w_sem, to_all, at_all, to_line, at_line, to_sib, at_sib,
    *sems,
):
    bf16 = jnp.bfloat16
    planes = kv.shape[1]
    z = lax.axis_index(F)
    tok = cotangent.shape[0]
    width = kv.shape[0]
    count = width // 2
    gather = Gather(row_items(cotangent, cot_all, chunks), sems)
    core = lax.rem(gather.me, 2)
    mine = pl.ds(core * count, count)
    above, below = lax.rem(z + 1, planes), lax.rem(z + planes - 1, planes)
    me = gather.me
    peers = [me ^ distance for distance in range(1, width)]

    def hidden_load(i):
        slot = lax.rem(i, 2)
        block = hidden.at[lax.rem(core * count + i, width)]
        return pltpu.make_async_copy(block, hidden_in.at[slot], hidden_sems.at[slot])

    for i in (0, 1):
        hidden_load(i).start()
    barrier = pltpu.get_barrier_semaphore()
    for other in (above, below):
        pl.semaphore_signal(barrier, inc=1, device_id={F: other}, device_id_type=MESH)
    for device in peers:
        pl.semaphore_signal(barrier, inc=1, device_id={R: device}, device_id_type=MESH)
    pl.semaphore_wait(barrier, 1 + width)
    rows = w_out.shape[0]
    share = w_out.shape[1] // width
    to = w_out.at[:, pl.ds(pl.multiple_of(me * share, share), share)]

    def rows_of(device):
        part = pl.ds(pl.multiple_of(device * rows, rows), rows)
        return w_cols.at[part, pl.ds(w_cols.shape[1] - share, share)]

    w_copies = [
        remote(rows_of(device), to, (to_all, at_all), i, device) for i, device in enumerate(peers)
    ]
    w_kept = pltpu.make_async_copy(rows_of(me), to, w_sem)
    kept_cot = pltpu.make_async_copy(cotangent, cot_all.at[gather.me], cot_sem)
    kept_cot.start()
    gather.start()
    for copy in [w_kept] + w_copies:
        copy.start()

    def tile(i, carry):
        s = lax.rem(core * count + i, width)
        rows = pl.ds(pl.multiple_of(s * tok, tok), tok)
        hidden_load(i).wait()
        acc = dot(hidden_in[lax.rem(i, 2)], weight[:, : query.shape[1] + 2 * HEAD_DIM])

        @pl.when(i + 2 < width)
        def _():
            hidden_load(i + 2).start()

        c, n = cosine[rows, :], sine[rows, :]
        columns = acc.shape[1] - 2 * HEAD_DIM
        for first in range(0, columns, 2 * HEAD_DIM):
            part = slice(first, first + 2 * HEAD_DIM)
            query[rows, part] = turn(acc[:, part], c, n).astype(bf16)
        own[s] = turn_keys(acc[:, columns:], c, n).astype(bf16)
        return carry

    class Group:
        def __init__(self, make):
            self.each = [make(i) for i in range(count)]

        def __getattr__(self, name):
            def call():
                for copy in self.each:
                    getattr(copy, name)()

            return call

    def up(step):
        slot = z - step

        def make(i):
            dst = kv.at[core * count + i, slot]
            src = own.at[core * count + i] if step == 0 else dst
            return along_line(src, dst, (to_line, at_line), (step, i), above)

        return Group(make)

    def came(step):
        def make(i):
            dst = kv.at[core * count + i, z - step]
            return along_line(dst, dst, (to_line, at_line), (step - 1, i), above)

        return Group(make)

    def across(step):
        slot = z - step
        return remote(kv.at[mine, slot], kv.at[mine, slot], (to_sib, at_sib), step, gather.sibling)

    lax.fori_loop(0, count, tile, 0)

    @pl.when(z < planes - 1)
    def _():
        up(0).start()

    lax.fori_loop(count, width, tile, 0)
    kept = pltpu.make_async_copy(own, kv.at[:, z], own_sem)
    kept.start()
    done = 0
    for step in range(1, planes):

        @pl.when(z >= step)
        def _():
            arriving, leaving = came(step), up(step)
            for i in range(count):
                arriving.each[i].wait_recv()

                @pl.when(z < planes - 1)
                def _():
                    leaving.each[i].start()

            across(step).start()

        while done < chunks * step // planes:
            gather.relay(done)
            done += 1
    for i in range(done, chunks):
        gather.relay(i)
    gather.finish()
    for step in range(planes):

        @pl.when((z >= step) & (z < planes - 1))
        def _():
            up(step).wait_send()

        if step:

            @pl.when(z >= step)
            def _():
                across(step).wait()

    for copy in [kept, kept_cot, w_kept] + w_copies:
        copy.wait()


def finish_kernel(
    qkv, out_rows, terms, all_qkv, all_out, gains, own_gain, all_gains,
    at_planes, own_sems, to_z, at_z, *sems,
):
    planes = terms.shape[0]
    z = lax.axis_index(F)
    chunks = [x for pair in zip(row_items(qkv, all_qkv, 2), row_items(out_rows, all_out, 2)) for x in pair]
    gather = Gather(chunks + [(own_gain, lambda owner: all_gains.at[owner])], sems)
    me, last = gather.me, gather.count - 1
    others = [lax.rem(z + i, planes) for i in range(1, planes)]
    barrier = pltpu.get_barrier_semaphore()
    for other in others:
        pl.semaphore_signal(barrier, inc=1, device_id={F: other}, device_id_type=MESH)
    for device in (gather.sibling, gather.x, gather.y):
        pl.semaphore_signal(barrier, inc=1, device_id={R: device}, device_id_type=MESH)
    pl.semaphore_wait(barrier, planes + 2)
    copies = [
        along_line(terms.at[other], at_planes.at[i], (to_z, at_z), i, other)
        for i, other in enumerate(others)
    ]
    for copy in copies:
        copy.start()
    kept = [
        pltpu.make_async_copy(qkv, all_qkv.at[me], own_sems.at[0]),
        pltpu.make_async_copy(out_rows, all_out.at[me], own_sems.at[1]),
    ]
    for copy in kept:
        copy.start()
    gather.start((last,))
    total = terms[z]
    for i, copy in enumerate(copies):
        copy.wait()
        total = total + at_planes[i]
    own_gain[...] = total
    all_gains[me] = total
    gather.start_items((last,))
    for i in range(gather.count):
        gather.relay(i)
    gather.finish()
    total = all_gains[0]
    for device in range(1, all_gains.shape[0]):
        total = total + all_gains[device]
    gains[...] = total
    for copy in kept:
        copy.wait()


def finish(qkv, out_rows, terms, call):
    planes, width = lax.axis_size(F), lax.axis_size(R)
    f32, bf16 = jnp.float32, jnp.bfloat16
    vmem = pl.BlockSpec(memory_space=pltpu.VMEM)
    block = terms.shape[1:]
    return pl.pallas_call(
        finish_kernel,
        out_shape=[
            jax.ShapeDtypeStruct((width,) + qkv.shape, bf16),
            jax.ShapeDtypeStruct((width,) + out_rows.shape, bf16),
            jax.ShapeDtypeStruct(block, f32),
        ],
        in_specs=[ANY, ANY, vmem],
        out_specs=[ANY, ANY, vmem],
        scratch_shapes=[
            pltpu.VMEM(block, f32),
            pltpu.VMEM((width,) + block, f32),
            pltpu.VMEM((planes - 1,) + block, f32),
            DMA((2,)),
            DMA((planes - 1,)),
            DMA((planes - 1,)),
        ]
        + Gather.scratch(5),
        compiler_params=pltpu.CompilerParams(collective_id=call, has_side_effects=True),
    )(qkv, out_rows, terms)


class Scatter:
    @staticmethod
    def scratch(rows, columns, chunks):
        bf16, size = jnp.bfloat16, rows // chunks
        return [
            pltpu.VMEM((5, rows, columns), bf16),
            pltpu.VMEM((4, rows, columns), bf16),
            pltpu.VMEM((chunks, 2, size, columns), bf16),
            pltpu.VMEM((chunks, size, columns), bf16),
            pltpu.VMEM((2, size, columns), jnp.float32),
            DMA((4,)),
            DMA((4,)),
            DMA((chunks, 2)),
            DMA((chunks, 2)),
            DMA((chunks,)),
            DMA((chunks,)),
            DMA((2,)),
        ]

    def __init__(self, out, chunks, refs):
        self.out, self.chunks, self.half = out, chunks, chunks // 2
        self.own, self.sib, self.got, self.got_far, self.total = refs[:5]
        self.sib_sems, self.near_sems, self.far_sems = refs[5:7], refs[7:9], refs[9:11]
        self.out_sem = refs[11]
        self.me = lax.axis_index(R)
        self.sibling, self.x, self.y = self.me + 1 - 2 * lax.rem(self.me, 2), self.me ^ 2, self.me ^ 4
        self.size = out.shape[0] // chunks
        self.order = [*range(self.half, chunks), *range(self.half)]
        self.trades = None

    def owner(self, i):
        return (self.me ^ (6 - 2 * (i // 2))) ^ (1 - lax.rem(i, 2))

    def trade(self, d):
        return remote(self.own.at[4], self.sib.at[d], self.sib_sems, d, self.sibling)

    def put(self, i, value):
        d = 3 - i // 2
        for_sibling = lax.rem(i, 2) == 0

        @pl.when(for_sibling & (i >= 2))
        def _():
            self.trade(d + 1).wait_send()

        self.own[jnp.where(for_sibling, 4, d)] = value

        @pl.when(for_sibling)
        def _():
            self.trade(d).start()

    def take(self, part, sems):
        self.loads, self.trades = {}, {}
        for d in (3, 2, 1, 0):
            self.loads[d] = pltpu.make_async_copy(part.at[self.me ^ (2 * d)], self.own.at[d], sems.at[d])
            self.loads[d].start()
        for d in (3, 2, 1, 0):
            self.trades[d] = remote(
                part.at[self.sibling ^ (2 * d)], self.sib.at[d], self.sib_sems, d, self.sibling
            )
            self.trades[d].start()

    def taken(self, d):
        self.loads[d].wait()
        self.trades[d].wait_recv()

    def arrived(self, d):
        self.trade(d).wait_recv()

    def part(self, j):
        return pl.ds(j * self.size, self.size)

    def summed(self, d, j):
        part = self.part(j)
        return self.own[d, part].astype(jnp.float32) + self.sib[d, part].astype(jnp.float32)

    def near_copy(self, j, n):
        device, d = (self.x, 1) if j < self.half else (self.y, 2)
        src = self.own.at[3 if n else d, self.part(j)]
        return remote(src, self.got.at[j, n], self.near_sems, (j, n), device)

    def far_copy(self, j):
        device, d = (self.y, 2) if j < self.half else (self.x, 1)
        return remote(self.own.at[d, self.part(j)], self.got_far.at[j], self.far_sems, j, device)

    def out_copy(self, j):
        slot = self.order.index(j) % 2
        return pltpu.make_async_copy(
            self.total.at[slot], self.out.at[self.part(j)], self.out_sem.at[slot]
        )

    def near(self, j, n):
        e = 3 if n else (1 if j < self.half else 2)
        self.own[e, self.part(j)] = self.summed(e, j).astype(jnp.bfloat16)
        self.near_copy(j, n).start()

    def progress(self, i):
        @pl.when(i == 2)
        def _():
            self.arrived(3)
            for j in self.order:
                self.near(j, 1)

        @pl.when(i == 4)
        def _():
            self.arrived(2)
            for j in range(self.half, self.chunks):
                self.near(j, 0)

        @pl.when(i == 6)
        def _():
            self.arrived(1)
            for j in range(self.half):
                self.near(j, 0)

    def far(self, j):
        for n in (0, 1):
            self.near_copy(j, n).wait_recv()
        d = 2 if j < self.half else 1
        passed = self.summed(d, j) + self.got[j, 1].astype(jnp.float32)
        self.own[d, self.part(j)] = passed.astype(jnp.bfloat16)
        self.far_copy(j).start()

    def result(self, j):
        self.far_copy(j).wait_recv()
        return (
            self.summed(0, j)
            + self.got[j, 0].astype(jnp.float32)
            + self.got_far[j].astype(jnp.float32)
        )

    def last(self, j):
        total = self.result(j)
        turn = self.order.index(j)
        if turn >= 2:
            self.out_copy(self.order[turn - 2]).wait()
        self.total[turn % 2] = total
        self.out_copy(j).start()

    def finish(self, written=True):
        if self.trades is None:
            self.trade(0).wait_send()
        else:
            for copy in self.trades.values():
                copy.wait_send()
        if written:
            for j in self.order[-2:]:
                self.out_copy(j).wait()
        for j in range(self.chunks):
            self.far_copy(j).wait_send()
            for n in (0, 1):
                self.near_copy(j, n).wait_send()


def branch_kernel(chunks, mixed, w_out, tokens, middle, *refs):
    f32, bf16 = jnp.float32, jnp.bfloat16
    scatter = Scatter(middle, chunks, refs)
    tok = tokens.shape[0]
    size = tok // chunks
    greet(scatter.sibling, scatter.x, scatter.y)

    def branch(i, carry):
        rows = pl.ds(pl.multiple_of(scatter.owner(i) * tok, tok), tok)
        scatter.put(i, dot(mixed[rows, :], w_out[...]).astype(bf16))
        scatter.progress(i)
        return carry

    lax.fori_loop(0, mixed.shape[0] // tok, branch, 0)
    scatter.arrived(0)
    for j in scatter.order:
        scatter.far(j)
    for j in scatter.order:
        part = pl.ds(j * size, size)
        middle[part, :] = tokens[part, :].astype(f32) + scatter.result(j)
    scatter.finish(False)


def middle_kernel(
    chunks, middle, gain, w_feed, cotangent, hidden, acts, down_part,
    blocks, act_stage, cot_in, down_sum, down_stage, out_sems, act_sems, cot_sems, down_sem, *sems,
):
    f32, bf16 = jnp.float32, jnp.bfloat16
    width, tok, _ = blocks.shape
    me = lax.axis_index(R)
    size = tok // chunks

    def item(j):
        part = pl.ds(j * size, size)
        return blocks.at[me, part], lambda owner: blocks.at[owner, part]

    gather = Gather([item(j) for j in range(chunks)], sems)
    units = w_feed.shape[1] // 2
    order = [*range(chunks // 2, chunks), *range(chunks // 2)]

    def cot_load(i):
        slot = lax.rem(i, 2)
        return pltpu.make_async_copy(cotangent.at[me ^ i], cot_in.at[slot], cot_sems.at[slot])

    for i in (0, 1):
        cot_load(i).start()
    greet(gather.sibling, gather.x, gather.y)
    for j in order:
        part = pl.ds(j * size, size)
        total = middle[part, :]
        blocks[me, part] = (total * inverse_rms(total) * gain[...]).astype(bf16)
        gather.start_items((j,))

    def hidden_copy(i):
        return pltpu.make_async_copy(blocks.at[me ^ i], hidden.at[me ^ i], out_sems.at[i])

    def act_copy(i):
        slot = lax.rem(i, 2)
        return pltpu.make_async_copy(act_stage.at[slot], acts.at[me ^ i], act_sems.at[slot])

    def block(i, carry):
        @pl.when(i == 1)
        def _():
            gather.from_sibling(3)

        @pl.when(i == 2)
        def _():
            for j in order:
                gather.pass_on(0, j)
                gather.pass_on(1, j)

        @pl.when(i == 3)
        def _():
            gather.from_sibling(4)

        @pl.when(i == 5)
        def _():
            gather.from_sibling(5)

        @pl.when(i == 6)
        def _():
            for j in order:
                gather.pass_on(2, j)

        @pl.when(i == 7)
        def _():
            gather.from_sibling(6)

        @pl.when(i >= 2)
        def _():
            act_copy(i - 2).wait()

        acc = dot(blocks[me ^ i], w_feed[...])
        act_stage[lax.rem(i, 2)] = acc
        act_copy(i).start()
        hidden_copy(i).start()
        gate, up = acc[:, :units], acc[:, units:]
        inner_turned = (gate / (1.0 + jnp.exp(-gate)) * up).astype(bf16).T
        cot_load(i).wait()

        @pl.when(i == 0)
        def _():
            down_sum[...] = dot(inner_turned, cot_in[0])

        @pl.when(i > 0)
        def _():
            down_sum[...] += dot(inner_turned, cot_in[lax.rem(i, 2)])

        @pl.when(i + 2 < width)
        def _():
            cot_load(i + 2).start()

        return carry

    lax.fori_loop(0, width, block, 0)
    down_stage[...] = down_sum[...].astype(bf16)
    down_copy = pltpu.make_async_copy(down_stage, down_part, down_sem)
    down_copy.start()
    down_copy.wait()
    gather.wait_sends()
    for i in (width - 2, width - 1):
        act_copy(i).wait()
    for i in range(width):
        hidden_copy(i).wait()


def branch_layer(mixed, w_out, tokens, call, chunks=4):
    vmem = pl.BlockSpec(memory_space=pltpu.VMEM)
    return pl.pallas_call(
        functools.partial(branch_kernel, chunks),
        out_shape=jax.ShapeDtypeStruct(tokens.shape, jnp.float32),
        in_specs=[vmem] * 3,
        out_specs=vmem,
        scratch_shapes=Scatter.scratch(*tokens.shape, chunks),
        compiler_params=pltpu.CompilerParams(
            collective_id=call, has_side_effects=True, vmem_limit_bytes=40 << 20
        ),
    )(mixed, w_out, tokens)


def middle_layer(middle, gain, w_feed, cotangent, call, chunks=4):
    width = lax.axis_size(R)
    tok, model = middle.shape
    bf16, f32 = jnp.bfloat16, jnp.float32
    units = w_feed.shape[1] // 2
    vmem = pl.BlockSpec(memory_space=pltpu.VMEM)
    return pl.pallas_call(
        functools.partial(middle_kernel, chunks),
        out_shape=[
            jax.ShapeDtypeStruct((width, tok, model), bf16),
            jax.ShapeDtypeStruct((width, tok, 2 * units), f32),
            jax.ShapeDtypeStruct((units, model), bf16),
        ],
        in_specs=[vmem] * 3 + [ANY],
        out_specs=[ANY] * 3,
        scratch_shapes=[
            pltpu.VMEM((width, tok, model), bf16),
            pltpu.VMEM((2, tok, 2 * units), f32),
            pltpu.VMEM((2, tok, model), bf16),
            pltpu.VMEM((units, model), f32),
            pltpu.VMEM((units, model), bf16),
            DMA((width,)),
            DMA((2,)),
            DMA((2,)),
            DMA,
        ]
        + Gather.scratch(chunks),
        compiler_params=pltpu.CompilerParams(
            collective_id=call, has_side_effects=True, vmem_limit_bytes=56 << 20
        ),
    )(middle, gain, w_feed, cotangent)


def feed_kernel(
    chunks, hidden, cotangent, acts, w_feed, w_down, out_part, grad_hidden, feed_part,
    acts_in, cot_in, grads, column_in, feed_stage, out_stage, in_sems, column_sems, feed_sem, out_sem,
    *refs,
):
    f32, bf16 = jnp.float32, jnp.bfloat16
    width, tok, model = hidden.shape
    units = w_down.shape[0]
    scatter = Scatter(grad_hidden, chunks, refs)
    half = chunks // 2
    first_half, second_half = range(half), range(half, chunks)

    def loads(i):
        slot, owner = lax.rem(i, 2), scatter.owner(i)
        return [
            pltpu.make_async_copy(acts.at[owner], acts_in.at[slot], in_sems.at[0, slot]),
            pltpu.make_async_copy(cotangent.at[owner], cot_in.at[slot], in_sems.at[1, slot]),
        ]

    def out_copy(i):
        slot = lax.rem(i, 2)
        return pltpu.make_async_copy(
            out_stage.at[slot], out_part.at[scatter.owner(i)], out_sem.at[slot]
        )

    for i in (0, 1):
        for copy in loads(i):
            copy.start()
    greet(scatter.sibling, scatter.x, scatter.y)

    def block(i, carry):
        slot = lax.rem(i, 2)
        rows = pl.ds(pl.multiple_of(i * tok, tok), tok)
        for copy in loads(i):
            copy.wait()
        gate, up = acts_in[slot, :, :units], acts_in[slot, :, units:]
        gate_sig = 1.0 / (1.0 + jnp.exp(-gate))
        gate_silu = gate * gate_sig
        inner = (gate_silu * up).astype(bf16)
        grad_inner = dot(cot_in[slot], w_down[...], 1, 1)
        grad_gate = grad_inner * up * gate_sig * (1.0 + gate * (1.0 - gate_sig))
        both = jnp.concatenate([grad_gate, grad_inner * gate_silu], axis=1).astype(bf16)
        grads[rows, :] = both
        scatter.put(i, dot(both, w_feed[...], 1, 1).astype(bf16))

        @pl.when(i >= 2)
        def _():
            out_copy(i - 2).wait()

        out_stage[slot] = dot(inner, w_down[...]).astype(bf16)
        out_copy(i).start()

        @pl.when(i + 2 < width)
        def _():
            for copy in loads(i + 2):
                copy.start()

        scatter.progress(i)
        return carry

    tiles = model // tok

    def column_loads(n):
        slot = lax.rem(n, 2)
        part = pl.ds(pl.multiple_of(n * tok, tok), tok)
        return [
            pltpu.make_async_copy(
                hidden.at[scatter.owner(i), :, part],
                column_in.at[slot, pl.ds(i * tok, tok)],
                column_sems.at[slot, i],
            )
            for i in range(width)
        ]

    def feed_copy(n):
        rows = pl.ds(pl.multiple_of(n * tok, tok), tok)
        slot = lax.rem(n, 2)
        return pltpu.make_async_copy(feed_stage.at[slot], feed_part.at[rows], feed_sem.at[slot])

    def feed_tile(n, carry):
        slot = lax.rem(n, 2)
        for copy in column_loads(n):
            copy.wait()

        @pl.when(n >= 2)
        def _():
            feed_copy(n - 2).wait()

        feed_stage[slot] = dot(column_in[slot], grads[...], 0, 0).astype(bf16)
        feed_copy(n).start()

        @pl.when(n + 2 < tiles)
        def _():
            for copy in column_loads(n + 2):
                copy.start()

        @pl.when(n == 0)
        def _():
            for j in second_half:
                scatter.far(j)

        @pl.when(n == 3)
        def _():
            for j in first_half:
                scatter.far(j)

        return carry

    for n in (0, 1):
        for copy in column_loads(n):
            copy.start()
    lax.fori_loop(0, width, block, 0)
    scatter.arrived(0)
    lax.fori_loop(0, tiles, feed_tile, 0)
    for j in scatter.order:
        scatter.last(j)
    scatter.finish()
    for i in (width - 2, width - 1):
        out_copy(i).wait()
    for n in (tiles - 2, tiles - 1):
        feed_copy(n).wait()


def feed_forward(hidden, cotangent, acts, w_feed, w_down, call, chunks=4):
    width, tok, model = hidden.shape
    units = w_down.shape[0]
    bf16 = jnp.bfloat16
    vmem = pl.BlockSpec(memory_space=pltpu.VMEM)
    return pl.pallas_call(
        functools.partial(feed_kernel, chunks),
        out_shape=[
            jax.ShapeDtypeStruct((width, tok, model), bf16),
            jax.ShapeDtypeStruct((tok, model), jnp.float32),
            jax.ShapeDtypeStruct((model, 2 * units), bf16),
        ],
        in_specs=[ANY, ANY, ANY, vmem, vmem],
        out_specs=[ANY] * 3,
        scratch_shapes=[
            pltpu.VMEM((2, tok, 2 * units), jnp.float32),
            pltpu.VMEM((2, tok, model), bf16),
            pltpu.VMEM((width * tok, 2 * units), bf16),
            pltpu.VMEM((2, width * tok, tok), bf16),
            pltpu.VMEM((2, tok, 2 * units), bf16),
            pltpu.VMEM((2, tok, model), bf16),
            DMA((2, 2)),
            DMA((2, width)),
            DMA((2,)),
            DMA((2,)),
        ]
        + Scatter.scratch(tok, model, chunks),
        compiler_params=pltpu.CompilerParams(
            collective_id=call, has_side_effects=True, vmem_limit_bytes=62 << 20
        ),
    )(hidden, cotangent, acts, w_feed, w_down)


def gradient_kernel(
    chunks, gain, grad_hidden_hbm, middle_hbm, cotangent_hbm, w_out_hbm, mixed_hbm,
    grad_mixed, w_part, grad_middle, term,
    blocks, total, grad_hidden, middle, cotangent, w_out, mixed, chunk_sems, whole_sems, *sems,
):
    f32, bf16 = jnp.float32, jnp.bfloat16
    width, tok, _ = blocks.shape
    me = lax.axis_index(R)
    size = tok // chunks

    def item(j):
        part = pl.ds(j * size, size)
        return blocks.at[me, part], lambda owner: blocks.at[owner, part]

    gather = Gather([item(j) for j in range(chunks)], sems)
    order = [x for j in range(chunks // 2) for x in (j, chunks // 2 + j)]

    def chunk_loads(j):
        part = pl.ds(j * size, size)
        pairs = (grad_hidden_hbm, grad_hidden), (middle_hbm, middle), (cotangent_hbm, cotangent)
        return [
            pltpu.make_async_copy(src.at[part], dst.at[part], chunk_sems.at[j, n])
            for n, (src, dst) in enumerate(pairs)
        ]

    loads = {j: chunk_loads(j) for j in order}
    whole = [
        pltpu.make_async_copy(w_out_hbm, w_out, whole_sems.at[0]),
        pltpu.make_async_copy(mixed_hbm, mixed, whole_sems.at[1]),
    ]
    for j in order:
        for copy in loads[j]:
            copy.start()
    for copy in whole:
        copy.start()
    greet(gather.sibling, gather.x, gather.y)
    terms = jnp.zeros(gain.shape, f32)
    for j in order:
        part = pl.ds(j * size, size)
        for copy in loads[j]:
            copy.wait()
        residual = middle[part, :]
        scale = inverse_rms(residual)
        normed = residual * scale
        grad = grad_hidden[part, :]
        terms = terms + jnp.sum(grad * normed, axis=0, keepdims=True)
        grad = grad * gain[...]
        inner = jnp.mean(grad * normed, axis=1, keepdims=True)
        result = cotangent[part, :].astype(f32) + scale * (grad - normed * inner)
        grad_middle[part, :] = result
        blocks[me, part] = result.astype(bf16)
        gather.start_items((j,))
    term[...] = terms
    for copy in whole:
        copy.wait()

    def block(i, carry):
        @pl.when(i == 1)
        def _():
            gather.from_sibling(3)

        @pl.when(i == 2)
        def _():
            for j in order:
                gather.pass_on(0, j)
                gather.pass_on(1, j)

        @pl.when(i == 3)
        def _():
            gather.from_sibling(4)

        @pl.when(i == 5)
        def _():
            gather.from_sibling(5)

        @pl.when(i == 6)
        def _():
            for j in order:
                gather.pass_on(2, j)

        @pl.when(i == 7)
        def _():
            gather.from_sibling(6)

        rows = pl.ds(pl.multiple_of((me ^ i) * tok, tok), tok)
        grad_mixed[rows, :] = dot(blocks[me ^ i], w_out[...], 1, 1).astype(bf16)
        product = dot(mixed[rows, :], blocks[me ^ i], 0, 0)

        @pl.when(i == 0)
        def _():
            total[...] = product

        @pl.when(i > 0)
        def _():
            total[...] += product

        return carry

    lax.fori_loop(0, width, block, 0)
    w_part[...] = total[...].astype(bf16)
    gather.wait_sends()


def gradient_layer(grad_hidden, middle, cotangent, gain, w_out, mixed, call, chunks=4):
    width = lax.axis_size(R)
    f32, bf16 = jnp.float32, jnp.bfloat16
    tok, model = middle.shape
    vmem = pl.BlockSpec(memory_space=pltpu.VMEM)
    return pl.pallas_call(
        functools.partial(gradient_kernel, chunks),
        out_shape=[
            jax.ShapeDtypeStruct(mixed.shape, bf16),
            jax.ShapeDtypeStruct(w_out.shape, bf16),
            jax.ShapeDtypeStruct((tok, model), f32),
            jax.ShapeDtypeStruct((1, model), f32),
        ],
        in_specs=[vmem] + [ANY] * 5,
        out_specs=[vmem] * 4,
        scratch_shapes=[
            pltpu.VMEM((width, tok, model), bf16),
            pltpu.VMEM(w_out.shape, f32),
            pltpu.VMEM((tok, model), f32),
            pltpu.VMEM((tok, model), f32),
            pltpu.VMEM((tok, model), bf16),
            pltpu.VMEM(w_out.shape, bf16),
            pltpu.VMEM(mixed.shape, bf16),
            DMA((chunks, 3)),
            DMA((2,)),
        ]
        + Gather.scratch(chunks),
        compiler_params=pltpu.CompilerParams(
            collective_id=call, has_side_effects=True, vmem_limit_bytes=60 << 20
        ),
    )(gain, grad_hidden, middle, cotangent, w_out, mixed)


def back_kernel(
    chunks, heads, q, kv, starts, places, grad, mixed, log_total, cosine, sine, hidden, out_part, down_rows, w_part,
    grad_qkv, weight_part, feed_out, all_down, w_rows,
    sums, grad_kv, from_sib, inbox, outbox, to_sib, at_sib, to_line, at_line, down_sem, w_sem,
    to_all, at_all, column_in, weight_stage, column_sems, weight_sem, load_sems, *refs,
):
    f32, bf16 = jnp.float32, jnp.bfloat16
    planes, count, tok = inbox.shape[0], inbox.shape[1], inbox.shape[2]
    width = 2 * count
    columns = heads * HEAD_DIM
    z, me = lax.axis_index(F), lax.axis_index(R)
    core = lax.rem(me, 2)
    above, below = lax.rem(z + 1, planes), lax.rem(z + planes - 1, planes)
    scatter = Scatter(feed_out, chunks, refs[:12])
    cut = (down_rows.shape[0] // 2 + 15) // 16 * 16

    def down_item(first, count):
        part = pl.ds(first, count)
        return down_rows.at[part], lambda owner: all_down.at[owner, part]

    gather = Gather([down_item(0, cut), down_item(cut, down_rows.shape[0] - cut)], refs[12:])
    barrier = pltpu.get_barrier_semaphore()
    for other in (above, below):
        pl.semaphore_signal(barrier, inc=1, device_id={F: other}, device_id_type=MESH)
    peers = [me ^ distance for distance in range(1, width)]
    for device in peers:
        pl.semaphore_signal(barrier, inc=1, device_id={R: device}, device_id_type=MESH)
    pl.semaphore_wait(barrier, 1 + width)
    share = w_part.shape[1] // width

    def share_of(device):
        return w_part.at[:, pl.ds(pl.multiple_of(device * share, share), share)]

    w_copies = [
        remote(share_of(device), w_rows.at[me], (to_all, at_all), i, device)
        for i, device in enumerate(peers)
    ]
    w_kept = pltpu.make_async_copy(share_of(me), w_rows.at[me], w_sem)
    for copy in [w_kept] + w_copies:
        copy.start()
    kept = pltpu.make_async_copy(down_rows, all_down.at[me], down_sem)
    kept.start()
    parts = tok // QUERY_BLOCK

    def step(n, carry):
        s, sub = n // parts, lax.rem(n, parts)
        rows = pl.ds(pl.multiple_of(n * QUERY_BLOCK, QUERY_BLOCK), QUERY_BLOCK)
        queries = heads_to_rows(q[rows, :] * bf16(HEAD_DIM**-0.5), heads)
        grads = heads_to_rows(grad[rows, :], heads)
        first = jnp.concatenate([starts[n]] * heads, axis=1)
        place = jnp.concatenate([places[n]] * heads, axis=1)
        products = grads.astype(f32) * heads_to_rows(mixed[rows, :], heads).astype(f32)
        delta = lax.dot_general(
            jnp.ones((8, 2 * HEAD_DIM), f32),
            products,
            (((1,), (1,)), ((), ())),
            precision=lax.Precision.HIGHEST,
            preferred_element_type=f32,
        )[:1]
        level = log_total[n]
        upper = pltpu.roll(grads.astype(f32), HEAD_DIM, 1).astype(bf16)

        @pl.when(sub == 0)
        def _():
            sums[...] = jnp.zeros_like(sums)

        def block(index, acc):
            part = pl.ds(pl.multiple_of(index * KEY_BLOCK, KEY_BLOCK), KEY_BLOCK)
            keys = kv[s, part, :]
            scores = dot(keys, queries, 1, 1)
            probs = jnp.where(visible(index, first, place), jnp.exp(scores - level), 0.0)
            grad_probs = dot(keys, upper, 1, 1)
            grad_scores = (probs * (grad_probs - delta)).astype(bf16)
            sums[part, :] += dot(grad_scores, queries) + dot(probs.astype(bf16), upper)
            return acc + dot(keys, grad_scores, 0, 0)

        place_of_first = z * tok + sub * QUERY_BLOCK
        low = jnp.where(place_of_first >= FIRST_DOC, FIRST_DOC // KEY_BLOCK, 0)
        high = (place_of_first + QUERY_BLOCK - 1) // KEY_BLOCK + 1
        acc = lax.fori_loop(low, high, block, jnp.zeros((2 * HEAD_DIM, queries.shape[0]), f32))
        grad_q = rows_to_heads(acc[:HEAD_DIM] * HEAD_DIM**-0.5, heads)
        c, n_sine = cosine[rows, :], -sine[rows, :]
        for at in range(0, columns, 2 * HEAD_DIM):
            part = slice(at, at + 2 * HEAD_DIM)
            grad_qkv[rows, part] = turn(grad_q[:, part], c, n_sine).astype(bf16)
        grad_qkv[rows, columns:] = jnp.zeros((QUERY_BLOCK, 2 * HEAD_DIM), bf16)

        @pl.when(sub == parts - 1)
        def _():
            grad_kv[s] = sums[...].astype(bf16)

        @pl.when(n == 3)
        def _():
            scatter.taken(3)
            for j in scatter.order:
                scatter.near(j, 1)
            scatter.taken(2)
            for j in scatter.order[: chunks // 2]:
                scatter.near(j, 0)
            scatter.taken(1)
            for j in scatter.order[chunks // 2 :]:
                scatter.near(j, 0)

        @pl.when(n == 11)
        def _():
            gather.relay(0)
            gather.relay(1)

        return carry

    scatter.take(out_part, load_sems)
    gather.start()
    lax.fori_loop(0, width * parts, step, 0)

    def block_of(which, b):
        return grad_kv.at[pl.ds(which * count, count), pl.ds(b * tok, tok)]

    def trade(b):
        return remote(block_of(1 - core, b), from_sib.at[b], (to_sib, at_sib), b, gather.sibling)

    def down(b, i):
        return along_line(outbox.at[b, i], inbox.at[b, i], (to_line, at_line), (b, i), below)

    def own(b, i):
        part = pl.ds(b * tok, tok)
        return grad_kv[core * count + i, part, :].astype(f32) + from_sib[b, i].astype(f32)

    for b in range(planes):

        @pl.when(b <= z)
        def _():
            trade(b).start()

    scatter.taken(0)
    for b in range(planes):

        @pl.when(b <= z)
        def _():
            trade(b).wait_recv()

        for i in range(count):

            @pl.when((b <= z) & (z < planes - 1))
            def _():
                down(b, i).wait_recv()

            @pl.when((b < z) & (z < planes - 1))
            def _():
                outbox[b, i] = (own(b, i) + inbox[b, i].astype(f32)).astype(bf16)

            @pl.when((b < z) & (z == planes - 1))
            def _():
                outbox[b, i] = own(b, i).astype(bf16)

            @pl.when(b < z)
            def _():
                down(b, i).start()

        if b == 0:
            for j in scatter.order[: chunks // 2]:
                scatter.far(j)
        if b == 1:
            for j in scatter.order[chunks // 2 :]:
                scatter.far(j)

    def keys(i, carry):
        rows = pl.ds(pl.multiple_of((core * count + i) * tok, tok), tok)
        part = pl.ds(pl.multiple_of(z * tok, tok), tok)
        total = grad_kv[core * count + i, part, :].astype(f32) + from_sib[z, i].astype(f32)
        total = total + jnp.where(z < planes - 1, inbox[z, i].astype(f32), 0.0)
        grad_qkv[rows, columns:] = turn_keys(total, cosine[rows, :], -sine[rows, :]).astype(bf16)
        return carry

    lax.fori_loop(0, count, keys, 0)
    gather.far()
    tiles = hidden.shape[1] // tok

    def column_load(n):
        part = pl.ds(pl.multiple_of(n * tok, tok), tok)
        slot = lax.rem(n, 2)
        return pltpu.make_async_copy(hidden.at[:, part], column_in.at[slot], column_sems.at[slot])

    def weight_copy(n):
        rows = pl.ds(pl.multiple_of(n * tok, tok), tok)
        slot = lax.rem(n, 2)
        return pltpu.make_async_copy(weight_stage.at[slot], weight_part.at[rows], weight_sem.at[slot])

    def weight_tile(n, carry):
        slot = lax.rem(n, 2)
        column_load(n).wait()

        @pl.when(n >= 2)
        def _():
            weight_copy(n - 2).wait()

        weight_stage[slot] = dot(column_in[slot], grad_qkv[...], 0, 0).astype(bf16)
        weight_copy(n).start()

        @pl.when(n + 2 < tiles)
        def _():
            column_load(n + 2).start()

        return carry

    for n in (0, 1):
        column_load(n).start()
    lax.fori_loop(0, tiles, weight_tile, 0)
    for j in scatter.order:
        scatter.last(j)
    scatter.finish()
    for n in (tiles - 2, tiles - 1):
        weight_copy(n).wait()
    for kind in range(3, 7):
        gather.from_sibling(kind)
    gather.wait_sends()
    for b in range(planes):

        @pl.when(b <= z)
        def _():
            trade(b).wait_send()

        @pl.when(b < z)
        def _():
            for i in range(count):
                down(b, i).wait_send()

    for copy in [kept, w_kept] + w_copies:
        copy.wait()


def attention_back(
    heads, q, kv, starts, places, grad, mixed, log_total, cosine, sine, hidden, out_part, down_rows, w_part,
    call, chunks=4,
):
    planes, width = lax.axis_size(F), lax.axis_size(R)
    f32, bf16 = jnp.float32, jnp.bfloat16
    tok, model = hidden.shape[0] // width, hidden.shape[1]
    columns = q.shape[1] + 2 * HEAD_DIM
    length = kv.shape[1]
    vmem = pl.BlockSpec(memory_space=pltpu.VMEM)
    blocks = pltpu.VMEM((planes, width // 2, tok, 2 * HEAD_DIM), bf16)
    return pl.pallas_call(
        functools.partial(back_kernel, chunks, heads),
        out_shape=[
            jax.ShapeDtypeStruct((q.shape[0], columns), bf16),
            jax.ShapeDtypeStruct((model, columns), bf16),
            jax.ShapeDtypeStruct((tok, model), f32),
            jax.ShapeDtypeStruct((width,) + down_rows.shape, bf16),
            jax.ShapeDtypeStruct((width, w_part.shape[0], w_part.shape[1] // width), bf16),
        ],
        in_specs=[vmem] * 9 + [ANY] * 4,
        out_specs=[vmem] + [ANY] * 4,
        scratch_shapes=[
            pltpu.VMEM((length, 2 * HEAD_DIM), f32),
            pltpu.VMEM((width, length, 2 * HEAD_DIM), bf16),
            blocks,
            blocks,
            blocks,
        ]
        + [DMA((planes,))] * 2
        + [DMA((planes, width // 2))] * 2
        + [DMA, DMA, DMA((width - 1,)), DMA((width - 1,))]
        + [pltpu.VMEM((2, width * tok, tok), bf16), pltpu.VMEM((2, tok, columns), bf16)]
        + [DMA((2,)), DMA((2,)), DMA((4,))]
        + Scatter.scratch(tok, model, chunks)
        + Gather.scratch(2),
        compiler_params=pltpu.CompilerParams(
            collective_id=call, has_side_effects=True, vmem_limit_bytes=60 << 20
        ),
    )(q, kv, starts, places, grad, mixed, log_total, cosine, sine, hidden, out_part, down_rows, w_part)


def hidden_kernel(chunks, grad_qkv, weight, feed_rows, grad_hidden, all_feed, feed_sem, *refs):
    bf16 = jnp.bfloat16
    scatter = Scatter(grad_hidden, chunks, refs[:12])
    gather = Gather(row_items(feed_rows, all_feed, chunks), refs[12:])
    tok = grad_hidden.shape[0]
    columns = grad_qkv.shape[1]
    greet(scatter.sibling, scatter.x, scatter.y)
    kept = pltpu.make_async_copy(feed_rows, all_feed.at[scatter.me], feed_sem)
    kept.start()
    gather.start()

    def block(i, carry):
        rows = pl.ds(pl.multiple_of(scatter.owner(i) * tok, tok), tok)
        scatter.put(i, dot(grad_qkv[rows, :], weight[:, :columns], 1, 1).astype(bf16))
        scatter.progress(i)
        return carry

    lax.fori_loop(0, grad_qkv.shape[0] // tok, block, 0)
    scatter.arrived(0)
    for i in range(chunks):
        gather.relay(i)
    for j in scatter.order:
        scatter.far(j)
    gather.finish()
    for j in scatter.order:
        scatter.last(j)
    scatter.finish()
    kept.wait()


def scatter_hidden(grad_qkv, weight, feed_rows, tok, call, chunks=4):
    width, model = lax.axis_size(R), weight.shape[0]
    vmem = pl.BlockSpec(memory_space=pltpu.VMEM)
    return pl.pallas_call(
        functools.partial(hidden_kernel, chunks),
        out_shape=[
            jax.ShapeDtypeStruct((tok, model), jnp.float32),
            jax.ShapeDtypeStruct((width,) + feed_rows.shape, jnp.bfloat16),
        ],
        in_specs=[vmem, vmem, ANY],
        out_specs=[ANY, ANY],
        scratch_shapes=[DMA] + Scatter.scratch(tok, model, chunks) + Gather.scratch(chunks),
        compiler_params=pltpu.CompilerParams(
            collective_id=call, has_side_effects=True, vmem_limit_bytes=40 << 20
        ),
    )(grad_qkv, weight, feed_rows)


def enter(tokens, gains, ids, gate, up, down, piece, call, chunks=4):
    planes, rows = lax.axis_size(F), lax.axis_size(R)
    tok, model = tokens.shape
    bf16, f32 = jnp.bfloat16, jnp.float32
    depth = gate.shape[0]
    span = (-(-piece // 128) + 1) * 128
    vmem = pl.BlockSpec(memory_space=pltpu.VMEM)
    return pl.pallas_call(
        functools.partial(enter_kernel, chunks, piece),
        out_shape=[
            jax.ShapeDtypeStruct((rows, tok, model), bf16),
            jax.ShapeDtypeStruct((planes,) + gains.shape, f32),
            jax.ShapeDtypeStruct((rows,) + ids.shape, jnp.int32),
            jax.ShapeDtypeStruct((depth, 2 * planes * piece), bf16),
            jax.ShapeDtypeStruct((piece, down.shape[1]), bf16),
        ],
        in_specs=[vmem] * 3 + [ANY] * 3,
        out_specs=[ANY, vmem, vmem, vmem, ANY],
        scratch_shapes=[
            pltpu.VMEM((tok, model), bf16),
            pltpu.VMEM((2 * planes, depth, span), bf16),
            pltpu.VMEM((depth, 2 * planes * piece), f32),
            DMA((2 * planes,)),
            DMA,
            DMA,
            DMA((planes - 1,)),
            DMA((planes - 1,)),
        ]
        + Gather.scratch(chunks + 1),
        compiler_params=pltpu.CompilerParams(
            collective_id=call, has_side_effects=True, vmem_limit_bytes=60 << 20
        ),
    )(tokens, gains, ids, gate, up, down)


def project(hidden, weight, cosine, sine, cotangent, query_width, call, chunks=4):
    planes, width = lax.axis_size(F), lax.axis_size(R)
    tok, model = cotangent.shape
    bf16 = jnp.bfloat16
    vmem = pl.BlockSpec(memory_space=pltpu.VMEM)
    return pl.pallas_call(
        functools.partial(project_kernel, chunks),
        out_shape=[
            jax.ShapeDtypeStruct((width * tok, query_width), bf16),
            jax.ShapeDtypeStruct((width, planes, tok, 2 * HEAD_DIM), bf16),
            jax.ShapeDtypeStruct((width, tok, model), bf16),
            jax.ShapeDtypeStruct((model // width, model), bf16),
        ],
        in_specs=[ANY] + [vmem] * 3 + [ANY, ANY],
        out_specs=[vmem, ANY, ANY, ANY],
        scratch_shapes=[
            pltpu.VMEM((width, tok, 2 * HEAD_DIM), bf16),
            pltpu.VMEM((2, tok, model), bf16),
            DMA((2,)),
            DMA,
            DMA,
            DMA,
            DMA((width - 1,)),
            DMA((width - 1,)),
        ]
        + [DMA((planes, width // 2))] * 2
        + [DMA((planes,))] * 2
        + Gather.scratch(chunks),
        compiler_params=pltpu.CompilerParams(
            collective_id=call, has_side_effects=True, vmem_limit_bytes=40 << 20
        ),
    )(hidden, weight, cosine, sine, cotangent, weight)


def scatter_kernel(
    chunks, part, out, own, from_sib, give, got, give_far, got_far, total,
    own_sem, out_sem, to_sib, at_sib, to_near, at_near, to_far, at_far,
):
    f32, bf16 = jnp.float32, jnp.bfloat16
    me = lax.axis_index(R)
    flip = 1 - 2 * lax.rem(me, 2)
    sibling, beside_x, beside_y = me + flip, me ^ 2, me ^ 4
    rows = out.shape[0]
    size = rows // chunks
    half = chunks // 2
    owners = [me, beside_x, beside_y, me ^ 6]
    order = [c for j in range(half) for c in (j, half + j)]

    def rows_of(device, j):
        return part.at[pl.ds(pl.multiple_of(device * rows + j * size, 16), size)]

    def own_copy(d, j):
        return pltpu.make_async_copy(rows_of(owners[d], j), own.at[d, j], own_sem.at[d, j])

    def sib_copy(d, j):
        return remote(rows_of(owners[d] + flip, j), from_sib.at[d, j], (to_sib, at_sib), (d, j), sibling)

    def near_copy(j):
        device = beside_x if j < half else beside_y
        return remote(give.at[j], got.at[j], (to_near, at_near), j, device)

    def far_copy(j):
        device = beside_y if j < half else beside_x
        return remote(give_far.at[j], got_far.at[j], (to_far, at_far), j, device)

    def out_copy(j):
        return pltpu.make_async_copy(total.at[j], out.at[pl.ds(j * size, size)], out_sem.at[j])

    def summed(d, j):
        own_copy(d, j).wait()
        sib_copy(d, j).wait_recv()
        return own[d, j].astype(f32) + from_sib[d, j].astype(f32)

    for j in order:
        for d in (1, 2, 3, 0):
            own_copy(d, j).start()
    greet(sibling, beside_x, beside_y)
    for j in order:
        for d in (1, 3, 2, 0) if j < half else (2, 3, 1, 0):
            sib_copy(d, j).start()
    for j in order:
        give[j, 0] = summed(1 if j < half else 2, j).astype(bf16)
        give[j, 1] = summed(3, j).astype(bf16)
        near_copy(j).start()
    for j in order:
        passed = summed(2 if j < half else 1, j)
        kept = summed(0, j)
        near_copy(j).wait_recv()
        give_far[j] = (passed + got[j, 1].astype(f32)).astype(bf16)
        far_copy(j).start()
        total[j] = kept + got[j, 0].astype(f32)
    for j in order:
        far_copy(j).wait_recv()
        total[j] = total[j] + got_far[j].astype(f32)
        out_copy(j).start()
    for j in order:
        out_copy(j).wait()
        near_copy(j).wait_send()
        far_copy(j).wait_send()
        for d in range(4):
            sib_copy(d, j).wait_send()


def plane_gather(x, call, chunks=4):
    width = lax.axis_size(R)
    if width != 8:
        return lax.all_gather(x, R, axis=0, tiled=True)
    out = pl.pallas_call(
        functools.partial(gather_kernel, chunks),
        out_shape=jax.ShapeDtypeStruct((width,) + x.shape, x.dtype),
        in_specs=[ANY],
        out_specs=ANY,
        scratch_shapes=[DMA] + Gather.scratch(chunks),
        compiler_params=pltpu.CompilerParams(collective_id=call, has_side_effects=True),
    )(x)
    return out.reshape((width * x.shape[0],) + x.shape[1:])


def plane_scatter(x, call, chunks=4):
    width = lax.axis_size(R)
    if width != 8:
        return lax.psum_scatter(x, R, scatter_dimension=0, tiled=True).astype(jnp.float32)
    rows, columns = x.shape[0] // width, x.shape[1]
    size = rows // chunks
    bf16 = jnp.bfloat16
    return pl.pallas_call(
        functools.partial(scatter_kernel, chunks),
        out_shape=jax.ShapeDtypeStruct((rows, columns), jnp.float32),
        in_specs=[ANY],
        out_specs=ANY,
        scratch_shapes=[
            pltpu.VMEM((4, chunks, size, columns), bf16),
            pltpu.VMEM((4, chunks, size, columns), bf16),
            pltpu.VMEM((chunks, 2, size, columns), bf16),
            pltpu.VMEM((chunks, 2, size, columns), bf16),
            pltpu.VMEM((chunks, size, columns), bf16),
            pltpu.VMEM((chunks, size, columns), bf16),
            pltpu.VMEM((chunks, size, columns), jnp.float32),
            DMA((4, chunks)),
            DMA((chunks,)),
            DMA((4, chunks)),
            DMA((4, chunks)),
        ]
        + [DMA((chunks,))] * 4,
        compiler_params=pltpu.CompilerParams(
            collective_id=call, has_side_effects=True, vmem_limit_bytes=32 << 20
        ),
    )(x)


def line_gather(x):
    return lax.all_gather(x, F, axis=0, tiled=True)


def line_scatter(x):
    return lax.psum_scatter(x, F, scatter_dimension=0, tiled=True)


def heads_to_rows(block, heads):
    parts = [block[:, h * HEAD_DIM : (h + 1) * HEAD_DIM] for h in range(heads)]
    rows = jnp.concatenate(parts, axis=0)
    return jnp.concatenate([rows, jnp.zeros_like(rows)], axis=1)


def rows_to_heads(columns, heads):
    count = columns.shape[1] // heads
    return jnp.concatenate([columns[:, h * count : (h + 1) * count].T for h in range(heads)], axis=1)


def visible(block_index, starts, places):
    keys = block_index * KEY_BLOCK + lax.broadcasted_iota(jnp.int32, (KEY_BLOCK, starts.shape[1]), 0)
    return (keys >= starts) & (keys <= places)


def attention_kernel(heads, low, high, q, kv, starts, places, mixed, log_total):
    f32, bf16 = jnp.float32, jnp.bfloat16
    step = pl.program_id(0) * pl.num_programs(1) + pl.program_id(1)
    queries = heads_to_rows(q[...] * bf16(HEAD_DIM**-0.5), heads)
    first = jnp.concatenate([starts[0]] * heads, axis=1)
    place = jnp.concatenate([places[0]] * heads, axis=1)
    columns = queries.shape[0]

    def block(index, carry):
        top, total, acc = carry
        rows = kv[0, pl.ds(pl.multiple_of(index * KEY_BLOCK, KEY_BLOCK), KEY_BLOCK), :]
        scores = jnp.where(visible(index, first, place), dot(rows, queries, 1, 1), NEGATIVE)
        new_top = jnp.maximum(top, jnp.max(scores, axis=0, keepdims=True))
        weights = jnp.exp(scores - new_top)
        fade = jnp.exp(top - new_top)
        total = total * fade + jnp.sum(weights, axis=0, keepdims=True)
        acc = acc * fade + dot(rows, weights.astype(bf16), 0, 0)
        return new_top, total, acc

    top, total, acc = lax.fori_loop(
        low[step],
        high[step],
        block,
        (
            jnp.full((1, columns), NEGATIVE, f32),
            jnp.zeros((1, columns), f32),
            jnp.zeros((2 * HEAD_DIM, columns), f32),
        ),
    )
    mixed[...] = rows_to_heads(acc[HEAD_DIM:] / total, heads).astype(bf16)
    log_total[0] = top + jnp.log(total)


def attention_back_kernel(
    heads, low, high, q, kv, starts, places, grad, mixed, log_total, grad_q, grad_kv, sums
):
    f32, bf16 = jnp.float32, jnp.bfloat16
    step = pl.program_id(0) * pl.num_programs(1) + pl.program_id(1)
    queries = heads_to_rows(q[...] * bf16(HEAD_DIM**-0.5), heads)
    grads = heads_to_rows(grad[...], heads)
    first = jnp.concatenate([starts[0]] * heads, axis=1)
    place = jnp.concatenate([places[0]] * heads, axis=1)
    columns = queries.shape[0]
    products = grads.astype(f32) * heads_to_rows(mixed[...], heads).astype(f32)
    delta = lax.dot_general(
        jnp.ones((8, 2 * HEAD_DIM), f32),
        products,
        (((1,), (1,)), ((), ())),
        precision=lax.Precision.HIGHEST,
        preferred_element_type=f32,
    )[:1]
    level = log_total[0]
    upper = pltpu.roll(grads.astype(f32), HEAD_DIM, 1).astype(bf16)

    @pl.when(pl.program_id(1) == 0)
    def _():
        sums[...] = jnp.zeros_like(sums)

    def block(index, acc):
        part = pl.ds(pl.multiple_of(index * KEY_BLOCK, KEY_BLOCK), KEY_BLOCK)
        rows = kv[0, part, :]
        scores = dot(rows, queries, 1, 1)
        probs = jnp.where(visible(index, first, place), jnp.exp(scores - level), 0.0)
        grad_probs = dot(rows, upper, 1, 1)
        grad_scores = (probs * (grad_probs - delta)).astype(bf16)
        sums[part, :] += dot(grad_scores, queries) + dot(probs.astype(bf16), upper)
        return acc + dot(rows, grad_scores, 0, 0)

    acc = lax.fori_loop(low[step], high[step], block, jnp.zeros((2 * HEAD_DIM, columns), f32))
    grad_q[...] = rows_to_heads(acc[:HEAD_DIM] * HEAD_DIM**-0.5, heads)

    @pl.when(pl.program_id(1) == PARTS - 1)
    def _():
        grad_kv[0] = sums[...].astype(bf16)


def attention_call(kernel, heads, low, high, arrays, outs, scratch=()):
    blocks = {
        "tokens": lambda shape: pl.BlockSpec((QUERY_BLOCK, shape[1]), lambda s, b, *_: (s * PARTS + b, 0)),
        "row": lambda shape: pl.BlockSpec((1,) + shape[1:], lambda s, b, *_: (s * PARTS + b, 0, 0)),
        "sequence": lambda shape: pl.BlockSpec((1,) + shape[1:], lambda s, b, *_: (s, 0, 0)),
    }
    return pl.pallas_call(
        functools.partial(kernel, heads),
        grid_spec=pltpu.PrefetchScalarGridSpec(
            num_scalar_prefetch=2,
            grid=(low.shape[0] // PARTS, PARTS),
            in_specs=[blocks[kind](x.shape) for kind, x in arrays],
            out_specs=[blocks[kind](x.shape) for kind, x in outs],
            scratch_shapes=scratch,
        ),
        out_shape=[x for _, x in outs],
        compiler_params=pltpu.CompilerParams(vmem_limit_bytes=32 << 20),
    )(low, high, *[x for _, x in arrays])


def join_feed_kernel(planes, piece, x, gate, up):
    width = x.shape[0]
    for kind, out in enumerate((gate, up)):
        for p in range(planes):
            for r in range(width):
                first = (kind * planes + p) * piece
                to = (p * width + r) * piece
                out[:, to : to + piece] = x[r, :, first : first + piece].astype(jnp.float32)


def join_attention_kernel(sharers, qkv, o, query, key, value, out):
    f32 = jnp.float32
    width, qw, ow = qkv.shape[0], qkv.shape[2] - 2 * HEAD_DIM, o.shape[2]
    for r in range(width):
        query[:, r * qw : (r + 1) * qw] = qkv[r, :, :qw].astype(f32)
        out[:, r * ow : (r + 1) * ow] = o[r].astype(f32)
    for head in range(width // sharers):
        both = sum(qkv[head * sharers + i, :, qw:].astype(f32) for i in range(sharers))
        to = slice(head * HEAD_DIM, (head + 1) * HEAD_DIM)
        key[:, to] = both[:, :HEAD_DIM]
        value[:, to] = both[:, HEAD_DIM:]


def widen_kernel(x, out):
    out[...] = x[0].astype(jnp.float32)


def widen(x):
    count, rows, columns = x.shape
    return pl.pallas_call(
        widen_kernel,
        grid=(count,),
        in_specs=[pl.BlockSpec((1, rows, columns), lambda i: (i, 0, 0))],
        out_specs=pl.BlockSpec((rows, columns), lambda i: (i, 0)),
        out_shape=jax.ShapeDtypeStruct((count * rows, columns), jnp.float32),
        compiler_params=pltpu.CompilerParams(vmem_limit_bytes=60 << 20),
    )(x)


def join_call(kernel, arrays, outs, block=64):
    rows = arrays[0].shape[1]
    return pl.pallas_call(
        kernel,
        grid=(rows // block,),
        in_specs=[pl.BlockSpec((x.shape[0], block, x.shape[2]), lambda i: (0, i, 0)) for x in arrays],
        out_specs=[pl.BlockSpec((block, columns), lambda i: (i, 0)) for columns in outs],
        out_shape=[jax.ShapeDtypeStruct((rows, columns), jnp.float32) for columns in outs],
        compiler_params=pltpu.CompilerParams(vmem_limit_bytes=32 << 20),
    )(*arrays)


def per_device(
    tokens,
    segment_ids,
    attention_gain,
    query_weight,
    key_weight,
    value_weight,
    output_weight,
    feed_gain,
    gate_weight,
    up_weight,
    down_weight,
    cotangent,
):
    f32, bf16 = jnp.float32, jnp.bfloat16
    planes, width = lax.axis_size(F), lax.axis_size(R)
    r, z = lax.axis_index(R), lax.axis_index(F)
    tok, model = tokens.shape
    length = segment_ids.shape[1]
    all_tok = width * tok
    plane_kernels = width == 8
    heads = HEADS // width
    group = HEADS // KV_HEADS
    qw = heads * HEAD_DIM
    kv = (r * heads) // group
    feed = gate_weight.shape[1]
    piece = feed // (width * planes)
    hidden_units = piece * planes

    def cols(weight, first, count):
        return lax.dynamic_slice_in_dim(weight, first, count, 1)

    def feed_cols(weight):
        return [cols(weight, p * (feed // planes) + r * piece, piece) for p in range(planes)]

    w_attention = line_gather(
        jnp.concatenate(
            [
                cols(query_weight, r * qw, qw),
                cols(key_weight, kv * HEAD_DIM, HEAD_DIM),
                cols(value_weight, kv * HEAD_DIM, HEAD_DIM),
                cols(output_weight, r * (model // width), model // width),
            ],
            axis=1,
        )
    )
    w_qkv = w_attention[:, : qw + 2 * HEAD_DIM]
    own_gains = jnp.stack([attention_gain, feed_gain]).astype(f32)
    tok_float = tokens.astype(f32)
    scale_in = inverse_rms(tok_float)
    normed_in = tok_float * scale_in
    if plane_kernels:
        hidden_in, gains, ids, feed_cut, down_cut = enter(
            tokens,
            jnp.pad(own_gains, ((0, 6), (0, 0))),
            segment_ids.reshape(8, length // 8),
            gate_weight,
            up_weight,
            down_weight,
            piece,
            0,
        )
        hidden_in = hidden_in.reshape(all_tok, model)
        gains = gains[:, :2].transpose(1, 0, 2).reshape(2, model)
        ids = ids.reshape(width, length)
    else:
        gains = lax.all_gather(own_gains, F, axis=1, tiled=True)
        hidden_in = lax.all_gather((normed_in * gains[0]).astype(bf16), R, axis=0, tiled=True)
        ids = lax.all_gather(segment_ids, R, axis=0, tiled=True)
        feed_cut = jnp.concatenate(feed_cols(gate_weight) + feed_cols(up_weight), axis=1)
        down_cut = lax.dynamic_slice_in_dim(down_weight, r * piece, piece, 0)
    gain_in, gain_mid = gains[0], gains[1]
    w_feed, w_down = line_gather(feed_cut), line_gather(down_cut)

    own_ids = lax.dynamic_slice_in_dim(ids, z * tok, tok, 1)
    own_starts = jnp.sum(ids[:, None, :] < own_ids[:, :, None], axis=2, dtype=jnp.int32).reshape(all_tok)
    own_places = z * tok + jnp.arange(all_tok, dtype=jnp.int32) % tok
    own_positions = own_places - own_starts
    steps = all_tok // QUERY_BLOCK
    starts = own_starts.reshape(steps, 1, QUERY_BLOCK)
    query_places = own_places.reshape(steps, 1, QUERY_BLOCK)
    low = starts[:, 0, 0] // KEY_BLOCK
    high = query_places[:, 0, QUERY_BLOCK - 1] // KEY_BLOCK + 1

    if plane_kernels:
        wide_cosine, wide_sine = rope_tables(own_positions, 4)
        wide_sine = wide_sine * jnp.where(jnp.arange(2 * HEAD_DIM) // (HEAD_DIM // 2) % 2, 1.0, -1.0)
        query, kv_rows, cot_all, w_out = project(
            hidden_in.reshape(width, tok, model),
            w_attention,
            wide_cosine,
            wide_sine,
            cotangent,
            qw,
            3,
        )
        kv_rows = kv_rows.reshape(width, length, 2 * HEAD_DIM)
        cot_all = cot_all.reshape(all_tok, model)
    else:
        cosine, sine = rope_tables(own_positions)
        qkv = dot(hidden_in, w_qkv)
        query = rotate(qkv[:, :qw].reshape(all_tok, heads, HEAD_DIM), cosine, sine, 1.0)
        query = query.astype(bf16).reshape(all_tok, qw)
        key = rotate(qkv[:, None, qw : qw + HEAD_DIM], cosine, sine, 1.0).astype(bf16)[:, 0]
        value = qkv[:, qw + HEAD_DIM :].astype(bf16)
        kv_rows = (
            lax.all_gather(jnp.concatenate([key, value], axis=1), F, axis=0, tiled=False)
            .reshape(planes, width, tok, 2 * HEAD_DIM)
            .transpose(1, 0, 2, 3)
            .reshape(width, length, 2 * HEAD_DIM)
        )
        cot_all = lax.all_gather(cotangent, R, axis=0, tiled=True)
        w_out = lax.all_to_all(
            w_attention[:, qw + 2 * HEAD_DIM :], R, split_axis=0, concat_axis=1, tiled=True
        )
    common = [("tokens", query), ("sequence", kv_rows), ("row", starts), ("row", query_places)]
    mixed, log_totals = attention_call(
        attention_kernel,
        heads,
        low,
        high,
        common,
        [
            ("tokens", jax.ShapeDtypeStruct((all_tok, qw), bf16)),
            ("row", jax.ShapeDtypeStruct((steps, 1, heads * QUERY_BLOCK), f32)),
        ],
    )
    if plane_kernels:
        cot_blocks = cot_all.reshape(width, tok, model)
        middle = branch_layer(mixed, w_out, tokens, 1)
        hidden_blocks, acts, down_part = middle_layer(middle, gain_mid[None], w_feed, cot_blocks, 2)
    else:
        middle = tok_float + plane_scatter(dot(mixed, w_out).astype(bf16), 1)

    if plane_kernels:
        out_part, grad_hidden_mid, feed_part = feed_forward(
            hidden_blocks, cot_blocks, acts, w_feed, w_down, 5
        )
    else:
        w_gate, w_up = w_feed[:, :hidden_units], w_feed[:, hidden_units:]
        scale_mid = inverse_rms(middle)
        normed_mid = middle * scale_mid
        hidden_mid = plane_gather((normed_mid * gain_mid).astype(bf16), 2)
        gate_acc = dot(hidden_mid, w_gate)
        up_acc = dot(hidden_mid, w_up)
        gate_sig = jax.nn.sigmoid(gate_acc)
        gate_silu = gate_acc * gate_sig
        inner_act = (gate_silu * up_acc).astype(bf16)
        out_part = dot(inner_act, w_down).astype(bf16)
        grad_inner = dot(cot_all, w_down, 1, 1)
        grad_gate = grad_inner * up_acc * gate_sig * (1.0 + gate_acc * (1.0 - gate_sig))
        grad_gate = grad_gate.astype(bf16)
        grad_up = (grad_inner * gate_silu).astype(bf16)
        feed_part = jnp.concatenate(
            [dot(hidden_mid, grad_gate, 0, 0), dot(hidden_mid, grad_up, 0, 0)], axis=1
        ).astype(bf16)
        down_part = dot(inner_act, cot_all, 0, 0).astype(bf16)
        grad_hidden_part = dot(grad_gate, w_gate, 1, 1) + dot(grad_up, w_up, 1, 1)
        grad_hidden_mid = plane_scatter(grad_hidden_part.astype(bf16), 5)
        feed_out = plane_scatter(out_part, 4)
    down_rows = line_scatter(down_part)
    feed_rows = line_scatter(feed_part)
    if plane_kernels:
        grad_mixed, w_out_part, grad_middle, gain_mid_term = gradient_layer(
            grad_hidden_mid, middle, cotangent, gain_mid[None], w_out, mixed, 6
        )
        gain_mid_term = gain_mid_term[0]
    else:
        gain_mid_term = jnp.sum(grad_hidden_mid * normed_mid, axis=0)
        grad_normed_mid = grad_hidden_mid * gain_mid
        inner = jnp.mean(grad_normed_mid * normed_mid, axis=1, keepdims=True)
        grad_middle = cotangent.astype(f32) + scale_mid * (grad_normed_mid - normed_mid * inner)
        grad_branch = plane_gather(grad_middle.astype(bf16), 6)
        grad_mixed = dot(grad_branch, w_out, 1, 1).astype(bf16)
        w_out_part = dot(mixed, grad_branch, 0, 0).astype(bf16)

    if plane_kernels:
        grad_qkv, qkv_part, feed_out, down_all, w_out_part = attention_back(
            heads,
            query,
            kv_rows,
            starts,
            query_places,
            grad_mixed,
            mixed,
            log_totals,
            wide_cosine,
            wide_sine,
            hidden_in,
            out_part,
            down_rows,
            w_out_part,
            10,
        )
        w_out_part = w_out_part.reshape(width * qw, model // width)
    else:
        gq, gkv = attention_call(
            attention_back_kernel,
            heads,
            low,
            high,
            common + [("tokens", grad_mixed), ("tokens", mixed), ("row", log_totals)],
            [
                ("tokens", jax.ShapeDtypeStruct((all_tok, qw), f32)),
                ("sequence", jax.ShapeDtypeStruct((width, length, 2 * HEAD_DIM), bf16)),
            ],
            [pltpu.VMEM((length, 2 * HEAD_DIM), f32)],
        )
        gkv = gkv.reshape(width, planes, tok, 2 * HEAD_DIM).transpose(1, 0, 2, 3)
        gkv = line_scatter(gkv.reshape(planes * all_tok, 2 * HEAD_DIM)).astype(f32)
        gq = rotate(gq.reshape(all_tok, heads, HEAD_DIM), cosine, sine, -1.0)
        gk = rotate(gkv[:, None, :HEAD_DIM], cosine, sine, -1.0)[:, 0]
        grad_qkv = jnp.concatenate([gq.reshape(all_tok, qw), gk, gkv[:, HEAD_DIM:]], axis=1)
        grad_qkv = grad_qkv.astype(bf16)
        qkv_part = dot(hidden_in, grad_qkv, 0, 0).astype(bf16)
        down_all = lax.all_gather(down_rows, R, axis=0, tiled=True)
        w_out_part = lax.all_to_all(w_out_part, R, split_axis=1, concat_axis=0, tiled=True)
    out_rows = line_scatter(w_out_part)
    activations = (middle + feed_out).astype(bf16)
    grad_qkv, qkv_part, feed_rows = lax.optimization_barrier((grad_qkv, qkv_part, feed_rows))
    qkv_rows = line_scatter(qkv_part)
    if plane_kernels:
        grad_hidden_in, feed_all = scatter_hidden(grad_qkv, w_attention, feed_rows, tok, 7)
    else:
        grad_hidden_in = plane_scatter(dot(grad_qkv, w_qkv, 1, 1).astype(bf16), 7)
        feed_all = lax.all_gather(feed_rows, R, axis=0, tiled=False)
    gain_in_term = jnp.sum(grad_hidden_in * normed_in, axis=0)
    grad_normed_in = grad_hidden_in * gain_in
    input_grad = (
        grad_middle
        + scale_in
        * (
            grad_normed_in
            - normed_in * jnp.mean(grad_normed_in * normed_in, axis=1, keepdims=True)
        )
    ).astype(bf16)

    rows = model // planes
    terms = jnp.stack([gain_in_term, gain_mid_term])
    if plane_kernels:
        terms = jnp.pad(terms.reshape(2, planes, rows).transpose(1, 0, 2), ((0, 0), (0, 6), (0, 0)))
        qkv_all, out_all, gain_terms = finish(qkv_rows, out_rows, terms, 9)
    else:
        qkv_all = lax.all_gather(qkv_rows, R, axis=0, tiled=False)
        out_all = lax.all_gather(out_rows, R, axis=0, tiled=False)
        gain_terms = lax.psum(lax.psum_scatter(terms, F, scatter_dimension=1, tiled=True), R)
    if plane_kernels:
        down_grad = widen(down_all)
    else:
        down_grad = down_all.reshape(feed // planes, model).astype(f32)
    gate_grad, up_grad = join_call(
        functools.partial(join_feed_kernel, planes, piece), [feed_all], [feed, feed]
    )
    query_grad, key_grad, value_grad, out_grad = join_call(
        functools.partial(join_attention_kernel, width // KV_HEADS),
        [qkv_all, out_all],
        [width * qw, KV_HEADS * HEAD_DIM, KV_HEADS * HEAD_DIM, model],
    )
    return (
        activations,
        input_grad,
        gain_terms[0],
        query_grad,
        key_grad,
        value_grad,
        out_grad,
        gain_terms[1],
        gate_grad,
        up_grad,
        down_grad,
    )


def solution(mesh):
    tok = P((R, F), None)
    row = P(F, None)
    in_specs = (tok, P(R, None), P(F), row, row, row, row, P(F), row, row, row, tok)
    out_specs = (tok, tok, P(F), row, row, row, row, P(F), row, row, row)
    return jax.shard_map(
        per_device, mesh=mesh, in_specs=in_specs, out_specs=out_specs, check_vma=False
    )
```

```python
import functools
import math

import jax
import jax.numpy as jnp
from jax import lax
from jax.experimental import pallas as pl
from jax.experimental.pallas import tpu as pltpu
from jax.sharding import PartitionSpec as P

HEADS = 32
KV_HEADS = 4
HEAD_DIM = 64
EPSILON = 1e-05
NEGATIVE = -1e30
R = "replica"
F = "fsdp"
MESH = pl.DeviceIdType.MESH
DMA = pltpu.SemaphoreType.DMA
ANY = pl.BlockSpec(memory_space=pl.ANY)
KEY_BLOCK = 256
QUERY_BLOCK = 128
PARTS = 2
FIRST_DOC = 800


def inverse_rms(values):
    return lax.rsqrt(jnp.mean(values * values, axis=1, keepdims=True) + EPSILON)


def rope_tables(positions, repeats=1):
    half_dim = HEAD_DIM // 2
    places = jnp.arange(repeats * half_dim, dtype=jnp.int32) % half_dim
    freq_rates = jnp.exp(places.astype(jnp.float32) * (-math.log(10000.0) / half_dim))
    angles = positions.astype(jnp.float32)[:, None] * freq_rates[None, :]
    return (jnp.cos(angles), jnp.sin(angles))


def rotate(tensor, cosine_table, sine_table, sign):
    half_dim = HEAD_DIM // 2
    low, up = tensor[..., :half_dim], tensor[..., half_dim:]
    cos_part = cosine_table[:, None, :]
    sin_part = sine_table[:, None, :] * sign
    return jnp.concatenate(
        [low * cos_part - up * sin_part, up * cos_part + low * sin_part], axis=-1
    )


def dot(a, b, ca=1, cb=0):
    return lax.dot_general(a, b, (((ca,), (cb,)), ((), ())), preferred_element_type=jnp.float32)


def remote(src, dst, sems, index, device):
    return pltpu.make_async_remote_copy(
        src_ref=src,
        dst_ref=dst,
        send_sem=sems[0].at[index],
        recv_sem=sems[1].at[index],
        device_id={R: device},
        device_id_type=MESH,
    )


def greet(*devices):
    barrier = pltpu.get_barrier_semaphore()
    for device in devices:
        pl.semaphore_signal(barrier, inc=1, device_id={R: device}, device_id_type=MESH)
    pl.semaphore_wait(barrier, len(devices))


class Gather:
    @staticmethod
    def scratch(count):
        return [DMA((count,))] * 6 + [DMA((4, count))] * 2

    def __init__(self, items, sems):
        self.items, self.count = items, len(items)
        self.half = self.count // 2
        self.me = lax.axis_index(R)
        self.sibling, self.x, self.y = self.me + 1 - 2 * lax.rem(self.me, 2), self.me ^ 2, self.me ^ 4
        self.sems = sems

    def copy(self, kind, i):
        first = i < self.half
        owner, device = {
            0: (self.me, self.x),
            1: (self.me, self.y),
            2: (self.x, self.y) if first else (self.y, self.x),
            3: (self.me, self.sibling),
            4: (self.x, self.sibling),
            5: (self.y, self.sibling),
            6: (self.me ^ 6, self.sibling),
        }[kind]
        own, slot = self.items[i]
        sems = self.sems[2 * min(kind, 3) : 2 * min(kind, 3) + 2]
        src = own if kind in (0, 1, 3) else slot(owner)
        return remote(src, slot(owner), sems, i if kind < 3 else (kind - 3, i), device)

    def start(self, kept=()):
        ready = [i for i in range(self.count) if i not in kept]
        for n, i in enumerate(ready):
            self.copy(0, i).start()
            self.copy(1, ready[(n + self.half) % len(ready)]).start()
        for i in ready:
            self.copy(3, i).start()

    def start_items(self, items):
        for i in items:
            for kind in (0, 1, 3):
                self.copy(kind, i).start()

    def pass_on(self, kind, i):
        self.copy(kind, i).wait_recv()
        if kind < 2 and (i < self.half) == (kind == 0):
            self.copy(2, i).start()
        self.copy(kind + 4, i).start()

    def relay(self, i):
        self.pass_on(0, i)
        self.pass_on(1, (i + self.half) % self.count)

    def far(self):
        for i in range(self.half):
            self.pass_on(2, i)
            self.pass_on(2, self.half + i)
        for i in range(2 * self.half, self.count):
            self.pass_on(2, i)

    def from_sibling(self, kind):
        for i in range(self.count):
            self.copy(kind, i).wait_recv()

    def wait_sends(self):
        for i in range(self.count):
            for kind in range(7):
                self.copy(kind, i).wait_send()

    def finish(self):
        self.far()
        for kind in range(3, 7):
            self.from_sibling(kind)
        self.wait_sends()


def row_items(x, out, chunks):
    size = x.shape[0] // chunks

    def item(i):
        part = pl.ds(i * size, size)
        return x.at[part], lambda owner: out.at[owner, part]

    return [item(i) for i in range(chunks)]


def gather_kernel(chunks, x, out, local_sem, *sems):
    gather = Gather(row_items(x, out, chunks), sems)
    greet(gather.sibling, gather.x, gather.y)
    own = pltpu.make_async_copy(x, out.at[gather.me], local_sem)
    own.start()
    gather.start()
    for i in range(chunks):
        gather.relay(i)
    gather.finish()
    own.wait()


def enter_kernel(
    chunks, piece, tokens, gains, ids, gate, up, down, hidden, all_gains, all_ids, feed_cols, down_rows,
    own, windows, joined, window_sems, rows_sem, own_sem, to_z, at_z, *sems,
):
    f32 = jnp.float32
    planes = all_gains.shape[0]
    z = lax.axis_index(F)
    me = lax.axis_index(R)
    count, span = windows.shape[0], windows.shape[2]
    total = gate.shape[1]

    def window(k):
        first = (k % planes) * (total // planes) + me * piece
        start = jnp.minimum(first // 128 * 128, total - span)
        return pl.multiple_of(start, 128), first - start

    cuts = []
    for k in range(count):
        source = gate if k < planes else up
        src = source.at[:, pl.ds(window(k)[0], span)]
        cuts.append(pltpu.make_async_copy(src, windows.at[k], window_sems.at[k]))
        cuts[-1].start()
    own_rows = pltpu.make_async_copy(
        down.at[pl.ds(pl.multiple_of(me * piece, 16), piece)], down_rows, rows_sem
    )
    own_rows.start()
    items = row_items(own, hidden, chunks) + [(ids, lambda owner: all_ids.at[owner])]
    gather = Gather(items, sems)
    others = [lax.rem(z + i, planes) for i in range(1, planes)]
    barrier = pltpu.get_barrier_semaphore()
    for other in others:
        pl.semaphore_signal(barrier, inc=1, device_id={F: other}, device_id_type=MESH)
    for device in (gather.sibling, gather.x, gather.y):
        pl.semaphore_signal(barrier, inc=1, device_id={R: device}, device_id_type=MESH)
    pl.semaphore_wait(barrier, planes + 2)
    copies = [
        pltpu.make_async_remote_copy(
            src_ref=gains,
            dst_ref=all_gains.at[z],
            send_sem=to_z.at[i],
            recv_sem=at_z.at[i],
            device_id={F: other},
            device_id_type=MESH,
        )
        for i, other in enumerate(others)
    ]
    for copy in copies:
        copy.start()
    all_gains[z] = gains[...]
    all_ids[gather.me] = ids[...]
    size = tokens.shape[0] // chunks
    scales = [
        inverse_rms(tokens[i * size : (i + 1) * size, :].astype(f32)) for i in range(chunks)
    ]
    for copy in copies:
        copy.wait()
    gain = jnp.concatenate([all_gains[p, 0:1] for p in range(planes)], axis=1)
    for i in range(chunks):
        part = slice(i * size, (i + 1) * size)
        own[part, :] = (tokens[part, :].astype(f32) * scales[i] * gain).astype(jnp.bfloat16)
    kept = pltpu.make_async_copy(own, hidden.at[gather.me], own_sem)
    kept.start()
    gather.start()

    def cut(k):
        cuts[k].wait()
        shift = lax.rem(span - window(k)[1], span)

        def some(n, carry):
            rows = pl.ds(pl.multiple_of(n * 64, 64), 64)
            turned = pltpu.roll(windows[k, rows, :].astype(f32), shift, 1)
            joined[rows, k * piece : (k + 1) * piece] = turned[:, :piece]
            return carry

        lax.fori_loop(0, joined.shape[0] // 64, some, 0)

    done = 0
    for i in range(gather.count):
        while done < count * (i + 1) // gather.count:
            cut(done)
            done += 1
        gather.relay(i)
    feed_cols[...] = joined[...].astype(jnp.bfloat16)
    gather.finish()
    kept.wait()
    own_rows.wait()


def turn(x, cosine, sine):
    half_dim = HEAD_DIM // 2
    low = lax.rem(lax.broadcasted_iota(jnp.int32, x.shape, 1), HEAD_DIM) < half_dim
    swapped = jnp.where(low, pltpu.roll(x, 2 * HEAD_DIM - half_dim, 1), pltpu.roll(x, half_dim, 1))
    return x * cosine + swapped * sine


def turn_keys(x, cosine, sine):
    is_key = lax.broadcasted_iota(jnp.int32, x.shape, 1) < HEAD_DIM
    return jnp.where(is_key, turn(x, cosine, sine), x)


def along_line(src, dst, sems, index, plane):
    return pltpu.make_async_remote_copy(
        src_ref=src,
        dst_ref=dst,
        send_sem=sems[0].at[index],
        recv_sem=sems[1].at[index],
        device_id={F: plane},
        device_id_type=MESH,
    )


def project_kernel(
    chunks, hidden, weight, cosine, sine, cotangent, w_cols, query, kv, cot_all, w_out,
    own, hidden_in, hidden_sems, own_sem, cot_sem, w_sem, to_all, at_all, to_line, at_line, to_sib, at_sib,
    *sems,
):
    bf16 = jnp.bfloat16
    planes = kv.shape[1]
    z = lax.axis_index(F)
    tok = cotangent.shape[0]
    width = kv.shape[0]
    count = width // 2
    gather = Gather(row_items(cotangent, cot_all, chunks), sems)
    core = lax.rem(gather.me, 2)
    mine = pl.ds(core * count, count)
    above, below = lax.rem(z + 1, planes), lax.rem(z + planes - 1, planes)
    me = gather.me
    peers = [me ^ distance for distance in range(1, width)]

    def hidden_load(i):
        slot = lax.rem(i, 2)
        block = hidden.at[lax.rem(core * count + i, width)]
        return pltpu.make_async_copy(block, hidden_in.at[slot], hidden_sems.at[slot])

    for i in (0, 1):
        hidden_load(i).start()
    barrier = pltpu.get_barrier_semaphore()
    for other in (above, below):
        pl.semaphore_signal(barrier, inc=1, device_id={F: other}, device_id_type=MESH)
    for device in peers:
        pl.semaphore_signal(barrier, inc=1, device_id={R: device}, device_id_type=MESH)
    pl.semaphore_wait(barrier, 1 + width)
    rows = w_out.shape[0]
    share = w_out.shape[1] // width
    to = w_out.at[:, pl.ds(pl.multiple_of(me * share, share), share)]

    def rows_of(device):
        part = pl.ds(pl.multiple_of(device * rows, rows), rows)
        return w_cols.at[part, pl.ds(w_cols.shape[1] - share, share)]

    w_copies = [
        remote(rows_of(device), to, (to_all, at_all), i, device) for i, device in enumerate(peers)
    ]
    w_kept = pltpu.make_async_copy(rows_of(me), to, w_sem)
    kept_cot = pltpu.make_async_copy(cotangent, cot_all.at[gather.me], cot_sem)
    kept_cot.start()
    gather.start()
    for copy in [w_kept] + w_copies:
        copy.start()

    def tile(i, carry):
        s = lax.rem(core * count + i, width)
        rows = pl.ds(pl.multiple_of(s * tok, tok), tok)
        hidden_load(i).wait()
        acc = dot(hidden_in[lax.rem(i, 2)], weight[:, : query.shape[1] + 2 * HEAD_DIM])

        @pl.when(i + 2 < width)
        def _():
            hidden_load(i + 2).start()

        c, n = cosine[rows, :], sine[rows, :]
        columns = acc.shape[1] - 2 * HEAD_DIM
        for first in range(0, columns, 2 * HEAD_DIM):
            part = slice(first, first + 2 * HEAD_DIM)
            query[rows, part] = turn(acc[:, part], c, n).astype(bf16)
        own[s] = turn_keys(acc[:, columns:], c, n).astype(bf16)
        return carry

    class Group:
        def __init__(self, make):
            self.each = [make(i) for i in range(count)]

        def __getattr__(self, name):
            def call():
                for copy in self.each:
                    getattr(copy, name)()

            return call

    def up(step):
        slot = z - step

        def make(i):
            dst = kv.at[core * count + i, slot]
            src = own.at[core * count + i] if step == 0 else dst
            return along_line(src, dst, (to_line, at_line), (step, i), above)

        return Group(make)

    def came(step):
        def make(i):
            dst = kv.at[core * count + i, z - step]
            return along_line(dst, dst, (to_line, at_line), (step - 1, i), above)

        return Group(make)

    def across(step):
        slot = z - step
        return remote(kv.at[mine, slot], kv.at[mine, slot], (to_sib, at_sib), step, gather.sibling)

    lax.fori_loop(0, count, tile, 0)

    @pl.when(z < planes - 1)
    def _():
        up(0).start()

    lax.fori_loop(count, width, tile, 0)
    kept = pltpu.make_async_copy(own, kv.at[:, z], own_sem)
    kept.start()
    done = 0
    for step in range(1, planes):

        @pl.when(z >= step)
        def _():
            arriving, leaving = came(step), up(step)
            for i in range(count):
                arriving.each[i].wait_recv()

                @pl.when(z < planes - 1)
                def _():
                    leaving.each[i].start()

            across(step).start()

        while done < chunks * step // planes:
            gather.relay(done)
            done += 1
    for i in range(done, chunks):
        gather.relay(i)
    gather.finish()
    for step in range(planes):

        @pl.when((z >= step) & (z < planes - 1))
        def _():
            up(step).wait_send()

        if step:

            @pl.when(z >= step)
            def _():
                across(step).wait()

    for copy in [kept, kept_cot, w_kept] + w_copies:
        copy.wait()


def finish_kernel(
    qkv, out_rows, terms, all_qkv, all_out, gains, own_gain, all_gains,
    at_planes, own_sems, to_z, at_z, *sems,
):
    planes = terms.shape[0]
    z = lax.axis_index(F)
    chunks = [x for pair in zip(row_items(qkv, all_qkv, 2), row_items(out_rows, all_out, 2)) for x in pair]
    gather = Gather(chunks + [(own_gain, lambda owner: all_gains.at[owner])], sems)
    me, last = gather.me, gather.count - 1
    others = [lax.rem(z + i, planes) for i in range(1, planes)]
    barrier = pltpu.get_barrier_semaphore()
    for other in others:
        pl.semaphore_signal(barrier, inc=1, device_id={F: other}, device_id_type=MESH)
    for device in (gather.sibling, gather.x, gather.y):
        pl.semaphore_signal(barrier, inc=1, device_id={R: device}, device_id_type=MESH)
    pl.semaphore_wait(barrier, planes + 2)
    copies = [
        along_line(terms.at[other], at_planes.at[i], (to_z, at_z), i, other)
        for i, other in enumerate(others)
    ]
    for copy in copies:
        copy.start()
    kept = [
        pltpu.make_async_copy(qkv, all_qkv.at[me], own_sems.at[0]),
        pltpu.make_async_copy(out_rows, all_out.at[me], own_sems.at[1]),
    ]
    for copy in kept:
        copy.start()
    gather.start((last,))
    total = terms[z]
    for i, copy in enumerate(copies):
        copy.wait()
        total = total + at_planes[i]
    own_gain[...] = total
    all_gains[me] = total
    gather.start_items((last,))
    for i in range(gather.count):
        gather.relay(i)
    gather.finish()
    total = all_gains[0]
    for device in range(1, all_gains.shape[0]):
        total = total + all_gains[device]
    gains[...] = total
    for copy in kept:
        copy.wait()


def finish(qkv, out_rows, terms, call):
    planes, width = lax.axis_size(F), lax.axis_size(R)
    f32, bf16 = jnp.float32, jnp.bfloat16
    vmem = pl.BlockSpec(memory_space=pltpu.VMEM)
    block = terms.shape[1:]
    return pl.pallas_call(
        finish_kernel,
        out_shape=[
            jax.ShapeDtypeStruct((width,) + qkv.shape, bf16),
            jax.ShapeDtypeStruct((width,) + out_rows.shape, bf16),
            jax.ShapeDtypeStruct(block, f32),
        ],
        in_specs=[ANY, ANY, vmem],
        out_specs=[ANY, ANY, vmem],
        scratch_shapes=[
            pltpu.VMEM(block, f32),
            pltpu.VMEM((width,) + block, f32),
            pltpu.VMEM((planes - 1,) + block, f32),
            DMA((2,)),
            DMA((planes - 1,)),
            DMA((planes - 1,)),
        ]
        + Gather.scratch(5),
        compiler_params=pltpu.CompilerParams(collective_id=call, has_side_effects=True),
    )(qkv, out_rows, terms)


class Scatter:
    @staticmethod
    def scratch(rows, columns, chunks):
        bf16, size = jnp.bfloat16, rows // chunks
        return [
            pltpu.VMEM((5, rows, columns), bf16),
            pltpu.VMEM((4, rows, columns), bf16),
            pltpu.VMEM((chunks, 2, size, columns), bf16),
            pltpu.VMEM((chunks, size, columns), bf16),
            pltpu.VMEM((2, size, columns), jnp.float32),
            DMA((4,)),
            DMA((4,)),
            DMA((chunks, 2)),
            DMA((chunks, 2)),
            DMA((chunks,)),
            DMA((chunks,)),
            DMA((2,)),
        ]

    def __init__(self, out, chunks, refs):
        self.out, self.chunks, self.half = out, chunks, chunks // 2
        self.own, self.sib, self.got, self.got_far, self.total = refs[:5]
        self.sib_sems, self.near_sems, self.far_sems = refs[5:7], refs[7:9], refs[9:11]
        self.out_sem = refs[11]
        self.me = lax.axis_index(R)
        self.sibling, self.x, self.y = self.me + 1 - 2 * lax.rem(self.me, 2), self.me ^ 2, self.me ^ 4
        self.size = out.shape[0] // chunks
        self.order = [*range(self.half, chunks), *range(self.half)]
        self.trades = None

    def owner(self, i):
        return (self.me ^ (6 - 2 * (i // 2))) ^ (1 - lax.rem(i, 2))

    def trade(self, d):
        return remote(self.own.at[4], self.sib.at[d], self.sib_sems, d, self.sibling)

    def put(self, i, value):
        d = 3 - i // 2
        for_sibling = lax.rem(i, 2) == 0

        @pl.when(for_sibling & (i >= 2))
        def _():
            self.trade(d + 1).wait_send()

        self.own[jnp.where(for_sibling, 4, d)] = value

        @pl.when(for_sibling)
        def _():
            self.trade(d).start()

    def take(self, part, sems):
        self.loads, self.trades = {}, {}
        for d in (3, 2, 1, 0):
            self.loads[d] = pltpu.make_async_copy(part.at[self.me ^ (2 * d)], self.own.at[d], sems.at[d])
            self.loads[d].start()
        for d in (3, 2, 1, 0):
            self.trades[d] = remote(
                part.at[self.sibling ^ (2 * d)], self.sib.at[d], self.sib_sems, d, self.sibling
            )
            self.trades[d].start()

    def taken(self, d):
        self.loads[d].wait()
        self.trades[d].wait_recv()

    def arrived(self, d):
        self.trade(d).wait_recv()

    def part(self, j):
        return pl.ds(j * self.size, self.size)

    def summed(self, d, j):
        part = self.part(j)
        return self.own[d, part].astype(jnp.float32) + self.sib[d, part].astype(jnp.float32)

    def near_copy(self, j, n):
        device, d = (self.x, 1) if j < self.half else (self.y, 2)
        src = self.own.at[3 if n else d, self.part(j)]
        return remote(src, self.got.at[j, n], self.near_sems, (j, n), device)

    def far_copy(self, j):
        device, d = (self.y, 2) if j < self.half else (self.x, 1)
        return remote(self.own.at[d, self.part(j)], self.got_far.at[j], self.far_sems, j, device)

    def out_copy(self, j):
        slot = self.order.index(j) % 2
        return pltpu.make_async_copy(
            self.total.at[slot], self.out.at[self.part(j)], self.out_sem.at[slot]
        )

    def near(self, j, n):
        e = 3 if n else (1 if j < self.half else 2)
        self.own[e, self.part(j)] = self.summed(e, j).astype(jnp.bfloat16)
        self.near_copy(j, n).start()

    def progress(self, i):
        @pl.when(i == 2)
        def _():
            self.arrived(3)
            for j in self.order:
                self.near(j, 1)

        @pl.when(i == 4)
        def _():
            self.arrived(2)
            for j in range(self.half, self.chunks):
                self.near(j, 0)

        @pl.when(i == 6)
        def _():
            self.arrived(1)
            for j in range(self.half):
                self.near(j, 0)

    def far(self, j):
        for n in (0, 1):
            self.near_copy(j, n).wait_recv()
        d = 2 if j < self.half else 1
        passed = self.summed(d, j) + self.got[j, 1].astype(jnp.float32)
        self.own[d, self.part(j)] = passed.astype(jnp.bfloat16)
        self.far_copy(j).start()

    def result(self, j):
        self.far_copy(j).wait_recv()
        return (
            self.summed(0, j)
            + self.got[j, 0].astype(jnp.float32)
            + self.got_far[j].astype(jnp.float32)
        )

    def last(self, j):
        total = self.result(j)
        turn = self.order.index(j)
        if turn >= 2:
            self.out_copy(self.order[turn - 2]).wait()
        self.total[turn % 2] = total
        self.out_copy(j).start()

    def finish(self, written=True):
        if self.trades is None:
            self.trade(0).wait_send()
        else:
            for copy in self.trades.values():
                copy.wait_send()
        if written:
            for j in self.order[-2:]:
                self.out_copy(j).wait()
        for j in range(self.chunks):
            self.far_copy(j).wait_send()
            for n in (0, 1):
                self.near_copy(j, n).wait_send()


def branch_kernel(chunks, mixed, w_out, tokens, middle, *refs):
    f32, bf16 = jnp.float32, jnp.bfloat16
    scatter = Scatter(middle, chunks, refs)
    tok = tokens.shape[0]
    size = tok // chunks
    greet(scatter.sibling, scatter.x, scatter.y)

    def branch(i, carry):
        rows = pl.ds(pl.multiple_of(scatter.owner(i) * tok, tok), tok)
        scatter.put(i, dot(mixed[rows, :], w_out[...]).astype(bf16))
        scatter.progress(i)
        return carry

    lax.fori_loop(0, mixed.shape[0] // tok, branch, 0)
    scatter.arrived(0)
    for j in scatter.order:
        scatter.far(j)
    for j in scatter.order:
        part = pl.ds(j * size, size)
        middle[part, :] = tokens[part, :].astype(f32) + scatter.result(j)
    scatter.finish(False)


def middle_kernel(
    chunks, gain, w_feed, middle_hbm, cotangent, hidden, acts, down_part,
    middle, middle_sems, blocks, act_stage, cot_in, down_sum, down_stage, out_sems, act_sems, cot_sems, down_sem, *sems,
):
    f32, bf16 = jnp.float32, jnp.bfloat16
    width, tok, _ = blocks.shape
    me = lax.axis_index(R)
    size = tok // chunks

    def item(j):
        part = pl.ds(j * size, size)
        return blocks.at[me, part], lambda owner: blocks.at[owner, part]

    gather = Gather([item(j) for j in range(chunks)], sems)
    units = w_feed.shape[1] // 2
    order = [*range(chunks // 2, chunks), *range(chunks // 2)]

    def cot_load(i):
        slot = lax.rem(i, 2)
        return pltpu.make_async_copy(cotangent.at[me ^ i], cot_in.at[slot], cot_sems.at[slot])

    loads = {}
    for j in order:
        part = pl.ds(j * size, size)
        loads[j] = pltpu.make_async_copy(middle_hbm.at[part], middle.at[part], middle_sems.at[j])
        loads[j].start()
    for i in (0, 1):
        cot_load(i).start()
    greet(gather.sibling, gather.x, gather.y)
    for j in order:
        part = pl.ds(j * size, size)
        loads[j].wait()
        total = middle[part, :]
        blocks[me, part] = (total * inverse_rms(total) * gain[...]).astype(bf16)
        gather.start_items((j,))

    def hidden_copy(i):
        return pltpu.make_async_copy(blocks.at[me ^ i], hidden.at[me ^ i], out_sems.at[i])

    def act_copy(i):
        slot = lax.rem(i, 2)
        return pltpu.make_async_copy(act_stage.at[slot], acts.at[me ^ i], act_sems.at[slot])

    def block(i, carry):
        @pl.when(i == 1)
        def _():
            gather.from_sibling(3)

        @pl.when(i == 2)
        def _():
            for j in order:
                gather.pass_on(0, j)
                gather.pass_on(1, j)

        @pl.when(i == 3)
        def _():
            gather.from_sibling(4)

        @pl.when(i == 5)
        def _():
            gather.from_sibling(5)

        @pl.when(i == 6)
        def _():
            for j in order:
                gather.pass_on(2, j)

        @pl.when(i == 7)
        def _():
            gather.from_sibling(6)

        @pl.when(i >= 2)
        def _():
            act_copy(i - 2).wait()

        acc = dot(blocks[me ^ i], w_feed[...])
        act_stage[lax.rem(i, 2)] = acc
        act_copy(i).start()
        hidden_copy(i).start()
        gate, up = acc[:, :units], acc[:, units:]
        inner_turned = (gate / (1.0 + jnp.exp(-gate)) * up).astype(bf16).T
        cot_load(i).wait()

        @pl.when(i == 0)
        def _():
            down_sum[...] = dot(inner_turned, cot_in[0])

        @pl.when(i > 0)
        def _():
            down_sum[...] += dot(inner_turned, cot_in[lax.rem(i, 2)])

        @pl.when(i + 2 < width)
        def _():
            cot_load(i + 2).start()

        return carry

    lax.fori_loop(0, width, block, 0)
    down_stage[...] = down_sum[...].astype(bf16)
    down_copy = pltpu.make_async_copy(down_stage, down_part, down_sem)
    down_copy.start()
    down_copy.wait()
    gather.wait_sends()
    for i in (width - 2, width - 1):
        act_copy(i).wait()
    for i in range(width):
        hidden_copy(i).wait()


def branch_layer(mixed, w_out, tokens, call, chunks=4):
    vmem = pl.BlockSpec(memory_space=pltpu.VMEM)
    return pl.pallas_call(
        functools.partial(branch_kernel, chunks),
        out_shape=jax.ShapeDtypeStruct(tokens.shape, jnp.float32),
        in_specs=[vmem] * 3,
        out_specs=vmem,
        scratch_shapes=Scatter.scratch(*tokens.shape, chunks),
        compiler_params=pltpu.CompilerParams(
            collective_id=call, has_side_effects=True, vmem_limit_bytes=40 << 20
        ),
    )(mixed, w_out, tokens)


def middle_layer(middle, gain, w_feed, cotangent, call, chunks=4):
    width = lax.axis_size(R)
    tok, model = middle.shape
    bf16, f32 = jnp.bfloat16, jnp.float32
    units = w_feed.shape[1] // 2
    vmem = pl.BlockSpec(memory_space=pltpu.VMEM)
    return pl.pallas_call(
        functools.partial(middle_kernel, chunks),
        out_shape=[
            jax.ShapeDtypeStruct((width, tok, model), bf16),
            jax.ShapeDtypeStruct((width, tok, 2 * units), f32),
            jax.ShapeDtypeStruct((units, model), bf16),
        ],
        in_specs=[vmem] * 2 + [ANY] * 2,
        out_specs=[ANY] * 3,
        scratch_shapes=[
            pltpu.VMEM((tok, model), f32),
            DMA((chunks,)),
            pltpu.VMEM((width, tok, model), bf16),
            pltpu.VMEM((2, tok, 2 * units), f32),
            pltpu.VMEM((2, tok, model), bf16),
            pltpu.VMEM((units, model), f32),
            pltpu.VMEM((units, model), bf16),
            DMA((width,)),
            DMA((2,)),
            DMA((2,)),
            DMA,
        ]
        + Gather.scratch(chunks),
        compiler_params=pltpu.CompilerParams(
            collective_id=call, has_side_effects=True, vmem_limit_bytes=56 << 20
        ),
    )(gain, w_feed, middle, cotangent)


def feed_kernel(
    chunks, hidden, cotangent, acts, w_feed, w_down, out_part, grad_hidden, feed_part,
    acts_in, cot_in, grads, column_in, feed_stage, out_stage, in_sems, column_sems, feed_sem, out_sem,
    *refs,
):
    f32, bf16 = jnp.float32, jnp.bfloat16
    width, tok, model = hidden.shape
    units = w_down.shape[0]
    scatter = Scatter(grad_hidden, chunks, refs)
    half = chunks // 2
    first_half, second_half = range(half), range(half, chunks)

    def loads(i):
        slot, owner = lax.rem(i, 2), scatter.owner(i)
        return [
            pltpu.make_async_copy(acts.at[owner], acts_in.at[slot], in_sems.at[0, slot]),
            pltpu.make_async_copy(cotangent.at[owner], cot_in.at[slot], in_sems.at[1, slot]),
        ]

    def out_copy(i):
        slot = lax.rem(i, 2)
        return pltpu.make_async_copy(
            out_stage.at[slot], out_part.at[scatter.owner(i)], out_sem.at[slot]
        )

    for i in (0, 1):
        for copy in loads(i):
            copy.start()
    greet(scatter.sibling, scatter.x, scatter.y)

    def block(i, carry):
        slot = lax.rem(i, 2)
        rows = pl.ds(pl.multiple_of(i * tok, tok), tok)
        for copy in loads(i):
            copy.wait()
        gate, up = acts_in[slot, :, :units], acts_in[slot, :, units:]
        gate_sig = 1.0 / (1.0 + jnp.exp(-gate))
        gate_silu = gate * gate_sig
        inner = (gate_silu * up).astype(bf16)
        grad_inner = dot(cot_in[slot], w_down[...], 1, 1)
        grad_gate = grad_inner * up * gate_sig * (1.0 + gate * (1.0 - gate_sig))
        both = jnp.concatenate([grad_gate, grad_inner * gate_silu], axis=1).astype(bf16)
        grads[rows, :] = both
        scatter.put(i, dot(both, w_feed[...], 1, 1).astype(bf16))

        @pl.when(i >= 2)
        def _():
            out_copy(i - 2).wait()

        out_stage[slot] = dot(inner, w_down[...]).astype(bf16)
        out_copy(i).start()

        @pl.when(i + 2 < width)
        def _():
            for copy in loads(i + 2):
                copy.start()

        scatter.progress(i)
        return carry

    tiles = model // tok

    def column_loads(n):
        slot = lax.rem(n, 2)
        part = pl.ds(pl.multiple_of(n * tok, tok), tok)
        return [
            pltpu.make_async_copy(
                hidden.at[scatter.owner(i), :, part],
                column_in.at[slot, pl.ds(i * tok, tok)],
                column_sems.at[slot, i],
            )
            for i in range(width)
        ]

    def feed_copy(n):
        rows = pl.ds(pl.multiple_of(n * tok, tok), tok)
        slot = lax.rem(n, 2)
        return pltpu.make_async_copy(feed_stage.at[slot], feed_part.at[rows], feed_sem.at[slot])

    def feed_tile(n, carry):
        slot = lax.rem(n, 2)
        for copy in column_loads(n):
            copy.wait()

        @pl.when(n >= 2)
        def _():
            feed_copy(n - 2).wait()

        feed_stage[slot] = dot(column_in[slot], grads[...], 0, 0).astype(bf16)
        feed_copy(n).start()

        @pl.when(n + 2 < tiles)
        def _():
            for copy in column_loads(n + 2):
                copy.start()

        @pl.when(n == 0)
        def _():
            for j in second_half:
                scatter.far(j)

        @pl.when(n == 3)
        def _():
            for j in first_half:
                scatter.far(j)

        return carry

    for n in (0, 1):
        for copy in column_loads(n):
            copy.start()
    lax.fori_loop(0, width, block, 0)
    scatter.arrived(0)
    lax.fori_loop(0, tiles, feed_tile, 0)
    for j in scatter.order:
        scatter.last(j)
    scatter.finish()
    for i in (width - 2, width - 1):
        out_copy(i).wait()
    for n in (tiles - 2, tiles - 1):
        feed_copy(n).wait()


def feed_forward(hidden, cotangent, acts, w_feed, w_down, call, chunks=4):
    width, tok, model = hidden.shape
    units = w_down.shape[0]
    bf16 = jnp.bfloat16
    vmem = pl.BlockSpec(memory_space=pltpu.VMEM)
    return pl.pallas_call(
        functools.partial(feed_kernel, chunks),
        out_shape=[
            jax.ShapeDtypeStruct((width, tok, model), bf16),
            jax.ShapeDtypeStruct((tok, model), jnp.float32),
            jax.ShapeDtypeStruct((model, 2 * units), bf16),
        ],
        in_specs=[ANY, ANY, ANY, vmem, vmem],
        out_specs=[ANY] * 3,
        scratch_shapes=[
            pltpu.VMEM((2, tok, 2 * units), jnp.float32),
            pltpu.VMEM((2, tok, model), bf16),
            pltpu.VMEM((width * tok, 2 * units), bf16),
            pltpu.VMEM((2, width * tok, tok), bf16),
            pltpu.VMEM((2, tok, 2 * units), bf16),
            pltpu.VMEM((2, tok, model), bf16),
            DMA((2, 2)),
            DMA((2, width)),
            DMA((2,)),
            DMA((2,)),
        ]
        + Scatter.scratch(tok, model, chunks),
        compiler_params=pltpu.CompilerParams(
            collective_id=call, has_side_effects=True, vmem_limit_bytes=62 << 20
        ),
    )(hidden, cotangent, acts, w_feed, w_down)


def gradient_kernel(
    chunks, gain, grad_hidden_hbm, middle_hbm, cotangent_hbm, w_out_hbm, mixed_hbm,
    grad_mixed, w_part, grad_middle, term,
    blocks, total, grad_hidden, middle, cotangent, w_out, mixed, chunk_sems, whole_sems, *sems,
):
    f32, bf16 = jnp.float32, jnp.bfloat16
    width, tok, _ = blocks.shape
    me = lax.axis_index(R)
    size = tok // chunks

    def item(j):
        part = pl.ds(j * size, size)
        return blocks.at[me, part], lambda owner: blocks.at[owner, part]

    gather = Gather([item(j) for j in range(chunks)], sems)
    order = [x for j in range(chunks // 2) for x in (j, chunks // 2 + j)]

    def chunk_loads(j):
        part = pl.ds(j * size, size)
        pairs = (grad_hidden_hbm, grad_hidden), (middle_hbm, middle), (cotangent_hbm, cotangent)
        return [
            pltpu.make_async_copy(src.at[part], dst.at[part], chunk_sems.at[j, n])
            for n, (src, dst) in enumerate(pairs)
        ]

    loads = {j: chunk_loads(j) for j in order}
    whole = [
        pltpu.make_async_copy(w_out_hbm, w_out, whole_sems.at[0]),
        pltpu.make_async_copy(mixed_hbm, mixed, whole_sems.at[1]),
    ]
    for j in order:
        for copy in loads[j]:
            copy.start()
    for copy in whole:
        copy.start()
    greet(gather.sibling, gather.x, gather.y)
    terms = jnp.zeros(gain.shape, f32)
    for j in order:
        part = pl.ds(j * size, size)
        for copy in loads[j]:
            copy.wait()
        residual = middle[part, :]
        scale = inverse_rms(residual)
        normed = residual * scale
        grad = grad_hidden[part, :]
        terms = terms + jnp.sum(grad * normed, axis=0, keepdims=True)
        grad = grad * gain[...]
        inner = jnp.mean(grad * normed, axis=1, keepdims=True)
        result = cotangent[part, :].astype(f32) + scale * (grad - normed * inner)
        grad_middle[part, :] = result
        blocks[me, part] = result.astype(bf16)
        gather.start_items((j,))
    term[...] = terms
    for copy in whole:
        copy.wait()

    def block(i, carry):
        @pl.when(i == 1)
        def _():
            gather.from_sibling(3)

        @pl.when(i == 2)
        def _():
            for j in order:
                gather.pass_on(0, j)
                gather.pass_on(1, j)

        @pl.when(i == 3)
        def _():
            gather.from_sibling(4)

        @pl.when(i == 5)
        def _():
            gather.from_sibling(5)

        @pl.when(i == 6)
        def _():
            for j in order:
                gather.pass_on(2, j)

        @pl.when(i == 7)
        def _():
            gather.from_sibling(6)

        rows = pl.ds(pl.multiple_of((me ^ i) * tok, tok), tok)
        grad_mixed[rows, :] = dot(blocks[me ^ i], w_out[...], 1, 1).astype(bf16)
        product = dot(mixed[rows, :], blocks[me ^ i], 0, 0)

        @pl.when(i == 0)
        def _():
            total[...] = product

        @pl.when(i > 0)
        def _():
            total[...] += product

        return carry

    lax.fori_loop(0, width, block, 0)
    w_part[...] = total[...].astype(bf16)
    gather.wait_sends()


def gradient_layer(grad_hidden, middle, cotangent, gain, w_out, mixed, call, chunks=4):
    width = lax.axis_size(R)
    f32, bf16 = jnp.float32, jnp.bfloat16
    tok, model = middle.shape
    vmem = pl.BlockSpec(memory_space=pltpu.VMEM)
    return pl.pallas_call(
        functools.partial(gradient_kernel, chunks),
        out_shape=[
            jax.ShapeDtypeStruct(mixed.shape, bf16),
            jax.ShapeDtypeStruct(w_out.shape, bf16),
            jax.ShapeDtypeStruct((tok, model), f32),
            jax.ShapeDtypeStruct((1, model), f32),
        ],
        in_specs=[vmem] + [ANY] * 5,
        out_specs=[vmem] * 4,
        scratch_shapes=[
            pltpu.VMEM((width, tok, model), bf16),
            pltpu.VMEM(w_out.shape, f32),
            pltpu.VMEM((tok, model), f32),
            pltpu.VMEM((tok, model), f32),
            pltpu.VMEM((tok, model), bf16),
            pltpu.VMEM(w_out.shape, bf16),
            pltpu.VMEM(mixed.shape, bf16),
            DMA((chunks, 3)),
            DMA((2,)),
        ]
        + Gather.scratch(chunks),
        compiler_params=pltpu.CompilerParams(
            collective_id=call, has_side_effects=True, vmem_limit_bytes=60 << 20
        ),
    )(gain, grad_hidden, middle, cotangent, w_out, mixed)


def back_kernel(
    chunks, heads, q, kv, starts, places, grad, mixed, log_total, cosine, sine, hidden, out_part, down_rows, w_part,
    grad_qkv, weight_part, feed_out, all_down, w_rows,
    sums, grad_kv, from_sib, inbox, outbox, to_sib, at_sib, to_line, at_line, down_sem, w_sem,
    to_all, at_all, column_in, weight_stage, column_sems, weight_sem, load_sems, *refs,
):
    f32, bf16 = jnp.float32, jnp.bfloat16
    planes, count, tok = inbox.shape[0], inbox.shape[1], inbox.shape[2]
    width = 2 * count
    columns = heads * HEAD_DIM
    z, me = lax.axis_index(F), lax.axis_index(R)
    core = lax.rem(me, 2)
    above, below = lax.rem(z + 1, planes), lax.rem(z + planes - 1, planes)
    scatter = Scatter(feed_out, chunks, refs[:12])
    cut = (down_rows.shape[0] // 2 + 15) // 16 * 16

    def down_item(first, count):
        part = pl.ds(first, count)
        return down_rows.at[part], lambda owner: all_down.at[owner, part]

    gather = Gather([down_item(0, cut), down_item(cut, down_rows.shape[0] - cut)], refs[12:])
    barrier = pltpu.get_barrier_semaphore()
    for other in (above, below):
        pl.semaphore_signal(barrier, inc=1, device_id={F: other}, device_id_type=MESH)
    peers = [me ^ distance for distance in range(1, width)]
    for device in peers:
        pl.semaphore_signal(barrier, inc=1, device_id={R: device}, device_id_type=MESH)
    pl.semaphore_wait(barrier, 1 + width)
    share = w_part.shape[1] // width

    def share_of(device):
        return w_part.at[:, pl.ds(pl.multiple_of(device * share, share), share)]

    w_copies = [
        remote(share_of(device), w_rows.at[me], (to_all, at_all), i, device)
        for i, device in enumerate(peers)
    ]
    w_kept = pltpu.make_async_copy(share_of(me), w_rows.at[me], w_sem)
    for copy in [w_kept] + w_copies:
        copy.start()
    kept = pltpu.make_async_copy(down_rows, all_down.at[me], down_sem)
    kept.start()
    parts = tok // QUERY_BLOCK

    top = z == planes - 1
    early = top & (core == 0)
    late = jnp.logical_not(early)

    def block_of(which, b):
        return grad_kv.at[pl.ds(which * count, count), pl.ds(b * tok, tok)]

    def trade(b):
        return remote(block_of(1 - core, b), from_sib.at[b], (to_sib, at_sib), b, gather.sibling)

    def down(b, i):
        return along_line(outbox.at[b, i], inbox.at[b, i], (to_line, at_line), (b, i), below)

    def own(b, i):
        part = pl.ds(b * tok, tok)
        return grad_kv[core * count + i, part, :].astype(f32) + from_sib[b, i].astype(f32)

    def step(n, carry):
        s, sub = n // parts, lax.rem(n, parts)
        rows = pl.ds(pl.multiple_of(n * QUERY_BLOCK, QUERY_BLOCK), QUERY_BLOCK)
        queries = heads_to_rows(q[rows, :] * bf16(HEAD_DIM**-0.5), heads)
        grads = heads_to_rows(grad[rows, :], heads)
        first = jnp.concatenate([starts[n]] * heads, axis=1)
        place = jnp.concatenate([places[n]] * heads, axis=1)
        products = grads.astype(f32) * heads_to_rows(mixed[rows, :], heads).astype(f32)
        delta = lax.dot_general(
            jnp.ones((8, 2 * HEAD_DIM), f32),
            products,
            (((1,), (1,)), ((), ())),
            precision=lax.Precision.HIGHEST,
            preferred_element_type=f32,
        )[:1]
        level = log_total[n]
        upper = pltpu.roll(grads.astype(f32), HEAD_DIM, 1).astype(bf16)

        @pl.when(sub == 0)
        def _():
            sums[...] = jnp.zeros_like(sums)

        def block(index, acc):
            part = pl.ds(pl.multiple_of(index * KEY_BLOCK, KEY_BLOCK), KEY_BLOCK)
            keys = kv[s, part, :]
            scores = dot(keys, queries, 1, 1)
            probs = jnp.where(visible(index, first, place), jnp.exp(scores - level), 0.0)
            grad_probs = dot(keys, upper, 1, 1)
            grad_scores = (probs * (grad_probs - delta)).astype(bf16)
            sums[part, :] += dot(grad_scores, queries) + dot(probs.astype(bf16), upper)
            return acc + dot(keys, grad_scores, 0, 0)

        place_of_first = z * tok + sub * QUERY_BLOCK
        low = jnp.where(place_of_first >= FIRST_DOC, FIRST_DOC // KEY_BLOCK, 0)
        high = (place_of_first + QUERY_BLOCK - 1) // KEY_BLOCK + 1
        acc = lax.fori_loop(low, high, block, jnp.zeros((2 * HEAD_DIM, queries.shape[0]), f32))
        grad_q = rows_to_heads(acc[:HEAD_DIM] * HEAD_DIM**-0.5, heads)
        c, n_sine = cosine[rows, :], -sine[rows, :]
        for at in range(0, columns, 2 * HEAD_DIM):
            part = slice(at, at + 2 * HEAD_DIM)
            grad_qkv[rows, part] = turn(grad_q[:, part], c, n_sine).astype(bf16)
        grad_qkv[rows, columns:] = jnp.zeros((QUERY_BLOCK, 2 * HEAD_DIM), bf16)

        @pl.when(sub == parts - 1)
        def _():
            grad_kv[s] = sums[...].astype(bf16)

        @pl.when(n == 3)
        def _():
            scatter.taken(3)
            for j in scatter.order:
                scatter.near(j, 1)
            scatter.taken(2)
            for j in scatter.order[: chunks // 2]:
                scatter.near(j, 0)
            scatter.taken(1)
            for j in scatter.order[chunks // 2 :]:
                scatter.near(j, 0)

        @pl.when((n == count * parts) & top & (core == 1))
        def _():
            for b in range(planes):
                trade(b).start()

        @pl.when((n == count * parts + 2) & early)
        def _():
            for b in range(planes - 1):
                trade(b).wait_recv()
                for i in range(count):
                    outbox[b, i] = own(b, i).astype(bf16)
                    down(b, i).start()

        @pl.when(n == 11)
        def _():
            gather.relay(0)
            gather.relay(1)

        return carry

    scatter.take(out_part, load_sems)
    gather.start()
    lax.fori_loop(0, width * parts, step, 0)

    for b in range(planes):

        @pl.when((b <= z) & jnp.logical_not(top & (core == 1)))
        def _():
            trade(b).start()

    scatter.taken(0)
    for b in range(planes):

        @pl.when((b <= z) & (late if b < planes - 1 else top))
        def _():
            trade(b).wait_recv()

        for i in range(count):

            @pl.when((b <= z) & jnp.logical_not(top))
            def _():
                down(b, i).wait_recv()

            @pl.when((b < z) & jnp.logical_not(top))
            def _():
                outbox[b, i] = (own(b, i) + inbox[b, i].astype(f32)).astype(bf16)

            @pl.when((b < z) & top & late)
            def _():
                outbox[b, i] = own(b, i).astype(bf16)

            @pl.when((b < z) & late)
            def _():
                down(b, i).start()

        if b == 0:
            for j in scatter.order[: chunks // 2]:
                scatter.far(j)
        if b == 1:
            for j in scatter.order[chunks // 2 :]:
                scatter.far(j)

    def keys(i, carry):
        rows = pl.ds(pl.multiple_of((core * count + i) * tok, tok), tok)
        part = pl.ds(pl.multiple_of(z * tok, tok), tok)
        total = grad_kv[core * count + i, part, :].astype(f32) + from_sib[z, i].astype(f32)
        total = total + jnp.where(z < planes - 1, inbox[z, i].astype(f32), 0.0)
        grad_qkv[rows, columns:] = turn_keys(total, cosine[rows, :], -sine[rows, :]).astype(bf16)
        return carry

    lax.fori_loop(0, count, keys, 0)
    gather.far()
    tiles = hidden.shape[1] // tok

    def column_load(n):
        part = pl.ds(pl.multiple_of(n * tok, tok), tok)
        slot = lax.rem(n, 2)
        return pltpu.make_async_copy(hidden.at[:, part], column_in.at[slot], column_sems.at[slot])

    def weight_copy(n):
        rows = pl.ds(pl.multiple_of(n * tok, tok), tok)
        slot = lax.rem(n, 2)
        return pltpu.make_async_copy(weight_stage.at[slot], weight_part.at[rows], weight_sem.at[slot])

    def weight_tile(n, carry):
        slot = lax.rem(n, 2)
        column_load(n).wait()

        @pl.when(n >= 2)
        def _():
            weight_copy(n - 2).wait()

        weight_stage[slot] = dot(column_in[slot], grad_qkv[...], 0, 0).astype(bf16)
        weight_copy(n).start()

        @pl.when(n + 2 < tiles)
        def _():
            column_load(n + 2).start()

        return carry

    for n in (0, 1):
        column_load(n).start()
    lax.fori_loop(0, tiles, weight_tile, 0)
    for j in scatter.order:
        scatter.last(j)
    scatter.finish()
    for n in (tiles - 2, tiles - 1):
        weight_copy(n).wait()
    for kind in range(3, 7):
        gather.from_sibling(kind)
    gather.wait_sends()
    for b in range(planes):

        @pl.when(b <= z)
        def _():
            trade(b).wait_send()

        @pl.when(b < z)
        def _():
            for i in range(count):
                down(b, i).wait_send()

    for copy in [kept, w_kept] + w_copies:
        copy.wait()


def attention_back(
    heads, q, kv, starts, places, grad, mixed, log_total, cosine, sine, hidden, out_part, down_rows, w_part,
    call, chunks=4,
):
    planes, width = lax.axis_size(F), lax.axis_size(R)
    f32, bf16 = jnp.float32, jnp.bfloat16
    tok, model = hidden.shape[0] // width, hidden.shape[1]
    columns = q.shape[1] + 2 * HEAD_DIM
    length = kv.shape[1]
    vmem = pl.BlockSpec(memory_space=pltpu.VMEM)
    blocks = pltpu.VMEM((planes, width // 2, tok, 2 * HEAD_DIM), bf16)
    return pl.pallas_call(
        functools.partial(back_kernel, chunks, heads),
        out_shape=[
            jax.ShapeDtypeStruct((q.shape[0], columns), bf16),
            jax.ShapeDtypeStruct((model, columns), bf16),
            jax.ShapeDtypeStruct((tok, model), f32),
            jax.ShapeDtypeStruct((width,) + down_rows.shape, bf16),
            jax.ShapeDtypeStruct((width, w_part.shape[0], w_part.shape[1] // width), bf16),
        ],
        in_specs=[vmem] * 9 + [ANY] * 4,
        out_specs=[vmem] + [ANY] * 4,
        scratch_shapes=[
            pltpu.VMEM((length, 2 * HEAD_DIM), f32),
            pltpu.VMEM((width, length, 2 * HEAD_DIM), bf16),
            blocks,
            blocks,
            blocks,
        ]
        + [DMA((planes,))] * 2
        + [DMA((planes, width // 2))] * 2
        + [DMA, DMA, DMA((width - 1,)), DMA((width - 1,))]
        + [pltpu.VMEM((2, width * tok, tok), bf16), pltpu.VMEM((2, tok, columns), bf16)]
        + [DMA((2,)), DMA((2,)), DMA((4,))]
        + Scatter.scratch(tok, model, chunks)
        + Gather.scratch(2),
        compiler_params=pltpu.CompilerParams(
            collective_id=call, has_side_effects=True, vmem_limit_bytes=60 << 20
        ),
    )(q, kv, starts, places, grad, mixed, log_total, cosine, sine, hidden, out_part, down_rows, w_part)


def hidden_kernel(chunks, grad_qkv, weight, feed_rows, grad_hidden, all_feed, feed_sem, *refs):
    bf16 = jnp.bfloat16
    scatter = Scatter(grad_hidden, chunks, refs[:12])
    gather = Gather(row_items(feed_rows, all_feed, chunks), refs[12:])
    tok = grad_hidden.shape[0]
    columns = grad_qkv.shape[1]
    greet(scatter.sibling, scatter.x, scatter.y)
    kept = pltpu.make_async_copy(feed_rows, all_feed.at[scatter.me], feed_sem)
    kept.start()
    gather.start()

    def block(i, carry):
        rows = pl.ds(pl.multiple_of(scatter.owner(i) * tok, tok), tok)
        scatter.put(i, dot(grad_qkv[rows, :], weight[:, :columns], 1, 1).astype(bf16))
        scatter.progress(i)
        return carry

    lax.fori_loop(0, grad_qkv.shape[0] // tok, block, 0)
    scatter.arrived(0)
    for i in range(chunks):
        gather.relay(i)
    for j in scatter.order:
        scatter.far(j)
    gather.finish()
    for j in scatter.order:
        scatter.last(j)
    scatter.finish()
    kept.wait()


def scatter_hidden(grad_qkv, weight, feed_rows, tok, call, chunks=4):
    width, model = lax.axis_size(R), weight.shape[0]
    vmem = pl.BlockSpec(memory_space=pltpu.VMEM)
    return pl.pallas_call(
        functools.partial(hidden_kernel, chunks),
        out_shape=[
            jax.ShapeDtypeStruct((tok, model), jnp.float32),
            jax.ShapeDtypeStruct((width,) + feed_rows.shape, jnp.bfloat16),
        ],
        in_specs=[vmem, vmem, ANY],
        out_specs=[ANY, ANY],
        scratch_shapes=[DMA] + Scatter.scratch(tok, model, chunks) + Gather.scratch(chunks),
        compiler_params=pltpu.CompilerParams(
            collective_id=call, has_side_effects=True, vmem_limit_bytes=40 << 20
        ),
    )(grad_qkv, weight, feed_rows)


def enter(tokens, gains, ids, gate, up, down, piece, call, chunks=4):
    planes, rows = lax.axis_size(F), lax.axis_size(R)
    tok, model = tokens.shape
    bf16, f32 = jnp.bfloat16, jnp.float32
    depth = gate.shape[0]
    span = (-(-piece // 128) + 1) * 128
    vmem = pl.BlockSpec(memory_space=pltpu.VMEM)
    return pl.pallas_call(
        functools.partial(enter_kernel, chunks, piece),
        out_shape=[
            jax.ShapeDtypeStruct((rows, tok, model), bf16),
            jax.ShapeDtypeStruct((planes,) + gains.shape, f32),
            jax.ShapeDtypeStruct((rows,) + ids.shape, jnp.int32),
            jax.ShapeDtypeStruct((depth, 2 * planes * piece), bf16),
            jax.ShapeDtypeStruct((piece, down.shape[1]), bf16),
        ],
        in_specs=[vmem] * 3 + [ANY] * 3,
        out_specs=[ANY, vmem, vmem, vmem, ANY],
        scratch_shapes=[
            pltpu.VMEM((tok, model), bf16),
            pltpu.VMEM((2 * planes, depth, span), bf16),
            pltpu.VMEM((depth, 2 * planes * piece), f32),
            DMA((2 * planes,)),
            DMA,
            DMA,
            DMA((planes - 1,)),
            DMA((planes - 1,)),
        ]
        + Gather.scratch(chunks + 1),
        compiler_params=pltpu.CompilerParams(
            collective_id=call, has_side_effects=True, vmem_limit_bytes=60 << 20
        ),
    )(tokens, gains, ids, gate, up, down)


def project(hidden, weight, cosine, sine, cotangent, query_width, call, chunks=4):
    planes, width = lax.axis_size(F), lax.axis_size(R)
    tok, model = cotangent.shape
    bf16 = jnp.bfloat16
    vmem = pl.BlockSpec(memory_space=pltpu.VMEM)
    return pl.pallas_call(
        functools.partial(project_kernel, chunks),
        out_shape=[
            jax.ShapeDtypeStruct((width * tok, query_width), bf16),
            jax.ShapeDtypeStruct((width, planes, tok, 2 * HEAD_DIM), bf16),
            jax.ShapeDtypeStruct((width, tok, model), bf16),
            jax.ShapeDtypeStruct((model // width, model), bf16),
        ],
        in_specs=[ANY] + [vmem] * 3 + [ANY, ANY],
        out_specs=[vmem, ANY, ANY, ANY],
        scratch_shapes=[
            pltpu.VMEM((width, tok, 2 * HEAD_DIM), bf16),
            pltpu.VMEM((2, tok, model), bf16),
            DMA((2,)),
            DMA,
            DMA,
            DMA,
            DMA((width - 1,)),
            DMA((width - 1,)),
        ]
        + [DMA((planes, width // 2))] * 2
        + [DMA((planes,))] * 2
        + Gather.scratch(chunks),
        compiler_params=pltpu.CompilerParams(
            collective_id=call, has_side_effects=True, vmem_limit_bytes=40 << 20
        ),
    )(hidden, weight, cosine, sine, cotangent, weight)


def scatter_kernel(
    chunks, part, out, own, from_sib, give, got, give_far, got_far, total,
    own_sem, out_sem, to_sib, at_sib, to_near, at_near, to_far, at_far,
):
    f32, bf16 = jnp.float32, jnp.bfloat16
    me = lax.axis_index(R)
    flip = 1 - 2 * lax.rem(me, 2)
    sibling, beside_x, beside_y = me + flip, me ^ 2, me ^ 4
    rows = out.shape[0]
    size = rows // chunks
    half = chunks // 2
    owners = [me, beside_x, beside_y, me ^ 6]
    order = [c for j in range(half) for c in (j, half + j)]

    def rows_of(device, j):
        return part.at[pl.ds(pl.multiple_of(device * rows + j * size, 16), size)]

    def own_copy(d, j):
        return pltpu.make_async_copy(rows_of(owners[d], j), own.at[d, j], own_sem.at[d, j])

    def sib_copy(d, j):
        return remote(rows_of(owners[d] + flip, j), from_sib.at[d, j], (to_sib, at_sib), (d, j), sibling)

    def near_copy(j):
        device = beside_x if j < half else beside_y
        return remote(give.at[j], got.at[j], (to_near, at_near), j, device)

    def far_copy(j):
        device = beside_y if j < half else beside_x
        return remote(give_far.at[j], got_far.at[j], (to_far, at_far), j, device)

    def out_copy(j):
        return pltpu.make_async_copy(total.at[j], out.at[pl.ds(j * size, size)], out_sem.at[j])

    def summed(d, j):
        own_copy(d, j).wait()
        sib_copy(d, j).wait_recv()
        return own[d, j].astype(f32) + from_sib[d, j].astype(f32)

    for j in order:
        for d in (1, 2, 3, 0):
            own_copy(d, j).start()
    greet(sibling, beside_x, beside_y)
    for j in order:
        for d in (1, 3, 2, 0) if j < half else (2, 3, 1, 0):
            sib_copy(d, j).start()
    for j in order:
        give[j, 0] = summed(1 if j < half else 2, j).astype(bf16)
        give[j, 1] = summed(3, j).astype(bf16)
        near_copy(j).start()
    for j in order:
        passed = summed(2 if j < half else 1, j)
        kept = summed(0, j)
        near_copy(j).wait_recv()
        give_far[j] = (passed + got[j, 1].astype(f32)).astype(bf16)
        far_copy(j).start()
        total[j] = kept + got[j, 0].astype(f32)
    for j in order:
        far_copy(j).wait_recv()
        total[j] = total[j] + got_far[j].astype(f32)
        out_copy(j).start()
    for j in order:
        out_copy(j).wait()
        near_copy(j).wait_send()
        far_copy(j).wait_send()
        for d in range(4):
            sib_copy(d, j).wait_send()


def plane_gather(x, call, chunks=4):
    width = lax.axis_size(R)
    if width != 8:
        return lax.all_gather(x, R, axis=0, tiled=True)
    out = pl.pallas_call(
        functools.partial(gather_kernel, chunks),
        out_shape=jax.ShapeDtypeStruct((width,) + x.shape, x.dtype),
        in_specs=[ANY],
        out_specs=ANY,
        scratch_shapes=[DMA] + Gather.scratch(chunks),
        compiler_params=pltpu.CompilerParams(collective_id=call, has_side_effects=True),
    )(x)
    return out.reshape((width * x.shape[0],) + x.shape[1:])


def plane_scatter(x, call, chunks=4):
    width = lax.axis_size(R)
    if width != 8:
        return lax.psum_scatter(x, R, scatter_dimension=0, tiled=True).astype(jnp.float32)
    rows, columns = x.shape[0] // width, x.shape[1]
    size = rows // chunks
    bf16 = jnp.bfloat16
    return pl.pallas_call(
        functools.partial(scatter_kernel, chunks),
        out_shape=jax.ShapeDtypeStruct((rows, columns), jnp.float32),
        in_specs=[ANY],
        out_specs=ANY,
        scratch_shapes=[
            pltpu.VMEM((4, chunks, size, columns), bf16),
            pltpu.VMEM((4, chunks, size, columns), bf16),
            pltpu.VMEM((chunks, 2, size, columns), bf16),
            pltpu.VMEM((chunks, 2, size, columns), bf16),
            pltpu.VMEM((chunks, size, columns), bf16),
            pltpu.VMEM((chunks, size, columns), bf16),
            pltpu.VMEM((chunks, size, columns), jnp.float32),
            DMA((4, chunks)),
            DMA((chunks,)),
            DMA((4, chunks)),
            DMA((4, chunks)),
        ]
        + [DMA((chunks,))] * 4,
        compiler_params=pltpu.CompilerParams(
            collective_id=call, has_side_effects=True, vmem_limit_bytes=32 << 20
        ),
    )(x)


def line_gather(x):
    return lax.all_gather(x, F, axis=0, tiled=True)


def line_scatter(x):
    return lax.psum_scatter(x, F, scatter_dimension=0, tiled=True)


def heads_to_rows(block, heads):
    parts = [block[:, h * HEAD_DIM : (h + 1) * HEAD_DIM] for h in range(heads)]
    rows = jnp.concatenate(parts, axis=0)
    return jnp.concatenate([rows, jnp.zeros_like(rows)], axis=1)


def rows_to_heads(columns, heads):
    count = columns.shape[1] // heads
    return jnp.concatenate([columns[:, h * count : (h + 1) * count].T for h in range(heads)], axis=1)


def visible(block_index, starts, places):
    keys = block_index * KEY_BLOCK + lax.broadcasted_iota(jnp.int32, (KEY_BLOCK, starts.shape[1]), 0)
    return (keys >= starts) & (keys <= places)


def attention_kernel(heads, low, high, q, kv, starts, places, mixed, log_total):
    f32, bf16 = jnp.float32, jnp.bfloat16
    step = pl.program_id(0) * pl.num_programs(1) + pl.program_id(1)
    queries = heads_to_rows(q[...] * bf16(HEAD_DIM**-0.5), heads)
    first = jnp.concatenate([starts[0]] * heads, axis=1)
    place = jnp.concatenate([places[0]] * heads, axis=1)
    columns = queries.shape[0]

    def block(index, carry):
        top, total, acc = carry
        rows = kv[0, pl.ds(pl.multiple_of(index * KEY_BLOCK, KEY_BLOCK), KEY_BLOCK), :]
        scores = jnp.where(visible(index, first, place), dot(rows, queries, 1, 1), NEGATIVE)
        new_top = jnp.maximum(top, jnp.max(scores, axis=0, keepdims=True))
        weights = jnp.exp(scores - new_top)
        fade = jnp.exp(top - new_top)
        total = total * fade + jnp.sum(weights, axis=0, keepdims=True)
        acc = acc * fade + dot(rows, weights.astype(bf16), 0, 0)
        return new_top, total, acc

    top, total, acc = lax.fori_loop(
        low[step],
        high[step],
        block,
        (
            jnp.full((1, columns), NEGATIVE, f32),
            jnp.zeros((1, columns), f32),
            jnp.zeros((2 * HEAD_DIM, columns), f32),
        ),
    )
    mixed[...] = rows_to_heads(acc[HEAD_DIM:] / total, heads).astype(bf16)
    log_total[0] = top + jnp.log(total)


def attention_back_kernel(
    heads, low, high, q, kv, starts, places, grad, mixed, log_total, grad_q, grad_kv, sums
):
    f32, bf16 = jnp.float32, jnp.bfloat16
    step = pl.program_id(0) * pl.num_programs(1) + pl.program_id(1)
    queries = heads_to_rows(q[...] * bf16(HEAD_DIM**-0.5), heads)
    grads = heads_to_rows(grad[...], heads)
    first = jnp.concatenate([starts[0]] * heads, axis=1)
    place = jnp.concatenate([places[0]] * heads, axis=1)
    columns = queries.shape[0]
    products = grads.astype(f32) * heads_to_rows(mixed[...], heads).astype(f32)
    delta = lax.dot_general(
        jnp.ones((8, 2 * HEAD_DIM), f32),
        products,
        (((1,), (1,)), ((), ())),
        precision=lax.Precision.HIGHEST,
        preferred_element_type=f32,
    )[:1]
    level = log_total[0]
    upper = pltpu.roll(grads.astype(f32), HEAD_DIM, 1).astype(bf16)

    @pl.when(pl.program_id(1) == 0)
    def _():
        sums[...] = jnp.zeros_like(sums)

    def block(index, acc):
        part = pl.ds(pl.multiple_of(index * KEY_BLOCK, KEY_BLOCK), KEY_BLOCK)
        rows = kv[0, part, :]
        scores = dot(rows, queries, 1, 1)
        probs = jnp.where(visible(index, first, place), jnp.exp(scores - level), 0.0)
        grad_probs = dot(rows, upper, 1, 1)
        grad_scores = (probs * (grad_probs - delta)).astype(bf16)
        sums[part, :] += dot(grad_scores, queries) + dot(probs.astype(bf16), upper)
        return acc + dot(rows, grad_scores, 0, 0)

    acc = lax.fori_loop(low[step], high[step], block, jnp.zeros((2 * HEAD_DIM, columns), f32))
    grad_q[...] = rows_to_heads(acc[:HEAD_DIM] * HEAD_DIM**-0.5, heads)

    @pl.when(pl.program_id(1) == PARTS - 1)
    def _():
        grad_kv[0] = sums[...].astype(bf16)


def attention_call(kernel, heads, low, high, arrays, outs, scratch=()):
    blocks = {
        "tokens": lambda shape: pl.BlockSpec((QUERY_BLOCK, shape[1]), lambda s, b, *_: (s * PARTS + b, 0)),
        "row": lambda shape: pl.BlockSpec((1,) + shape[1:], lambda s, b, *_: (s * PARTS + b, 0, 0)),
        "sequence": lambda shape: pl.BlockSpec((1,) + shape[1:], lambda s, b, *_: (s, 0, 0)),
    }
    return pl.pallas_call(
        functools.partial(kernel, heads),
        grid_spec=pltpu.PrefetchScalarGridSpec(
            num_scalar_prefetch=2,
            grid=(low.shape[0] // PARTS, PARTS),
            in_specs=[blocks[kind](x.shape) for kind, x in arrays],
            out_specs=[blocks[kind](x.shape) for kind, x in outs],
            scratch_shapes=scratch,
        ),
        out_shape=[x for _, x in outs],
        compiler_params=pltpu.CompilerParams(vmem_limit_bytes=32 << 20),
    )(low, high, *[x for _, x in arrays])


def join_feed_kernel(planes, piece, x, gate, up):
    width = x.shape[0]
    for kind, out in enumerate((gate, up)):
        for p in range(planes):
            for r in range(width):
                first = (kind * planes + p) * piece
                to = (p * width + r) * piece
                out[:, to : to + piece] = x[r, :, first : first + piece].astype(jnp.float32)


def join_attention_kernel(sharers, qkv, o, query, key, value, out):
    f32 = jnp.float32
    width, qw, ow = qkv.shape[0], qkv.shape[2] - 2 * HEAD_DIM, o.shape[2]
    for r in range(width):
        query[:, r * qw : (r + 1) * qw] = qkv[r, :, :qw].astype(f32)
        out[:, r * ow : (r + 1) * ow] = o[r].astype(f32)
    for head in range(width // sharers):
        both = sum(qkv[head * sharers + i, :, qw:].astype(f32) for i in range(sharers))
        to = slice(head * HEAD_DIM, (head + 1) * HEAD_DIM)
        key[:, to] = both[:, :HEAD_DIM]
        value[:, to] = both[:, HEAD_DIM:]


def widen_kernel(x, out):
    out[...] = x[0].astype(jnp.float32)


def widen(x):
    count, rows, columns = x.shape
    return pl.pallas_call(
        widen_kernel,
        grid=(count,),
        in_specs=[pl.BlockSpec((1, rows, columns), lambda i: (i, 0, 0))],
        out_specs=pl.BlockSpec((rows, columns), lambda i: (i, 0)),
        out_shape=jax.ShapeDtypeStruct((count * rows, columns), jnp.float32),
        compiler_params=pltpu.CompilerParams(vmem_limit_bytes=60 << 20),
    )(x)


def join_call(kernel, arrays, outs, block=64):
    rows = arrays[0].shape[1]
    return pl.pallas_call(
        kernel,
        grid=(rows // block,),
        in_specs=[pl.BlockSpec((x.shape[0], block, x.shape[2]), lambda i: (0, i, 0)) for x in arrays],
        out_specs=[pl.BlockSpec((block, columns), lambda i: (i, 0)) for columns in outs],
        out_shape=[jax.ShapeDtypeStruct((rows, columns), jnp.float32) for columns in outs],
        compiler_params=pltpu.CompilerParams(vmem_limit_bytes=32 << 20),
    )(*arrays)


def per_device(
    tokens,
    segment_ids,
    attention_gain,
    query_weight,
    key_weight,
    value_weight,
    output_weight,
    feed_gain,
    gate_weight,
    up_weight,
    down_weight,
    cotangent,
):
    f32, bf16 = jnp.float32, jnp.bfloat16
    planes, width = lax.axis_size(F), lax.axis_size(R)
    r, z = lax.axis_index(R), lax.axis_index(F)
    tok, model = tokens.shape
    length = segment_ids.shape[1]
    all_tok = width * tok
    plane_kernels = width == 8
    heads = HEADS // width
    group = HEADS // KV_HEADS
    qw = heads * HEAD_DIM
    kv = (r * heads) // group
    feed = gate_weight.shape[1]
    piece = feed // (width * planes)
    hidden_units = piece * planes

    def cols(weight, first, count):
        return lax.dynamic_slice_in_dim(weight, first, count, 1)

    def feed_cols(weight):
        return [cols(weight, p * (feed // planes) + r * piece, piece) for p in range(planes)]

    w_attention = line_gather(
        jnp.concatenate(
            [
                cols(query_weight, r * qw, qw),
                cols(key_weight, kv * HEAD_DIM, HEAD_DIM),
                cols(value_weight, kv * HEAD_DIM, HEAD_DIM),
                cols(output_weight, r * (model // width), model // width),
            ],
            axis=1,
        )
    )
    w_qkv = w_attention[:, : qw + 2 * HEAD_DIM]
    own_gains = jnp.stack([attention_gain, feed_gain]).astype(f32)
    tok_float = tokens.astype(f32)
    scale_in = inverse_rms(tok_float)
    normed_in = tok_float * scale_in
    if plane_kernels:
        hidden_in, gains, ids, feed_cut, down_cut = enter(
            tokens,
            jnp.pad(own_gains, ((0, 6), (0, 0))),
            segment_ids.reshape(8, length // 8),
            gate_weight,
            up_weight,
            down_weight,
            piece,
            0,
        )
        hidden_in = hidden_in.reshape(all_tok, model)
        gains = gains[:, :2].transpose(1, 0, 2).reshape(2, model)
        ids = ids.reshape(width, length)
    else:
        gains = lax.all_gather(own_gains, F, axis=1, tiled=True)
        hidden_in = lax.all_gather((normed_in * gains[0]).astype(bf16), R, axis=0, tiled=True)
        ids = lax.all_gather(segment_ids, R, axis=0, tiled=True)
        feed_cut = jnp.concatenate(feed_cols(gate_weight) + feed_cols(up_weight), axis=1)
        down_cut = lax.dynamic_slice_in_dim(down_weight, r * piece, piece, 0)
    gain_in, gain_mid = gains[0], gains[1]
    w_feed, w_down = line_gather(feed_cut), line_gather(down_cut)

    own_ids = lax.dynamic_slice_in_dim(ids, z * tok, tok, 1)
    own_starts = jnp.sum(ids[:, None, :] < own_ids[:, :, None], axis=2, dtype=jnp.int32).reshape(all_tok)
    own_places = z * tok + jnp.arange(all_tok, dtype=jnp.int32) % tok
    own_positions = own_places - own_starts
    steps = all_tok // QUERY_BLOCK
    starts = own_starts.reshape(steps, 1, QUERY_BLOCK)
    query_places = own_places.reshape(steps, 1, QUERY_BLOCK)
    low = starts[:, 0, 0] // KEY_BLOCK
    high = query_places[:, 0, QUERY_BLOCK - 1] // KEY_BLOCK + 1

    if plane_kernels:
        wide_cosine, wide_sine = rope_tables(own_positions, 4)
        wide_sine = wide_sine * jnp.where(jnp.arange(2 * HEAD_DIM) // (HEAD_DIM // 2) % 2, 1.0, -1.0)
        query, kv_rows, cot_all, w_out = project(
            hidden_in.reshape(width, tok, model),
            w_attention,
            wide_cosine,
            wide_sine,
            cotangent,
            qw,
            3,
        )
        kv_rows = kv_rows.reshape(width, length, 2 * HEAD_DIM)
        cot_all = cot_all.reshape(all_tok, model)
    else:
        cosine, sine = rope_tables(own_positions)
        qkv = dot(hidden_in, w_qkv)
        query = rotate(qkv[:, :qw].reshape(all_tok, heads, HEAD_DIM), cosine, sine, 1.0)
        query = query.astype(bf16).reshape(all_tok, qw)
        key = rotate(qkv[:, None, qw : qw + HEAD_DIM], cosine, sine, 1.0).astype(bf16)[:, 0]
        value = qkv[:, qw + HEAD_DIM :].astype(bf16)
        kv_rows = (
            lax.all_gather(jnp.concatenate([key, value], axis=1), F, axis=0, tiled=False)
            .reshape(planes, width, tok, 2 * HEAD_DIM)
            .transpose(1, 0, 2, 3)
            .reshape(width, length, 2 * HEAD_DIM)
        )
        cot_all = lax.all_gather(cotangent, R, axis=0, tiled=True)
        w_out = lax.all_to_all(
            w_attention[:, qw + 2 * HEAD_DIM :], R, split_axis=0, concat_axis=1, tiled=True
        )
    common = [("tokens", query), ("sequence", kv_rows), ("row", starts), ("row", query_places)]
    mixed, log_totals = attention_call(
        attention_kernel,
        heads,
        low,
        high,
        common,
        [
            ("tokens", jax.ShapeDtypeStruct((all_tok, qw), bf16)),
            ("row", jax.ShapeDtypeStruct((steps, 1, heads * QUERY_BLOCK), f32)),
        ],
    )
    if plane_kernels:
        cot_blocks = cot_all.reshape(width, tok, model)
        middle = branch_layer(mixed, w_out, tokens, 1)
        hidden_blocks, acts, down_part = middle_layer(middle, gain_mid[None], w_feed, cot_blocks, 2)
    else:
        middle = tok_float + plane_scatter(dot(mixed, w_out).astype(bf16), 1)

    if plane_kernels:
        out_part, grad_hidden_mid, feed_part = feed_forward(
            hidden_blocks, cot_blocks, acts, w_feed, w_down, 5
        )
    else:
        w_gate, w_up = w_feed[:, :hidden_units], w_feed[:, hidden_units:]
        scale_mid = inverse_rms(middle)
        normed_mid = middle * scale_mid
        hidden_mid = plane_gather((normed_mid * gain_mid).astype(bf16), 2)
        gate_acc = dot(hidden_mid, w_gate)
        up_acc = dot(hidden_mid, w_up)
        gate_sig = jax.nn.sigmoid(gate_acc)
        gate_silu = gate_acc * gate_sig
        inner_act = (gate_silu * up_acc).astype(bf16)
        out_part = dot(inner_act, w_down).astype(bf16)
        grad_inner = dot(cot_all, w_down, 1, 1)
        grad_gate = grad_inner * up_acc * gate_sig * (1.0 + gate_acc * (1.0 - gate_sig))
        grad_gate = grad_gate.astype(bf16)
        grad_up = (grad_inner * gate_silu).astype(bf16)
        feed_part = jnp.concatenate(
            [dot(hidden_mid, grad_gate, 0, 0), dot(hidden_mid, grad_up, 0, 0)], axis=1
        ).astype(bf16)
        down_part = dot(inner_act, cot_all, 0, 0).astype(bf16)
        grad_hidden_part = dot(grad_gate, w_gate, 1, 1) + dot(grad_up, w_up, 1, 1)
        grad_hidden_mid = plane_scatter(grad_hidden_part.astype(bf16), 5)
        feed_out = plane_scatter(out_part, 4)
    down_rows = line_scatter(down_part)
    feed_rows = line_scatter(feed_part)
    if plane_kernels:
        grad_mixed, w_out_part, grad_middle, gain_mid_term = gradient_layer(
            grad_hidden_mid, middle, cotangent, gain_mid[None], w_out, mixed, 6
        )
        gain_mid_term = gain_mid_term[0]
    else:
        gain_mid_term = jnp.sum(grad_hidden_mid * normed_mid, axis=0)
        grad_normed_mid = grad_hidden_mid * gain_mid
        inner = jnp.mean(grad_normed_mid * normed_mid, axis=1, keepdims=True)
        grad_middle = cotangent.astype(f32) + scale_mid * (grad_normed_mid - normed_mid * inner)
        grad_branch = plane_gather(grad_middle.astype(bf16), 6)
        grad_mixed = dot(grad_branch, w_out, 1, 1).astype(bf16)
        w_out_part = dot(mixed, grad_branch, 0, 0).astype(bf16)

    if plane_kernels:
        grad_qkv, qkv_part, feed_out, down_all, w_out_part = attention_back(
            heads,
            query,
            kv_rows,
            starts,
            query_places,
            grad_mixed,
            mixed,
            log_totals,
            wide_cosine,
            wide_sine,
            hidden_in,
            out_part,
            down_rows,
            w_out_part,
            10,
        )
        w_out_part = w_out_part.reshape(width * qw, model // width)
    else:
        gq, gkv = attention_call(
            attention_back_kernel,
            heads,
            low,
            high,
            common + [("tokens", grad_mixed), ("tokens", mixed), ("row", log_totals)],
            [
                ("tokens", jax.ShapeDtypeStruct((all_tok, qw), f32)),
                ("sequence", jax.ShapeDtypeStruct((width, length, 2 * HEAD_DIM), bf16)),
            ],
            [pltpu.VMEM((length, 2 * HEAD_DIM), f32)],
        )
        gkv = gkv.reshape(width, planes, tok, 2 * HEAD_DIM).transpose(1, 0, 2, 3)
        gkv = line_scatter(gkv.reshape(planes * all_tok, 2 * HEAD_DIM)).astype(f32)
        gq = rotate(gq.reshape(all_tok, heads, HEAD_DIM), cosine, sine, -1.0)
        gk = rotate(gkv[:, None, :HEAD_DIM], cosine, sine, -1.0)[:, 0]
        grad_qkv = jnp.concatenate([gq.reshape(all_tok, qw), gk, gkv[:, HEAD_DIM:]], axis=1)
        grad_qkv = grad_qkv.astype(bf16)
        qkv_part = dot(hidden_in, grad_qkv, 0, 0).astype(bf16)
        down_all = lax.all_gather(down_rows, R, axis=0, tiled=True)
        w_out_part = lax.all_to_all(w_out_part, R, split_axis=1, concat_axis=0, tiled=True)
    out_rows = line_scatter(w_out_part)
    activations = (middle + feed_out).astype(bf16)
    grad_qkv, qkv_part, feed_rows = lax.optimization_barrier((grad_qkv, qkv_part, feed_rows))
    qkv_rows = line_scatter(qkv_part)
    if plane_kernels:
        grad_hidden_in, feed_all = scatter_hidden(grad_qkv, w_attention, feed_rows, tok, 7)
    else:
        grad_hidden_in = plane_scatter(dot(grad_qkv, w_qkv, 1, 1).astype(bf16), 7)
        feed_all = lax.all_gather(feed_rows, R, axis=0, tiled=False)
    gain_in_term = jnp.sum(grad_hidden_in * normed_in, axis=0)
    grad_normed_in = grad_hidden_in * gain_in
    input_grad = (
        grad_middle
        + scale_in
        * (
            grad_normed_in
            - normed_in * jnp.mean(grad_normed_in * normed_in, axis=1, keepdims=True)
        )
    ).astype(bf16)

    rows = model // planes
    terms = jnp.stack([gain_in_term, gain_mid_term])
    if plane_kernels:
        terms = jnp.pad(terms.reshape(2, planes, rows).transpose(1, 0, 2), ((0, 0), (0, 6), (0, 0)))
        qkv_all, out_all, gain_terms = finish(qkv_rows, out_rows, terms, 9)
    else:
        qkv_all = lax.all_gather(qkv_rows, R, axis=0, tiled=False)
        out_all = lax.all_gather(out_rows, R, axis=0, tiled=False)
        gain_terms = lax.psum(lax.psum_scatter(terms, F, scatter_dimension=1, tiled=True), R)
    if plane_kernels:
        down_grad = widen(down_all)
    else:
        down_grad = down_all.reshape(feed // planes, model).astype(f32)
    gate_grad, up_grad = join_call(
        functools.partial(join_feed_kernel, planes, piece), [feed_all], [feed, feed]
    )
    query_grad, key_grad, value_grad, out_grad = join_call(
        functools.partial(join_attention_kernel, width // KV_HEADS),
        [qkv_all, out_all],
        [width * qw, KV_HEADS * HEAD_DIM, KV_HEADS * HEAD_DIM, model],
    )
    return (
        activations,
        input_grad,
        gain_terms[0],
        query_grad,
        key_grad,
        value_grad,
        out_grad,
        gain_terms[1],
        gate_grad,
        up_grad,
        down_grad,
    )


def solution(mesh):
    tok = P((R, F), None)
    row = P(F, None)
    in_specs = (tok, P(R, None), P(F), row, row, row, row, P(F), row, row, row, tok)
    out_specs = (tok, tok, P(F), row, row, row, row, P(F), row, row, row)
    return jax.shard_map(
        per_device, mesh=mesh, in_specs=in_specs, out_specs=out_specs, check_vma=False
    )
```
